32 devices in a mesh: row: 4 (over y, core), gz: 2 (over x), vert: 4 (over z).
Axes of the slice: x: 2, y: 2, z: 4, core: 2. Of those that a mesh axis runs over, the one named last changes fastest.
Arguments:
- distribution: float32 [32, 32, 110592], P('row', 'gz', 'vert'), may hold values from 0 to 10, as said below
- z_order: int32 [48], P('vert'), may hold values from 0 to 47, as said below
- edge_codes: int32 [2, 4], P(None, 'row'), may hold values from 0 to 2, as said below
Outputs:
- new_distribution: float32 [32, 32, 110592], P('row', 'gz', 'vert')
- macroscopic: float32 [8, 32, 32], P(None, 'row', 'gz')
- boundary_flux: float32 [2, 32], P('gz', 'row')
The draws below stay inside these ranges and needn't reach their ends.
Inputs may be any that keep to these rules, and one draw needn't show every extreme that they name: `z_order`: a permutation of 0 to 47. `edge_codes`: row 0 holds 0 (diffuse wall) or 1 (evaporating film), row 1 holds 0 (diffuse wall) or 2 (outflow); the first column's bottom is film and the last column's top is outflow. `distribution`: every entry is positive.
All inputs are finite; a program needn't handle non-finite values.
Results may differ from the reference program's by a relative error of at most 0.0003.
Values sent between devices are 32-bit elements; how exact they have to be, the bound alone decides.
No kernel may reach another device: no remote copies, remote signals or barrier semaphores. Data moves between devices by JAX's collectives and lax.ppermute only.
A program may use at most 256 MiB of HBM per device.

```python
import math
import jax
import jax.numpy as jnp
import numpy as np
from jax import lax

NODES = 8
NVR = 48
NVT = 48
NVZ = 48
STEPS = 2
NER = 4
OUTWARD_COUNT = 32
LENGTHWISE_COUNT = 32
NV = 110592


SPEED_LIMIT = 5.0


def axial_order(key):
    return jax.random.permutation(jax.random.fold_in(key, 11), NVZ).astype(jnp.int32)


def draw_z_order(key, part):
    return axial_order(key)


def draw_edge_codes(key, part):
    bottom = jax.random.randint(jax.random.fold_in(key, 21), (NER,), 0, 2).astype(jnp.int32)
    bottom = bottom.at[0].set(1)
    top_codes = 2 * jax.random.randint(jax.random.fold_in(key, 22), (NER,), 0, 2).astype(jnp.int32)
    top_codes = top_codes.at[NER - 1].set(2)
    return jnp.stack([bottom, top_codes]).astype(jnp.int32)


def uniform_grid(point_count):
    return -SPEED_LIMIT + (jnp.arange(point_count, dtype=jnp.float32) + 0.5) * (2.0 * SPEED_LIMIT / point_count)


def draw_distribution(key, part):
    slot_order = axial_order(key)
    grid_z = uniform_grid(NVZ)
    z_speeds = jnp.sum(jnp.where(slot_order[:, None] == jnp.arange(NVZ)[None, :], grid_z[None, :], 0.0), 1)
    grid_r = uniform_grid(NVR)
    grid_t = uniform_grid(NVT)
    particle_concentration = jnp.exp(jax.random.uniform(jax.random.fold_in(key, 31), (OUTWARD_COUNT, LENGTHWISE_COUNT), jnp.float32, math.log(0.5), math.log(2.0)))
    vapour_warmth = jax.random.uniform(jax.random.fold_in(key, 32), (OUTWARD_COUNT, LENGTHWISE_COUNT), jnp.float32, 0.7, 1.4)
    drift_speed = jax.random.uniform(jax.random.fold_in(key, 33), (3, OUTWARD_COUNT, LENGTHWISE_COUNT), jnp.float32, -0.3, 0.3)
    jitter_scaling = jnp.clip(0.12 * jax.random.normal(jax.random.fold_in(key, 34), (OUTWARD_COUNT, LENGTHWISE_COUNT, NVZ, NVR, NVT), jnp.float32), -0.3, 0.3)
    conduction_strength = jax.random.uniform(jax.random.fold_in(key, 35), (3, OUTWARD_COUNT, LENGTHWISE_COUNT), jnp.float32, 0.15, 0.35)
    conduction_unit_heading = (2 * jax.random.randint(jax.random.fold_in(key, 36), (3, OUTWARD_COUNT, LENGTHWISE_COUNT), 0, 2) - 1).astype(jnp.float32)
    conduction_components = conduction_strength * conduction_unit_heading * (particle_concentration * vapour_warmth ** 1.5)[None]
    fivefold_warmth = vapour_warmth[:, :, None, None, None]
    fivefold_crowding = particle_concentration[:, :, None, None, None]
    pec_z = z_speeds[None, None, :, None, None] - drift_speed[2][:, :, None, None, None]
    pec_r = grid_r[None, None, None, :, None] - drift_speed[0][:, :, None, None, None]
    pec_t = grid_t[None, None, None, None, :] - drift_speed[1][:, :, None, None, None]
    thermal_norm_local = pec_r * pec_r + pec_t * pec_t + pec_z * pec_z
    projected_conduction = pec_r * conduction_components[0][:, :, None, None, None] + pec_t * conduction_components[1][:, :, None, None, None] + pec_z * conduction_components[2][:, :, None, None, None]
    conduction_coefficient = jnp.clip(1.0 + projected_conduction * (thermal_norm_local / fivefold_warmth - 5.0) / (5.0 * fivefold_crowding * fivefold_warmth ** 2), 0.05, 6.0)
    field_entries = fivefold_crowding * fivefold_warmth ** (-1.5) * jnp.exp(-thermal_norm_local / (2 * fivefold_warmth)) * conduction_coefficient * (1.0 + jitter_scaling)
    return field_entries.reshape(OUTWARD_COUNT, LENGTHWISE_COUNT, NVZ * NVR * NVT).astype(jnp.float32)


def setup_inputs(seed: int = 0) -> dict:
    splits = jax.random.split(jax.random.key(seed), 4)
    distribution = draw_distribution(jax.random.fold_in(splits[3], 71), 0)
    z_order = draw_z_order(jax.random.fold_in(splits[3], 71), 0)
    edge_codes = draw_edge_codes(jax.random.fold_in(splits[3], 71), 0)
    return {"distribution": distribution, "z_order": z_order, "edge_codes": edge_codes}


ELEMENT_WIDTH = 4.0
TIME_STEP = 1e-3
KNUDSEN = 0.005
VISCOUS_RATIO = 2.0 / 3.0
SAT_DENSITY = 1.5
SPEED_LIMIT = 5.0
HIGHEST_PRECISION = lax.Precision.HIGHEST


def legendre_pair(position, point_count):
    previous = 1.0
    current = position
    for degree in range(2, point_count + 1):
        previous, current = current, ((2 * degree - 1) * position * current - (degree - 1) * previous) / degree
    slope = point_count * (position * current - previous) / (position * position - 1.0)
    return current, slope


def dg_tables(point_count):
    point_list = []
    weight_list = []
    for number in range(point_count):
        position = math.cos(math.pi * (number + 0.75) / (point_count + 0.5))
        for sweep in range(60):
            value, slope = legendre_pair(position, point_count)
            position = position - value / slope
        value, slope = legendre_pair(position, point_count)
        point_list.append(position)
        weight_list.append(2.0 / ((1.0 - position * position) * slope * slope))
    point_list = point_list[::-1]
    weight_list = weight_list[::-1]
    products = []
    for row_number in range(point_count):
        product_value = 1.0
        for other in range(point_count):
            if other != row_number:
                product_value = product_value * (point_list[row_number] - point_list[other])
        products.append(product_value)
    derivative_rows = []
    for row_number in range(point_count):
        entries = []
        for column in range(point_count):
            if column == row_number:
                total_value = 0.0
                for other in range(point_count):
                    if other != row_number:
                        total_value = total_value + 1.0 / (point_list[row_number] - point_list[other])
                entries.append(total_value)
            else:
                entries.append(products[row_number] / products[column] / (point_list[row_number] - point_list[column]))
        derivative_rows.append(entries)
    right_list = []
    left_list = []
    for column in range(point_count):
        right_value = 1.0
        left_value = 1.0
        for other in range(point_count):
            if other != column:
                right_value = right_value * (1.0 - point_list[other])
                left_value = left_value * (-1.0 - point_list[other])
        right_list.append(right_value / products[column])
        left_list.append(left_value / products[column])
    points = np.array(point_list)
    quad_weights = np.array(weight_list)
    derivative = np.array(derivative_rows)
    end_right = np.array(right_list)
    end_left = np.array(left_list)
    return (points, jnp.asarray(derivative, jnp.float32), jnp.asarray(end_right / quad_weights, jnp.float32),
            jnp.asarray(end_left / quad_weights, jnp.float32), jnp.asarray(end_right, jnp.float32),
            jnp.asarray(end_left, jnp.float32))


def speed_grid(point_count):
    return -SPEED_LIMIT + (np.arange(point_count) + 0.5) * (2.0 * SPEED_LIMIT / point_count)


def velocity_constants():
    weight = (2 * SPEED_LIMIT / NVR) * (2 * SPEED_LIMIT / NVT) * (2 * SPEED_LIMIT / NVZ) / (2 * math.pi) ** 1.5
    grid_r = speed_grid(NVR)
    grid_t = speed_grid(NVT)
    grid_z = speed_grid(NVZ)
    half_flux = weight * np.sum(np.exp(-grid_r ** 2 / 2)) * np.sum(np.exp(-grid_t ** 2 / 2)) * np.sum(
        np.maximum(grid_z, 0.0) * np.exp(-grid_z ** 2 / 2))
    return float(weight), float(half_flux), grid_r, grid_t, grid_z


def shift_velocity(field_entries, offset, keep_mask):
    padding = jnp.zeros(field_entries.shape[:-1] + (abs(offset),), field_entries.dtype)
    if offset > 0:
        shifted = jnp.concatenate([field_entries[..., offset:], padding], -1)
    else:
        shifted = jnp.concatenate([padding, field_entries[..., :offset]], -1)
    return jnp.where(keep_mask, shifted, 0.0)


def rotation_term(field_entries, vel_r, vel_t, radius, a_index, b_index):
    step_r = 2 * SPEED_LIMIT / NVR
    step_t = 2 * SPEED_LIMIT / NVT
    grad_r = (shift_velocity(field_entries, NVT, a_index < NVR - 1) - shift_velocity(field_entries, -NVT, a_index > 0)) / (2 * step_r)
    grad_t = (shift_velocity(field_entries, 1, b_index < NVT - 1) - shift_velocity(field_entries, -1, b_index > 0)) / (2 * step_t)
    return (vel_t * vel_t * grad_r - vel_r * vel_t * grad_t) / radius


def shakhov_term(field_entries, vel_r, vel_t, vel_z, fluid_observables):
    particle_concentration, drift_outward, drift_around, drift_lengthwise, vapour_warmth, conduction_outward, conduction_around, conduction_lengthwise = fluid_observables
    peculiar_r = vel_r - drift_outward
    peculiar_t = vel_t - drift_around
    peculiar_z = vel_z - drift_lengthwise
    thermal_norm_square = peculiar_r ** 2 + peculiar_t ** 2 + peculiar_z ** 2
    projected_conduction = peculiar_r * conduction_outward + peculiar_t * conduction_around + peculiar_z * conduction_lengthwise
    gaussian_resting_state = particle_concentration * vapour_warmth ** -1.5 * jnp.exp(-thermal_norm_square / (2 * vapour_warmth))
    collision_goal_state = gaussian_resting_state * (1.0 + (1.0 - VISCOUS_RATIO) * projected_conduction / (5.0 * particle_concentration * vapour_warmth ** 2) * (thermal_norm_square / vapour_warmth - 5.0))
    return particle_concentration / KNUDSEN * (collision_goal_state - field_entries)


def reference_moments(slabs, z_speeds, vel_r, vel_t, weight, end_right, end_left):
    def first_pass(integral_sums_table, slab_item):
        plane_slab, z_speed = slab_item
        bottom = jnp.einsum('j,rjp->rp', end_left, plane_slab[:, :NODES], precision=HIGHEST_PRECISION)
        top_trace = jnp.einsum('j,rjp->rp', end_right, plane_slab[:, LENGTHWISE_COUNT - NODES:], precision=HIGHEST_PRECISION)
        speed_sq = vel_r ** 2 + vel_t ** 2 + z_speed ** 2
        plain = jnp.sum(plane_slab, -1)
        return (integral_sums_table[0] + weight * plain,
                integral_sums_table[1] + weight * jnp.sum(plane_slab * vel_r, -1),
                integral_sums_table[2] + weight * jnp.sum(plane_slab * vel_t, -1),
                integral_sums_table[3] + weight * z_speed * plain,
                integral_sums_table[4] + 0.5 * weight * jnp.sum(plane_slab * speed_sq, -1),
                integral_sums_table[5] + weight * jnp.maximum(-z_speed, 0.0) * jnp.sum(bottom, -1),
                integral_sums_table[6] + weight * jnp.maximum(z_speed, 0.0) * jnp.sum(top_trace, -1),
                integral_sums_table[7] + weight * jnp.maximum(-z_speed, 0.0) * jnp.sum(top_trace, -1)), None

    node_zeros = jnp.zeros((OUTWARD_COUNT, LENGTHWISE_COUNT), jnp.float32)
    edge_zeros = jnp.zeros((OUTWARD_COUNT,), jnp.float32)
    start = (node_zeros,) * 5 + (edge_zeros,) * 3
    integral_sums_table, _ = lax.scan(first_pass, start, (slabs, z_speeds))
    particle_concentration = integral_sums_table[0]
    drift_outward = integral_sums_table[1] / particle_concentration
    drift_around = integral_sums_table[2] / particle_concentration
    drift_lengthwise = integral_sums_table[3] / particle_concentration
    vapour_warmth = (2.0 * integral_sums_table[4] / particle_concentration - (drift_outward ** 2 + drift_around ** 2 + drift_lengthwise ** 2)) / 3.0

    def second_pass(heat_totals, slab_item):
        plane_slab, z_speed = slab_item
        peculiar_r = vel_r - drift_outward[:, :, None]
        peculiar_t = vel_t - drift_around[:, :, None]
        peculiar_z = z_speed - drift_lengthwise[:, :, None]
        weighted = plane_slab * (peculiar_r ** 2 + peculiar_t ** 2 + peculiar_z ** 2)
        return (heat_totals[0] + 0.5 * weight * jnp.sum(weighted * peculiar_r, -1),
                heat_totals[1] + 0.5 * weight * jnp.sum(weighted * peculiar_t, -1),
                heat_totals[2] + 0.5 * weight * jnp.sum(weighted * peculiar_z, -1)), None

    conduction_integral, _ = lax.scan(second_pass, (node_zeros,) * 3, (slabs, z_speeds))
    fluid_observables = (particle_concentration, drift_outward, drift_around, drift_lengthwise, vapour_warmth, conduction_integral[0], conduction_integral[1], conduction_integral[2])
    return fluid_observables, (integral_sums_table[5], integral_sums_table[6], integral_sums_table[7])


def reference(distribution, z_order, edge_codes):
    points, derivative, lift_right, lift_left, end_right, end_left = dg_tables(NODES)
    weight, half_flux, grid_r, grid_t, grid_z = velocity_constants()
    plane_size = NVR * NVT
    vel_r = jnp.asarray(np.repeat(grid_r, NVT), jnp.float32)
    vel_t = jnp.asarray(np.tile(grid_t, NVR), jnp.float32)
    plane_index = jnp.arange(plane_size, dtype=jnp.int32)
    a_index = plane_index // NVT
    b_index = plane_index % NVT
    z_speeds = jnp.asarray(grid_z, jnp.float32)[z_order]
    elements = OUTWARD_COUNT // NODES
    columns = LENGTHWISE_COUNT // NODES
    radius = ((jnp.arange(elements, dtype=jnp.float32)[:, None] + (1.0 + jnp.asarray(points, jnp.float32))[None, :] / 2)
              * ELEMENT_WIDTH).reshape(OUTWARD_COUNT)
    code_bottom = jnp.repeat(edge_codes[0], NODES)
    code_top = jnp.repeat(edge_codes[1], NODES)
    slabs = distribution.reshape(OUTWARD_COUNT, LENGTHWISE_COUNT, NVZ, plane_size).transpose(2, 0, 1, 3)

    for step_index in range(STEPS):
        fluid_observables, edge_sums = reference_moments(slabs, z_speeds, vel_r, vel_t, weight, end_right, end_left)
        bottom_density = jnp.where(code_bottom == 1, SAT_DENSITY, edge_sums[0] / half_flux)
        top_density = edge_sums[1] / half_flux
        node_stats = tuple(entry[:, :, None] for entry in fluid_observables)

        def advance_slab(slab_item):
            plane_slab, z_speed = slab_item
            maxwell_wall = jnp.exp(-(vel_r ** 2 + vel_t ** 2 + z_speed ** 2) / 2)
            grouped = plane_slab.reshape(elements, NODES, LENGTHWISE_COUNT, plane_size)
            volume = jnp.einsum('ij,ejzp->eizp', derivative, grouped, precision=HIGHEST_PRECISION)
            trace_hi = jnp.einsum('j,ejzp->ezp', end_right, grouped, precision=HIGHEST_PRECISION)
            trace_lo = jnp.einsum('j,ejzp->ezp', end_left, grouped, precision=HIGHEST_PRECISION)
            mirror = trace_lo[0].reshape(LENGTHWISE_COUNT, NVR, NVT)[:, ::-1, :].reshape(LENGTHWISE_COUNT, plane_size)
            plus_side = jnp.concatenate([mirror[None], trace_hi], 0)
            minus_side = jnp.concatenate([trace_lo, trace_hi[-1:]], 0)
            face_values = jnp.where(vel_r > 0, plus_side, minus_side)
            radial = (2.0 / ELEMENT_WIDTH) * vel_r * (volume
                                                      + lift_right[None, :, None, None] * (face_values[1:] - trace_hi)[:, None]
                                                      - lift_left[None, :, None, None] * (face_values[:-1] - trace_lo)[:, None])
            radial = radial.reshape(OUTWARD_COUNT, LENGTHWISE_COUNT, plane_size)
            grouped = plane_slab.reshape(OUTWARD_COUNT, columns, NODES, plane_size)
            volume = jnp.einsum('ij,rejp->reip', derivative, grouped, precision=HIGHEST_PRECISION)
            trace_hi = jnp.einsum('j,rejp->rep', end_right, grouped, precision=HIGHEST_PRECISION)
            trace_lo = jnp.einsum('j,rejp->rep', end_left, grouped, precision=HIGHEST_PRECISION)
            bottom_ghost = bottom_density[:, None] * maxwell_wall
            top_ghost = jnp.where(code_top[:, None] == 2, trace_hi[:, -1], top_density[:, None] * maxwell_wall)
            plus_side = jnp.concatenate([bottom_ghost[:, None], trace_hi], 1)
            minus_side = jnp.concatenate([trace_lo, top_ghost[:, None]], 1)
            face_values = jnp.where(z_speed > 0, plus_side, minus_side)
            axial_term = (2.0 / ELEMENT_WIDTH) * z_speed * (volume
                                                            + lift_right[None, None, :, None] * (face_values[:, 1:] - trace_hi)[:, :, None]
                                                            - lift_left[None, None, :, None] * (face_values[:, :-1] - trace_lo)[:, :, None])
            axial_term = axial_term.reshape(OUTWARD_COUNT, LENGTHWISE_COUNT, plane_size)
            rotation = rotation_term(plane_slab, vel_r, vel_t, radius[:, None, None], a_index, b_index)
            collide = shakhov_term(plane_slab, vel_r, vel_t, z_speed, node_stats)
            return plane_slab + TIME_STEP * (collide - radial - axial_term - rotation)

        slabs = lax.map(advance_slab, (slabs, z_speeds))

    fluid_observables, edge_sums = reference_moments(slabs, z_speeds, vel_r, vel_t, weight, end_right, end_left)
    macroscopic = jnp.stack(fluid_observables)
    bottom_row = jnp.where(code_bottom == 1, SAT_DENSITY * half_flux - edge_sums[0], 0.0)
    top_row = jnp.where(code_top == 2, edge_sums[1] - edge_sums[2], 0.0)
    boundary_flux = jnp.stack([bottom_row, top_row])
    new_distribution = slabs.transpose(1, 2, 0, 3).reshape(OUTWARD_COUNT, LENGTHWISE_COUNT, NV)
    return new_distribution, macroscopic, boundary_flux
```

```python
import math

import jax
import jax.numpy as jnp
import ml_dtypes
import numpy as np
from jax import lax
from jax.experimental import pallas as pl
from jax.experimental.pallas import tpu as pltpu
from jax.sharding import PartitionSpec as P

NODES = 8
NVR = 48
NVT = 48
NVZ = 48
STEPS = 2

ELEMENT_WIDTH = 4.0
TIME_STEP = 0.001
KNUDSEN = 0.005
VISCOUS_RATIO = 2.0 / 3.0
SAT_DENSITY = 1.5
SPEED_LIMIT = 5.0

PLANE = NVR * NVT
HALF = PLANE // 2
LOCAL_Z = 2 * NODES
NODE_COUNT = NODES * LOCAL_Z
TILE = 256
WINDOW = 512
GHOST_ROWS = 32
MOMENTS = 16
F32 = jnp.float32
BF16 = jnp.bfloat16
PIECES = [(t, TILE, 0) for t in range(0, 1024, TILE)] + [(1024, 128, 0), (1152, 128, 1)] + [
    (t, TILE, 1) for t in range(1280, PLANE, TILE)
]


def legendre_pair(position, point_count):
    previous = 1.0
    current = position
    for degree in range(2, point_count + 1):
        previous, current = (
            current,
            ((2 * degree - 1) * position * current - (degree - 1) * previous) / degree,
        )
    slope = point_count * (position * current - previous) / (position * position - 1.0)
    return (current, slope)


def dg_tables(point_count):
    point_list = []
    weight_list = []
    for number in range(point_count):
        position = math.cos(math.pi * (number + 0.75) / (point_count + 0.5))
        for sweep in range(60):
            value, slope = legendre_pair(position, point_count)
            position = position - value / slope
        value, slope = legendre_pair(position, point_count)
        point_list.append(position)
        weight_list.append(2.0 / ((1.0 - position * position) * slope * slope))
    point_list = point_list[::-1]
    weight_list = weight_list[::-1]
    points = np.array(point_list)
    derivative = np.zeros((point_count, point_count))
    right = np.zeros(point_count)
    left = np.zeros(point_count)
    products = [
        np.prod([points[i] - points[j] for j in range(point_count) if j != i])
        for i in range(point_count)
    ]
    for i in range(point_count):
        others = [j for j in range(point_count) if j != i]
        derivative[i, i] = sum(1.0 / (points[i] - points[j]) for j in others)
        for j in others:
            derivative[i, j] = products[i] / products[j] / (points[i] - points[j])
        right[i] = np.prod([1.0 - points[j] for j in others]) / products[i]
        left[i] = np.prod([-1.0 - points[j] for j in others]) / products[i]
    return points, np.array(weight_list), derivative, right, left


def speed_grid(point_count):
    return -SPEED_LIMIT + (np.arange(point_count) + 0.5) * (2.0 * SPEED_LIMIT / point_count)


POINTS, QUAD, DERIV, END_R, END_L = dg_tables(NODES)
LIFT_R = END_R / QUAD
LIFT_L = END_L / QUAD
GRID_R = speed_grid(NVR)
GRID_T = speed_grid(NVT)
GRID_Z = speed_grid(NVZ)
STEP_V = 2 * SPEED_LIMIT / NVR
WEIGHT = STEP_V**3 / (2 * math.pi) ** 1.5
HALF_FLUX = float(
    WEIGHT
    * np.sum(np.exp(-(GRID_R**2) / 2))
    * np.sum(np.exp(-(GRID_T**2) / 2))
    * np.sum(np.maximum(GRID_Z, 0.0) * np.exp(-(GRID_Z**2) / 2))
)
SCALE = TIME_STEP * 2.0 / ELEMENT_WIDTH


def transport_tables():
    ident = np.eye(NODES)
    up = DERIV + np.outer(LIFT_L, END_L)
    down = DERIV - np.outer(LIFT_R, END_R)
    zero = np.zeros((NODES, NODES))
    wide = np.eye(LOCAL_Z)
    radial = np.stack([np.kron(down, wide), np.kron(up, wide), np.kron(DERIV, wide)])
    zup = np.block([[up, zero], [-np.outer(LIFT_L, END_R), up]])
    zdown = np.block([[down, np.outer(LIFT_R, END_L)], [zero, down]])
    zout = np.block([[down, np.outer(LIFT_R, END_L)], [zero, DERIV]])
    axial = np.stack([np.kron(ident, zdown), np.kron(ident, zup), np.kron(ident, zout)])
    ghost_r = np.zeros((2, NODE_COUNT, 128))
    ghost_z = np.zeros((2, NODE_COUNT, 128))
    for r in range(NODES):
        for z in range(LOCAL_Z):
            n = r * LOCAL_Z + z
            ghost_r[0, n, z] = -LIFT_R[r]
            ghost_r[1, n, z] = LIFT_L[r]
            if z >= NODES:
                ghost_z[0, n, LOCAL_Z + r] = LIFT_R[z - NODES]
            else:
                ghost_z[1, n, LOCAL_Z + r] = LIFT_L[z]
    trace = np.zeros((2, 2, GHOST_ROWS, NODE_COUNT))
    for side in range(2):
        radial_row = END_R if side == 1 else END_L
        for place in range(2):
            for z in range(LOCAL_Z):
                for r in range(NODES):
                    trace[side, place, z, r * LOCAL_Z + z] = radial_row[r]
            for r in range(NODES):
                for k in range(NODES):
                    if place == 0:
                        trace[side, place, LOCAL_Z + r, r * LOCAL_Z + NODES + k] = END_R[k]
                    else:
                        trace[side, place, LOCAL_Z + r, r * LOCAL_Z + k] = END_L[k]
    return (
        (-SCALE * radial).astype(ml_dtypes.bfloat16),
        (-SCALE * axial).astype(np.float32),
        (SCALE * ghost_r).astype(np.float32),
        (SCALE * ghost_z).astype(np.float32),
        trace.astype(ml_dtypes.bfloat16),
    )


def rotation_table():
    full = np.zeros((PLANE + 2 * TILE, PLANE))
    factor = TIME_STEP / (2 * STEP_V)
    for a in range(NVR):
        for b in range(NVT):
            n = a * NVT + b
            first = factor * GRID_T[b] * GRID_T[b]
            second = factor * GRID_R[a] * GRID_T[b]
            if a + 1 < NVR:
                full[TILE + n + NVT, n] = -first
            if a > 0:
                full[TILE + n - NVT, n] = first
            if b + 1 < NVT:
                full[TILE + n + 1, n] = second
            if b > 0:
                full[TILE + n - 1, n] = -second
    tiles = [full[TILE + t - 128 : TILE + t - 128 + WINDOW, t : t + TILE] for t in range(0, PLANE, TILE)]
    return np.stack(tiles).astype(ml_dtypes.bfloat16)


def mirror_table():
    table = np.zeros((HALF, HALF))
    groups = NVR // 2
    for g in range(groups):
        for b in range(NVT):
            table[(groups - 1 - g) * NVT + b, g * NVT + b] = 1.0
    return table.astype(ml_dtypes.bfloat16)


def plane_rows():
    vr = np.repeat(GRID_R, NVT)
    vt = np.tile(GRID_T, NVR)
    rows = np.zeros((8, PLANE))
    rows[0] = vr
    rows[1] = vt
    rows[2] = np.exp(-(vr**2 + vt**2) / 2)
    return rows.astype(np.float32)


def edge_table():
    table = np.zeros((2, NODE_COUNT, 128))
    for r in range(NODES):
        for k in range(NODES):
            table[0, r * LOCAL_Z + k, r] = END_L[k]
            table[1, r * LOCAL_Z + NODES + k, r] = END_R[k]
    return table.astype(np.float32)


def node_columns():
    table = np.zeros((NODE_COUNT, 128))
    for r in range(NODES):
        table[r * LOCAL_Z : (r + 1) * LOCAL_Z, :] = (1.0 + POINTS[r]) / 2
    return table.astype(np.float32)


RADIAL_M, AXIAL_M, GHOST_R, GHOST_Z, TRACE_M = transport_tables()
ROTATION_M = rotation_table()
MIRROR_M = mirror_table()
ROWS = plane_rows()
EDGE = edge_table()
NODE_POS = node_columns()


def slot_speed(ints, slot):
    return (ints[slot].astype(F32) + 0.5) * (2 * SPEED_LIMIT / NVZ) - SPEED_LIMIT


def macroscopic_of(m):
    rho = m(0)
    inv = 1.0 / rho
    ur, ut, uz = m(1) * inv, m(2) * inv, m(3) * inv
    rr, tt, rt, zz, rz, tz = (m(k) for k in range(4, 10))
    energy = rr + tt + zz
    speed = ur * ur + ut * ut + uz * uz
    temp = (energy * inv - speed) * (1.0 / 3.0)
    tail = 2.0 * rho * speed - energy
    qr = 0.5 * (m(10) - 2.0 * (ur * rr + ut * rt + uz * rz) + ur * tail)
    qt = 0.5 * (m(11) - 2.0 * (ur * rt + ut * tt + uz * tz) + ut * tail)
    qz = 0.5 * (m(12) - 2.0 * (ur * rz + ut * tz + uz * zz) + uz * tail)
    return rho, ur, ut, uz, temp, qr, qt, qz


def add_speed_sums(field, vz, sums):
    one = field * vz
    two = one * vz
    return [
        sums[0] + field,
        sums[1] + one,
        sums[2] + two,
        sums[3] + two * vz,
        sums[4] + field * jnp.abs(vz),
    ]


def finish_moments(sums_ref, rows_ref, table_ref, out_ref):
    lane = lax.broadcasted_iota(jnp.int32, (LOCAL_Z, 128), 1)

    def one_radius(r, carry):
        acc = [jnp.zeros((LOCAL_Z, 128), F32) for _ in range(14)]
        for j in range(PLANE // 128):
            at = pl.ds(j * 128, 128)
            vr = rows_ref[0:1, at]
            vt = rows_ref[1:2, at]
            g0, g1, g2, g3, g4 = (sums_ref[k, r, :, at] for k in range(5))
            a = vr * g0
            b = vt * g0
            aa = vr * a
            bb = vt * b
            c = vr * g1
            d = vt * g1
            perp = aa + bb + g2
            new = [g0, a, b, g1, aa, bb, vr * b, g2, c, d, vr * perp, vt * perp, vr * c + vt * d + g3, g4]
            acc = [x + y for x, y in zip(acc, new)]
        block = jnp.zeros((LOCAL_Z, 128), F32)
        for k in range(14):
            block = jnp.where(lane == k, WEIGHT * jnp.sum(acc[k], axis=1, keepdims=True), block)
        table_ref[pl.ds(pl.multiple_of(r * LOCAL_Z, LOCAL_Z), LOCAL_Z), :] = block
        return carry

    lax.fori_loop(0, NODES, one_radius, 0)
    out_ref[...] = jnp.transpose(table_ref[...])[0:MOMENTS, :]


def send_traces(slot_count, ints, narrow_ref, trace_ref, mirror_ref, right_ref, left_ref, turned_ref, axial_ref, info):
    place = ints[info + 1]
    for s in range(slot_count):
        for first, lanes, side in PIECES:
            got = jnp.dot(
                trace_ref[side, place],
                narrow_ref[s, :, first : first + lanes],
                preferred_element_type=F32,
            )
            if side == 1:
                right_ref[s, :, first - HALF : first - HALF + lanes] = got[0:LOCAL_Z]
            else:
                left_ref[s, :, first : first + lanes] = got[0:LOCAL_Z]
            axial_ref[s, :, first : first + lanes] = got[LOCAL_Z : LOCAL_Z + NODES]

    at_axis = ints[info] == 0

    @pl.when(at_axis)
    def _():
        flat = left_ref[...].reshape(slot_count * LOCAL_Z, HALF).astype(BF16)
        for first in range(0, HALF, 128):
            low = max(0, (HALF - first - 128 - 48) // 128 * 128)
            high = min(HALF, -((first - HALF - 48) // 128) * 128)
            got = jnp.dot(
                flat[:, low:high], mirror_ref[low:high, first : first + 128], preferred_element_type=F32
            )
            turned_ref[:, :, first : first + 128] = got.reshape(slot_count, LOCAL_Z, 128)

    @pl.when(jnp.logical_not(at_axis))
    def _():
        turned_ref[...] = jnp.zeros(turned_ref.shape, F32)


def first_kernel(
    slot_count, info, ints, f_ref, rows_ref, trace_ref, mirror_ref,
    right_ref, left_ref, turned_ref, axial_ref, mom_ref, sums_ref, narrow_ref, table_ref,
):
    step = pl.program_id(0)

    @pl.when(step == 0)
    def _():
        sums_ref[...] = jnp.zeros(sums_ref.shape, F32)

    speeds = [slot_speed(ints, step * slot_count + s) for s in range(slot_count)]

    def one_radius(r, carry):
        for j in range(PLANE // 128):
            at = pl.ds(j * 128, 128)
            sums = [sums_ref[k, r, :, at] for k in range(5)]
            for s in range(slot_count):
                field = f_ref[r, :, pl.ds(s * PLANE + j * 128, 128)]
                sums = add_speed_sums(field, speeds[s], sums)
                narrow_ref[s, pl.ds(pl.multiple_of(r * LOCAL_Z, LOCAL_Z), LOCAL_Z), at] = field.astype(BF16)
            for k in range(5):
                sums_ref[k, r, :, at] = sums[k]
        return carry

    lax.fori_loop(0, NODES, one_radius, 0)
    send_traces(
        slot_count, ints, narrow_ref, trace_ref, mirror_ref, right_ref, left_ref, turned_ref, axial_ref, info
    )

    @pl.when(step == pl.num_programs(0) - 1)
    def _():
        finish_moments(sums_ref, rows_ref, table_ref, mom_ref)


def total_of(parts):
    while len(parts) > 1:
        parts = [parts[k] + parts[k + 1] for k in range(0, len(parts), 2)]
    return parts[0]


def step_kernel(slot_count, info, part_count, last, ints, *refs):
    part_refs, refs = refs[:part_count], refs[part_count:]
    (
        f_ref, in_left_ref, in_turned_ref, in_right_ref, in_axial_ref,
        rows_ref, pos_ref, edge_ref, radial_ref, axial_m_ref, ghost_r_ref, ghost_z_ref, rot_ref,
    ) = refs[:13]
    refs = refs[13:]
    if last:
        (out_ref, mom_ref), refs = refs[:2], refs[2:]
    else:
        (trace_ref, mirror_ref), refs = refs[:2], refs[2:]
        (out_ref, right_ref, left_ref, turned_ref, axial_ref, mom_ref), refs = refs[:6], refs[6:]
    (
        plane_ref, node_ref, wall_ref, slot_ref, sums_ref, work_ref, pad_ref, lhs_ref, ghost_ref, narrow_ref, table_ref,
    ) = refs
    step = pl.program_id(0)
    row = ints[info]
    place = ints[info + 1]
    code_bottom = ints[info + 2]
    code_top = ints[info + 3]
    last_row = ints[info + 4]

    @pl.when(step == 0)
    def _():
        sums_ref[...] = jnp.zeros(sums_ref.shape, F32)
        pad_ref[:, 0:128] = jnp.zeros((NODE_COUNT, 128), BF16)
        pad_ref[:, 128 + PLANE :] = jnp.zeros((NODE_COUNT, 128), BF16)
        total = total_of([p[...] for p in part_refs])
        wide = jnp.concatenate([total, jnp.zeros((128 - MOMENTS, 128), F32)], axis=0)
        table_ref[...] = jnp.transpose(wide)
        rho, ur, ut, uz, temp, qr, qt, qz = macroscopic_of(lambda k: table_ref[:, k : k + 1])
        inv_t = 1.0 / temp
        beta = ((1.0 - VISCOUS_RATIO) / 5.0) / (rho * temp * temp)
        kappa = rho * (TIME_STEP / KNUDSEN)
        peak = kappa * rho * inv_t * jnp.sqrt(inv_t)
        columns = [uz, -0.5 * inv_t, qz * beta, inv_t, peak, 1.0 - kappa, ur, ut, qr * beta, qt * beta]
        for k, column in enumerate(columns):
            node_ref[k] = jnp.broadcast_to(column, (NODE_COUNT, 128))
        radius = ELEMENT_WIDTH * (row.astype(F32) + pos_ref[...])
        node_ref[10] = 1.0 / radius
        net = table_ref[:, 3:4]
        gross = table_ref[:, 13:14]
        to_bottom = 0.5 * (gross - net)
        to_top = 0.5 * (gross + net)
        incident = jnp.sum(edge_ref[0] * to_bottom, axis=0, keepdims=True)
        upward = jnp.sum(edge_ref[1] * to_top, axis=0, keepdims=True)
        bottom = jnp.where(code_bottom == 1, SAT_DENSITY, incident * (1.0 / HALF_FLUX))
        top = jnp.where(code_top == 2, 0.0, upward * (1.0 / HALF_FLUX))
        density = jnp.where(place == 0, bottom, top)
        square = jnp.transpose(jnp.broadcast_to(density, (128, 128)))
        wall_ref[...] = square[0:NODES, :]

        def one_radius(r, carry):
            rows = pl.ds(pl.multiple_of(r * LOCAL_Z, LOCAL_Z), LOCAL_Z)
            n_half, n_inv = node_ref[1, rows, :], node_ref[3, rows, :]
            n_ur, n_ut = node_ref[6, rows, :], node_ref[7, rows, :]
            n_qr, n_qt = node_ref[8, rows, :], node_ref[9, rows, :]
            for j in range(PLANE // 128):
                at = pl.ds(j * 128, 128)
                cr = rows_ref[0:1, at] - n_ur
                ct = rows_ref[1:2, at] - n_ut
                square = cr * cr + ct * ct
                gauss = jnp.exp(square * n_half)
                along = cr * n_qr + ct * n_qt
                reach = square * n_inv - 5.0
                plane_ref[0, rows, at] = gauss
                plane_ref[1, rows, at] = gauss * along
                plane_ref[2, rows, at] = gauss * reach
                plane_ref[3, rows, at] = gauss * along * reach
            return carry

        lax.fori_loop(0, NODES, one_radius, 0)

    speeds = [slot_speed(ints, step * slot_count + s) for s in range(slot_count)]
    kind_minus = jnp.where(row == last_row, 2, 0)
    kind_out = jnp.where(jnp.logical_and(place == 1, code_top == 2), 2, 0)

    for s in range(slot_count):
        vz = speeds[s]
        positive = vz > 0
        cz = vz - node_ref[0]
        lam = node_ref[4] * jnp.exp(cz * cz * node_ref[1])
        alpha = cz * node_ref[2]
        reach = cz * cz * node_ref[3]
        slot_ref[s, 0] = lam * (1.0 + alpha * reach)
        slot_ref[s, 1] = lam * reach
        slot_ref[s, 2] = lam * alpha
        slot_ref[s, 3] = lam

        sign = jnp.where(positive, 1, 0)
        kind = jnp.where(positive, 1, kind_out)
        lhs_ref[0] = (vz * axial_m_ref[kind]).astype(BF16)
        lean = jnp.abs(vz) * ghost_z_ref[sign]
        lhs_ref[1] = (ghost_r_ref[0] + lean).astype(BF16)
        lhs_ref[2] = (ghost_r_ref[1] + lean).astype(BF16)

        own = (place == 0) == positive
        strength = jnp.exp(-0.5 * vz * vz + jnp.zeros((NODES, 128), F32)) * wall_ref[...]
        for j in range(PLANE // 128):
            at = pl.ds(j * 128, 128)
            vr = rows_ref[0:1, at]
            if j * 128 < HALF:
                radial = in_right_ref[s, :, at]
            else:
                back = pl.ds(j * 128 - HALF, 128)
                radial = in_left_ref[s, :, back] + in_turned_ref[s, :, back]
            wall = strength * rows_ref[2:3, at]
            axial = jnp.where(own, wall, in_axial_ref[s, :, at])
            rows = jnp.concatenate([vr * radial, axial, jnp.zeros((8, 128), F32)], axis=0)
            ghost_ref[:, at] = rows.astype(BF16)

        inverse = node_ref[10]
        for j in range(PLANE // 128):
            at = pl.ds(s * PLANE + j * 128, 128)
            field = f_ref[:, :, at].reshape(NODE_COUNT, 128)
            pad_ref[:, 128 + j * 128 : 256 + j * 128] = (field * inverse).astype(BF16)

        lane = lax.broadcasted_iota(jnp.int32, (NODE_COUNT, 128), 1)
        for first, lanes, side in PIECES:
            tile = first // TILE
            inside = first - tile * TILE
            field = f_ref[:, :, s * PLANE + first : s * PLANE + first + lanes].reshape(NODE_COUNT, lanes)
            narrow = field.astype(BF16)
            moved = (field * rows_ref[0:1, first : first + lanes]).astype(BF16)
            start = tile * TILE
            edge = jnp.where(lane < GHOST_ROWS, lhs_ref[1 + side], pad_ref[:, start : start + 128])
            left = jnp.concatenate(
                [radial_ref[1] if side else radial_ref[kind_minus], lhs_ref[0], edge, pad_ref[:, start + 128 : start + WINDOW]],
                axis=1,
            )
            right = jnp.concatenate(
                [
                    moved,
                    narrow,
                    ghost_ref[:, first : first + lanes],
                    rot_ref[tile, GHOST_ROWS:, inside : inside + lanes],
                ],
                axis=0,
            )
            work_ref[s, :, first : first + lanes] = jnp.dot(left, right, preferred_element_type=F32)

    def update(r, carry):
        rows = pl.ds(pl.multiple_of(r * LOCAL_Z, LOCAL_Z), LOCAL_Z)
        keep = node_ref[5, rows, :]
        factor = [[slot_ref[s, k, rows, :] for k in range(4)] for s in range(slot_count)]
        for j in range(PLANE // 128):
            at = pl.ds(j * 128, 128)
            planes = [plane_ref[k, rows, at] for k in range(4)]
            sums = [sums_ref[k, r, :, at] for k in range(5)]
            for s in range(slot_count):
                here = pl.ds(s * PLANE + j * 128, 128)
                new = f_ref[r, :, here] * keep + work_ref[s, rows, at]
                for k in range(4):
                    new = new + planes[k] * factor[s][k]
                out_ref[r, :, here] = new
                sums = add_speed_sums(new, speeds[s], sums)
                if not last:
                    narrow_ref[s, rows, at] = new.astype(BF16)
            for k in range(5):
                sums_ref[k, r, :, at] = sums[k]
        return carry

    lax.fori_loop(0, NODES, update, 0)
    if not last:
        send_traces(
            slot_count, ints, narrow_ref, trace_ref, mirror_ref, right_ref, left_ref, turned_ref, axial_ref, info
        )

    @pl.when(step == pl.num_programs(0) - 1)
    def _():
        finish_moments(sums_ref, rows_ref, table_ref, mom_ref)


def last_kernel(info, part_count, ints, *refs):
    total_ref = total_of([p[...] for p in refs[:part_count]])
    edge_ref, macro_ref, flux_ref = refs[part_count:]
    values = macroscopic_of(lambda k: total_ref[k : k + 1, :])
    for k in range(8):
        macro_ref[k : k + 1, :] = values[k]
    net, gross = total_ref[3:4, :], total_ref[13:14, :]
    to_bottom = jnp.broadcast_to(0.5 * (gross - net), (8, 128))
    to_top = jnp.broadcast_to(0.5 * (gross + net), (8, 128))
    dot = lambda x, y: jnp.dot(x, y, precision=lax.Precision.HIGHEST, preferred_element_type=F32)
    incident = dot(to_bottom, edge_ref[0])
    upward = dot(to_top, edge_ref[1])
    downward = dot(to_bottom, edge_ref[1])
    bottom = jnp.where(ints[info + 2] == 1, SAT_DENSITY * HALF_FLUX - incident, 0.0)
    top = jnp.where(ints[info + 3] == 2, upward - downward, 0.0)
    flux_ref[...] = jnp.where(ints[info + 1] == 0, bottom, top)


def whole(shape):
    return pl.BlockSpec(shape, lambda *a: (0,) * len(shape), pipeline_mode=pl.Buffered(1))


def on_device(distribution, z_order, edge_codes):
    local_r, local_z, vdev = distribution.shape
    assert local_r == NODES and local_z == LOCAL_Z
    slots = vdev // PLANE
    group = math.gcd(slots, 3)
    steps = slots // group
    rows_total = lax.axis_size("row")
    places = lax.axis_size("gz")
    verts = lax.axis_size("vert")
    assert places == 2
    info = slots
    ints = jnp.concatenate(
        [
            z_order,
            jnp.stack(
                [
                    lax.axis_index("row"),
                    lax.axis_index("gz"),
                    edge_codes[0, 0],
                    edge_codes[1, 0],
                    jnp.int32(rows_total - 1),
                ]
            ),
        ]
    )
    rows, pos, edge = jnp.asarray(ROWS), jnp.asarray(NODE_POS), jnp.asarray(EDGE)
    radial_m, axial_m = jnp.asarray(RADIAL_M), jnp.asarray(AXIAL_M)
    ghost_r, ghost_z = jnp.asarray(GHOST_R), jnp.asarray(GHOST_Z)
    trace_m, mirror_m, rot_m = jnp.asarray(TRACE_M), jnp.asarray(MIRROR_M), jnp.asarray(ROTATION_M)

    big = pl.BlockSpec((NODES, LOCAL_Z, group * PLANE), lambda i, n: (0, 0, i))
    radial_spec = pl.BlockSpec((group, LOCAL_Z, HALF), lambda i, n: (i, 0, 0))
    axial_spec = pl.BlockSpec((group, NODES, PLANE), lambda i, n: (i, 0, 0))
    mom_spec = whole((MOMENTS, 128))
    radial_shape = jax.ShapeDtypeStruct((slots, LOCAL_Z, HALF), F32)
    axial_shape = jax.ShapeDtypeStruct((slots, NODES, PLANE), F32)
    mom_shape = jax.ShapeDtypeStruct((MOMENTS, 128), F32)
    big_shape = jax.ShapeDtypeStruct(distribution.shape, F32)
    trace_specs = [radial_spec, radial_spec, radial_spec, axial_spec, mom_spec]
    trace_shapes = [radial_shape, radial_shape, radial_shape, axial_shape, mom_shape]
    sums_scratch = pltpu.VMEM((5, NODES, LOCAL_Z, PLANE), F32)
    narrow_scratch = pltpu.VMEM((group, NODE_COUNT, PLANE), BF16)
    table_scratch = pltpu.VMEM((NODE_COUNT, 128), F32)
    params = pltpu.CompilerParams(vmem_limit_bytes=56 * 1024 * 1024)

    def start(f):
        return pl.pallas_call(
            lambda *a: first_kernel(group, info, *a),
            grid_spec=pltpu.PrefetchScalarGridSpec(
                num_scalar_prefetch=1,
                grid=(steps,),
                in_specs=[big] + [whole(x.shape) for x in (rows, trace_m, mirror_m)],
                out_specs=trace_specs,
                scratch_shapes=[sums_scratch, narrow_scratch, table_scratch],
            ),
            out_shape=trace_shapes,
            compiler_params=params,
            name="moments_and_traces",
        )(ints, f, rows, trace_m, mirror_m)

    def advance(f, parts, left, turned, right, axial, last):
        tables = [rows, pos, edge, radial_m, axial_m, ghost_r, ghost_z, rot_m]
        if not last:
            tables += [trace_m, mirror_m]
        return pl.pallas_call(
            lambda *a: step_kernel(group, info, len(parts), last, *a),
            grid_spec=pltpu.PrefetchScalarGridSpec(
                num_scalar_prefetch=1,
                grid=(steps,),
                in_specs=[mom_spec] * len(parts)
                + [big, radial_spec, radial_spec, radial_spec, axial_spec]
                + [whole(x.shape) for x in tables],
                out_specs=[big] + ([mom_spec] if last else trace_specs),
                scratch_shapes=[
                    pltpu.VMEM((4, NODE_COUNT, PLANE), F32),
                    pltpu.VMEM((11, NODE_COUNT, 128), F32),
                    pltpu.VMEM((NODES, 128), F32),
                    pltpu.VMEM((group, 4, NODE_COUNT, 128), F32),
                    sums_scratch,
                    pltpu.VMEM((group, NODE_COUNT, PLANE), F32),
                    pltpu.VMEM((NODE_COUNT, PLANE + 256), BF16),
                    pltpu.VMEM((3, NODE_COUNT, 128), BF16),
                    pltpu.VMEM((GHOST_ROWS, PLANE), BF16),
                    narrow_scratch,
                    table_scratch,
                ],
            ),
            out_shape=[big_shape] + ([mom_shape] if last else trace_shapes),
            compiler_params=params,
            name="last_step" if last else "step",
        )(ints, *parts, f, left, turned, right, axial, *tables)

    def spread(moments):
        parts = [moments]
        for shift in range(1, verts):
            parts.append(lax.ppermute(moments, "vert", [(i, i ^ shift) for i in range(verts)]))
        return parts

    def halo(right, left, axial):
        from_left = lax.ppermute(right, "row", [(i, i + 1) for i in range(rows_total - 1)])
        from_right = lax.ppermute(left, "row", [(i + 1, i) for i in range(rows_total - 1)])
        from_axial = lax.ppermute(axial, "gz", [(0, 1), (1, 0)])
        return from_left, from_right, from_axial

    right, left, turned, axial, moments = start(distribution)
    current = distribution
    for number in range(STEPS):
        from_left, from_right, from_axial = halo(right, left, axial)
        parts = spread(moments)
        last = number == STEPS - 1
        out = advance(current, parts, from_left, turned, from_right, from_axial, last)
        if last:
            current, moments = out
        else:
            current, right, left, turned, axial, moments = out
    parts = spread(moments)
    macro, flux = pl.pallas_call(
        lambda *a: last_kernel(info, len(parts), *a),
        grid_spec=pltpu.PrefetchScalarGridSpec(
            num_scalar_prefetch=1,
            grid=(1,),
            in_specs=[mom_spec] * len(parts) + [whole(edge.shape)],
            out_specs=[whole((8, 128)), whole((8, 128))],
        ),
        out_shape=[jax.ShapeDtypeStruct((8, 128), F32), jax.ShapeDtypeStruct((8, 128), F32)],
        name="macroscopic",
    )(ints, *parts, edge)
    return (current, macro.reshape(8, local_r, local_z), flux[0:1, 0:local_r])


def solution(mesh):
    in_specs = (P("row", "gz", "vert"), P("vert"), P(None, "row"))
    out_specs = (P("row", "gz", "vert"), P(None, "row", "gz"), P("gz", "row"))
    return jax.shard_map(
        on_device, mesh=mesh, in_specs=in_specs, out_specs=out_specs, check_vma=False
    )
```

```python
import math

import jax
import jax.numpy as jnp
import ml_dtypes
import numpy as np
from jax import lax
from jax.experimental import pallas as pl
from jax.experimental.pallas import tpu as pltpu
from jax.sharding import PartitionSpec as P

NODES = 8
NVR = 48
NVT = 48
NVZ = 48
STEPS = 2

ELEMENT_WIDTH = 4.0
TIME_STEP = 0.001
KNUDSEN = 0.005
VISCOUS_RATIO = 2.0 / 3.0
SAT_DENSITY = 1.5
SPEED_LIMIT = 5.0

PLANE = NVR * NVT
HALF = PLANE // 2
LOCAL_Z = 2 * NODES
NODE_COUNT = NODES * LOCAL_Z
TILE = 256
WINDOW = 512
GHOST_ROWS = 32
MOMENTS = 16
PARTS_W = 3
F32 = jnp.float32
BF16 = jnp.bfloat16
PIECES = [(t, TILE, 0) for t in range(0, 1024, TILE)] + [(1024, 128, 0), (1152, 128, 1)] + [
    (t, TILE, 1) for t in range(1280, PLANE, TILE)
]


def legendre_pair(position, point_count):
    previous = 1.0
    current = position
    for degree in range(2, point_count + 1):
        previous, current = (
            current,
            ((2 * degree - 1) * position * current - (degree - 1) * previous) / degree,
        )
    slope = point_count * (position * current - previous) / (position * position - 1.0)
    return (current, slope)


def dg_tables(point_count):
    point_list = []
    weight_list = []
    for number in range(point_count):
        position = math.cos(math.pi * (number + 0.75) / (point_count + 0.5))
        for sweep in range(60):
            value, slope = legendre_pair(position, point_count)
            position = position - value / slope
        value, slope = legendre_pair(position, point_count)
        point_list.append(position)
        weight_list.append(2.0 / ((1.0 - position * position) * slope * slope))
    point_list = point_list[::-1]
    weight_list = weight_list[::-1]
    points = np.array(point_list)
    derivative = np.zeros((point_count, point_count))
    right = np.zeros(point_count)
    left = np.zeros(point_count)
    products = [
        np.prod([points[i] - points[j] for j in range(point_count) if j != i])
        for i in range(point_count)
    ]
    for i in range(point_count):
        others = [j for j in range(point_count) if j != i]
        derivative[i, i] = sum(1.0 / (points[i] - points[j]) for j in others)
        for j in others:
            derivative[i, j] = products[i] / products[j] / (points[i] - points[j])
        right[i] = np.prod([1.0 - points[j] for j in others]) / products[i]
        left[i] = np.prod([-1.0 - points[j] for j in others]) / products[i]
    return points, np.array(weight_list), derivative, right, left


def speed_grid(point_count):
    return -SPEED_LIMIT + (np.arange(point_count) + 0.5) * (2.0 * SPEED_LIMIT / point_count)


POINTS, QUAD, DERIV, END_R, END_L = dg_tables(NODES)
LIFT_R = END_R / QUAD
LIFT_L = END_L / QUAD
GRID_R = speed_grid(NVR)
GRID_T = speed_grid(NVT)
GRID_Z = speed_grid(NVZ)
STEP_V = 2 * SPEED_LIMIT / NVR
WEIGHT = STEP_V**3 / (2 * math.pi) ** 1.5
HALF_FLUX = float(
    WEIGHT
    * np.sum(np.exp(-(GRID_R**2) / 2))
    * np.sum(np.exp(-(GRID_T**2) / 2))
    * np.sum(np.maximum(GRID_Z, 0.0) * np.exp(-(GRID_Z**2) / 2))
)
SCALE = TIME_STEP * 2.0 / ELEMENT_WIDTH


def transport_tables():
    ident = np.eye(NODES)
    up = DERIV + np.outer(LIFT_L, END_L)
    down = DERIV - np.outer(LIFT_R, END_R)
    zero = np.zeros((NODES, NODES))
    wide = np.eye(LOCAL_Z)
    radial = np.stack([np.kron(down, wide), np.kron(up, wide), np.kron(DERIV, wide)])
    zup = np.block([[up, zero], [-np.outer(LIFT_L, END_R), up]])
    zdown = np.block([[down, np.outer(LIFT_R, END_L)], [zero, down]])
    zout = np.block([[down, np.outer(LIFT_R, END_L)], [zero, DERIV]])
    axial = np.stack([np.kron(ident, zdown), np.kron(ident, zup), np.kron(ident, zout)])
    ghost_r = np.zeros((2, NODE_COUNT, 128))
    ghost_z = np.zeros((2, NODE_COUNT, 128))
    for r in range(NODES):
        for z in range(LOCAL_Z):
            n = r * LOCAL_Z + z
            ghost_r[0, n, z] = -LIFT_R[r]
            ghost_r[1, n, z] = LIFT_L[r]
            if z >= NODES:
                ghost_z[0, n, LOCAL_Z + r] = LIFT_R[z - NODES]
            else:
                ghost_z[1, n, LOCAL_Z + r] = LIFT_L[z]
    trace = np.zeros((2, 2, GHOST_ROWS, NODE_COUNT))
    for side in range(2):
        radial_row = END_R if side == 1 else END_L
        for place in range(2):
            for z in range(LOCAL_Z):
                for r in range(NODES):
                    trace[side, place, z, r * LOCAL_Z + z] = radial_row[r]
            for r in range(NODES):
                for k in range(NODES):
                    if place == 0:
                        trace[side, place, LOCAL_Z + r, r * LOCAL_Z + NODES + k] = END_R[k]
                    else:
                        trace[side, place, LOCAL_Z + r, r * LOCAL_Z + k] = END_L[k]
    return (
        (-SCALE * radial).astype(ml_dtypes.bfloat16),
        (-SCALE * axial).astype(np.float32),
        (SCALE * ghost_r).astype(np.float32),
        (SCALE * ghost_z).astype(np.float32),
        trace.astype(ml_dtypes.bfloat16),
    )


def rotation_table():
    full = np.zeros((PLANE + 2 * TILE, PLANE))
    factor = TIME_STEP / (2 * STEP_V)
    for a in range(NVR):
        for b in range(NVT):
            n = a * NVT + b
            first = factor * GRID_T[b] * GRID_T[b]
            second = factor * GRID_R[a] * GRID_T[b]
            if a + 1 < NVR:
                full[TILE + n + NVT, n] = -first
            if a > 0:
                full[TILE + n - NVT, n] = first
            if b + 1 < NVT:
                full[TILE + n + 1, n] = second
            if b > 0:
                full[TILE + n - 1, n] = -second
    tiles = [full[TILE + t - 128 : TILE + t - 128 + WINDOW, t : t + TILE] for t in range(0, PLANE, TILE)]
    return np.stack(tiles).astype(ml_dtypes.bfloat16)


def mirror_table():
    table = np.zeros((HALF, HALF))
    groups = NVR // 2
    for g in range(groups):
        for b in range(NVT):
            table[(groups - 1 - g) * NVT + b, g * NVT + b] = 1.0
    return table.astype(ml_dtypes.bfloat16)


def plane_rows():
    vr = np.repeat(GRID_R, NVT)
    vt = np.tile(GRID_T, NVR)
    rows = np.zeros((8, PLANE))
    rows[0] = vr
    rows[1] = vt
    rows[2] = np.exp(-(vr**2 + vt**2) / 2)
    return rows.astype(np.float32)


def weight_table():
    vr = np.repeat(GRID_R, NVT)
    vt = np.tile(GRID_T, NVR)
    square = vr**2 + vt**2
    columns = [np.ones(PLANE), vr, vt, vr**2, vt**2, vr * vt, vr * square, vt * square]
    table = np.zeros((PLANE, 128))
    for k, column in enumerate(columns):
        rest = column.copy()
        for part in range(PARTS_W):
            piece = rest.astype(ml_dtypes.bfloat16).astype(np.float64)
            table[:, k + 8 * part] = piece
            rest = rest - piece
    return table.astype(ml_dtypes.bfloat16)


def edge_table():
    table = np.zeros((2, NODE_COUNT, 128))
    for r in range(NODES):
        for k in range(NODES):
            table[0, r * LOCAL_Z + k, r] = END_L[k]
            table[1, r * LOCAL_Z + NODES + k, r] = END_R[k]
    return table.astype(np.float32)


def node_columns():
    table = np.zeros((NODE_COUNT, 128))
    for r in range(NODES):
        table[r * LOCAL_Z : (r + 1) * LOCAL_Z, :] = (1.0 + POINTS[r]) / 2
    return table.astype(np.float32)


RADIAL_M, AXIAL_M, GHOST_R, GHOST_Z, TRACE_M = transport_tables()
ROTATION_M = rotation_table()
MIRROR_M = mirror_table()
ROWS = plane_rows()
WEIGHT_M = weight_table()
EDGE = edge_table()
NODE_POS = node_columns()


def slot_speed(order, slot):
    return (order[slot].astype(F32) + 0.5) * (2 * SPEED_LIMIT / NVZ) - SPEED_LIMIT


def dot(x, y):
    return jnp.dot(x, y, preferred_element_type=F32)


def split(x):
    high = x.astype(BF16)
    return high, (x - high.astype(F32)).astype(BF16)


def macroscopic_of(m):
    rho = m(0)
    inv = 1.0 / rho
    ur, ut, uz = m(1) * inv, m(2) * inv, m(3) * inv
    rr, tt, rt, zz, rz, tz = (m(k) for k in range(4, 10))
    energy = rr + tt + zz
    speed = ur * ur + ut * ut + uz * uz
    temp = (energy * inv - speed) * (1.0 / 3.0)
    tail = 2.0 * rho * speed - energy
    qr = 0.5 * (m(10) - 2.0 * (ur * rr + ut * rt + uz * rz) + ur * tail)
    qt = 0.5 * (m(11) - 2.0 * (ur * rt + ut * tt + uz * tz) + ut * tail)
    qz = 0.5 * (m(12) - 2.0 * (ur * rz + ut * tz + uz * zz) + uz * tail)
    return rho, ur, ut, uz, temp, qr, qt, qz


def add_speed_sums(sums_ref, sums, vz):
    one = vz * sums
    two = vz * one
    for k, value in enumerate([sums, one, two, vz * two, jnp.abs(vz) * sums]):
        sums_ref[k] += value


def moment_rows(sums_ref):
    lane = lax.broadcasted_iota(jnp.int32, (NODE_COUNT, 128), 1)
    e = []
    for k in range(5):
        x = sums_ref[k]
        e.append(x + pltpu.roll(x, 120, 1) + pltpu.roll(x, 112, 1))
    pick = lambda k, c: e[k][:, c : c + 1]
    columns = [
        pick(0, 0), pick(0, 1), pick(0, 2), pick(1, 0),
        pick(0, 3), pick(0, 4), pick(0, 5), pick(2, 0), pick(1, 1), pick(1, 2),
        pick(0, 6) + pick(2, 1), pick(0, 7) + pick(2, 2), pick(1, 3) + pick(1, 4) + pick(3, 0), pick(4, 0),
    ]
    table = jnp.zeros((NODE_COUNT, 128), F32)
    for k, column in enumerate(columns):
        table = jnp.where(lane == k, WEIGHT * column, table)
    return jnp.transpose(table)[0:MOMENTS, :]


def places_of():
    return lax.axis_index("row"), lax.axis_index("gz")


def send_piece(s, first, lanes, side, place, narrow, trace_ref, right_ref, left_ref, axial_ref):
    got = dot(trace_ref[side, place], narrow)
    if side == 1:
        right_ref[s, :, first - HALF : first - HALF + lanes] = got[0:LOCAL_Z]
    else:
        left_ref[s, :, first : first + lanes] = got[0:LOCAL_Z]
    axial_ref[s, :, first : first + lanes] = got[LOCAL_Z : LOCAL_Z + NODES]


def turn_traces(count, row, mirror_ref, left_ref, turned_ref):
    @pl.when(row == 0)
    def _():
        flat = left_ref[...].reshape(count * LOCAL_Z, HALF).astype(BF16)
        for first in range(0, HALF, 128):
            low = max(0, (HALF - first - 128 - 48) // 128 * 128)
            high = min(HALF, -((first - HALF - 48) // 128) * 128)
            got = dot(flat[:, low:high], mirror_ref[low:high, first : first + 128])
            turned_ref[:, :, first : first + 128] = got.reshape(count, LOCAL_Z, 128)

    @pl.when(row != 0)
    def _():
        turned_ref[...] = jnp.zeros(turned_ref.shape, F32)


def nodes_of(ref, first, lanes):
    return ref[:, :, first : first + lanes].reshape(NODE_COUNT, lanes)


def first_kernel(
    count, order, codes, f_ref, weight_ref, trace_ref, mirror_ref,
    right_ref, left_ref, turned_ref, axial_ref, mom_ref, sums_ref,
):
    step = pl.program_id(0)
    row, place = places_of()

    @pl.when(step == 0)
    def _():
        sums_ref[...] = jnp.zeros(sums_ref.shape, F32)

    for s in range(count):
        sums = jnp.zeros((NODE_COUNT, 128), F32)
        for first, lanes, side in PIECES:
            high, low = split(nodes_of(f_ref, s * PLANE + first, lanes))
            weights = weight_ref[first : first + lanes, :]
            sums = sums + dot(
                jnp.concatenate([high, low], axis=1), jnp.concatenate([weights, weights], axis=0)
            )
            send_piece(s, first, lanes, side, place, high, trace_ref, right_ref, left_ref, axial_ref)
        add_speed_sums(sums_ref, sums, slot_speed(order, step * count + s))
    turn_traces(count, row, mirror_ref, left_ref, turned_ref)

    @pl.when(step == pl.num_programs(0) - 1)
    def _():
        mom_ref[...] = moment_rows(sums_ref)


def inner_kernel(
    count, order, codes, f_ref, rows_ref, pos_ref, weight_ref, radial_ref, axial_m_ref, rot_ref,
    out_ref, mom_ref, sums_ref, inverse_ref, pad_ref, lhs_ref,
):
    step = pl.program_id(0)
    row, place = places_of()

    @pl.when(step == 0)
    def _():
        sums_ref[...] = jnp.zeros(sums_ref.shape, F32)
        pad_ref[:, 0:128] = jnp.zeros((NODE_COUNT, 128), BF16)
        pad_ref[:, 128 + PLANE :] = jnp.zeros((NODE_COUNT, 128), BF16)
        inverse_ref[...] = 1.0 / (ELEMENT_WIDTH * (row.astype(F32) + pos_ref[...]))
        lhs_ref[0, :, 0:128] = radial_ref[jnp.where(row == lax.axis_size("row") - 1, 2, 0)]
        lhs_ref[1, :, 0:128] = radial_ref[1]

    kind_out = jnp.where(jnp.logical_and(place == 1, codes[1, 0] == 2), 2, 0)
    inverse = inverse_ref[...]
    for s in range(count):
        vz = slot_speed(order, step * count + s)
        axial = (vz * axial_m_ref[jnp.where(vz > 0, 1, kind_out)]).astype(BF16)
        lhs_ref[0, :, 128:256] = axial
        lhs_ref[1, :, 128:256] = axial
        for j in range(PLANE // 128):
            field = nodes_of(f_ref, s * PLANE + j * 128, 128)
            pad_ref[:, 128 + j * 128 : 256 + j * 128] = (field * inverse).astype(BF16)
        sums = jnp.zeros((NODE_COUNT, 128), F32)
        for first, lanes, side in PIECES:
            tile = first // TILE
            inside = first - tile * TILE
            start = tile * TILE
            field = nodes_of(f_ref, s * PLANE + first, lanes)
            moved = (field * rows_ref[0:1, first : first + lanes]).astype(BF16)
            left = jnp.concatenate([lhs_ref[side], pad_ref[:, start : start + WINDOW]], axis=1)
            right = jnp.concatenate(
                [moved, field.astype(BF16), rot_ref[tile, :, inside : inside + lanes]], axis=0
            )
            change = dot(left, right).astype(BF16)
            out_ref[:, :, s * PLANE + first : s * PLANE + first + lanes] = change.reshape(
                NODES, LOCAL_Z, lanes
            )
            sums = sums + dot(change, weight_ref[first : first + lanes, :])
        add_speed_sums(sums_ref, sums, vz)

    @pl.when(step == pl.num_programs(0) - 1)
    def _():
        mom_ref[...] = moment_rows(sums_ref)


def total_of(parts):
    while len(parts) > 1:
        parts = [parts[k] + parts[k + 1] for k in range(0, len(parts), 2)]
    return parts[0]


def total_moments(part_refs, base_ref):
    total = total_of([p[...] for p in part_refs])
    return total if base_ref is None else total + base_ref[...]


def prepare_nodes(total, codes, place, rows_ref, edge_ref, table_ref, node_ref, wall_ref, plane_ref):
    wide = jnp.concatenate([total, jnp.zeros((128 - MOMENTS, 128), F32)], axis=0)
    table_ref[...] = jnp.transpose(wide)
    rho, ur, ut, uz, temp, qr, qt, qz = macroscopic_of(lambda k: table_ref[:, k : k + 1])
    inv_t = 1.0 / temp
    beta = ((1.0 - VISCOUS_RATIO) / 5.0) / (rho * temp * temp)
    kappa = rho * (TIME_STEP / KNUDSEN)
    peak = kappa * rho * inv_t * jnp.sqrt(inv_t)
    columns = [uz, -0.5 * inv_t, qz * beta, inv_t, peak, 1.0 - kappa, ur, ut, qr * beta, qt * beta]
    for k, column in enumerate(columns):
        node_ref[k] = jnp.broadcast_to(column, (NODE_COUNT, 128))
    net = table_ref[:, 3:4]
    gross = table_ref[:, 13:14]
    to_bottom = 0.5 * (gross - net)
    to_top = 0.5 * (gross + net)
    incident = jnp.sum(edge_ref[0] * to_bottom, axis=0, keepdims=True)
    upward = jnp.sum(edge_ref[1] * to_top, axis=0, keepdims=True)
    bottom = jnp.where(codes[0, 0] == 1, SAT_DENSITY, incident * (1.0 / HALF_FLUX))
    top = jnp.where(codes[1, 0] == 2, 0.0, upward * (1.0 / HALF_FLUX))
    density = jnp.where(place == 0, bottom, top)
    wall_ref[...] = jnp.transpose(jnp.broadcast_to(density, (128, 128)))[0:NODES, :]

    def one_radius(r, carry):
        rows = pl.ds(pl.multiple_of(r * LOCAL_Z, LOCAL_Z), LOCAL_Z)
        n_half, n_inv = node_ref[1, rows, :], node_ref[3, rows, :]
        n_ur, n_ut = node_ref[6, rows, :], node_ref[7, rows, :]
        n_qr, n_qt = node_ref[8, rows, :], node_ref[9, rows, :]
        for j in range(PLANE // 128):
            at = pl.ds(j * 128, 128)
            cr = rows_ref[0:1, at] - n_ur
            ct = rows_ref[1:2, at] - n_ut
            square = cr * cr + ct * ct
            gauss = jnp.exp(square * n_half)
            along = cr * n_qr + ct * n_qt
            reach = square * n_inv - 5.0
            tilted = gauss * along
            plane_ref[0, rows, at] = gauss
            plane_ref[1, rows, at] = tilted
            plane_ref[2, rows, at] = gauss * reach
            plane_ref[3, rows, at] = tilted * reach
        return carry

    lax.fori_loop(0, NODES, one_radius, 0)


def slot_factors(vz, node_ref):
    cz = vz - node_ref[0]
    lam = node_ref[4] * jnp.exp(cz * cz * node_ref[1])
    alpha = cz * node_ref[2]
    reach = cz * cz * node_ref[3]
    return lam * (1.0 + alpha * reach), lam * reach, lam * alpha, lam


def ghost_lifts(vz, ghost_r_ref, ghost_z_ref, lhs_ref):
    lean = jnp.abs(vz) * ghost_z_ref[jnp.where(vz > 0, 1, 0)]
    lhs_ref[0] = (ghost_r_ref[0] + lean).astype(BF16)
    lhs_ref[1] = (ghost_r_ref[1] + lean).astype(BF16)


def ghost_rows(s, vz, place, in_left_ref, in_turned_ref, in_right_ref, in_axial_ref, rows_ref, wall_ref, ghost_ref):
    own = (place == 0) == (vz > 0)
    strength = jnp.exp(-0.5 * vz * vz + jnp.zeros((NODES, 128), F32)) * wall_ref[...]
    for j in range(PLANE // 128):
        at = pl.ds(j * 128, 128)
        if j * 128 < HALF:
            radial = in_right_ref[s, :, at]
        else:
            back = pl.ds(j * 128 - HALF, 128)
            radial = in_left_ref[s, :, back] + in_turned_ref[s, :, back]
        axial = jnp.where(own, strength * rows_ref[2:3, at], in_axial_ref[s, :, at])
        rows = jnp.concatenate([rows_ref[0:1, at] * radial, axial, jnp.zeros((8, 128), F32)], axis=0)
        ghost_ref[:, at] = rows.astype(BF16)


def outer_kernel(count, part_count, based, last, order, codes, *refs):
    part_refs, refs = refs[:part_count], refs[part_count:]
    base_ref = None
    if based:
        base_ref, refs = refs[0], refs[1:]
    f_ref, inner_ref, in_left_ref, in_turned_ref, in_right_ref, in_axial_ref = refs[:6]
    rows_ref, edge_ref, ghost_r_ref, ghost_z_ref = refs[6:10]
    refs = refs[10:]
    if last:
        out_ref, refs = refs[0], refs[1:]
    else:
        (trace_ref, mirror_ref, out_ref, right_ref, left_ref, turned_ref, axial_ref), refs = refs[:7], refs[7:]
    plane_ref, node_ref, wall_ref, slot_ref, lhs_ref, ghost_ref, table_ref = refs
    step = pl.program_id(0)
    row, place = places_of()

    @pl.when(step == 0)
    def _():
        total = total_moments(part_refs, base_ref)
        prepare_nodes(total, codes, place, rows_ref, edge_ref, table_ref, node_ref, wall_ref, plane_ref)

    for s in range(count):
        vz = slot_speed(order, step * count + s)
        for k, value in enumerate(slot_factors(vz, node_ref)):
            slot_ref[k] = value
        ghost_lifts(vz, ghost_r_ref, ghost_z_ref, lhs_ref)
        ghost_rows(
            s, vz, place, in_left_ref, in_turned_ref, in_right_ref, in_axial_ref, rows_ref, wall_ref, ghost_ref
        )
        for first, lanes, side in PIECES:
            lifted = dot(lhs_ref[side, :, 0:GHOST_ROWS], ghost_ref[:, first : first + lanes])
            pieces = []
            for inside in range(0, lanes, 128):
                here = s * PLANE + first + inside
                at = pl.ds(first + inside, 128)
                new = nodes_of(f_ref, here, 128) * node_ref[5] + nodes_of(inner_ref, here, 128).astype(F32)
                new = new + lifted[:, inside : inside + 128]
                for k in range(4):
                    new = new + plane_ref[k, :, at] * slot_ref[k]
                out_ref[:, :, here : here + 128] = new.reshape(NODES, LOCAL_Z, 128)
                pieces.append(new.astype(BF16))
            if not last:
                narrow = jnp.concatenate(pieces, axis=1) if len(pieces) > 1 else pieces[0]
                send_piece(s, first, lanes, side, place, narrow, trace_ref, right_ref, left_ref, axial_ref)
    if not last:
        turn_traces(count, row, mirror_ref, left_ref, turned_ref)


def moment_kernel(count, part_count, based, order, codes, *refs):
    part_refs, refs = refs[:part_count], refs[part_count:]
    base_ref = None
    if based:
        base_ref, refs = refs[0], refs[1:]
    inner_mom_ref, in_left_ref, in_turned_ref, in_right_ref, in_axial_ref = refs[:5]
    rows_ref, edge_ref, ghost_r_ref, ghost_z_ref, weight_ref = refs[5:10]
    share_ref, kept_ref = refs[10:12]
    plane_ref, node_ref, wall_ref, lhs_ref, ghost_ref, table_ref, sums_ref, plane_sums_ref = refs[12:]
    step = pl.program_id(0)
    row, place = places_of()

    @pl.when(step == 0)
    def _():
        sums_ref[...] = jnp.zeros(sums_ref.shape, F32)
        total = total_moments(part_refs, base_ref)
        kept_ref[...] = total * (1.0 - total[0:1, :] * (TIME_STEP / KNUDSEN))
        prepare_nodes(total, codes, place, rows_ref, edge_ref, table_ref, node_ref, wall_ref, plane_ref)
        for k in range(4):
            high, low = split(plane_ref[k])
            plane_sums_ref[k] = dot(high, weight_ref[...]) + dot(low, weight_ref[...])

    for s in range(count):
        vz = slot_speed(order, step * count + s)
        sums = jnp.zeros((NODE_COUNT, 128), F32)
        for k, value in enumerate(slot_factors(vz, node_ref)):
            sums = sums + plane_sums_ref[k] * value
        ghost_lifts(vz, ghost_r_ref, ghost_z_ref, lhs_ref)
        ghost_rows(
            s, vz, place, in_left_ref, in_turned_ref, in_right_ref, in_axial_ref, rows_ref, wall_ref, ghost_ref
        )
        for side in range(2):
            span = pl.ds(side * HALF, HALF)
            high, low = split(dot(ghost_ref[:, span], weight_ref[span, :]))
            lift = lhs_ref[side, :, 0:GHOST_ROWS]
            sums = sums + dot(lift, high) + dot(lift, low)
        add_speed_sums(sums_ref, sums, vz)

    @pl.when(step == pl.num_programs(0) - 1)
    def _():
        share_ref[...] = moment_rows(sums_ref) + inner_mom_ref[...]


def last_kernel(part_count, codes, *refs):
    total_ref = total_moments(refs[:part_count], refs[part_count])
    edge_ref, macro_ref, flux_ref = refs[part_count + 1 :]
    row, place = places_of()
    values = macroscopic_of(lambda k: total_ref[k : k + 1, :])
    for k in range(8):
        for r in range(NODES):
            macro_ref[k, r : r + 1, :] = values[k][:, r * LOCAL_Z : (r + 1) * LOCAL_Z]
    net, gross = total_ref[3:4, :], total_ref[13:14, :]
    to_bottom = jnp.broadcast_to(0.5 * (gross - net), (8, 128))
    to_top = jnp.broadcast_to(0.5 * (gross + net), (8, 128))
    exact = lambda x, y: jnp.dot(x, y, precision=lax.Precision.HIGHEST, preferred_element_type=F32)
    incident = exact(to_bottom, edge_ref[0])
    upward = exact(to_top, edge_ref[1])
    downward = exact(to_bottom, edge_ref[1])
    bottom = jnp.where(codes[0, 0] == 1, SAT_DENSITY * HALF_FLUX - incident, 0.0)
    top = jnp.where(codes[1, 0] == 2, upward - downward, 0.0)
    flux_ref[...] = jnp.where(place == 0, bottom, top)[0:1, 0:NODES]


def whole(shape):
    return pl.BlockSpec(shape, lambda *a: (0,) * len(shape), pipeline_mode=pl.Buffered(1))


def on_device(distribution, z_order, edge_codes):
    local_r, local_z, vdev = distribution.shape
    assert local_r == NODES and local_z == LOCAL_Z
    slots = vdev // PLANE
    group = math.gcd(slots, 3)
    steps = slots // group
    rows_total = lax.axis_size("row")
    verts = lax.axis_size("vert")
    assert lax.axis_size("gz") == 2
    rows, pos, edge = jnp.asarray(ROWS), jnp.asarray(NODE_POS), jnp.asarray(EDGE)
    radial_m, axial_m = jnp.asarray(RADIAL_M), jnp.asarray(AXIAL_M)
    ghost_r, ghost_z = jnp.asarray(GHOST_R), jnp.asarray(GHOST_Z)
    trace_m, mirror_m, rot_m = jnp.asarray(TRACE_M), jnp.asarray(MIRROR_M), jnp.asarray(ROTATION_M)
    weight_m = jnp.asarray(WEIGHT_M)

    big = pl.BlockSpec((NODES, LOCAL_Z, group * PLANE), lambda i, *n: (0, 0, i))
    radial_spec = pl.BlockSpec((group, LOCAL_Z, HALF), lambda i, *n: (i, 0, 0))
    axial_spec = pl.BlockSpec((group, NODES, PLANE), lambda i, *n: (i, 0, 0))
    mom_spec = whole((MOMENTS, 128))
    radial_shape = jax.ShapeDtypeStruct((slots, LOCAL_Z, HALF), F32)
    axial_shape = jax.ShapeDtypeStruct((slots, NODES, PLANE), F32)
    mom_shape = jax.ShapeDtypeStruct((MOMENTS, 128), F32)
    big_shape = jax.ShapeDtypeStruct(distribution.shape, F32)
    trace_specs = [radial_spec, radial_spec, radial_spec, axial_spec]
    trace_shapes = [radial_shape, radial_shape, radial_shape, axial_shape]
    ghost_specs = [radial_spec, radial_spec, radial_spec, axial_spec]
    square = pltpu.VMEM((NODE_COUNT, 128), F32)
    sums_scratch = pltpu.VMEM((5, NODE_COUNT, 128), F32)
    node_scratch = [
        pltpu.VMEM((4, NODE_COUNT, PLANE), F32),
        pltpu.VMEM((10, NODE_COUNT, 128), F32),
        pltpu.VMEM((NODES, 128), F32),
    ]
    ghost_scratch = [
        pltpu.VMEM((2, NODE_COUNT, 128), BF16),
        pltpu.VMEM((GHOST_ROWS, PLANE), BF16),
        square,
    ]

    def call(body, name, in_specs, out_specs, out_shape, scratch, args):
        return pl.pallas_call(
            body,
            grid_spec=pltpu.PrefetchScalarGridSpec(
                num_scalar_prefetch=2,
                grid=(steps,),
                in_specs=in_specs,
                out_specs=out_specs,
                scratch_shapes=scratch,
            ),
            out_shape=out_shape,
            compiler_params=pltpu.CompilerParams(vmem_limit_bytes=56 * 1024 * 1024),
            name=name,
        )(z_order, edge_codes, *args)

    def all_whole(tables):
        return [whole(x.shape) for x in tables]

    def first(f):
        tables = [weight_m, trace_m, mirror_m]
        return call(
            lambda *a: first_kernel(group, *a), "moments_and_traces", [big] + all_whole(tables),
            trace_specs + [mom_spec], trace_shapes + [mom_shape], [sums_scratch], [f] + tables,
        )

    def inner(f):
        tables = [rows, pos, weight_m, radial_m, axial_m, rot_m]
        scratch = [
            sums_scratch,
            square,
            pltpu.VMEM((NODE_COUNT, PLANE + 256), BF16),
            pltpu.VMEM((2, NODE_COUNT, 256), BF16),
        ]
        return call(
            lambda *a: inner_kernel(group, *a), "inner_increments", [big] + all_whole(tables),
            [big, mom_spec], [jax.ShapeDtypeStruct(f.shape, BF16), mom_shape], scratch, [f] + tables,
        )

    def outer(f, change, ghosts, parts, base, last):
        bases = [] if base is None else [base]
        tables = [rows, edge, ghost_r, ghost_z] + ([] if last else [trace_m, mirror_m])
        return call(
            lambda *a: outer_kernel(group, len(parts), bool(bases), last, *a),
            "last_update" if last else "update",
            [mom_spec] * (len(parts) + len(bases)) + [big, big] + ghost_specs + all_whole(tables),
            [big] + ([] if last else trace_specs),
            [big_shape] + ([] if last else trace_shapes),
            node_scratch + [pltpu.VMEM((4, NODE_COUNT, 128), F32)] + ghost_scratch,
            [*parts, *bases, f, change, *ghosts, *tables],
        )

    def share(change_moments, ghosts, parts, base):
        bases = [] if base is None else [base]
        tables = [rows, edge, ghost_r, ghost_z, weight_m]
        return call(
            lambda *a: moment_kernel(group, len(parts), bool(bases), *a),
            "moment_share",
            [mom_spec] * (len(parts) + len(bases) + 1) + ghost_specs + all_whole(tables),
            [mom_spec, mom_spec],
            [mom_shape, mom_shape],
            node_scratch + ghost_scratch + [sums_scratch, pltpu.VMEM((4, NODE_COUNT, 128), F32)],
            [*parts, *bases, change_moments, *ghosts, *tables],
        )

    def spread(moments):
        parts = [moments]
        for shift in range(1, verts):
            parts.append(lax.ppermute(moments, "vert", [(i, i ^ shift) for i in range(verts)]))
        return parts

    def halo(right, left, turned, axial):
        from_axial = lax.ppermute(axial, "gz", [(0, 1), (1, 0)])
        from_left = lax.ppermute(right, "row", [(i, i + 1) for i in range(rows_total - 1)])
        from_right = lax.ppermute(left, "row", [(i + 1, i) for i in range(rows_total - 1)])
        return from_left, turned, from_right, from_axial

    current = distribution
    *traces, moments = first(current)
    base = None
    for number in range(STEPS):
        last = number == STEPS - 1
        ghosts = halo(*traces)
        parts = spread(moments)
        change, change_moments = inner(current)
        moments, next_base = share(change_moments, ghosts, parts, base)
        current, *traces = outer(current, change, ghosts, parts, base, last)
        base = next_base
    parts = spread(moments)
    macro, flux = pl.pallas_call(
        lambda *a: last_kernel(len(parts), *a),
        grid_spec=pltpu.PrefetchScalarGridSpec(
            num_scalar_prefetch=1,
            grid=(1,),
            in_specs=[mom_spec] * (len(parts) + 1) + [whole(edge.shape)],
            out_specs=[whole((8, NODES, LOCAL_Z)), whole((1, NODES))],
        ),
        out_shape=[
            jax.ShapeDtypeStruct((8, NODES, LOCAL_Z), F32),
            jax.ShapeDtypeStruct((1, NODES), F32),
        ],
        name="macroscopic",
    )(edge_codes, *parts, base, edge)
    return (current, macro, flux)


def solution(mesh):
    in_specs = (P("row", "gz", "vert"), P("vert"), P(None, "row"))
    out_specs = (P("row", "gz", "vert"), P(None, "row", "gz"), P("gz", "row"))
    return jax.shard_map(
        on_device, mesh=mesh, in_specs=in_specs, out_specs=out_specs, check_vma=False
    )
```

```python
import math

import jax
import jax.numpy as jnp
import ml_dtypes
import numpy as np
from jax import lax
from jax.experimental import pallas as pl
from jax.experimental.pallas import tpu as pltpu
from jax.sharding import PartitionSpec as P

NODES = 8
NVR = 48
NVT = 48
NVZ = 48
STEPS = 2

ELEMENT_WIDTH = 4.0
TIME_STEP = 0.001
KNUDSEN = 0.005
VISCOUS_RATIO = 2.0 / 3.0
SAT_DENSITY = 1.5
SPEED_LIMIT = 5.0

PLANE = NVR * NVT
HALF = PLANE // 2
LOCAL_Z = 2 * NODES
NODE_COUNT = NODES * LOCAL_Z
TILE = 256
WINDOW = 512
GHOST_ROWS = 32
MOMENTS = 16
F32 = jnp.float32
BF16 = jnp.bfloat16
PIECES = [(t, TILE, 0) for t in range(0, 1024, TILE)] + [(1024, 128, 0), (1152, 128, 1)] + [
    (t, TILE, 1) for t in range(1280, PLANE, TILE)
]


def legendre_pair(position, point_count):
    previous = 1.0
    current = position
    for degree in range(2, point_count + 1):
        previous, current = (
            current,
            ((2 * degree - 1) * position * current - (degree - 1) * previous) / degree,
        )
    slope = point_count * (position * current - previous) / (position * position - 1.0)
    return (current, slope)


def dg_tables(point_count):
    point_list = []
    weight_list = []
    for number in range(point_count):
        position = math.cos(math.pi * (number + 0.75) / (point_count + 0.5))
        for sweep in range(60):
            value, slope = legendre_pair(position, point_count)
            position = position - value / slope
        value, slope = legendre_pair(position, point_count)
        point_list.append(position)
        weight_list.append(2.0 / ((1.0 - position * position) * slope * slope))
    point_list = point_list[::-1]
    weight_list = weight_list[::-1]
    points = np.array(point_list)
    derivative = np.zeros((point_count, point_count))
    right = np.zeros(point_count)
    left = np.zeros(point_count)
    products = [
        np.prod([points[i] - points[j] for j in range(point_count) if j != i])
        for i in range(point_count)
    ]
    for i in range(point_count):
        others = [j for j in range(point_count) if j != i]
        derivative[i, i] = sum(1.0 / (points[i] - points[j]) for j in others)
        for j in others:
            derivative[i, j] = products[i] / products[j] / (points[i] - points[j])
        right[i] = np.prod([1.0 - points[j] for j in others]) / products[i]
        left[i] = np.prod([-1.0 - points[j] for j in others]) / products[i]
    return points, np.array(weight_list), derivative, right, left


def speed_grid(point_count):
    return -SPEED_LIMIT + (np.arange(point_count) + 0.5) * (2.0 * SPEED_LIMIT / point_count)


POINTS, QUAD, DERIV, END_R, END_L = dg_tables(NODES)
LIFT_R = END_R / QUAD
LIFT_L = END_L / QUAD
GRID_R = speed_grid(NVR)
GRID_T = speed_grid(NVT)
GRID_Z = speed_grid(NVZ)
STEP_V = 2 * SPEED_LIMIT / NVR
WEIGHT = STEP_V**3 / (2 * math.pi) ** 1.5
HALF_FLUX = float(
    WEIGHT
    * np.sum(np.exp(-(GRID_R**2) / 2))
    * np.sum(np.exp(-(GRID_T**2) / 2))
    * np.sum(np.maximum(GRID_Z, 0.0) * np.exp(-(GRID_Z**2) / 2))
)
SCALE = TIME_STEP * 2.0 / ELEMENT_WIDTH


def transport_tables():
    ident = np.eye(NODES)
    up = DERIV + np.outer(LIFT_L, END_L)
    down = DERIV - np.outer(LIFT_R, END_R)
    zero = np.zeros((NODES, NODES))
    wide = np.eye(LOCAL_Z)
    radial = np.stack([np.kron(down, wide), np.kron(up, wide), np.kron(DERIV, wide)])
    zup = np.block([[up, zero], [-np.outer(LIFT_L, END_R), up]])
    zdown = np.block([[down, np.outer(LIFT_R, END_L)], [zero, down]])
    zout = np.block([[down, np.outer(LIFT_R, END_L)], [zero, DERIV]])
    axial = np.stack([np.kron(ident, zdown), np.kron(ident, zup), np.kron(ident, zout)])
    ghost_r = np.zeros((2, NODE_COUNT, 128))
    ghost_z = np.zeros((2, NODE_COUNT, 128))
    for r in range(NODES):
        for z in range(LOCAL_Z):
            n = r * LOCAL_Z + z
            ghost_r[0, n, z] = -LIFT_R[r]
            ghost_r[1, n, z] = LIFT_L[r]
            if z >= NODES:
                ghost_z[0, n, LOCAL_Z + r] = LIFT_R[z - NODES]
            else:
                ghost_z[1, n, LOCAL_Z + r] = LIFT_L[z]
    trace = np.zeros((2, 2, GHOST_ROWS, NODE_COUNT))
    for side in range(2):
        radial_row = END_R if side == 1 else END_L
        for place in range(2):
            for z in range(LOCAL_Z):
                for r in range(NODES):
                    trace[side, place, z, r * LOCAL_Z + z] = radial_row[r]
            for r in range(NODES):
                for k in range(NODES):
                    if place == 0:
                        trace[side, place, LOCAL_Z + r, r * LOCAL_Z + NODES + k] = END_R[k]
                    else:
                        trace[side, place, LOCAL_Z + r, r * LOCAL_Z + k] = END_L[k]
    return (
        (-SCALE * radial).astype(ml_dtypes.bfloat16),
        (-SCALE * axial).astype(np.float32),
        (SCALE * ghost_r).astype(np.float32),
        (SCALE * ghost_z).astype(np.float32),
        trace.astype(ml_dtypes.bfloat16),
    )


def rotation_table():
    full = np.zeros((PLANE + 2 * TILE, PLANE))
    factor = TIME_STEP / (2 * STEP_V)
    for a in range(NVR):
        for b in range(NVT):
            n = a * NVT + b
            first = factor * GRID_T[b] * GRID_T[b]
            second = factor * GRID_R[a] * GRID_T[b]
            if a + 1 < NVR:
                full[TILE + n + NVT, n] = -first
            if a > 0:
                full[TILE + n - NVT, n] = first
            if b + 1 < NVT:
                full[TILE + n + 1, n] = second
            if b > 0:
                full[TILE + n - 1, n] = -second
    tiles = [full[TILE + t - 128 : TILE + t - 128 + WINDOW, t : t + TILE] for t in range(0, PLANE, TILE)]
    return np.stack(tiles).astype(ml_dtypes.bfloat16)


def mirror_table():
    table = np.zeros((HALF, HALF))
    groups = NVR // 2
    for g in range(groups):
        for b in range(NVT):
            table[(groups - 1 - g) * NVT + b, g * NVT + b] = 1.0
    return table.astype(ml_dtypes.bfloat16)


def plane_rows():
    vr = np.repeat(GRID_R, NVT)
    vt = np.tile(GRID_T, NVR)
    rows = np.zeros((8, PLANE))
    rows[0] = vr
    rows[1] = vt
    rows[2] = np.exp(-(vr**2 + vt**2) / 2)
    return rows.astype(np.float32)


def edge_table():
    table = np.zeros((2, NODE_COUNT, 128))
    for r in range(NODES):
        for k in range(NODES):
            table[0, r * LOCAL_Z + k, r] = END_L[k]
            table[1, r * LOCAL_Z + NODES + k, r] = END_R[k]
    return table.astype(np.float32)


def node_columns():
    table = np.zeros((NODE_COUNT, 128))
    for r in range(NODES):
        table[r * LOCAL_Z : (r + 1) * LOCAL_Z, :] = (1.0 + POINTS[r]) / 2
    return table.astype(np.float32)


RADIAL_M, AXIAL_M, GHOST_R, GHOST_Z, TRACE_M = transport_tables()
ROTATION_M = rotation_table()
MIRROR_M = mirror_table()
ROWS = plane_rows()
EDGE = edge_table()
NODE_POS = node_columns()


def slot_speed(order, slot):
    return (order[slot].astype(F32) + 0.5) * (2 * SPEED_LIMIT / NVZ) - SPEED_LIMIT


def dot(x, y):
    return jnp.dot(x, y, preferred_element_type=F32)


def macroscopic_of(m):
    rho = m(0)
    inv = 1.0 / rho
    ur, ut, uz = m(1) * inv, m(2) * inv, m(3) * inv
    rr, tt, rt, zz, rz, tz = (m(k) for k in range(4, 10))
    energy = rr + tt + zz
    speed = ur * ur + ut * ut + uz * uz
    temp = (energy * inv - speed) * (1.0 / 3.0)
    tail = 2.0 * rho * speed - energy
    qr = 0.5 * (m(10) - 2.0 * (ur * rr + ut * rt + uz * rz) + ur * tail)
    qt = 0.5 * (m(11) - 2.0 * (ur * rt + ut * tt + uz * tz) + ut * tail)
    qz = 0.5 * (m(12) - 2.0 * (ur * rz + ut * tz + uz * zz) + uz * tail)
    return rho, ur, ut, uz, temp, qr, qt, qz


def add_speed_sums(field, vz, sums):
    one = field * vz
    two = one * vz
    return [
        sums[0] + field,
        sums[1] + one,
        sums[2] + two,
        sums[3] + two * vz,
        sums[4] + field * jnp.abs(vz),
    ]


def finish_moments(sums_ref, rows_ref, table_ref, out_ref):
    lane = lax.broadcasted_iota(jnp.int32, (LOCAL_Z, 128), 1)

    def one_radius(r, carry):
        acc = [jnp.zeros((LOCAL_Z, 128), F32) for _ in range(14)]
        for j in range(PLANE // 128):
            at = pl.ds(j * 128, 128)
            vr = rows_ref[0:1, at]
            vt = rows_ref[1:2, at]
            g0, g1, g2, g3, g4 = (sums_ref[k, r, :, at] for k in range(5))
            a = vr * g0
            b = vt * g0
            aa = vr * a
            bb = vt * b
            c = vr * g1
            d = vt * g1
            perp = aa + bb + g2
            new = [g0, a, b, g1, aa, bb, vr * b, g2, c, d, vr * perp, vt * perp, vr * c + vt * d + g3, g4]
            acc = [x + y for x, y in zip(acc, new)]
        block = jnp.zeros((LOCAL_Z, 128), F32)
        for k in range(14):
            block = jnp.where(lane == k, WEIGHT * jnp.sum(acc[k], axis=1, keepdims=True), block)
        table_ref[pl.ds(pl.multiple_of(r * LOCAL_Z, LOCAL_Z), LOCAL_Z), :] = block
        return carry

    lax.fori_loop(0, NODES, one_radius, 0)
    out_ref[...] = jnp.transpose(table_ref[...])[0:MOMENTS, :]


def clear_sums(sums_ref):
    sums_ref[...] = jnp.zeros(sums_ref.shape, F32)


def places_of():
    return lax.axis_index("row"), lax.axis_index("gz")


def send_piece(s, first, lanes, side, place, narrow, trace_ref, right_ref, left_ref, axial_ref):
    got = dot(trace_ref[side, place], narrow)
    if side == 1:
        right_ref[s, :, first - HALF : first - HALF + lanes] = got[0:LOCAL_Z]
    else:
        left_ref[s, :, first : first + lanes] = got[0:LOCAL_Z]
    axial_ref[s, :, first : first + lanes] = got[LOCAL_Z : LOCAL_Z + NODES]


def turn_traces(count, row, mirror_ref, left_ref, turned_ref):
    @pl.when(row == 0)
    def _():
        flat = left_ref[...].reshape(count * LOCAL_Z, HALF).astype(BF16)
        for first in range(0, HALF, 128):
            low = max(0, (HALF - first - 128 - 48) // 128 * 128)
            high = min(HALF, -((first - HALF - 48) // 128) * 128)
            got = dot(flat[:, low:high], mirror_ref[low:high, first : first + 128])
            turned_ref[:, :, first : first + 128] = got.reshape(count, LOCAL_Z, 128)

    @pl.when(row != 0)
    def _():
        turned_ref[...] = jnp.zeros(turned_ref.shape, F32)


def nodes_of(ref, first, lanes):
    return ref[:, :, first : first + lanes].reshape(NODE_COUNT, lanes)


def send_traces(count, place, narrow_ref, trace_ref, right_ref, left_ref, axial_ref):
    for s in range(count):
        for first, lanes, side in PIECES:
            narrow = narrow_ref[s, :, first : first + lanes]
            send_piece(s, first, lanes, side, place, narrow, trace_ref, right_ref, left_ref, axial_ref)


def first_kernel(
    count, order, codes, f_ref, rows_ref, trace_ref, mirror_ref,
    right_ref, left_ref, turned_ref, axial_ref, mom_ref, sums_ref, table_ref,
):
    step = pl.program_id(0)
    row, place = places_of()

    @pl.when(step == 0)
    def _():
        clear_sums(sums_ref)

    speeds = [slot_speed(order, step * count + s) for s in range(count)]
    for first, lanes, side in PIECES:
        narrow = [[] for s in range(count)]
        for inside in range(0, lanes, 128):
            at = pl.ds(first + inside, 128)
            column = [[] for s in range(count)]
            for r in range(NODES):
                sums = [sums_ref[k, r, :, at] for k in range(5)]
                for s in range(count):
                    field = f_ref[r, :, pl.ds(s * PLANE + first + inside, 128)]
                    sums = add_speed_sums(field, speeds[s], sums)
                    column[s].append(field.astype(BF16))
                for k in range(5):
                    sums_ref[k, r, :, at] = sums[k]
            for s in range(count):
                narrow[s].append(jnp.concatenate(column[s], axis=0))
        for s in range(count):
            block = jnp.concatenate(narrow[s], axis=1) if len(narrow[s]) > 1 else narrow[s][0]
            send_piece(s, first, lanes, side, place, block, trace_ref, right_ref, left_ref, axial_ref)
    turn_traces(count, row, mirror_ref, left_ref, turned_ref)

    @pl.when(step == pl.num_programs(0) - 1)
    def _():
        finish_moments(sums_ref, rows_ref, table_ref, mom_ref)


def inner_kernel(
    count, order, codes, f_ref, rows_ref, pos_ref, radial_ref, axial_m_ref, rot_ref,
    out_ref, inverse_ref, pad_ref, lhs_ref,
):
    step = pl.program_id(0)
    row, place = places_of()

    @pl.when(step == 0)
    def _():
        pad_ref[:, :, 0:128] = jnp.zeros((count, NODE_COUNT, 128), BF16)
        pad_ref[:, :, 128 + PLANE :] = jnp.zeros((count, NODE_COUNT, 128), BF16)
        inverse_ref[...] = 1.0 / (ELEMENT_WIDTH * (row.astype(F32) + pos_ref[...]))
        minus = radial_ref[jnp.where(row == lax.axis_size("row") - 1, 2, 0)]
        for s in range(count):
            lhs_ref[s, 0, 0:NODE_COUNT] = minus
            lhs_ref[s, 1, 0:NODE_COUNT] = radial_ref[1]

    kind_out = jnp.where(jnp.logical_and(place == 1, codes[1, 0] == 2), 2, 0)
    inverse = inverse_ref[...]
    for s in range(count):
        vz = slot_speed(order, step * count + s)
        axial = (vz * axial_m_ref[jnp.where(vz > 0, 1, kind_out)]).astype(BF16)
        lhs_ref[s, 0, NODE_COUNT:] = axial
        lhs_ref[s, 1, NODE_COUNT:] = axial
        for j in range(PLANE // 128):
            field = nodes_of(f_ref, s * PLANE + j * 128, 128)
            pad_ref[s, :, 128 + j * 128 : 256 + j * 128] = (field * inverse).astype(BF16)

    for tile in range(PLANE // TILE):
        start = tile * TILE
        turned = dot(pad_ref[:, :, start : start + WINDOW].reshape(count * NODE_COUNT, WINDOW), rot_ref[tile])
        for first, lanes, side in PIECES:
            if first // TILE != tile:
                continue
            vr = rows_ref[0:1, first : first + lanes]
            inside = first - start
            for s in range(count):
                here = s * PLANE + first
                moved = dot(lhs_ref[s, side], nodes_of(f_ref, here, lanes).astype(BF16))
                change = turned[s * NODE_COUNT : (s + 1) * NODE_COUNT, inside : inside + lanes]
                change = change + vr * moved[0:NODE_COUNT] + moved[NODE_COUNT:]
                out_ref[:, :, here : here + lanes] = change.astype(BF16).reshape(NODES, LOCAL_Z, lanes)


def total_of(parts):
    while len(parts) > 1:
        parts = [parts[k] + parts[k + 1] for k in range(0, len(parts), 2)]
    return parts[0]


def prepare_nodes(total, codes, place, rows_ref, edge_ref, table_ref, node_ref, wall_ref, plane_ref):
    wide = jnp.concatenate([total, jnp.zeros((128 - MOMENTS, 128), F32)], axis=0)
    table_ref[...] = jnp.transpose(wide)
    rho, ur, ut, uz, temp, qr, qt, qz = macroscopic_of(lambda k: table_ref[:, k : k + 1])
    inv_t = 1.0 / temp
    beta = ((1.0 - VISCOUS_RATIO) / 5.0) / (rho * temp * temp)
    kappa = rho * (TIME_STEP / KNUDSEN)
    peak = kappa * rho * inv_t * jnp.sqrt(inv_t)
    columns = [uz, -0.5 * inv_t, qz * beta, inv_t, peak, 1.0 - kappa, ur, ut, qr * beta, qt * beta]
    for k, column in enumerate(columns):
        node_ref[k] = jnp.broadcast_to(column, (NODE_COUNT, 128))
    net = table_ref[:, 3:4]
    gross = table_ref[:, 13:14]
    to_bottom = 0.5 * (gross - net)
    to_top = 0.5 * (gross + net)
    incident = jnp.sum(edge_ref[0] * to_bottom, axis=0, keepdims=True)
    upward = jnp.sum(edge_ref[1] * to_top, axis=0, keepdims=True)
    bottom = jnp.where(codes[0, 0] == 1, SAT_DENSITY, incident * (1.0 / HALF_FLUX))
    top = jnp.where(codes[1, 0] == 2, 0.0, upward * (1.0 / HALF_FLUX))
    density = jnp.where(place == 0, bottom, top)
    wall_ref[...] = jnp.transpose(jnp.broadcast_to(density, (128, 128)))[0:NODES, :]

    def one_radius(r, carry):
        rows = pl.ds(pl.multiple_of(r * LOCAL_Z, LOCAL_Z), LOCAL_Z)
        n_half, n_inv = node_ref[1, rows, :], node_ref[3, rows, :]
        n_ur, n_ut = node_ref[6, rows, :], node_ref[7, rows, :]
        n_qr, n_qt = node_ref[8, rows, :], node_ref[9, rows, :]
        for j in range(PLANE // 128):
            at = pl.ds(j * 128, 128)
            cr = rows_ref[0:1, at] - n_ur
            ct = rows_ref[1:2, at] - n_ut
            square = cr * cr + ct * ct
            gauss = jnp.exp(square * n_half)
            along = cr * n_qr + ct * n_qt
            reach = square * n_inv - 5.0
            tilted = gauss * along
            plane_ref[0, rows, at] = gauss
            plane_ref[1, rows, at] = tilted
            plane_ref[2, rows, at] = gauss * reach
            plane_ref[3, rows, at] = tilted * reach
        return carry

    lax.fori_loop(0, NODES, one_radius, 0)


def slot_factors(vz, node_ref):
    cz = vz - node_ref[0]
    lam = node_ref[4] * jnp.exp(cz * cz * node_ref[1])
    alpha = cz * node_ref[2]
    reach = cz * cz * node_ref[3]
    return lam * (1.0 + alpha * reach), lam * reach, lam * alpha, lam


def ghost_lifts(vz, ghost_r_ref, ghost_z_ref, lhs_ref):
    lean = jnp.abs(vz) * ghost_z_ref[jnp.where(vz > 0, 1, 0)]
    lhs_ref[0] = (ghost_r_ref[0] + lean).astype(BF16)
    lhs_ref[1] = (ghost_r_ref[1] + lean).astype(BF16)


def ghost_rows(s, vz, place, in_left_ref, in_turned_ref, in_right_ref, in_axial_ref, rows_ref, wall_ref, ghost_ref):
    own = (place == 0) == (vz > 0)
    strength = jnp.exp(-0.5 * vz * vz + jnp.zeros((NODES, 128), F32)) * wall_ref[...]
    for j in range(PLANE // 128):
        at = pl.ds(j * 128, 128)
        if j * 128 < HALF:
            radial = in_right_ref[s, :, at]
        else:
            back = pl.ds(j * 128 - HALF, 128)
            radial = in_left_ref[s, :, back] + in_turned_ref[s, :, back]
        axial = jnp.where(own, strength * rows_ref[2:3, at], in_axial_ref[s, :, at])
        rows = jnp.concatenate([rows_ref[0:1, at] * radial, axial, jnp.zeros((8, 128), F32)], axis=0)
        ghost_ref[:, at] = rows.astype(BF16)


def outer_kernel(count, part_count, last, order, codes, *refs):
    part_refs, refs = refs[:part_count], refs[part_count:]
    f_ref, inner_ref, in_left_ref, in_turned_ref, in_right_ref, in_axial_ref = refs[:6]
    rows_ref, edge_ref, ghost_r_ref, ghost_z_ref = refs[6:10]
    refs = refs[10:]
    if last:
        (out_ref, mom_ref), refs = refs[:2], refs[2:]
    else:
        (trace_ref, mirror_ref, out_ref, right_ref, left_ref, turned_ref, axial_ref, mom_ref), refs = refs[:8], refs[8:]
        narrow_ref, refs = refs[0], refs[1:]
    plane_ref, node_ref, wall_ref, slot_ref, work_ref, sums_ref, lhs_ref, ghost_ref, table_ref = refs
    step = pl.program_id(0)
    row, place = places_of()

    @pl.when(step == 0)
    def _():
        clear_sums(sums_ref)
        total = total_of([p[...] for p in part_refs])
        prepare_nodes(total, codes, place, rows_ref, edge_ref, table_ref, node_ref, wall_ref, plane_ref)

    speeds = [slot_speed(order, step * count + s) for s in range(count)]
    for s in range(count):
        vz = speeds[s]
        for k, value in enumerate(slot_factors(vz, node_ref)):
            slot_ref[s, k] = value
        ghost_lifts(vz, ghost_r_ref, ghost_z_ref, lhs_ref)
        ghost_rows(
            s, vz, place, in_left_ref, in_turned_ref, in_right_ref, in_axial_ref, rows_ref, wall_ref, ghost_ref
        )
        for first, lanes, side in PIECES:
            work_ref[s, :, first : first + lanes] = dot(
                lhs_ref[side, :, 0:GHOST_ROWS], ghost_ref[:, first : first + lanes]
            )

    def update(r, carry):
        rows = pl.ds(pl.multiple_of(r * LOCAL_Z, LOCAL_Z), LOCAL_Z)
        keep = node_ref[5, rows, :]
        factor = [[slot_ref[s, k, rows, :] for k in range(4)] for s in range(count)]
        for j in range(PLANE // 128):
            at = pl.ds(j * 128, 128)
            planes = [plane_ref[k, rows, at] for k in range(4)]
            sums = [sums_ref[k, r, :, at] for k in range(5)]
            for s in range(count):
                here = pl.ds(s * PLANE + j * 128, 128)
                new = f_ref[r, :, here] * keep + work_ref[s, rows, at] + inner_ref[r, :, here].astype(F32)
                for k in range(4):
                    new = new + planes[k] * factor[s][k]
                out_ref[r, :, here] = new
                sums = add_speed_sums(new, speeds[s], sums)
                if not last:
                    narrow_ref[s, rows, at] = new.astype(BF16)
            for k in range(5):
                sums_ref[k, r, :, at] = sums[k]
        return carry

    lax.fori_loop(0, NODES, update, 0)
    if not last:
        send_traces(count, place, narrow_ref, trace_ref, right_ref, left_ref, axial_ref)
        turn_traces(count, row, mirror_ref, left_ref, turned_ref)

    @pl.when(step == pl.num_programs(0) - 1)
    def _():
        finish_moments(sums_ref, rows_ref, table_ref, mom_ref)


def last_kernel(part_count, codes, *refs):
    total_ref = total_of([p[...] for p in refs[:part_count]])
    edge_ref, macro_ref, flux_ref = refs[part_count:]
    row, place = places_of()
    values = macroscopic_of(lambda k: total_ref[k : k + 1, :])
    for k in range(8):
        for r in range(NODES):
            macro_ref[k, r : r + 1, :] = values[k][:, r * LOCAL_Z : (r + 1) * LOCAL_Z]
    net, gross = total_ref[3:4, :], total_ref[13:14, :]
    to_bottom = jnp.broadcast_to(0.5 * (gross - net), (8, 128))
    to_top = jnp.broadcast_to(0.5 * (gross + net), (8, 128))
    exact = lambda x, y: jnp.dot(x, y, precision=lax.Precision.HIGHEST, preferred_element_type=F32)
    incident = exact(to_bottom, edge_ref[0])
    upward = exact(to_top, edge_ref[1])
    downward = exact(to_bottom, edge_ref[1])
    bottom = jnp.where(codes[0, 0] == 1, SAT_DENSITY * HALF_FLUX - incident, 0.0)
    top = jnp.where(codes[1, 0] == 2, upward - downward, 0.0)
    flux_ref[...] = jnp.where(place == 0, bottom, top)[0:1, 0:NODES]


def whole(shape):
    return pl.BlockSpec(shape, lambda *a: (0,) * len(shape), pipeline_mode=pl.Buffered(1))


def on_device(distribution, z_order, edge_codes):
    local_r, local_z, vdev = distribution.shape
    assert local_r == NODES and local_z == LOCAL_Z
    slots = vdev // PLANE
    group = math.gcd(slots, 3)
    steps = slots // group
    rows_total = lax.axis_size("row")
    verts = lax.axis_size("vert")
    assert lax.axis_size("gz") == 2
    rows, pos, edge = jnp.asarray(ROWS), jnp.asarray(NODE_POS), jnp.asarray(EDGE)
    radial_m, axial_m = jnp.asarray(RADIAL_M), jnp.asarray(AXIAL_M)
    ghost_r, ghost_z = jnp.asarray(GHOST_R), jnp.asarray(GHOST_Z)
    trace_m, mirror_m, rot_m = jnp.asarray(TRACE_M), jnp.asarray(MIRROR_M), jnp.asarray(ROTATION_M)

    big = pl.BlockSpec((NODES, LOCAL_Z, group * PLANE), lambda i, *n: (0, 0, i))
    radial_spec = pl.BlockSpec((group, LOCAL_Z, HALF), lambda i, *n: (i, 0, 0))
    axial_spec = pl.BlockSpec((group, NODES, PLANE), lambda i, *n: (i, 0, 0))
    mom_spec = whole((MOMENTS, 128))
    radial_shape = jax.ShapeDtypeStruct((slots, LOCAL_Z, HALF), F32)
    axial_shape = jax.ShapeDtypeStruct((slots, NODES, PLANE), F32)
    mom_shape = jax.ShapeDtypeStruct((MOMENTS, 128), F32)
    big_shape = jax.ShapeDtypeStruct(distribution.shape, F32)
    trace_specs = [radial_spec, radial_spec, radial_spec, axial_spec]
    trace_shapes = [radial_shape, radial_shape, radial_shape, axial_shape]
    ghost_specs = [radial_spec, radial_spec, radial_spec, axial_spec]
    square = pltpu.VMEM((NODE_COUNT, 128), F32)
    sums_scratch = pltpu.VMEM((5, NODES, LOCAL_Z, PLANE), F32)
    narrow_scratch = pltpu.VMEM((group, NODE_COUNT, PLANE), BF16)
    node_scratch = [
        pltpu.VMEM((4, NODE_COUNT, PLANE), F32),
        pltpu.VMEM((10, NODE_COUNT, 128), F32),
        pltpu.VMEM((NODES, 128), F32),
    ]
    ghost_scratch = [
        pltpu.VMEM((2, NODE_COUNT, 128), BF16),
        pltpu.VMEM((GHOST_ROWS, PLANE), BF16),
        square,
    ]

    def call(body, name, in_specs, out_specs, out_shape, scratch, args):
        return pl.pallas_call(
            body,
            grid_spec=pltpu.PrefetchScalarGridSpec(
                num_scalar_prefetch=2,
                grid=(steps,),
                in_specs=in_specs,
                out_specs=out_specs,
                scratch_shapes=scratch,
            ),
            out_shape=out_shape,
            compiler_params=pltpu.CompilerParams(vmem_limit_bytes=56 * 1024 * 1024),
            name=name,
        )(z_order, edge_codes, *args)

    def all_whole(tables):
        return [whole(x.shape) for x in tables]

    def first(f):
        tables = [rows, trace_m, mirror_m]
        return call(
            lambda *a: first_kernel(group, *a), "moments_and_traces", [big] + all_whole(tables),
            trace_specs + [mom_spec], trace_shapes + [mom_shape], [sums_scratch, square], [f] + tables,
        )

    def inner(f):
        tables = [rows, pos, radial_m, axial_m, rot_m]
        scratch = [
            square,
            pltpu.VMEM((group, NODE_COUNT, PLANE + 256), BF16),
            pltpu.VMEM((group, 2, 2 * NODE_COUNT, 128), BF16),
        ]
        return call(
            lambda *a: inner_kernel(group, *a), "inner_increments", [big] + all_whole(tables),
            [big], [jax.ShapeDtypeStruct(f.shape, BF16)], scratch, [f] + tables,
        )[0]

    def outer(f, change, ghosts, parts, last):
        tables = [rows, edge, ghost_r, ghost_z] + ([] if last else [trace_m, mirror_m])
        scratch = node_scratch + [
            pltpu.VMEM((group, 4, NODE_COUNT, 128), F32),
            pltpu.VMEM((group, NODE_COUNT, PLANE), F32),
            sums_scratch,
        ]
        return call(
            lambda *a: outer_kernel(group, len(parts), last, *a),
            "last_update" if last else "update",
            [mom_spec] * len(parts) + [big, big] + ghost_specs + all_whole(tables),
            [big] + ([] if last else trace_specs) + [mom_spec],
            [big_shape] + ([] if last else trace_shapes) + [mom_shape],
            ([] if last else [narrow_scratch]) + scratch + ghost_scratch,
            [*parts, f, change, *ghosts, *tables],
        )

    def spread(moments):
        parts = [moments]
        for shift in range(1, verts):
            parts.append(lax.ppermute(moments, "vert", [(i, i ^ shift) for i in range(verts)]))
        return parts

    def halo(right, left, turned, axial):
        from_axial = lax.ppermute(axial, "gz", [(0, 1), (1, 0)])
        from_left = lax.ppermute(right, "row", [(i, i + 1) for i in range(rows_total - 1)])
        from_right = lax.ppermute(left, "row", [(i + 1, i) for i in range(rows_total - 1)])
        return from_left, turned, from_right, from_axial

    current = distribution
    *traces, moments = first(current)
    for number in range(STEPS):
        last = number == STEPS - 1
        ghosts = halo(*traces)
        parts = spread(moments)
        change = inner(current)
        current, *traces, moments = outer(current, change, ghosts, parts, last)
    parts = spread(moments)
    macro, flux = pl.pallas_call(
        lambda *a: last_kernel(len(parts), *a),
        grid_spec=pltpu.PrefetchScalarGridSpec(
            num_scalar_prefetch=1,
            grid=(1,),
            in_specs=[mom_spec] * len(parts) + [whole(edge.shape)],
            out_specs=[whole((8, NODES, LOCAL_Z)), whole((1, NODES))],
        ),
        out_shape=[
            jax.ShapeDtypeStruct((8, NODES, LOCAL_Z), F32),
            jax.ShapeDtypeStruct((1, NODES), F32),
        ],
        name="macroscopic",
    )(edge_codes, *parts, edge)
    return (current, macro, flux)


def solution(mesh):
    in_specs = (P("row", "gz", "vert"), P("vert"), P(None, "row"))
    out_specs = (P("row", "gz", "vert"), P(None, "row", "gz"), P("gz", "row"))
    return jax.shard_map(
        on_device, mesh=mesh, in_specs=in_specs, out_specs=out_specs, check_vma=False
    )
```

```python
import math

import jax
import jax.numpy as jnp
import ml_dtypes
import numpy as np
from jax import lax
from jax.experimental import pallas as pl
from jax.experimental.pallas import tpu as pltpu
from jax.sharding import PartitionSpec as P

NODES = 8
NVR = 48
NVT = 48
NVZ = 48
STEPS = 2

ELEMENT_WIDTH = 4.0
TIME_STEP = 0.001
KNUDSEN = 0.005
VISCOUS_RATIO = 2.0 / 3.0
SAT_DENSITY = 1.5
SPEED_LIMIT = 5.0

PLANE = NVR * NVT
HALF = PLANE // 2
LOCAL_Z = 2 * NODES
NODE_COUNT = NODES * LOCAL_Z
TILE = 256
CHUNK = 384
CHUNKS = PLANE // CHUNK
WINDOW = 512
GHOST_ROWS = 32
MOMENTS = 16
F32 = jnp.float32
BF16 = jnp.bfloat16
PIECES = [(t, TILE, 0) for t in range(0, 1024, TILE)] + [(1024, 128, 0), (1152, 128, 1)] + [
    (t, TILE, 1) for t in range(1280, PLANE, TILE)
]


def legendre_pair(position, point_count):
    previous = 1.0
    current = position
    for degree in range(2, point_count + 1):
        previous, current = (
            current,
            ((2 * degree - 1) * position * current - (degree - 1) * previous) / degree,
        )
    slope = point_count * (position * current - previous) / (position * position - 1.0)
    return (current, slope)


def dg_tables(point_count):
    point_list = []
    weight_list = []
    for number in range(point_count):
        position = math.cos(math.pi * (number + 0.75) / (point_count + 0.5))
        for sweep in range(60):
            value, slope = legendre_pair(position, point_count)
            position = position - value / slope
        value, slope = legendre_pair(position, point_count)
        point_list.append(position)
        weight_list.append(2.0 / ((1.0 - position * position) * slope * slope))
    point_list = point_list[::-1]
    weight_list = weight_list[::-1]
    points = np.array(point_list)
    derivative = np.zeros((point_count, point_count))
    right = np.zeros(point_count)
    left = np.zeros(point_count)
    products = [
        np.prod([points[i] - points[j] for j in range(point_count) if j != i])
        for i in range(point_count)
    ]
    for i in range(point_count):
        others = [j for j in range(point_count) if j != i]
        derivative[i, i] = sum(1.0 / (points[i] - points[j]) for j in others)
        for j in others:
            derivative[i, j] = products[i] / products[j] / (points[i] - points[j])
        right[i] = np.prod([1.0 - points[j] for j in others]) / products[i]
        left[i] = np.prod([-1.0 - points[j] for j in others]) / products[i]
    return points, np.array(weight_list), derivative, right, left


def speed_grid(point_count):
    return -SPEED_LIMIT + (np.arange(point_count) + 0.5) * (2.0 * SPEED_LIMIT / point_count)


POINTS, QUAD, DERIV, END_R, END_L = dg_tables(NODES)
LIFT_R = END_R / QUAD
LIFT_L = END_L / QUAD
GRID_R = speed_grid(NVR)
GRID_T = speed_grid(NVT)
GRID_Z = speed_grid(NVZ)
STEP_V = 2 * SPEED_LIMIT / NVR
WEIGHT = STEP_V**3 / (2 * math.pi) ** 1.5
HALF_FLUX = float(
    WEIGHT
    * np.sum(np.exp(-(GRID_R**2) / 2))
    * np.sum(np.exp(-(GRID_T**2) / 2))
    * np.sum(np.maximum(GRID_Z, 0.0) * np.exp(-(GRID_Z**2) / 2))
)
SCALE = TIME_STEP * 2.0 / ELEMENT_WIDTH


def transport_tables():
    ident = np.eye(NODES)
    up = DERIV + np.outer(LIFT_L, END_L)
    down = DERIV - np.outer(LIFT_R, END_R)
    zero = np.zeros((NODES, NODES))
    wide = np.eye(LOCAL_Z)
    radial = np.stack([np.kron(down, wide), np.kron(up, wide), np.kron(DERIV, wide)])
    zup = np.block([[up, zero], [-np.outer(LIFT_L, END_R), up]])
    zdown = np.block([[down, np.outer(LIFT_R, END_L)], [zero, down]])
    zout = np.block([[down, np.outer(LIFT_R, END_L)], [zero, DERIV]])
    axial = np.stack([np.kron(ident, zdown), np.kron(ident, zup), np.kron(ident, zout)])
    ghost_r = np.zeros((2, NODE_COUNT, 128))
    ghost_z = np.zeros((2, NODE_COUNT, 128))
    for r in range(NODES):
        for z in range(LOCAL_Z):
            n = r * LOCAL_Z + z
            ghost_r[0, n, z] = -LIFT_R[r]
            ghost_r[1, n, z] = LIFT_L[r]
            if z >= NODES:
                ghost_z[0, n, LOCAL_Z + r] = LIFT_R[z - NODES]
            else:
                ghost_z[1, n, LOCAL_Z + r] = LIFT_L[z]
    trace = np.zeros((2, 2, GHOST_ROWS, NODE_COUNT))
    for side in range(2):
        radial_row = END_R if side == 1 else END_L
        for place in range(2):
            for z in range(LOCAL_Z):
                for r in range(NODES):
                    trace[side, place, z, r * LOCAL_Z + z] = radial_row[r]
            for r in range(NODES):
                for k in range(NODES):
                    if place == 0:
                        trace[side, place, LOCAL_Z + r, r * LOCAL_Z + NODES + k] = END_R[k]
                    else:
                        trace[side, place, LOCAL_Z + r, r * LOCAL_Z + k] = END_L[k]
    return (
        (-SCALE * radial).astype(ml_dtypes.bfloat16),
        (-SCALE * axial).astype(np.float32),
        (SCALE * ghost_r).astype(np.float32),
        (SCALE * ghost_z).astype(np.float32),
        trace.astype(ml_dtypes.bfloat16),
    )


def rotation_table():
    full = np.zeros((PLANE + 2 * TILE, PLANE))
    factor = TIME_STEP / (2 * STEP_V)
    for a in range(NVR):
        for b in range(NVT):
            n = a * NVT + b
            first = factor * GRID_T[b] * GRID_T[b]
            second = factor * GRID_R[a] * GRID_T[b]
            if a + 1 < NVR:
                full[TILE + n + NVT, n] = -first
            if a > 0:
                full[TILE + n - NVT, n] = first
            if b + 1 < NVT:
                full[TILE + n + 1, n] = second
            if b > 0:
                full[TILE + n - 1, n] = -second
    tiles = [full[TILE + t - 128 : TILE + t - 128 + WINDOW, t : t + TILE] for t in range(0, PLANE, TILE)]
    return np.stack(tiles).astype(ml_dtypes.bfloat16)


def mirror_table():
    table = np.zeros((HALF, HALF))
    groups = NVR // 2
    for g in range(groups):
        for b in range(NVT):
            table[(groups - 1 - g) * NVT + b, g * NVT + b] = 1.0
    return table.astype(ml_dtypes.bfloat16)


def plane_rows():
    vr = np.repeat(GRID_R, NVT)
    vt = np.tile(GRID_T, NVR)
    rows = np.zeros((8, PLANE))
    rows[0] = vr
    rows[1] = vt
    rows[2] = np.exp(-(vr**2 + vt**2) / 2)
    return rows.astype(np.float32)


def edge_table():
    table = np.zeros((2, NODE_COUNT, 128))
    for r in range(NODES):
        for k in range(NODES):
            table[0, r * LOCAL_Z + k, r] = END_L[k]
            table[1, r * LOCAL_Z + NODES + k, r] = END_R[k]
    return table.astype(np.float32)


def node_columns():
    table = np.zeros((NODE_COUNT, 128))
    for r in range(NODES):
        table[r * LOCAL_Z : (r + 1) * LOCAL_Z, :] = (1.0 + POINTS[r]) / 2
    return table.astype(np.float32)


RADIAL_M, AXIAL_M, GHOST_R, GHOST_Z, TRACE_M = transport_tables()
ROTATION_M = rotation_table()
MIRROR_M = mirror_table()
ROWS = plane_rows()
EDGE = edge_table()
NODE_POS = node_columns()


def slot_speed(order, slot):
    return (order[slot].astype(F32) + 0.5) * (2 * SPEED_LIMIT / NVZ) - SPEED_LIMIT


def dot(x, y):
    return jnp.dot(x, y, preferred_element_type=F32)


def macroscopic_of(m):
    rho = m(0)
    inv = 1.0 / rho
    ur, ut, uz = m(1) * inv, m(2) * inv, m(3) * inv
    rr, tt, rt, zz, rz, tz = (m(k) for k in range(4, 10))
    energy = rr + tt + zz
    speed = ur * ur + ut * ut + uz * uz
    temp = (energy * inv - speed) * (1.0 / 3.0)
    tail = 2.0 * rho * speed - energy
    qr = 0.5 * (m(10) - 2.0 * (ur * rr + ut * rt + uz * rz) + ur * tail)
    qt = 0.5 * (m(11) - 2.0 * (ur * rt + ut * tt + uz * tz) + ut * tail)
    qz = 0.5 * (m(12) - 2.0 * (ur * rz + ut * tz + uz * zz) + uz * tail)
    return rho, ur, ut, uz, temp, qr, qt, qz


def add_speed_sums(field, vz, sums):
    one = field * vz
    two = one * vz
    return [
        sums[0] + field,
        sums[1] + one,
        sums[2] + two,
        sums[3] + two * vz,
        sums[4] + field * jnp.abs(vz),
    ]


def add_moments(acc, vr, vt, sums):
    g0, g1, g2, g3, g4 = sums
    a = vr * g0
    b = vt * g0
    aa = vr * a
    bb = vt * b
    c = vr * g1
    d = vt * g1
    perp = aa + bb + g2
    new = [g0, a, b, g1, aa, bb, vr * b, g2, c, d, vr * perp, vt * perp, vr * c + vt * d + g3, g4]
    return new if acc is None else [x + y for x, y in zip(acc, new)]


def finish_moments(sums_ref, table_ref, out_ref):
    lane = lax.broadcasted_iota(jnp.int32, (LOCAL_Z, 128), 1)

    def one_radius(r, carry):
        rows = radius_rows(r)
        block = jnp.zeros((LOCAL_Z, 128), F32)
        for k in range(14):
            block = jnp.where(lane == k, WEIGHT * jnp.sum(sums_ref[k, rows, :], axis=1, keepdims=True), block)
        table_ref[rows, :] = block
        return carry

    lax.fori_loop(0, NODES, one_radius, 0)
    out_ref[...] = jnp.transpose(table_ref[...])[0:MOMENTS, :]


def radius_rows(r):
    return pl.ds(pl.multiple_of(r * LOCAL_Z, LOCAL_Z), LOCAL_Z)


def clear_sums(sums_ref):
    sums_ref[...] = jnp.zeros(sums_ref.shape, F32)


def places_of():
    return lax.axis_index("row"), lax.axis_index("gz")


def send_traces(count, step, place, narrow_ref, trace_ref, right_ref, left_ref, axial_ref, mirrored_ref):
    for side in range(2):

        @pl.when((step >= CHUNKS // 2) == (side == 1))
        def _():
            for s in range(count):
                got = dot(trace_ref[side, place], narrow_ref[s])
                axial_ref[s] = got[LOCAL_Z : LOCAL_Z + NODES]
                if side == 1:
                    right_ref[s] = got[0:LOCAL_Z]
                else:
                    left_ref[s] = got[0:LOCAL_Z]
                    at = pl.ds(pl.multiple_of(step * CHUNK, CHUNK), CHUNK)
                    mirrored_ref[s * LOCAL_Z : (s + 1) * LOCAL_Z, at] = got[0:LOCAL_Z].astype(BF16)


def turn_traces(count, row, mirror_ref, mirrored_ref, turned_ref):
    @pl.when(row == 0)
    def _():
        for first in range(0, HALF, 128):
            low = max(0, (HALF - first - 128 - 48) // 128 * 128)
            high = min(HALF, -((first - HALF - 48) // 128) * 128)
            got = dot(mirrored_ref[:, low:high], mirror_ref[low:high, first : first + 128])
            turned_ref[:, :, first : first + 128] = got.reshape(count, LOCAL_Z, 128)

    @pl.when(row != 0)
    def _():
        turned_ref[...] = jnp.zeros(turned_ref.shape, F32)


def first_kernel(count, order, codes, *refs):
    f_refs, refs = refs[:count], refs[count:]
    (
        rows_ref, trace_ref, mirror_ref, right_ref, left_ref, turned_ref, axial_ref, mom_ref,
        sums_ref, narrow_ref, mirrored_ref, table_ref,
    ) = refs
    step = pl.program_id(0)
    row, place = places_of()

    @pl.when(step == 0)
    def _():
        clear_sums(sums_ref)

    speeds = [slot_speed(order, s) for s in range(count)]

    def one_radius(r, carry):
        rows = radius_rows(r)
        acc = None
        for j in range(0, CHUNK, 128):
            at = pl.ds(j, 128)
            sums = [jnp.zeros((LOCAL_Z, 128), F32) for _ in range(5)]
            for s in range(count):
                field = f_refs[s][r, :, at]
                sums = add_speed_sums(field, speeds[s], sums)
                narrow_ref[s, rows, at] = field.astype(BF16)
            acc = add_moments(acc, rows_ref[0:1, at], rows_ref[1:2, at], sums)
        for k in range(14):
            sums_ref[k, rows, :] += acc[k]
        return carry

    lax.fori_loop(0, NODES, one_radius, 0)
    send_traces(count, step, place, narrow_ref, trace_ref, right_ref, left_ref, axial_ref, mirrored_ref)

    @pl.when(step == CHUNKS - 1)
    def _():
        turn_traces(count, row, mirror_ref, mirrored_ref, turned_ref)
        finish_moments(sums_ref, table_ref, mom_ref)


def inner_kernel(
    count, split, order, codes, f_ref, rows_ref, pos_ref, radial_ref, axial_m_ref, rot_ref,
    out_ref, inverse_ref, pad_ref, lhs_ref,
):
    def nodes_of(s, first, lanes):
        if split:
            return f_ref[s, :, :, first : first + lanes].reshape(NODE_COUNT, lanes)
        return f_ref[:, :, s * PLANE + first : s * PLANE + first + lanes].reshape(NODE_COUNT, lanes)

    step = pl.program_id(0)
    row, place = places_of()

    @pl.when(step == 0)
    def _():
        pad_ref[:, :, 0:128] = jnp.zeros((count, NODE_COUNT, 128), BF16)
        pad_ref[:, :, 128 + PLANE :] = jnp.zeros((count, NODE_COUNT, 128), BF16)
        inverse_ref[...] = 1.0 / (ELEMENT_WIDTH * (row.astype(F32) + pos_ref[...]))
        minus = radial_ref[jnp.where(row == lax.axis_size("row") - 1, 2, 0)]
        for s in range(count):
            lhs_ref[s, 0, 0:NODE_COUNT] = minus
            lhs_ref[s, 1, 0:NODE_COUNT] = radial_ref[1]

    kind_out = jnp.where(jnp.logical_and(place == 1, codes[1, 0] == 2), 2, 0)
    inverse = inverse_ref[...]
    for s in range(count):
        vz = slot_speed(order, step * count + s)
        axial = (vz * axial_m_ref[jnp.where(vz > 0, 1, kind_out)]).astype(BF16)
        lhs_ref[s, 0, NODE_COUNT:] = axial
        lhs_ref[s, 1, NODE_COUNT:] = axial
        for j in range(PLANE // 128):
            field = nodes_of(s, j * 128, 128)
            pad_ref[s, :, 128 + j * 128 : 256 + j * 128] = (field * inverse).astype(BF16)

    for tile in range(PLANE // TILE):
        start = tile * TILE
        turned = dot(pad_ref[:, :, start : start + WINDOW].reshape(count * NODE_COUNT, WINDOW), rot_ref[tile])
        for first, lanes, side in PIECES:
            if first // TILE != tile:
                continue
            vr = rows_ref[0:1, first : first + lanes]
            inside = first - start
            for s in range(count):
                moved = dot(lhs_ref[s, side], nodes_of(s, first, lanes).astype(BF16))
                change = turned[s * NODE_COUNT : (s + 1) * NODE_COUNT, inside : inside + lanes]
                change = change + vr * moved[0:NODE_COUNT] + moved[NODE_COUNT:]
                out_ref[s, :, :, first : first + lanes] = change.astype(BF16).reshape(NODES, LOCAL_Z, lanes)


def total_of(parts_ref):
    parts = [parts_ref[k : k + MOMENTS, :] for k in range(0, parts_ref.shape[0], MOMENTS)]
    while len(parts) > 1:
        parts = [parts[k] + parts[k + 1] for k in range(0, len(parts), 2)]
    return parts[0]


def prepare_nodes(total, codes, place, edge_ref, table_ref, node_ref, wall_ref):
    wide = jnp.concatenate([total, jnp.zeros((128 - MOMENTS, 128), F32)], axis=0)
    table_ref[...] = jnp.transpose(wide)
    rho, ur, ut, uz, temp, qr, qt, qz = macroscopic_of(lambda k: table_ref[:, k : k + 1])
    inv_t = 1.0 / temp
    beta = ((1.0 - VISCOUS_RATIO) / 5.0) / (rho * temp * temp)
    kappa = rho * (TIME_STEP / KNUDSEN)
    peak = kappa * rho * inv_t * jnp.sqrt(inv_t)
    columns = [uz, -0.5 * inv_t, qz * beta, inv_t, peak, 1.0 - kappa, ur, ut, qr * beta, qt * beta]
    for k, column in enumerate(columns):
        node_ref[k] = jnp.broadcast_to(column, (NODE_COUNT, 128))
    net = table_ref[:, 3:4]
    gross = table_ref[:, 13:14]
    to_bottom = 0.5 * (gross - net)
    to_top = 0.5 * (gross + net)
    incident = jnp.sum(edge_ref[0] * to_bottom, axis=0, keepdims=True)
    upward = jnp.sum(edge_ref[1] * to_top, axis=0, keepdims=True)
    bottom = jnp.where(codes[0, 0] == 1, SAT_DENSITY, incident * (1.0 / HALF_FLUX))
    top = jnp.where(codes[1, 0] == 2, 0.0, upward * (1.0 / HALF_FLUX))
    density = jnp.where(place == 0, bottom, top)
    wall_ref[...] = jnp.transpose(jnp.broadcast_to(density, (128, 128)))[0:NODES, :]


def slot_factors(vz, node_ref):
    cz = vz - node_ref[0]
    square = cz * cz
    return node_ref[4] * jnp.exp(square * node_ref[1]), cz * node_ref[2], square * node_ref[3] - 5.0


def ghost_lifts(vz, ghost_r_ref, ghost_z_ref, lhs_ref, s):
    lean = jnp.abs(vz) * ghost_z_ref[jnp.where(vz > 0, 1, 0)]
    lhs_ref[s, 0] = (ghost_r_ref[0] + lean).astype(BF16)
    lhs_ref[s, 1] = (ghost_r_ref[1] + lean).astype(BF16)


def outer_kernel(count, split, last, order, codes, parts_ref, *refs):
    if split:
        f_ref, refs = refs[0], refs[1:]
        field_of = lambda s, r, at: f_ref[s, r, :, at]
    else:
        f_refs, refs = refs[:count], refs[count:]
        field_of = lambda s, r, at: f_refs[s][r, :, at]
    inner_ref, in_left_ref, in_turned_ref, in_right_ref, in_axial_ref = refs[:5]
    rows_ref, edge_ref, ghost_r_ref, ghost_z_ref = refs[5:9]
    refs = refs[9:]
    if last:
        (out_hbm, mom_ref, out_buf, out_sem), refs = refs[:4], refs[4:]
    else:
        (trace_ref, mirror_ref, out_ref, right_ref, left_ref, turned_ref, axial_ref, mom_ref), refs = refs[:8], refs[8:]
        (narrow_ref, mirrored_ref), refs = refs[:2], refs[2:]
    node_ref, wall_ref, slot_ref, work_ref, sums_ref, lhs_ref, ghost_ref, table_ref = refs
    step = pl.program_id(0)
    row, place = places_of()
    speeds = [slot_speed(order, s) for s in range(count)]

    @pl.when(step == 0)
    def _():
        clear_sums(sums_ref)
        prepare_nodes(total_of(parts_ref), codes, place, edge_ref, table_ref, node_ref, wall_ref)
        for s in range(count):
            for k, value in enumerate(slot_factors(speeds[s], node_ref)):
                slot_ref[s, k] = value
            ghost_lifts(speeds[s], ghost_r_ref, ghost_z_ref, lhs_ref, s)

    side = jnp.where(step >= CHUNKS // 2, 1, 0)
    inward = step < CHUNKS // 2
    for s in range(count):
        vz = speeds[s]
        own = (place == 0) == (vz > 0)
        strength = jnp.exp(-0.5 * vz * vz + jnp.zeros((NODES, 128), F32)) * wall_ref[...]
        for j in range(0, CHUNK, 128):
            at = pl.ds(j, 128)
            radial = jnp.where(inward, in_right_ref[s, :, at], in_left_ref[s, :, at] + in_turned_ref[s, :, at])
            axial = jnp.where(own, strength * rows_ref[2:3, at], in_axial_ref[s, :, at])
            rows = jnp.concatenate([rows_ref[0:1, at] * radial, axial, jnp.zeros((8, 128), F32)], axis=0)
            ghost_ref[s, :, at] = rows.astype(BF16)
        work_ref[s] = dot(lhs_ref[s, side, :, 0:GHOST_ROWS], ghost_ref[s])

    def copy_out(s, chunk):
        at = pl.ds(pl.multiple_of(s * PLANE + chunk * CHUNK, CHUNK), CHUNK)
        slot = lax.rem(chunk, 2)
        return pltpu.make_async_copy(out_buf.at[slot, s], out_hbm.at[:, :, at], out_sem.at[slot, s])

    if last:

        @pl.when(step >= 2)
        def _():
            for s in range(count):
                copy_out(s, step - 2).wait()

        buffer = lax.rem(step, 2)

    def update(r, carry):
        rows = radius_rows(r)
        acc = None
        for j in range(0, CHUNK, 128):
            at = pl.ds(j, 128)
            vr, vt = rows_ref[0:1, at], rows_ref[1:2, at]
            cr = vr - node_ref[6, rows, :]
            ct = vt - node_ref[7, rows, :]
            square = cr * cr + ct * ct
            gauss = jnp.exp(square * node_ref[1, rows, :])
            along = cr * node_ref[8, rows, :] + ct * node_ref[9, rows, :]
            reach = square * node_ref[3, rows, :]
            keep = node_ref[5, rows, :]
            sums = [jnp.zeros((LOCAL_Z, 128), F32) for _ in range(5)]
            for s in range(count):
                new = field_of(s, r, at) * keep + work_ref[s, rows, at] + inner_ref[s, r, :, at].astype(F32)
                bend = (along + slot_ref[s, 1, rows, :]) * (reach + slot_ref[s, 2, rows, :]) + 1.0
                new = new + (gauss * slot_ref[s, 0, rows, :]) * bend
                if last:
                    out_buf[buffer, s, r, :, at] = new
                else:
                    out_ref[s, r, :, at] = new
                    narrow_ref[s, rows, at] = new.astype(BF16)
                sums = add_speed_sums(new, speeds[s], sums)
            acc = add_moments(acc, vr, vt, sums)
        for k in range(14):
            sums_ref[k, rows, :] += acc[k]
        return carry

    lax.fori_loop(0, NODES, update, 0)
    if last:
        for s in range(count):
            copy_out(s, step).start()

        @pl.when(step == CHUNKS - 1)
        def _():
            for s in range(count):
                copy_out(s, step - 1).wait()
                copy_out(s, step).wait()

    else:
        send_traces(count, step, place, narrow_ref, trace_ref, right_ref, left_ref, axial_ref, mirrored_ref)

    @pl.when(step == CHUNKS - 1)
    def _():
        if not last:
            turn_traces(count, row, mirror_ref, mirrored_ref, turned_ref)
        finish_moments(sums_ref, table_ref, mom_ref)


def last_kernel(codes, parts_ref, edge_ref, macro_ref, flux_ref):
    total_ref = total_of(parts_ref)
    row, place = places_of()
    values = macroscopic_of(lambda k: total_ref[k : k + 1, :])
    for k in range(8):
        for r in range(NODES):
            macro_ref[k, r : r + 1, :] = values[k][:, r * LOCAL_Z : (r + 1) * LOCAL_Z]
    net, gross = total_ref[3:4, :], total_ref[13:14, :]
    to_bottom = jnp.broadcast_to(0.5 * (gross - net), (8, 128))
    to_top = jnp.broadcast_to(0.5 * (gross + net), (8, 128))
    exact = lambda x, y: jnp.dot(x, y, precision=lax.Precision.HIGHEST, preferred_element_type=F32)
    incident = exact(to_bottom, edge_ref[0])
    upward = exact(to_top, edge_ref[1])
    downward = exact(to_bottom, edge_ref[1])
    bottom = jnp.where(codes[0, 0] == 1, SAT_DENSITY * HALF_FLUX - incident, 0.0)
    top = jnp.where(codes[1, 0] == 2, upward - downward, 0.0)
    flux_ref[...] = jnp.where(place == 0, bottom, top)[0:1, 0:NODES]


def whole(shape):
    return pl.BlockSpec(shape, lambda *a: (0,) * len(shape), pipeline_mode=pl.Buffered(1))


def on_device(distribution, z_order, edge_codes):
    local_r, local_z, vdev = distribution.shape
    assert local_r == NODES and local_z == LOCAL_Z
    slots = vdev // PLANE
    group = math.gcd(slots, 3)
    steps = slots // group
    rows_total = lax.axis_size("row")
    verts = lax.axis_size("vert")
    assert lax.axis_size("gz") == 2
    rows, pos, edge = jnp.asarray(ROWS), jnp.asarray(NODE_POS), jnp.asarray(EDGE)
    radial_m, axial_m = jnp.asarray(RADIAL_M), jnp.asarray(AXIAL_M)
    ghost_r, ghost_z = jnp.asarray(GHOST_R), jnp.asarray(GHOST_Z)
    trace_m, mirror_m, rot_m = jnp.asarray(TRACE_M), jnp.asarray(MIRROR_M), jnp.asarray(ROTATION_M)

    everything = verts * MOMENTS
    slab = pl.BlockSpec((NODES, LOCAL_Z, group * PLANE), lambda i, *n: (0, 0, i))
    slot_slab = pl.BlockSpec((group, NODES, LOCAL_Z, PLANE), lambda i, *n: (i, 0, 0, 0))
    chunk_specs = [
        pl.BlockSpec((NODES, LOCAL_Z, CHUNK), lambda i, *n, s=s: (0, 0, s * CHUNKS + i)) for s in range(slots)
    ]
    slot_chunk = pl.BlockSpec((slots, NODES, LOCAL_Z, CHUNK), lambda i, *n: (0, 0, 0, i))
    half = CHUNKS // 2
    outward_spec = pl.BlockSpec((slots, LOCAL_Z, CHUNK), lambda i, *n: (0, 0, jnp.maximum(i - half, 0)))
    inward_spec = pl.BlockSpec((slots, LOCAL_Z, CHUNK), lambda i, *n: (0, 0, jnp.minimum(i, half - 1)))
    axial_spec = pl.BlockSpec((slots, NODES, CHUNK), lambda i, *n: (0, 0, i))
    rows_spec = pl.BlockSpec((8, CHUNK), lambda i, *n: (0, i))
    mom_spec = whole((MOMENTS, 128))
    radial_shape = jax.ShapeDtypeStruct((slots, LOCAL_Z, HALF), F32)
    axial_shape = jax.ShapeDtypeStruct((slots, NODES, PLANE), F32)
    mom_shape = jax.ShapeDtypeStruct((MOMENTS, 128), F32)
    inner_shape = (slots, NODES, LOCAL_Z, PLANE)
    trace_specs = [outward_spec, inward_spec, whole(radial_shape.shape), axial_spec]
    trace_shapes = [radial_shape, radial_shape, radial_shape, axial_shape]
    ghost_specs = [outward_spec, outward_spec, inward_spec, axial_spec]
    square = pltpu.VMEM((NODE_COUNT, 128), F32)
    sums_scratch = pltpu.VMEM((14, NODE_COUNT, 128), F32)
    trace_scratch = [
        pltpu.VMEM((slots, NODE_COUNT, CHUNK), BF16),
        pltpu.VMEM((slots * LOCAL_Z, HALF), BF16),
    ]

    def call(body, name, grid, in_specs, out_specs, out_shape, scratch, args):
        return pl.pallas_call(
            body,
            grid_spec=pltpu.PrefetchScalarGridSpec(
                num_scalar_prefetch=2,
                grid=(grid,),
                in_specs=in_specs,
                out_specs=out_specs,
                scratch_shapes=scratch,
            ),
            out_shape=out_shape,
            compiler_params=pltpu.CompilerParams(vmem_limit_bytes=56 * 1024 * 1024),
            name=name,
        )(z_order, edge_codes, *args)

    def all_whole(tables):
        return [whole(x.shape) for x in tables]

    def first(f):
        return call(
            lambda *a: first_kernel(slots, *a), "moments_and_traces", CHUNKS,
            chunk_specs + [rows_spec] + all_whole([trace_m, mirror_m]),
            trace_specs + [mom_spec], trace_shapes + [mom_shape],
            [sums_scratch] + trace_scratch + [square],
            [f] * slots + [rows, trace_m, mirror_m],
        )

    def inner(f, split):
        tables = [rows, pos, radial_m, axial_m, rot_m]
        scratch = [
            square,
            pltpu.VMEM((group, NODE_COUNT, PLANE + 256), BF16),
            pltpu.VMEM((group, 2, 2 * NODE_COUNT, 128), BF16),
        ]
        return call(
            lambda *a: inner_kernel(group, split, *a), "inner_increments", steps,
            [slot_slab if split else slab] + all_whole(tables),
            [slot_slab], [jax.ShapeDtypeStruct(inner_shape, BF16)], scratch, [f] + tables,
        )[0]

    def outer(f, split, change, ghosts, parts, last):
        more = [] if last else [trace_m, mirror_m]
        if last:
            outs = [pl.BlockSpec(memory_space=pl.ANY)]
            out_shapes = [jax.ShapeDtypeStruct(distribution.shape, F32)]
            scratch = [
                pltpu.VMEM((2, slots, NODES, LOCAL_Z, CHUNK), F32),
                pltpu.SemaphoreType.DMA((2, slots)),
            ]
        else:
            outs = [slot_chunk] + trace_specs
            out_shapes = [jax.ShapeDtypeStruct(inner_shape, F32)] + trace_shapes
            scratch = trace_scratch
        scratch = scratch + [
            pltpu.VMEM((10, NODE_COUNT, 128), F32),
            pltpu.VMEM((NODES, 128), F32),
            pltpu.VMEM((slots, 3, NODE_COUNT, 128), F32),
            pltpu.VMEM((slots, NODE_COUNT, CHUNK), F32),
            sums_scratch,
            pltpu.VMEM((slots, 2, NODE_COUNT, 128), BF16),
            pltpu.VMEM((slots, GHOST_ROWS, CHUNK), BF16),
            square,
        ]
        return call(
            lambda *a: outer_kernel(slots, split, last, *a),
            "last_update" if last else "update",
            CHUNKS,
            [whole((everything, 128))]
            + ([slot_chunk] if split else chunk_specs)
            + [slot_chunk] + ghost_specs + [rows_spec] + all_whole([edge, ghost_r, ghost_z] + more),
            outs + [mom_spec],
            out_shapes + [mom_shape],
            scratch,
            [parts] + [f] * (1 if split else slots) + [change, *ghosts, rows, edge, ghost_r, ghost_z] + more,
        )

    def spread(moments):
        return lax.all_gather(moments, "vert", tiled=True)

    def halo(right, left, turned, axial):
        from_axial = lax.ppermute(axial, "gz", [(0, 1), (1, 0)])
        from_left = lax.ppermute(right, "row", [(i, i + 1) for i in range(rows_total - 1)])
        from_right = lax.ppermute(left, "row", [(i + 1, i) for i in range(rows_total - 1)])
        return from_left, turned, from_right, from_axial

    current = distribution
    *traces, moments = first(current)
    for number in range(STEPS):
        last = number == STEPS - 1
        ghosts = halo(*traces)
        parts = spread(moments)
        change = inner(current, number > 0)
        current, *traces, moments = outer(current, number > 0, change, ghosts, parts, last)
    parts = spread(moments)
    macro, flux = pl.pallas_call(
        last_kernel,
        grid_spec=pltpu.PrefetchScalarGridSpec(
            num_scalar_prefetch=1,
            grid=(1,),
            in_specs=[whole((everything, 128)), whole(edge.shape)],
            out_specs=[whole((8, NODES, LOCAL_Z)), whole((1, NODES))],
        ),
        out_shape=[
            jax.ShapeDtypeStruct((8, NODES, LOCAL_Z), F32),
            jax.ShapeDtypeStruct((1, NODES), F32),
        ],
        name="macroscopic",
    )(edge_codes, parts, edge)
    return (current, macro, flux)


def solution(mesh):
    in_specs = (P("row", "gz", "vert"), P("vert"), P(None, "row"))
    out_specs = (P("row", "gz", "vert"), P(None, "row", "gz"), P("gz", "row"))
    return jax.shard_map(
        on_device, mesh=mesh, in_specs=in_specs, out_specs=out_specs, check_vma=False
    )
```

```python
import math

import jax
import jax.numpy as jnp
import ml_dtypes
import numpy as np
from jax import lax
from jax.experimental import pallas as pl
from jax.experimental.pallas import tpu as pltpu
from jax.sharding import PartitionSpec as P

NODES = 8
NVR = 48
NVT = 48
NVZ = 48
STEPS = 2

ELEMENT_WIDTH = 4.0
TIME_STEP = 0.001
KNUDSEN = 0.005
VISCOUS_RATIO = 2.0 / 3.0
SAT_DENSITY = 1.5
SPEED_LIMIT = 5.0

PLANE = NVR * NVT
HALF = PLANE // 2
LOCAL_Z = 2 * NODES
NODE_COUNT = NODES * LOCAL_Z
TILE = 256
CHUNK = 384
CHUNKS = PLANE // CHUNK
WINDOW = 512
GHOST_ROWS = 32
MOMENTS = 16
PARTS_W = 3
F32 = jnp.float32
BF16 = jnp.bfloat16
PIECES = [(t, TILE, 0) for t in range(0, 1024, TILE)] + [(1024, 128, 0), (1152, 128, 1)] + [
    (t, TILE, 1) for t in range(1280, PLANE, TILE)
]


def legendre_pair(position, point_count):
    previous = 1.0
    current = position
    for degree in range(2, point_count + 1):
        previous, current = (
            current,
            ((2 * degree - 1) * position * current - (degree - 1) * previous) / degree,
        )
    slope = point_count * (position * current - previous) / (position * position - 1.0)
    return (current, slope)


def dg_tables(point_count):
    point_list = []
    weight_list = []
    for number in range(point_count):
        position = math.cos(math.pi * (number + 0.75) / (point_count + 0.5))
        for sweep in range(60):
            value, slope = legendre_pair(position, point_count)
            position = position - value / slope
        value, slope = legendre_pair(position, point_count)
        point_list.append(position)
        weight_list.append(2.0 / ((1.0 - position * position) * slope * slope))
    point_list = point_list[::-1]
    weight_list = weight_list[::-1]
    points = np.array(point_list)
    derivative = np.zeros((point_count, point_count))
    right = np.zeros(point_count)
    left = np.zeros(point_count)
    products = [
        np.prod([points[i] - points[j] for j in range(point_count) if j != i])
        for i in range(point_count)
    ]
    for i in range(point_count):
        others = [j for j in range(point_count) if j != i]
        derivative[i, i] = sum(1.0 / (points[i] - points[j]) for j in others)
        for j in others:
            derivative[i, j] = products[i] / products[j] / (points[i] - points[j])
        right[i] = np.prod([1.0 - points[j] for j in others]) / products[i]
        left[i] = np.prod([-1.0 - points[j] for j in others]) / products[i]
    return points, np.array(weight_list), derivative, right, left


def speed_grid(point_count):
    return -SPEED_LIMIT + (np.arange(point_count) + 0.5) * (2.0 * SPEED_LIMIT / point_count)


POINTS, QUAD, DERIV, END_R, END_L = dg_tables(NODES)
LIFT_R = END_R / QUAD
LIFT_L = END_L / QUAD
GRID_R = speed_grid(NVR)
GRID_T = speed_grid(NVT)
GRID_Z = speed_grid(NVZ)
STEP_V = 2 * SPEED_LIMIT / NVR
WEIGHT = STEP_V**3 / (2 * math.pi) ** 1.5
HALF_FLUX = float(
    WEIGHT
    * np.sum(np.exp(-(GRID_R**2) / 2))
    * np.sum(np.exp(-(GRID_T**2) / 2))
    * np.sum(np.maximum(GRID_Z, 0.0) * np.exp(-(GRID_Z**2) / 2))
)
SCALE = TIME_STEP * 2.0 / ELEMENT_WIDTH


def transport_tables():
    ident = np.eye(NODES)
    up = DERIV + np.outer(LIFT_L, END_L)
    down = DERIV - np.outer(LIFT_R, END_R)
    zero = np.zeros((NODES, NODES))
    wide = np.eye(LOCAL_Z)
    radial = np.stack([np.kron(down, wide), np.kron(up, wide), np.kron(DERIV, wide)])
    zup = np.block([[up, zero], [-np.outer(LIFT_L, END_R), up]])
    zdown = np.block([[down, np.outer(LIFT_R, END_L)], [zero, down]])
    zout = np.block([[down, np.outer(LIFT_R, END_L)], [zero, DERIV]])
    axial = np.stack([np.kron(ident, zdown), np.kron(ident, zup), np.kron(ident, zout)])
    ghost_r = np.zeros((2, NODE_COUNT, 128))
    ghost_z = np.zeros((2, NODE_COUNT, 128))
    for r in range(NODES):
        for z in range(LOCAL_Z):
            n = r * LOCAL_Z + z
            ghost_r[0, n, z] = -LIFT_R[r]
            ghost_r[1, n, z] = LIFT_L[r]
            if z >= NODES:
                ghost_z[0, n, LOCAL_Z + r] = LIFT_R[z - NODES]
            else:
                ghost_z[1, n, LOCAL_Z + r] = LIFT_L[z]
    trace = np.zeros((2, 2, GHOST_ROWS, NODE_COUNT))
    for side in range(2):
        radial_row = END_R if side == 1 else END_L
        for place in range(2):
            for z in range(LOCAL_Z):
                for r in range(NODES):
                    trace[side, place, z, r * LOCAL_Z + z] = radial_row[r]
            for r in range(NODES):
                for k in range(NODES):
                    if place == 0:
                        trace[side, place, LOCAL_Z + r, r * LOCAL_Z + NODES + k] = END_R[k]
                    else:
                        trace[side, place, LOCAL_Z + r, r * LOCAL_Z + k] = END_L[k]
    return (
        (-SCALE * radial).astype(ml_dtypes.bfloat16),
        (-SCALE * axial).astype(np.float32),
        (SCALE * ghost_r).astype(np.float32),
        (SCALE * ghost_z).astype(np.float32),
        trace.astype(ml_dtypes.bfloat16),
    )


def rotation_table():
    full = np.zeros((PLANE + 2 * TILE, PLANE))
    factor = TIME_STEP / (2 * STEP_V)
    for a in range(NVR):
        for b in range(NVT):
            n = a * NVT + b
            first = factor * GRID_T[b] * GRID_T[b]
            second = factor * GRID_R[a] * GRID_T[b]
            if a + 1 < NVR:
                full[TILE + n + NVT, n] = -first
            if a > 0:
                full[TILE + n - NVT, n] = first
            if b + 1 < NVT:
                full[TILE + n + 1, n] = second
            if b > 0:
                full[TILE + n - 1, n] = -second
    tiles = [full[TILE + t - 128 : TILE + t - 128 + WINDOW, t : t + TILE] for t in range(0, PLANE, TILE)]
    return np.stack(tiles).astype(ml_dtypes.bfloat16)


def mirror_table():
    table = np.zeros((HALF, HALF))
    groups = NVR // 2
    for g in range(groups):
        for b in range(NVT):
            table[(groups - 1 - g) * NVT + b, g * NVT + b] = 1.0
    return table.astype(ml_dtypes.bfloat16)


def plane_rows():
    vr = np.repeat(GRID_R, NVT)
    vt = np.tile(GRID_T, NVR)
    rows = np.zeros((8, PLANE))
    rows[0] = vr
    rows[1] = vt
    rows[2] = np.exp(-(vr**2 + vt**2) / 2)
    return rows.astype(np.float32)


def weight_table():
    vr = np.repeat(GRID_R, NVT)
    vt = np.tile(GRID_T, NVR)
    square = vr**2 + vt**2
    columns = [np.ones(PLANE), vr, vt, vr**2, vt**2, vr * vt, vr * square, vt * square]
    table = np.zeros((PLANE, 128))
    for k, column in enumerate(columns):
        rest = column.copy()
        for part in range(PARTS_W):
            piece = rest.astype(ml_dtypes.bfloat16).astype(np.float64)
            table[:, k + 8 * part] = piece
            rest = rest - piece
    return table.astype(ml_dtypes.bfloat16)


def edge_table():
    table = np.zeros((2, NODE_COUNT, 128))
    for r in range(NODES):
        for k in range(NODES):
            table[0, r * LOCAL_Z + k, r] = END_L[k]
            table[1, r * LOCAL_Z + NODES + k, r] = END_R[k]
    return table.astype(np.float32)


def node_columns():
    table = np.zeros((NODE_COUNT, 128))
    for r in range(NODES):
        table[r * LOCAL_Z : (r + 1) * LOCAL_Z, :] = (1.0 + POINTS[r]) / 2
    return table.astype(np.float32)


RADIAL_M, AXIAL_M, GHOST_R, GHOST_Z, TRACE_M = transport_tables()
ROTATION_M = rotation_table()
MIRROR_M = mirror_table()
ROWS = plane_rows()
WEIGHT_M = weight_table()
EDGE = edge_table()
NODE_POS = node_columns()


def slot_speed(order, slot):
    return (order[slot].astype(F32) + 0.5) * (2 * SPEED_LIMIT / NVZ) - SPEED_LIMIT


def dot(x, y):
    return jnp.dot(x, y, preferred_element_type=F32)


def split(x):
    high = x.astype(BF16)
    return high, (x - high.astype(F32)).astype(BF16)


def macroscopic_of(m):
    rho = m(0)
    inv = 1.0 / rho
    ur, ut, uz = m(1) * inv, m(2) * inv, m(3) * inv
    rr, tt, rt, zz, rz, tz = (m(k) for k in range(4, 10))
    energy = rr + tt + zz
    speed = ur * ur + ut * ut + uz * uz
    temp = (energy * inv - speed) * (1.0 / 3.0)
    tail = 2.0 * rho * speed - energy
    qr = 0.5 * (m(10) - 2.0 * (ur * rr + ut * rt + uz * rz) + ur * tail)
    qt = 0.5 * (m(11) - 2.0 * (ur * rt + ut * tt + uz * tz) + ut * tail)
    qz = 0.5 * (m(12) - 2.0 * (ur * rz + ut * tz + uz * zz) + uz * tail)
    return rho, ur, ut, uz, temp, qr, qt, qz


def add_speed_sums(sums_ref, sums, vz):
    one = vz * sums
    two = vz * one
    for k, value in enumerate([sums, one, two, vz * two, jnp.abs(vz) * sums]):
        sums_ref[k] += value


def moment_rows(sums_ref):
    lane = lax.broadcasted_iota(jnp.int32, (NODE_COUNT, 128), 1)
    e = []
    for k in range(5):
        x = sums_ref[k]
        e.append(x + pltpu.roll(x, 120, 1) + pltpu.roll(x, 112, 1))
    pick = lambda k, c: e[k][:, c : c + 1]
    columns = [
        pick(0, 0), pick(0, 1), pick(0, 2), pick(1, 0),
        pick(0, 3), pick(0, 4), pick(0, 5), pick(2, 0), pick(1, 1), pick(1, 2),
        pick(0, 6) + pick(2, 1), pick(0, 7) + pick(2, 2), pick(1, 3) + pick(1, 4) + pick(3, 0), pick(4, 0),
    ]
    table = jnp.zeros((NODE_COUNT, 128), F32)
    for k, column in enumerate(columns):
        table = jnp.where(lane == k, WEIGHT * column, table)
    return jnp.transpose(table)[0:MOMENTS, :]


def radius_rows(r):
    return pl.ds(pl.multiple_of(r * LOCAL_Z, LOCAL_Z), LOCAL_Z)


def clear(ref):
    ref[...] = jnp.zeros(ref.shape, ref.dtype)


def places_of():
    return lax.axis_index("row"), lax.axis_index("gz")


def send_traces(count, step, place, narrow_ref, trace_ref, right_ref, left_ref, axial_ref, mirrored_ref):
    for side in range(2):

        @pl.when((step >= CHUNKS // 2) == (side == 1))
        def _():
            for s in range(count):
                got = dot(trace_ref[side, place], narrow_ref[s])
                axial_ref[s] = got[LOCAL_Z : LOCAL_Z + NODES]
                if side == 1:
                    right_ref[s] = got[0:LOCAL_Z]
                else:
                    left_ref[s] = got[0:LOCAL_Z]
                    at = pl.ds(pl.multiple_of(step * CHUNK, CHUNK), CHUNK)
                    mirrored_ref[s * LOCAL_Z : (s + 1) * LOCAL_Z, at] = got[0:LOCAL_Z].astype(BF16)


def turn_traces(count, row, mirror_ref, mirrored_ref, turned_ref):
    @pl.when(row == 0)
    def _():
        for first in range(0, HALF, 128):
            low = max(0, (HALF - first - 128 - 48) // 128 * 128)
            high = min(HALF, -((first - HALF - 48) // 128) * 128)
            got = dot(mirrored_ref[:, low:high], mirror_ref[low:high, first : first + 128])
            turned_ref[:, :, first : first + 128] = got.reshape(count, LOCAL_Z, 128)

    @pl.when(row != 0)
    def _():
        turned_ref[...] = jnp.zeros(turned_ref.shape, F32)


def first_kernel(count, order, codes, *refs):
    f_refs, refs = refs[:count], refs[count:]
    (
        weight_ref, trace_ref, mirror_ref, right_ref, left_ref, turned_ref, axial_ref, mom_ref,
        sums_ref, slot_sums_ref, narrow_ref, mirrored_ref, low_ref,
    ) = refs
    step = pl.program_id(0)
    row, place = places_of()

    @pl.when(step == 0)
    def _():
        clear(slot_sums_ref)

    def one_radius(r, carry):
        rows = radius_rows(r)
        for j in range(0, CHUNK, 128):
            at = pl.ds(j, 128)
            for s in range(count):
                high, low = split(f_refs[s][r, :, at])
                narrow_ref[s, rows, at] = high
                low_ref[s, rows, at] = low
        return carry

    lax.fori_loop(0, NODES, one_radius, 0)
    send_traces(count, step, place, narrow_ref, trace_ref, right_ref, left_ref, axial_ref, mirrored_ref)
    every = (count * NODE_COUNT, CHUNK)
    found = dot(narrow_ref[...].reshape(every), weight_ref[...]) + dot(low_ref[...].reshape(every), weight_ref[...])
    slot_sums_ref[...] += found.reshape(count, NODE_COUNT, 128)

    @pl.when(step == CHUNKS - 1)
    def _():
        turn_traces(count, row, mirror_ref, mirrored_ref, turned_ref)
        clear(sums_ref)
        for s in range(count):
            add_speed_sums(sums_ref, slot_sums_ref[s], slot_speed(order, s))
        mom_ref[...] = moment_rows(sums_ref)


def inner_kernel(
    count, slotted, order, codes, f_ref, rows_ref, pos_ref, weight_ref, radial_ref, axial_m_ref, rot_ref,
    out_ref, mom_ref, sums_ref, slot_sums_ref, inverse_ref, pad_ref, lhs_ref,
):
    def nodes_of(s, first, lanes):
        if slotted:
            return f_ref[s, :, :, first : first + lanes].reshape(NODE_COUNT, lanes)
        return f_ref[:, :, s * PLANE + first : s * PLANE + first + lanes].reshape(NODE_COUNT, lanes)

    step = pl.program_id(0)
    row, place = places_of()

    clear(slot_sums_ref)

    @pl.when(step == 0)
    def _():
        clear(sums_ref)
        pad_ref[:, :, 0:128] = jnp.zeros((count, NODE_COUNT, 128), BF16)
        pad_ref[:, :, 128 + PLANE :] = jnp.zeros((count, NODE_COUNT, 128), BF16)
        inverse_ref[...] = 1.0 / (ELEMENT_WIDTH * (row.astype(F32) + pos_ref[...]))
        minus = radial_ref[jnp.where(row == lax.axis_size("row") - 1, 2, 0)]
        for s in range(count):
            lhs_ref[s, 0, 0:NODE_COUNT] = minus
            lhs_ref[s, 1, 0:NODE_COUNT] = radial_ref[1]

    kind_out = jnp.where(jnp.logical_and(place == 1, codes[1, 0] == 2), 2, 0)
    inverse = inverse_ref[...]
    for s in range(count):
        vz = slot_speed(order, step * count + s)
        axial = (vz * axial_m_ref[jnp.where(vz > 0, 1, kind_out)]).astype(BF16)
        lhs_ref[s, 0, NODE_COUNT:] = axial
        lhs_ref[s, 1, NODE_COUNT:] = axial
        for j in range(PLANE // 128):
            field = nodes_of(s, j * 128, 128)
            pad_ref[s, :, 128 + j * 128 : 256 + j * 128] = (field * inverse).astype(BF16)

    for tile in range(PLANE // TILE):
        start = tile * TILE
        turned = dot(pad_ref[:, :, start : start + WINDOW].reshape(count * NODE_COUNT, WINDOW), rot_ref[tile])
        for first, lanes, side in PIECES:
            if first // TILE != tile:
                continue
            vr = rows_ref[0:1, first : first + lanes]
            inside = first - start
            changes = []
            for s in range(count):
                moved = dot(lhs_ref[s, side], nodes_of(s, first, lanes).astype(BF16))
                change = turned[s * NODE_COUNT : (s + 1) * NODE_COUNT, inside : inside + lanes]
                change = change + vr * moved[0:NODE_COUNT] + moved[NODE_COUNT:]
                changes.append(change.astype(BF16))
                out_ref[s, :, :, first : first + lanes] = changes[s].reshape(NODES, LOCAL_Z, lanes)
            found = dot(jnp.concatenate(changes, axis=0), weight_ref[first : first + lanes, :])
            slot_sums_ref[...] += found.reshape(count, NODE_COUNT, 128)

    for s in range(count):
        add_speed_sums(sums_ref, slot_sums_ref[s], slot_speed(order, step * count + s))

    @pl.when(step == pl.num_programs(0) - 1)
    def _():
        mom_ref[...] = moment_rows(sums_ref)


def total_of(part_refs, base_ref):
    parts = [p[...] for p in part_refs]
    while len(parts) > 1:
        parts = [parts[k] + parts[k + 1] for k in range(0, len(parts), 2)]
    return parts[0] if base_ref is None else parts[0] + base_ref[...]


def prepare_nodes(total, codes, place, edge_ref, table_ref, node_ref, wall_ref):
    wide = jnp.concatenate([total, jnp.zeros((128 - MOMENTS, 128), F32)], axis=0)
    table_ref[...] = jnp.transpose(wide)
    rho, ur, ut, uz, temp, qr, qt, qz = macroscopic_of(lambda k: table_ref[:, k : k + 1])
    inv_t = 1.0 / temp
    beta = ((1.0 - VISCOUS_RATIO) / 5.0) / (rho * temp * temp)
    kappa = rho * (TIME_STEP / KNUDSEN)
    peak = kappa * rho * inv_t * jnp.sqrt(inv_t)
    columns = [uz, -0.5 * inv_t, qz * beta, inv_t, peak, 1.0 - kappa, ur, ut, qr * beta, qt * beta]
    for k, column in enumerate(columns):
        node_ref[k] = jnp.broadcast_to(column, (NODE_COUNT, 128))
    net = table_ref[:, 3:4]
    gross = table_ref[:, 13:14]
    to_bottom = 0.5 * (gross - net)
    to_top = 0.5 * (gross + net)
    incident = jnp.sum(edge_ref[0] * to_bottom, axis=0, keepdims=True)
    upward = jnp.sum(edge_ref[1] * to_top, axis=0, keepdims=True)
    bottom = jnp.where(codes[0, 0] == 1, SAT_DENSITY, incident * (1.0 / HALF_FLUX))
    top = jnp.where(codes[1, 0] == 2, 0.0, upward * (1.0 / HALF_FLUX))
    density = jnp.where(place == 0, bottom, top)
    wall_ref[...] = jnp.transpose(jnp.broadcast_to(density, (128, 128)))[0:NODES, :]


def slot_factors(vz, node_ref):
    cz = vz - node_ref[0]
    square = cz * cz
    return node_ref[4] * jnp.exp(square * node_ref[1]), cz * node_ref[2], square * node_ref[3] - 5.0


def ghost_lifts(vz, ghost_r_ref, ghost_z_ref, lhs_ref, s):
    lean = jnp.abs(vz) * ghost_z_ref[jnp.where(vz > 0, 1, 0)]
    lhs_ref[s, 0] = (ghost_r_ref[0] + lean).astype(BF16)
    lhs_ref[s, 1] = (ghost_r_ref[1] + lean).astype(BF16)


def outer_kernel(count, part_count, slotted, last, order, codes, *refs):
    part_refs, refs = refs[:part_count], refs[part_count:]
    base_ref = None
    if slotted:
        base_ref, refs = refs[0], refs[1:]
    inner_mom_ref, refs = refs[0], refs[1:]
    if slotted:
        f_ref, refs = refs[0], refs[1:]
        field_of = lambda s, r, at: f_ref[s, r, :, at]
    else:
        f_refs, refs = refs[:count], refs[count:]
        field_of = lambda s, r, at: f_refs[s][r, :, at]
    inner_ref, in_left_ref, in_turned_ref, in_right_ref, in_axial_ref = refs[:5]
    rows_ref, weight_ref, edge_ref, ghost_r_ref, ghost_z_ref = refs[5:10]
    refs = refs[10:]
    if last:
        (out_hbm, share_ref, kept_ref, out_buf, out_sem), refs = refs[:5], refs[5:]
    else:
        (trace_ref, mirror_ref, out_ref, right_ref, left_ref, turned_ref, axial_ref), refs = refs[:7], refs[7:]
        (share_ref, kept_ref, narrow_ref, mirrored_ref), refs = refs[:4], refs[4:]
    (
        node_ref, wall_ref, slot_ref, work_ref, sums_ref, lhs_ref, ghost_ref, table_ref,
        plane_ref, plane_sums_ref, ghost_sums_ref,
    ) = refs
    step = pl.program_id(0)
    row, place = places_of()
    speeds = [slot_speed(order, s) for s in range(count)]

    @pl.when(step == 0)
    def _():
        clear(plane_sums_ref)
        clear(ghost_sums_ref)
        total = total_of(part_refs, base_ref)
        kept_ref[...] = total * (1.0 - total[0:1, :] * (TIME_STEP / KNUDSEN))
        prepare_nodes(total, codes, place, edge_ref, table_ref, node_ref, wall_ref)
        for s in range(count):
            for k, value in enumerate(slot_factors(speeds[s], node_ref)):
                slot_ref[s, k] = value
            ghost_lifts(speeds[s], ghost_r_ref, ghost_z_ref, lhs_ref, s)

    side = jnp.where(step >= CHUNKS // 2, 1, 0)
    inward = step < CHUNKS // 2
    for s in range(count):
        vz = speeds[s]
        own = (place == 0) == (vz > 0)
        strength = jnp.exp(-0.5 * vz * vz + jnp.zeros((NODES, 128), F32)) * wall_ref[...]
        for j in range(0, CHUNK, 128):
            at = pl.ds(j, 128)
            radial = jnp.where(inward, in_right_ref[s, :, at], in_left_ref[s, :, at] + in_turned_ref[s, :, at])
            axial = jnp.where(own, strength * rows_ref[2:3, at], in_axial_ref[s, :, at])
            rows = jnp.concatenate([rows_ref[0:1, at] * radial, axial, jnp.zeros((8, 128), F32)], axis=0)
            ghost_ref[s, :, at] = rows.astype(BF16)
        work_ref[s] = dot(lhs_ref[s, side, :, 0:GHOST_ROWS], ghost_ref[s])
    ghost_sums_ref[side] += dot(ghost_ref[...].reshape(count * GHOST_ROWS, CHUNK), weight_ref[...])

    def copy_out(s, chunk):
        at = pl.ds(pl.multiple_of(s * PLANE + chunk * CHUNK, CHUNK), CHUNK)
        slot = lax.rem(chunk, 2)
        return pltpu.make_async_copy(out_buf.at[slot, s], out_hbm.at[:, :, at], out_sem.at[slot, s])

    if last:

        @pl.when(step >= 2)
        def _():
            for s in range(count):
                copy_out(s, step - 2).wait()

        buffer = lax.rem(step, 2)

    def update(r, carry):
        rows = radius_rows(r)
        for j in range(0, CHUNK, 128):
            at = pl.ds(j, 128)
            cr = rows_ref[0:1, at] - node_ref[6, rows, :]
            ct = rows_ref[1:2, at] - node_ref[7, rows, :]
            square = cr * cr + ct * ct
            gauss = jnp.exp(square * node_ref[1, rows, :])
            along = cr * node_ref[8, rows, :] + ct * node_ref[9, rows, :]
            reach = square * node_ref[3, rows, :]
            keep = node_ref[5, rows, :]
            tilted = gauss * along
            for k, plane in enumerate([gauss, tilted, gauss * reach, tilted * reach]):
                high, low = split(plane)
                plane_ref[k, rows, at] = high
                plane_ref[4 + k, rows, at] = low
            for s in range(count):
                new = field_of(s, r, at) * keep + work_ref[s, rows, at] + inner_ref[s, r, :, at].astype(F32)
                bend = (along + slot_ref[s, 1, rows, :]) * (reach + slot_ref[s, 2, rows, :]) + 1.0
                new = new + (gauss * slot_ref[s, 0, rows, :]) * bend
                if last:
                    out_buf[buffer, s, r, :, at] = new
                else:
                    out_ref[s, r, :, at] = new
                    narrow_ref[s, rows, at] = new.astype(BF16)
        return carry

    lax.fori_loop(0, NODES, update, 0)
    if last:
        for s in range(count):
            copy_out(s, step).start()

        @pl.when(step == CHUNKS - 1)
        def _():
            for s in range(count):
                copy_out(s, step - 1).wait()
                copy_out(s, step).wait()

    else:
        send_traces(count, step, place, narrow_ref, trace_ref, right_ref, left_ref, axial_ref, mirrored_ref)

    found = dot(plane_ref[...].reshape(8 * NODE_COUNT, CHUNK), weight_ref[...]).reshape(8, NODE_COUNT, 128)
    plane_sums_ref[...] += found[0:4] + found[4:8]

    @pl.when(step == CHUNKS - 1)
    def _():
        if not last:
            turn_traces(count, row, mirror_ref, mirrored_ref, turned_ref)
        clear(sums_ref)
        for s in range(count):
            peak, heat, reach = (slot_ref[s, k] for k in range(3))
            sums = plane_sums_ref[0] * (1.0 + heat * reach) + plane_sums_ref[1] * reach
            sums = peak * (sums + plane_sums_ref[2] * heat + plane_sums_ref[3])
            for edge_side in range(2):
                lift = lhs_ref[s, edge_side, :, 0:GHOST_ROWS]
                high, low = split(ghost_sums_ref[edge_side, s * GHOST_ROWS : (s + 1) * GHOST_ROWS, :])
                sums = sums + dot(lift, high) + dot(lift, low)
            add_speed_sums(sums_ref, sums, speeds[s])
        share_ref[...] = moment_rows(sums_ref) + inner_mom_ref[...]


def last_kernel(part_count, codes, *refs):
    total_ref = total_of(refs[:part_count], refs[part_count])
    edge_ref, macro_ref, flux_ref = refs[part_count + 1 :]
    row, place = places_of()
    values = macroscopic_of(lambda k: total_ref[k : k + 1, :])
    for k in range(8):
        for r in range(NODES):
            macro_ref[k, r : r + 1, :] = values[k][:, r * LOCAL_Z : (r + 1) * LOCAL_Z]
    net, gross = total_ref[3:4, :], total_ref[13:14, :]
    to_bottom = jnp.broadcast_to(0.5 * (gross - net), (8, 128))
    to_top = jnp.broadcast_to(0.5 * (gross + net), (8, 128))
    exact = lambda x, y: jnp.dot(x, y, precision=lax.Precision.HIGHEST, preferred_element_type=F32)
    incident = exact(to_bottom, edge_ref[0])
    upward = exact(to_top, edge_ref[1])
    downward = exact(to_bottom, edge_ref[1])
    bottom = jnp.where(codes[0, 0] == 1, SAT_DENSITY * HALF_FLUX - incident, 0.0)
    top = jnp.where(codes[1, 0] == 2, upward - downward, 0.0)
    flux_ref[...] = jnp.where(place == 0, bottom, top)[0:1, 0:NODES]


def whole(shape):
    return pl.BlockSpec(shape, lambda *a: (0,) * len(shape), pipeline_mode=pl.Buffered(1))


def on_device(distribution, z_order, edge_codes):
    local_r, local_z, vdev = distribution.shape
    assert local_r == NODES and local_z == LOCAL_Z
    slots = vdev // PLANE
    group = math.gcd(slots, 3)
    steps = slots // group
    rows_total = lax.axis_size("row")
    verts = lax.axis_size("vert")
    assert lax.axis_size("gz") == 2
    rows, pos, edge = jnp.asarray(ROWS), jnp.asarray(NODE_POS), jnp.asarray(EDGE)
    radial_m, axial_m = jnp.asarray(RADIAL_M), jnp.asarray(AXIAL_M)
    ghost_r, ghost_z = jnp.asarray(GHOST_R), jnp.asarray(GHOST_Z)
    trace_m, mirror_m, rot_m = jnp.asarray(TRACE_M), jnp.asarray(MIRROR_M), jnp.asarray(ROTATION_M)

    weight_m = jnp.asarray(WEIGHT_M)
    slab = pl.BlockSpec((NODES, LOCAL_Z, group * PLANE), lambda i, *n: (0, 0, i))
    slot_slab = pl.BlockSpec((group, NODES, LOCAL_Z, PLANE), lambda i, *n: (i, 0, 0, 0))
    chunk_specs = [
        pl.BlockSpec((NODES, LOCAL_Z, CHUNK), lambda i, *n, s=s: (0, 0, s * CHUNKS + i)) for s in range(slots)
    ]
    slot_chunk = pl.BlockSpec((slots, NODES, LOCAL_Z, CHUNK), lambda i, *n: (0, 0, 0, i))
    half = CHUNKS // 2
    outward_spec = pl.BlockSpec((slots, LOCAL_Z, CHUNK), lambda i, *n: (0, 0, jnp.maximum(i - half, 0)))
    inward_spec = pl.BlockSpec((slots, LOCAL_Z, CHUNK), lambda i, *n: (0, 0, jnp.minimum(i, half - 1)))
    axial_spec = pl.BlockSpec((slots, NODES, CHUNK), lambda i, *n: (0, 0, i))
    rows_spec = pl.BlockSpec((8, CHUNK), lambda i, *n: (0, i))
    weight_spec = pl.BlockSpec((CHUNK, 128), lambda i, *n: (i, 0))
    mom_spec = whole((MOMENTS, 128))
    radial_shape = jax.ShapeDtypeStruct((slots, LOCAL_Z, HALF), F32)
    axial_shape = jax.ShapeDtypeStruct((slots, NODES, PLANE), F32)
    mom_shape = jax.ShapeDtypeStruct((MOMENTS, 128), F32)
    inner_shape = (slots, NODES, LOCAL_Z, PLANE)
    trace_specs = [outward_spec, inward_spec, whole(radial_shape.shape), axial_spec]
    trace_shapes = [radial_shape, radial_shape, radial_shape, axial_shape]
    ghost_specs = [outward_spec, outward_spec, inward_spec, axial_spec]
    square = pltpu.VMEM((NODE_COUNT, 128), F32)
    sums_scratch = pltpu.VMEM((5, NODE_COUNT, 128), F32)
    trace_scratch = [
        pltpu.VMEM((slots, NODE_COUNT, CHUNK), BF16),
        pltpu.VMEM((slots * LOCAL_Z, HALF), BF16),
    ]

    def call(body, name, grid, in_specs, out_specs, out_shape, scratch, args):
        return pl.pallas_call(
            body,
            grid_spec=pltpu.PrefetchScalarGridSpec(
                num_scalar_prefetch=2,
                grid=(grid,),
                in_specs=in_specs,
                out_specs=out_specs,
                scratch_shapes=scratch,
            ),
            out_shape=out_shape,
            compiler_params=pltpu.CompilerParams(vmem_limit_bytes=56 * 1024 * 1024),
            name=name,
        )(z_order, edge_codes, *args)

    def all_whole(tables):
        return [whole(x.shape) for x in tables]

    def first(f):
        return call(
            lambda *a: first_kernel(slots, *a), "moments_and_traces", CHUNKS,
            chunk_specs + [weight_spec] + all_whole([trace_m, mirror_m]),
            trace_specs + [mom_spec], trace_shapes + [mom_shape],
            [sums_scratch, pltpu.VMEM((slots, NODE_COUNT, 128), F32)] + trace_scratch + trace_scratch[:1],
            [f] * slots + [weight_m, trace_m, mirror_m],
        )

    def inner(f, split):
        tables = [rows, pos, weight_m, radial_m, axial_m, rot_m]
        scratch = [
            sums_scratch,
            pltpu.VMEM((group, NODE_COUNT, 128), F32),
            square,
            pltpu.VMEM((group, NODE_COUNT, PLANE + 256), BF16),
            pltpu.VMEM((group, 2, 2 * NODE_COUNT, 128), BF16),
        ]
        return call(
            lambda *a: inner_kernel(group, split, *a), "inner_increments", steps,
            [slot_slab if split else slab] + all_whole(tables),
            [slot_slab, mom_spec], [jax.ShapeDtypeStruct(inner_shape, BF16), mom_shape], scratch, [f] + tables,
        )

    def outer(f, base, change, change_moments, ghosts, parts, last):
        split = base is not None
        more = [] if last else [trace_m, mirror_m]
        if last:
            outs = [pl.BlockSpec(memory_space=pl.ANY)]
            out_shapes = [jax.ShapeDtypeStruct(distribution.shape, F32)]
            scratch = [
                pltpu.VMEM((2, slots, NODES, LOCAL_Z, CHUNK), F32),
                pltpu.SemaphoreType.DMA((2, slots)),
            ]
        else:
            outs = [slot_chunk] + trace_specs
            out_shapes = [jax.ShapeDtypeStruct(inner_shape, F32)] + trace_shapes
            scratch = trace_scratch
        scratch = scratch + [
            pltpu.VMEM((10, NODE_COUNT, 128), F32),
            pltpu.VMEM((NODES, 128), F32),
            pltpu.VMEM((slots, 3, NODE_COUNT, 128), F32),
            pltpu.VMEM((slots, NODE_COUNT, CHUNK), F32),
            sums_scratch,
            pltpu.VMEM((slots, 2, NODE_COUNT, 128), BF16),
            pltpu.VMEM((slots, GHOST_ROWS, CHUNK), BF16),
            square,
            pltpu.VMEM((8, NODE_COUNT, CHUNK), BF16),
            pltpu.VMEM((4, NODE_COUNT, 128), F32),
            pltpu.VMEM((2, slots * GHOST_ROWS, 128), F32),
        ]
        return call(
            lambda *a: outer_kernel(slots, len(parts), split, last, *a),
            "last_update" if last else "update",
            CHUNKS,
            [mom_spec] * (len(parts) + (2 if split else 1))
            + ([slot_chunk] if split else chunk_specs)
            + [slot_chunk] + ghost_specs + [rows_spec, weight_spec] + all_whole([edge, ghost_r, ghost_z] + more),
            outs + [mom_spec, mom_spec],
            out_shapes + [mom_shape, mom_shape],
            scratch,
            [*parts] + ([base] if split else []) + [change_moments] + [f] * (1 if split else slots)
            + [change, *ghosts, rows, weight_m, edge, ghost_r, ghost_z] + more,
        )

    def spread(moments):
        parts = [moments]
        for shift in range(1, verts):
            parts.append(lax.ppermute(moments, "vert", [(i, i ^ shift) for i in range(verts)]))
        return parts

    def halo(right, left, turned, axial):
        from_axial = lax.ppermute(axial, "gz", [(0, 1), (1, 0)])
        from_left = lax.ppermute(right, "row", [(i, i + 1) for i in range(rows_total - 1)])
        from_right = lax.ppermute(left, "row", [(i + 1, i) for i in range(rows_total - 1)])
        return from_left, turned, from_right, from_axial

    current = distribution
    *traces, moments = first(current)
    base = None
    for number in range(STEPS):
        last = number == STEPS - 1
        ghosts = halo(*traces)
        parts = spread(moments)
        change, change_moments = inner(current, number > 0)
        current, *traces, moments, base = outer(current, base, change, change_moments, ghosts, parts, last)
    parts = spread(moments)
    macro, flux = pl.pallas_call(
        lambda *a: last_kernel(len(parts), *a),
        grid_spec=pltpu.PrefetchScalarGridSpec(
            num_scalar_prefetch=1,
            grid=(1,),
            in_specs=[mom_spec] * (len(parts) + 1) + [whole(edge.shape)],
            out_specs=[whole((8, NODES, LOCAL_Z)), whole((1, NODES))],
        ),
        out_shape=[
            jax.ShapeDtypeStruct((8, NODES, LOCAL_Z), F32),
            jax.ShapeDtypeStruct((1, NODES), F32),
        ],
        name="macroscopic",
    )(edge_codes, *parts, base, edge)
    return (current, macro, flux)


def solution(mesh):
    in_specs = (P("row", "gz", "vert"), P("vert"), P(None, "row"))
    out_specs = (P("row", "gz", "vert"), P(None, "row", "gz"), P("gz", "row"))
    return jax.shard_map(
        on_device, mesh=mesh, in_specs=in_specs, out_specs=out_specs, check_vma=False
    )
```

```python
import math

import jax
import jax.numpy as jnp
import ml_dtypes
import numpy as np
from jax import lax
from jax.experimental import pallas as pl
from jax.experimental.pallas import tpu as pltpu
from jax.sharding import PartitionSpec as P

NODES = 8
NVR = 48
NVT = 48
NVZ = 48
STEPS = 2

ELEMENT_WIDTH = 4.0
TIME_STEP = 0.001
KNUDSEN = 0.005
VISCOUS_RATIO = 2.0 / 3.0
SAT_DENSITY = 1.5
SPEED_LIMIT = 5.0

PLANE = NVR * NVT
HALF = PLANE // 2
LOCAL_Z = 2 * NODES
NODE_COUNT = NODES * LOCAL_Z
TILE = 256
WINDOW = 512
GHOST_ROWS = 32
MOMENTS = 16
F32 = jnp.float32
BF16 = jnp.bfloat16
PIECES = [(t, TILE, 0) for t in range(0, 1024, TILE)] + [(1024, 128, 0), (1152, 128, 1)] + [
    (t, TILE, 1) for t in range(1280, PLANE, TILE)
]


def legendre_pair(position, point_count):
    previous = 1.0
    current = position
    for degree in range(2, point_count + 1):
        previous, current = (
            current,
            ((2 * degree - 1) * position * current - (degree - 1) * previous) / degree,
        )
    slope = point_count * (position * current - previous) / (position * position - 1.0)
    return (current, slope)


def dg_tables(point_count):
    point_list = []
    weight_list = []
    for number in range(point_count):
        position = math.cos(math.pi * (number + 0.75) / (point_count + 0.5))
        for sweep in range(60):
            value, slope = legendre_pair(position, point_count)
            position = position - value / slope
        value, slope = legendre_pair(position, point_count)
        point_list.append(position)
        weight_list.append(2.0 / ((1.0 - position * position) * slope * slope))
    point_list = point_list[::-1]
    weight_list = weight_list[::-1]
    points = np.array(point_list)
    derivative = np.zeros((point_count, point_count))
    right = np.zeros(point_count)
    left = np.zeros(point_count)
    products = [
        np.prod([points[i] - points[j] for j in range(point_count) if j != i])
        for i in range(point_count)
    ]
    for i in range(point_count):
        others = [j for j in range(point_count) if j != i]
        derivative[i, i] = sum(1.0 / (points[i] - points[j]) for j in others)
        for j in others:
            derivative[i, j] = products[i] / products[j] / (points[i] - points[j])
        right[i] = np.prod([1.0 - points[j] for j in others]) / products[i]
        left[i] = np.prod([-1.0 - points[j] for j in others]) / products[i]
    return points, np.array(weight_list), derivative, right, left


def speed_grid(point_count):
    return -SPEED_LIMIT + (np.arange(point_count) + 0.5) * (2.0 * SPEED_LIMIT / point_count)


POINTS, QUAD, DERIV, END_R, END_L = dg_tables(NODES)
LIFT_R = END_R / QUAD
LIFT_L = END_L / QUAD
GRID_R = speed_grid(NVR)
GRID_T = speed_grid(NVT)
GRID_Z = speed_grid(NVZ)
STEP_V = 2 * SPEED_LIMIT / NVR
WEIGHT = STEP_V**3 / (2 * math.pi) ** 1.5
HALF_FLUX = float(
    WEIGHT
    * np.sum(np.exp(-(GRID_R**2) / 2))
    * np.sum(np.exp(-(GRID_T**2) / 2))
    * np.sum(np.maximum(GRID_Z, 0.0) * np.exp(-(GRID_Z**2) / 2))
)
SCALE = TIME_STEP * 2.0 / ELEMENT_WIDTH


def transport_tables():
    ident = np.eye(NODES)
    up = DERIV + np.outer(LIFT_L, END_L)
    down = DERIV - np.outer(LIFT_R, END_R)
    zero = np.zeros((NODES, NODES))
    wide = np.eye(LOCAL_Z)
    radial = np.stack([np.kron(down, wide), np.kron(up, wide), np.kron(DERIV, wide)])
    zup = np.block([[up, zero], [-np.outer(LIFT_L, END_R), up]])
    zdown = np.block([[down, np.outer(LIFT_R, END_L)], [zero, down]])
    zout = np.block([[down, np.outer(LIFT_R, END_L)], [zero, DERIV]])
    axial = np.stack([np.kron(ident, zdown), np.kron(ident, zup), np.kron(ident, zout)])
    ghost_r = np.zeros((2, NODE_COUNT, 128))
    ghost_z = np.zeros((2, NODE_COUNT, 128))
    for r in range(NODES):
        for z in range(LOCAL_Z):
            n = r * LOCAL_Z + z
            ghost_r[0, n, z] = -LIFT_R[r]
            ghost_r[1, n, z] = LIFT_L[r]
            if z >= NODES:
                ghost_z[0, n, LOCAL_Z + r] = LIFT_R[z - NODES]
            else:
                ghost_z[1, n, LOCAL_Z + r] = LIFT_L[z]
    trace = np.zeros((2, 2, GHOST_ROWS, NODE_COUNT))
    for side in range(2):
        radial_row = END_R if side == 1 else END_L
        for place in range(2):
            for z in range(LOCAL_Z):
                for r in range(NODES):
                    trace[side, place, z, r * LOCAL_Z + z] = radial_row[r]
            for r in range(NODES):
                for k in range(NODES):
                    if place == 0:
                        trace[side, place, LOCAL_Z + r, r * LOCAL_Z + NODES + k] = END_R[k]
                    else:
                        trace[side, place, LOCAL_Z + r, r * LOCAL_Z + k] = END_L[k]
    return (
        (-SCALE * radial).astype(ml_dtypes.bfloat16),
        (-SCALE * axial).astype(np.float32),
        (SCALE * ghost_r).astype(np.float32),
        (SCALE * ghost_z).astype(np.float32),
        trace.astype(ml_dtypes.bfloat16),
    )


def rotation_table():
    full = np.zeros((PLANE + 2 * TILE, PLANE))
    factor = TIME_STEP / (2 * STEP_V)
    for a in range(NVR):
        for b in range(NVT):
            n = a * NVT + b
            first = factor * GRID_T[b] * GRID_T[b]
            second = factor * GRID_R[a] * GRID_T[b]
            if a + 1 < NVR:
                full[TILE + n + NVT, n] = -first
            if a > 0:
                full[TILE + n - NVT, n] = first
            if b + 1 < NVT:
                full[TILE + n + 1, n] = second
            if b > 0:
                full[TILE + n - 1, n] = -second
    tiles = [full[TILE + t - 128 : TILE + t - 128 + WINDOW, t : t + TILE] for t in range(0, PLANE, TILE)]
    return np.stack(tiles).astype(ml_dtypes.bfloat16)


def mirror_table():
    table = np.zeros((HALF, HALF))
    groups = NVR // 2
    for g in range(groups):
        for b in range(NVT):
            table[(groups - 1 - g) * NVT + b, g * NVT + b] = 1.0
    return table.astype(ml_dtypes.bfloat16)


def plane_rows():
    vr = np.repeat(GRID_R, NVT)
    vt = np.tile(GRID_T, NVR)
    rows = np.zeros((8, PLANE))
    rows[0] = vr
    rows[1] = vt
    rows[2] = np.exp(-(vr**2 + vt**2) / 2)
    return rows.astype(np.float32)


def edge_table():
    table = np.zeros((2, NODE_COUNT, 128))
    for r in range(NODES):
        for k in range(NODES):
            table[0, r * LOCAL_Z + k, r] = END_L[k]
            table[1, r * LOCAL_Z + NODES + k, r] = END_R[k]
    return table.astype(np.float32)


def node_columns():
    table = np.zeros((NODE_COUNT, 128))
    for r in range(NODES):
        table[r * LOCAL_Z : (r + 1) * LOCAL_Z, :] = (1.0 + POINTS[r]) / 2
    return table.astype(np.float32)


RADIAL_M, AXIAL_M, GHOST_R, GHOST_Z, TRACE_M = transport_tables()
ROTATION_M = rotation_table()
MIRROR_M = mirror_table()
ROWS = plane_rows()
EDGE = edge_table()
NODE_POS = node_columns()


def slot_speed(order, slot):
    return (order[slot].astype(F32) + 0.5) * (2 * SPEED_LIMIT / NVZ) - SPEED_LIMIT


def dot(x, y):
    return jnp.dot(x, y, preferred_element_type=F32)


def macroscopic_of(m):
    rho = m(0)
    inv = 1.0 / rho
    ur, ut, uz = m(1) * inv, m(2) * inv, m(3) * inv
    rr, tt, rt, zz, rz, tz = (m(k) for k in range(4, 10))
    energy = rr + tt + zz
    speed = ur * ur + ut * ut + uz * uz
    temp = (energy * inv - speed) * (1.0 / 3.0)
    tail = 2.0 * rho * speed - energy
    qr = 0.5 * (m(10) - 2.0 * (ur * rr + ut * rt + uz * rz) + ur * tail)
    qt = 0.5 * (m(11) - 2.0 * (ur * rt + ut * tt + uz * tz) + ut * tail)
    qz = 0.5 * (m(12) - 2.0 * (ur * rz + ut * tz + uz * zz) + uz * tail)
    return rho, ur, ut, uz, temp, qr, qt, qz


def add_speed_sums(field, vz, sums):
    one = field * vz
    two = one * vz
    return [
        sums[0] + field,
        sums[1] + one,
        sums[2] + two,
        sums[3] + two * vz,
        sums[4] + field * jnp.abs(vz),
    ]


def finish_moments(sums_ref, rows_ref, table_ref, out_ref):
    lane = lax.broadcasted_iota(jnp.int32, (LOCAL_Z, 128), 1)

    def one_radius(r, carry):
        acc = [jnp.zeros((LOCAL_Z, 128), F32) for _ in range(14)]
        for j in range(PLANE // 128):
            at = pl.ds(j * 128, 128)
            vr = rows_ref[0:1, at]
            vt = rows_ref[1:2, at]
            g0, g1, g2, g3, g4 = (sums_ref[k, r, :, at] for k in range(5))
            a = vr * g0
            b = vt * g0
            aa = vr * a
            bb = vt * b
            c = vr * g1
            d = vt * g1
            perp = aa + bb + g2
            new = [g0, a, b, g1, aa, bb, vr * b, g2, c, d, vr * perp, vt * perp, vr * c + vt * d + g3, g4]
            acc = [x + y for x, y in zip(acc, new)]
        block = jnp.zeros((LOCAL_Z, 128), F32)
        for k in range(14):
            block = jnp.where(lane == k, WEIGHT * jnp.sum(acc[k], axis=1, keepdims=True), block)
        table_ref[pl.ds(pl.multiple_of(r * LOCAL_Z, LOCAL_Z), LOCAL_Z), :] = block
        return carry

    lax.fori_loop(0, NODES, one_radius, 0)
    out_ref[...] = jnp.transpose(table_ref[...])[0:MOMENTS, :]


def clear_sums(sums_ref):
    sums_ref[...] = jnp.zeros(sums_ref.shape, F32)


def places_of():
    return lax.axis_index("row"), lax.axis_index("gz")


def send_piece(s, first, lanes, side, place, narrow, trace_ref, right_ref, left_ref, axial_ref):
    got = dot(trace_ref[side, place], narrow)
    if side == 1:
        right_ref[s, :, first - HALF : first - HALF + lanes] = got[0:LOCAL_Z]
    else:
        left_ref[s, :, first : first + lanes] = got[0:LOCAL_Z]
    axial_ref[s, :, first : first + lanes] = got[LOCAL_Z : LOCAL_Z + NODES]


def turn_traces(count, row, mirror_ref, left_ref, turned_ref):
    @pl.when(row == 0)
    def _():
        flat = left_ref[...].reshape(count * LOCAL_Z, HALF).astype(BF16)
        for first in range(0, HALF, 128):
            low = max(0, (HALF - first - 128 - 48) // 128 * 128)
            high = min(HALF, -((first - HALF - 48) // 128) * 128)
            got = dot(flat[:, low:high], mirror_ref[low:high, first : first + 128])
            turned_ref[:, :, first : first + 128] = got.reshape(count, LOCAL_Z, 128)

    @pl.when(row != 0)
    def _():
        turned_ref[...] = jnp.zeros(turned_ref.shape, F32)


def nodes_of(ref, first, lanes):
    return ref[:, :, first : first + lanes].reshape(NODE_COUNT, lanes)


def trace_kernel(
    count, order, codes, f_ref, trace_ref, mirror_ref, right_ref, left_ref, turned_ref, axial_ref
):
    row, place = places_of()
    for s in range(count):
        for first, lanes, side in PIECES:
            narrow = nodes_of(f_ref, s * PLANE + first, lanes).astype(BF16)
            send_piece(s, first, lanes, side, place, narrow, trace_ref, right_ref, left_ref, axial_ref)
    turn_traces(count, row, mirror_ref, left_ref, turned_ref)


def moment_kernel(count, order, codes, f_ref, rows_ref, mom_ref, sums_ref, table_ref):
    step = pl.program_id(0)

    @pl.when(step == 0)
    def _():
        clear_sums(sums_ref)

    speeds = [slot_speed(order, step * count + s) for s in range(count)]
    for j in range(0, PLANE, 128):
        at = pl.ds(j, 128)
        for r in range(NODES):
            sums = [sums_ref[k, r, :, at] for k in range(5)]
            for s in range(count):
                sums = add_speed_sums(f_ref[r, :, pl.ds(s * PLANE + j, 128)], speeds[s], sums)
            for k in range(5):
                sums_ref[k, r, :, at] = sums[k]

    @pl.when(step == pl.num_programs(0) - 1)
    def _():
        finish_moments(sums_ref, rows_ref, table_ref, mom_ref)


def inner_kernel(
    count, order, codes, f_ref, rows_ref, pos_ref, radial_ref, axial_m_ref, rot_ref,
    out_ref, inverse_ref, pad_ref, lhs_ref,
):
    step = pl.program_id(0)
    row, place = places_of()

    @pl.when(step == 0)
    def _():
        pad_ref[:, :, 0:128] = jnp.zeros((count, NODE_COUNT, 128), BF16)
        pad_ref[:, :, 128 + PLANE :] = jnp.zeros((count, NODE_COUNT, 128), BF16)
        inverse_ref[...] = 1.0 / (ELEMENT_WIDTH * (row.astype(F32) + pos_ref[...]))
        minus = radial_ref[jnp.where(row == lax.axis_size("row") - 1, 2, 0)]
        for s in range(count):
            lhs_ref[s, 0, :, 0:NODE_COUNT] = minus
            lhs_ref[s, 1, :, 0:NODE_COUNT] = radial_ref[1]

    kind_out = jnp.where(jnp.logical_and(place == 1, codes[1, 0] == 2), 2, 0)
    inverse = inverse_ref[...]
    for s in range(count):
        vz = slot_speed(order, step * count + s)
        axial = (vz * axial_m_ref[jnp.where(vz > 0, 1, kind_out)]).astype(BF16)
        lhs_ref[s, 0, :, NODE_COUNT:] = axial
        lhs_ref[s, 1, :, NODE_COUNT:] = axial
        for j in range(PLANE // 128):
            field = nodes_of(f_ref, s * PLANE + j * 128, 128)
            pad_ref[s, :, 128 + j * 128 : 256 + j * 128] = (field * inverse).astype(BF16)

    for tile in range(PLANE // TILE):
        start = tile * TILE
        turned = dot(pad_ref[:, :, start : start + WINDOW].reshape(count * NODE_COUNT, WINDOW), rot_ref[tile])
        for first, lanes, side in PIECES:
            if first // TILE != tile:
                continue
            vr = rows_ref[0:1, first : first + lanes]
            inside = first - start
            for s in range(count):
                here = s * PLANE + first
                field = nodes_of(f_ref, here, lanes)
                both = jnp.concatenate([(field * vr).astype(BF16), field.astype(BF16)], axis=0)
                change = turned[s * NODE_COUNT : (s + 1) * NODE_COUNT, inside : inside + lanes]
                change = change + dot(lhs_ref[s, side], both)
                out_ref[:, :, here : here + lanes] = change.astype(BF16).reshape(NODES, LOCAL_Z, lanes)


def total_of(parts):
    while len(parts) > 1:
        parts = [parts[k] + parts[k + 1] for k in range(0, len(parts), 2)]
    return parts[0]


def prepare_nodes(total, codes, place, rows_ref, edge_ref, table_ref, node_ref, wall_ref, plane_ref):
    wide = jnp.concatenate([total, jnp.zeros((128 - MOMENTS, 128), F32)], axis=0)
    table_ref[...] = jnp.transpose(wide)
    rho, ur, ut, uz, temp, qr, qt, qz = macroscopic_of(lambda k: table_ref[:, k : k + 1])
    inv_t = 1.0 / temp
    beta = ((1.0 - VISCOUS_RATIO) / 5.0) / (rho * temp * temp)
    kappa = rho * (TIME_STEP / KNUDSEN)
    peak = kappa * rho * inv_t * jnp.sqrt(inv_t)
    columns = [uz, -0.5 * inv_t, qz * beta, inv_t, peak, 1.0 - kappa, ur, ut, qr * beta, qt * beta]
    for k, column in enumerate(columns):
        node_ref[k] = jnp.broadcast_to(column, (NODE_COUNT, 128))
    net = table_ref[:, 3:4]
    gross = table_ref[:, 13:14]
    to_bottom = 0.5 * (gross - net)
    to_top = 0.5 * (gross + net)
    incident = jnp.sum(edge_ref[0] * to_bottom, axis=0, keepdims=True)
    upward = jnp.sum(edge_ref[1] * to_top, axis=0, keepdims=True)
    bottom = jnp.where(codes[0, 0] == 1, SAT_DENSITY, incident * (1.0 / HALF_FLUX))
    top = jnp.where(codes[1, 0] == 2, 0.0, upward * (1.0 / HALF_FLUX))
    density = jnp.where(place == 0, bottom, top)
    wall_ref[...] = jnp.transpose(jnp.broadcast_to(density, (128, 128)))[0:NODES, :]

    def one_radius(r, carry):
        rows = pl.ds(pl.multiple_of(r * LOCAL_Z, LOCAL_Z), LOCAL_Z)
        n_half, n_inv = node_ref[1, rows, :], node_ref[3, rows, :]
        n_ur, n_ut = node_ref[6, rows, :], node_ref[7, rows, :]
        n_qr, n_qt = node_ref[8, rows, :], node_ref[9, rows, :]
        for j in range(PLANE // 128):
            at = pl.ds(j * 128, 128)
            cr = rows_ref[0:1, at] - n_ur
            ct = rows_ref[1:2, at] - n_ut
            square = cr * cr + ct * ct
            gauss = jnp.exp(square * n_half)
            along = cr * n_qr + ct * n_qt
            plane_ref[0, rows, at] = gauss
            plane_ref[1, rows, at] = along
            plane_ref[2, rows, at] = square * n_inv
        return carry

    lax.fori_loop(0, NODES, one_radius, 0)


def slot_factors(vz, node_ref):
    cz = vz - node_ref[0]
    square = cz * cz
    return node_ref[4] * jnp.exp(square * node_ref[1]), cz * node_ref[2], square * node_ref[3] - 5.0


def ghost_lifts(vz, ghost_r_ref, ghost_z_ref, lhs_ref):
    lean = jnp.abs(vz) * ghost_z_ref[jnp.where(vz > 0, 1, 0)]
    lhs_ref[0] = (ghost_r_ref[0] + lean).astype(BF16)
    lhs_ref[1] = (ghost_r_ref[1] + lean).astype(BF16)


def ghost_rows(s, vz, place, in_left_ref, in_turned_ref, in_right_ref, in_axial_ref, rows_ref, wall_ref, ghost_ref):
    own = (place == 0) == (vz > 0)
    strength = jnp.exp(-0.5 * vz * vz + jnp.zeros((NODES, 128), F32)) * wall_ref[...]
    for j in range(PLANE // 128):
        at = pl.ds(j * 128, 128)
        if j * 128 < HALF:
            radial = in_right_ref[s, :, at]
        else:
            back = pl.ds(j * 128 - HALF, 128)
            radial = in_left_ref[s, :, back] + in_turned_ref[s, :, back]
        axial = jnp.where(own, strength * rows_ref[2:3, at], in_axial_ref[s, :, at])
        rows = jnp.concatenate([rows_ref[0:1, at] * radial, axial, jnp.zeros((8, 128), F32)], axis=0)
        ghost_ref[:, at] = rows.astype(BF16)


def outer_kernel(part_count, last, order, codes, *refs):
    part_refs, refs = refs[:part_count], refs[part_count:]
    f_ref, inner_ref, in_left_ref, in_turned_ref, in_right_ref, in_axial_ref = refs[:6]
    rows_ref, edge_ref, ghost_r_ref, ghost_z_ref = refs[6:10]
    refs = refs[10:]
    if last:
        out_ref, refs = refs[0], refs[1:]
    else:
        (trace_ref, mirror_ref, out_ref, right_ref, left_ref, turned_ref, axial_ref), refs = refs[:7], refs[7:]
    plane_ref, node_ref, wall_ref, slot_ref, lhs_ref, ghost_ref, table_ref = refs
    step = pl.program_id(0)
    row, place = places_of()

    @pl.when(step == 0)
    def _():
        total = total_of([p[...] for p in part_refs])
        prepare_nodes(total, codes, place, rows_ref, edge_ref, table_ref, node_ref, wall_ref, plane_ref)

    vz = slot_speed(order, step)
    for k, value in enumerate(slot_factors(vz, node_ref)):
        slot_ref[k] = value
    ghost_lifts(vz, ghost_r_ref, ghost_z_ref, lhs_ref)
    ghost_rows(0, vz, place, in_left_ref, in_turned_ref, in_right_ref, in_axial_ref, rows_ref, wall_ref, ghost_ref)
    for first, lanes, side in PIECES:
        lifted = dot(lhs_ref[side, :, 0:GHOST_ROWS], ghost_ref[:, first : first + lanes])
        pieces = []
        for inside in range(0, lanes, 128):
            here = first + inside
            at = pl.ds(here, 128)
            new = nodes_of(f_ref, here, 128) * node_ref[5] + nodes_of(inner_ref, here, 128).astype(F32)
            new = new + lifted[:, inside : inside + 128]
            bend = (plane_ref[1, :, at] + slot_ref[1]) * (plane_ref[2, :, at] + slot_ref[2]) + 1.0
            new = new + (plane_ref[0, :, at] * slot_ref[0]) * bend
            out_ref[:, :, here : here + 128] = new.reshape(NODES, LOCAL_Z, 128)
            pieces.append(new.astype(BF16))
        if not last:
            narrow = jnp.concatenate(pieces, axis=1) if len(pieces) > 1 else pieces[0]
            send_piece(0, first, lanes, side, place, narrow, trace_ref, right_ref, left_ref, axial_ref)
    if not last:
        turn_traces(1, row, mirror_ref, left_ref, turned_ref)


def last_kernel(part_count, codes, *refs):
    total_ref = total_of([p[...] for p in refs[:part_count]])
    edge_ref, macro_ref, flux_ref = refs[part_count:]
    row, place = places_of()
    values = macroscopic_of(lambda k: total_ref[k : k + 1, :])
    for k in range(8):
        for r in range(NODES):
            macro_ref[k, r : r + 1, :] = values[k][:, r * LOCAL_Z : (r + 1) * LOCAL_Z]
    net, gross = total_ref[3:4, :], total_ref[13:14, :]
    to_bottom = jnp.broadcast_to(0.5 * (gross - net), (8, 128))
    to_top = jnp.broadcast_to(0.5 * (gross + net), (8, 128))
    exact = lambda x, y: jnp.dot(x, y, precision=lax.Precision.HIGHEST, preferred_element_type=F32)
    incident = exact(to_bottom, edge_ref[0])
    upward = exact(to_top, edge_ref[1])
    downward = exact(to_bottom, edge_ref[1])
    bottom = jnp.where(codes[0, 0] == 1, SAT_DENSITY * HALF_FLUX - incident, 0.0)
    top = jnp.where(codes[1, 0] == 2, upward - downward, 0.0)
    flux_ref[...] = jnp.where(place == 0, bottom, top)[0:1, 0:NODES]


def whole(shape):
    return pl.BlockSpec(shape, lambda *a: (0,) * len(shape), pipeline_mode=pl.Buffered(1))


def on_device(distribution, z_order, edge_codes):
    local_r, local_z, vdev = distribution.shape
    assert local_r == NODES and local_z == LOCAL_Z
    slots = vdev // PLANE
    group = math.gcd(slots, 3)
    rows_total = lax.axis_size("row")
    verts = lax.axis_size("vert")
    assert lax.axis_size("gz") == 2
    rows, pos, edge = jnp.asarray(ROWS), jnp.asarray(NODE_POS), jnp.asarray(EDGE)
    radial_m, axial_m = jnp.asarray(RADIAL_M), jnp.asarray(AXIAL_M)
    ghost_r, ghost_z = jnp.asarray(GHOST_R), jnp.asarray(GHOST_Z)
    trace_m, mirror_m, rot_m = jnp.asarray(TRACE_M), jnp.asarray(MIRROR_M), jnp.asarray(ROTATION_M)

    def slab(count):
        return pl.BlockSpec((NODES, LOCAL_Z, count * PLANE), lambda i, *n: (0, 0, i))

    def radial_spec(count):
        return pl.BlockSpec((count, LOCAL_Z, HALF), lambda i, *n: (i, 0, 0))

    def axial_spec(count):
        return pl.BlockSpec((count, NODES, PLANE), lambda i, *n: (i, 0, 0))

    def trace_specs(count):
        return [radial_spec(count), radial_spec(count), radial_spec(count), axial_spec(count)]

    mom_spec = whole((MOMENTS, 128))
    radial_shape = jax.ShapeDtypeStruct((slots, LOCAL_Z, HALF), F32)
    axial_shape = jax.ShapeDtypeStruct((slots, NODES, PLANE), F32)
    mom_shape = jax.ShapeDtypeStruct((MOMENTS, 128), F32)
    big_shape = jax.ShapeDtypeStruct(distribution.shape, F32)
    trace_shapes = [radial_shape, radial_shape, radial_shape, axial_shape]
    square = pltpu.VMEM((NODE_COUNT, 128), F32)

    def call(body, name, count, limit, in_specs, out_specs, out_shape, scratch, args):
        return pl.pallas_call(
            body,
            grid_spec=pltpu.PrefetchScalarGridSpec(
                num_scalar_prefetch=2,
                grid=(slots // count,),
                in_specs=in_specs,
                out_specs=out_specs,
                scratch_shapes=scratch,
            ),
            out_shape=out_shape,
            compiler_params=pltpu.CompilerParams(vmem_limit_bytes=limit * 1024 * 1024),
            name=name,
        )(z_order, edge_codes, *args)

    def all_whole(tables):
        return [whole(x.shape) for x in tables]

    def traces_of(f):
        return call(
            lambda *a: trace_kernel(group, *a), "traces", group, 20, [slab(group)] + all_whole([trace_m, mirror_m]),
            trace_specs(group), trace_shapes, [], [f, trace_m, mirror_m],
        )

    def moments_of(f):
        return call(
            lambda *a: moment_kernel(group, *a), "moments", group, 20, [slab(group)] + all_whole([rows]),
            mom_spec, mom_shape, [pltpu.VMEM((5, NODES, LOCAL_Z, PLANE), F32), square], [f, rows],
        )

    def inner(f):
        tables = [rows, pos, radial_m, axial_m, rot_m]
        scratch = [
            square,
            pltpu.VMEM((group, NODE_COUNT, PLANE + 256), BF16),
            pltpu.VMEM((group, 2, NODE_COUNT, 2 * NODE_COUNT), BF16),
        ]
        return call(
            lambda *a: inner_kernel(group, *a), "inner_increments", group, 22, [slab(group)] + all_whole(tables),
            slab(group), jax.ShapeDtypeStruct(f.shape, BF16), scratch, [f] + tables,
        )

    def outer(f, change, ghosts, parts, last):
        tables = [rows, edge, ghost_r, ghost_z] + ([] if last else [trace_m, mirror_m])
        scratch = [
            pltpu.VMEM((3, NODE_COUNT, PLANE), F32),
            pltpu.VMEM((10, NODE_COUNT, 128), F32),
            pltpu.VMEM((NODES, 128), F32),
            pltpu.VMEM((3, NODE_COUNT, 128), F32),
            pltpu.VMEM((2, NODE_COUNT, 128), BF16),
            pltpu.VMEM((GHOST_ROWS, PLANE), BF16),
            square,
        ]
        out = call(
            lambda *a: outer_kernel(len(parts), last, *a),
            "last_update" if last else "update", 1, 20,
            [mom_spec] * len(parts) + [slab(1), slab(1)] + trace_specs(1) + all_whole(tables),
            [slab(1)] + ([] if last else trace_specs(1)),
            [big_shape] + ([] if last else trace_shapes),
            scratch,
            [*parts, f, change, *ghosts, *tables],
        )
        return out[0], out[1:]

    def spread(moments):
        parts = [moments]
        for shift in range(1, verts):
            parts.append(lax.ppermute(moments, "vert", [(i, i ^ shift) for i in range(verts)]))
        return parts

    def halo(right, left, turned, axial):
        from_axial = lax.ppermute(axial, "gz", [(0, 1), (1, 0)])
        from_left = lax.ppermute(right, "row", [(i, i + 1) for i in range(rows_total - 1)])
        from_right = lax.ppermute(left, "row", [(i + 1, i) for i in range(rows_total - 1)])
        return from_left, turned, from_right, from_axial

    current = distribution
    traces = traces_of(current)
    for number in range(STEPS):
        ghosts = halo(*traces)
        parts = spread(moments_of(current))
        change = inner(current)
        current, traces = outer(current, change, ghosts, parts, number == STEPS - 1)
    parts = spread(moments_of(current))
    macro, flux = pl.pallas_call(
        lambda *a: last_kernel(len(parts), *a),
        grid_spec=pltpu.PrefetchScalarGridSpec(
            num_scalar_prefetch=1,
            grid=(1,),
            in_specs=[mom_spec] * len(parts) + [whole(edge.shape)],
            out_specs=[whole((8, NODES, LOCAL_Z)), whole((1, NODES))],
        ),
        out_shape=[
            jax.ShapeDtypeStruct((8, NODES, LOCAL_Z), F32),
            jax.ShapeDtypeStruct((1, NODES), F32),
        ],
        name="macroscopic",
    )(edge_codes, *parts, edge)
    return (current, macro, flux)


def solution(mesh):
    in_specs = (P("row", "gz", "vert"), P("vert"), P(None, "row"))
    out_specs = (P("row", "gz", "vert"), P(None, "row", "gz"), P("gz", "row"))
    return jax.shard_map(
        on_device, mesh=mesh, in_specs=in_specs, out_specs=out_specs, check_vma=False
    )
```

```python
import math

import jax
import jax.numpy as jnp
import ml_dtypes
import numpy as np
from jax import lax
from jax.experimental import pallas as pl
from jax.experimental.pallas import tpu as pltpu
from jax.sharding import PartitionSpec as P

NODES = 8
NVR = 48
NVT = 48
NVZ = 48
STEPS = 2

ELEMENT_WIDTH = 4.0
TIME_STEP = 0.001
KNUDSEN = 0.005
VISCOUS_RATIO = 2.0 / 3.0
SAT_DENSITY = 1.5
SPEED_LIMIT = 5.0

PLANE = NVR * NVT
HALF = PLANE // 2
THIRD = HALF // 3
BOTTOM, TOP = 0, 1
LOCAL_Z = 2 * NODES
NODE_COUNT = NODES * LOCAL_Z
TILE = 256
WINDOW = 512
GHOST_ROWS = 32
MOMENTS = 16
F32 = jnp.float32
BF16 = jnp.bfloat16
PIECES = [(t, TILE, 0) for t in range(0, 1024, TILE)] + [(1024, 128, 0), (1152, 128, 1)] + [
    (t, TILE, 1) for t in range(1280, PLANE, TILE)
]


def legendre_pair(position, point_count):
    previous = 1.0
    current = position
    for degree in range(2, point_count + 1):
        previous, current = (
            current,
            ((2 * degree - 1) * position * current - (degree - 1) * previous) / degree,
        )
    slope = point_count * (position * current - previous) / (position * position - 1.0)
    return (current, slope)


def dg_tables(point_count):
    point_list = []
    weight_list = []
    for number in range(point_count):
        position = math.cos(math.pi * (number + 0.75) / (point_count + 0.5))
        for sweep in range(60):
            value, slope = legendre_pair(position, point_count)
            position = position - value / slope
        value, slope = legendre_pair(position, point_count)
        point_list.append(position)
        weight_list.append(2.0 / ((1.0 - position * position) * slope * slope))
    point_list = point_list[::-1]
    weight_list = weight_list[::-1]
    points = np.array(point_list)
    derivative = np.zeros((point_count, point_count))
    right = np.zeros(point_count)
    left = np.zeros(point_count)
    products = [
        np.prod([points[i] - points[j] for j in range(point_count) if j != i])
        for i in range(point_count)
    ]
    for i in range(point_count):
        others = [j for j in range(point_count) if j != i]
        derivative[i, i] = sum(1.0 / (points[i] - points[j]) for j in others)
        for j in others:
            derivative[i, j] = products[i] / products[j] / (points[i] - points[j])
        right[i] = np.prod([1.0 - points[j] for j in others]) / products[i]
        left[i] = np.prod([-1.0 - points[j] for j in others]) / products[i]
    return points, np.array(weight_list), derivative, right, left


def speed_grid(point_count):
    return -SPEED_LIMIT + (np.arange(point_count) + 0.5) * (2.0 * SPEED_LIMIT / point_count)


POINTS, QUAD, DERIV, END_R, END_L = dg_tables(NODES)
LIFT_R = END_R / QUAD
LIFT_L = END_L / QUAD
GRID_R = speed_grid(NVR)
GRID_T = speed_grid(NVT)
GRID_Z = speed_grid(NVZ)
STEP_V = 2 * SPEED_LIMIT / NVR
WEIGHT = STEP_V**3 / (2 * math.pi) ** 1.5
HALF_FLUX = float(
    WEIGHT
    * np.sum(np.exp(-(GRID_R**2) / 2))
    * np.sum(np.exp(-(GRID_T**2) / 2))
    * np.sum(np.maximum(GRID_Z, 0.0) * np.exp(-(GRID_Z**2) / 2))
)
SCALE = TIME_STEP * 2.0 / ELEMENT_WIDTH


def transport_tables():
    ident = np.eye(NODES)
    up = DERIV + np.outer(LIFT_L, END_L)
    down = DERIV - np.outer(LIFT_R, END_R)
    zero = np.zeros((NODES, NODES))
    wide = np.eye(LOCAL_Z)
    radial = np.stack([np.kron(down, wide), np.kron(up, wide), np.kron(DERIV, wide)])
    zup = np.block([[up, zero], [-np.outer(LIFT_L, END_R), up]])
    zdown = np.block([[down, np.outer(LIFT_R, END_L)], [zero, down]])
    zout = np.block([[down, np.outer(LIFT_R, END_L)], [zero, DERIV]])
    axial = np.stack([np.kron(ident, zdown), np.kron(ident, zup), np.kron(ident, zout)])
    ghost_r = np.zeros((2, NODE_COUNT, 128))
    ghost_z = np.zeros((2, NODE_COUNT, 128))
    for r in range(NODES):
        for z in range(LOCAL_Z):
            n = r * LOCAL_Z + z
            ghost_r[0, n, z] = -LIFT_R[r]
            ghost_r[1, n, z] = LIFT_L[r]
            if z >= NODES:
                ghost_z[0, n, LOCAL_Z + r] = LIFT_R[z - NODES]
            else:
                ghost_z[1, n, LOCAL_Z + r] = LIFT_L[z]
    trace = np.zeros((2, 2, GHOST_ROWS, NODE_COUNT))
    for side in range(2):
        radial_row = END_R if side == 1 else END_L
        for place in range(2):
            for z in range(LOCAL_Z):
                for r in range(NODES):
                    trace[side, place, z, r * LOCAL_Z + z] = radial_row[r]
            for r in range(NODES):
                for k in range(NODES):
                    if place == 0:
                        trace[side, place, LOCAL_Z + r, r * LOCAL_Z + NODES + k] = END_R[k]
                    else:
                        trace[side, place, LOCAL_Z + r, r * LOCAL_Z + k] = END_L[k]
    return (
        (-SCALE * radial).astype(ml_dtypes.bfloat16),
        (-SCALE * axial).astype(np.float32),
        (SCALE * ghost_r).astype(np.float32),
        (SCALE * ghost_z).astype(np.float32),
        trace.astype(ml_dtypes.bfloat16),
    )


def rotation_table():
    full = np.zeros((PLANE + 2 * TILE, PLANE))
    factor = TIME_STEP / (2 * STEP_V)
    for a in range(NVR):
        for b in range(NVT):
            n = a * NVT + b
            first = factor * GRID_T[b] * GRID_T[b]
            second = factor * GRID_R[a] * GRID_T[b]
            if a + 1 < NVR:
                full[TILE + n + NVT, n] = -first
            if a > 0:
                full[TILE + n - NVT, n] = first
            if b + 1 < NVT:
                full[TILE + n + 1, n] = second
            if b > 0:
                full[TILE + n - 1, n] = -second
    tiles = [full[TILE + t - 128 : TILE + t - 128 + WINDOW, t : t + TILE] for t in range(0, PLANE, TILE)]
    return np.stack(tiles).astype(ml_dtypes.bfloat16)


def mirror_table():
    table = np.zeros((THIRD, THIRD))
    groups = THIRD // NVT
    for g in range(groups):
        for b in range(NVT):
            table[(groups - 1 - g) * NVT + b, g * NVT + b] = 1.0
    return table.astype(ml_dtypes.bfloat16)


def plane_rows():
    vr = np.repeat(GRID_R, NVT)
    vt = np.tile(GRID_T, NVR)
    rows = np.zeros((8, PLANE))
    rows[0] = vr
    rows[1] = vt
    rows[2] = np.exp(-(vr**2 + vt**2) / 2)
    return rows.astype(np.float32)


def edge_table():
    table = np.zeros((2, NODE_COUNT, 128))
    for r in range(NODES):
        for k in range(NODES):
            table[0, r * LOCAL_Z + k, r] = END_L[k]
            table[1, r * LOCAL_Z + NODES + k, r] = END_R[k]
    return table.astype(np.float32)


def node_columns():
    table = np.zeros((NODE_COUNT, 128))
    for r in range(NODES):
        table[r * LOCAL_Z : (r + 1) * LOCAL_Z, :] = (1.0 + POINTS[r]) / 2
    return table.astype(np.float32)


RADIAL_M, AXIAL_M, GHOST_R, GHOST_Z, TRACE_M = transport_tables()
ROTATION_M = rotation_table()
MIRROR_M = mirror_table()
ROWS = plane_rows()
EDGE = edge_table()
NODE_POS = node_columns()


def slot_speed(order, slot):
    return (order[slot].astype(F32) + 0.5) * (2 * SPEED_LIMIT / NVZ) - SPEED_LIMIT


def dot(x, y):
    return jnp.dot(x, y, preferred_element_type=F32)


def macroscopic_of(m):
    rho = m(0)
    inv = 1.0 / rho
    ur, ut, uz = m(1) * inv, m(2) * inv, m(3) * inv
    rr, tt, rt, zz, rz, tz = (m(k) for k in range(4, 10))
    energy = rr + tt + zz
    speed = ur * ur + ut * ut + uz * uz
    temp = (energy * inv - speed) * (1.0 / 3.0)
    tail = 2.0 * rho * speed - energy
    qr = 0.5 * (m(10) - 2.0 * (ur * rr + ut * rt + uz * rz) + ur * tail)
    qt = 0.5 * (m(11) - 2.0 * (ur * rt + ut * tt + uz * tz) + ut * tail)
    qz = 0.5 * (m(12) - 2.0 * (ur * rz + ut * tz + uz * zz) + uz * tail)
    return rho, ur, ut, uz, temp, qr, qt, qz


def add_speed_sums(field, vz, sums):
    one = field * vz
    two = one * vz
    return [
        sums[0] + field,
        sums[1] + one,
        sums[2] + two,
        sums[3] + two * vz,
        sums[4] + field * jnp.abs(vz),
    ]


def finish_moments(sums_ref, rows_ref, table_ref, out_ref):
    lane = lax.broadcasted_iota(jnp.int32, (LOCAL_Z, 128), 1)

    def one_radius(r, carry):
        acc = [jnp.zeros((LOCAL_Z, 128), F32) for _ in range(14)]
        for j in range(PLANE // 128):
            at = pl.ds(j * 128, 128)
            vr = rows_ref[0:1, at]
            vt = rows_ref[1:2, at]
            g0, g1, g2, g3, g4 = (sums_ref[k, r, :, at] for k in range(5))
            a = vr * g0
            b = vt * g0
            aa = vr * a
            bb = vt * b
            c = vr * g1
            d = vt * g1
            perp = aa + bb + g2
            new = [g0, a, b, g1, aa, bb, vr * b, g2, c, d, vr * perp, vt * perp, vr * c + vt * d + g3, g4]
            acc = [x + y for x, y in zip(acc, new)]
        block = jnp.zeros((LOCAL_Z, 128), F32)
        for k in range(14):
            block = jnp.where(lane == k, WEIGHT * jnp.sum(acc[k], axis=1, keepdims=True), block)
        table_ref[pl.ds(pl.multiple_of(r * LOCAL_Z, LOCAL_Z), LOCAL_Z), :] = block
        return carry

    lax.fori_loop(0, NODES, one_radius, 0)
    out_ref[...] = jnp.transpose(table_ref[...])[0:MOMENTS, :]


def clear_sums(sums_ref):
    sums_ref[...] = jnp.zeros(sums_ref.shape, F32)


def places_of():
    return lax.axis_index("row"), lax.axis_index("gz")


def send_piece(s, first, lanes, side, place, narrow, trace_ref, right_ref, left_ref, axial_ref):
    got = dot(trace_ref[side, place], narrow)
    if side == 1:
        right_ref[s, :, first - HALF : first - HALF + lanes] = got[0:LOCAL_Z]
    else:
        left_ref[s, :, first : first + lanes] = got[0:LOCAL_Z]
    axial_ref[s, :, first : first + lanes] = got[LOCAL_Z : LOCAL_Z + NODES]


def turn_traces(count, row, mirror_ref, left_ref, turned_ref):
    @pl.when(row == 0)
    def _():
        for part in range(3):
            start = (2 - part) * THIRD
            flat = left_ref[:, :, start : start + THIRD].reshape(count * LOCAL_Z, THIRD).astype(BF16)
            got = dot(flat, mirror_ref[...])
            turned_ref[:, :, part * THIRD : (part + 1) * THIRD] = got.reshape(count, LOCAL_Z, THIRD)

    @pl.when(row != 0)
    def _():
        turned_ref[...] = jnp.zeros(turned_ref.shape, F32)


def nodes_of(ref, first, lanes):
    return ref[:, :, first : first + lanes].reshape(NODE_COUNT, lanes)


def trace_kernel(
    count, order, codes, f_ref, trace_ref, mirror_ref, right_ref, left_ref, turned_ref, axial_ref
):
    row, place = places_of()
    for s in range(count):
        for first, lanes, side in PIECES:
            narrow = nodes_of(f_ref, s * PLANE + first, lanes).astype(BF16)
            send_piece(s, first, lanes, side, place, narrow, trace_ref, right_ref, left_ref, axial_ref)
    turn_traces(count, row, mirror_ref, left_ref, turned_ref)


def moment_kernel(count, order, codes, f_ref, rows_ref, mom_ref, sums_ref, table_ref):
    step = pl.program_id(0)

    @pl.when(step == 0)
    def _():
        clear_sums(sums_ref)

    speeds = [slot_speed(order, step * count + s) for s in range(count)]
    for j in range(0, PLANE, 128):
        at = pl.ds(j, 128)
        for r in range(NODES):
            sums = [sums_ref[k, r, :, at] for k in range(5)]
            for s in range(count):
                sums = add_speed_sums(f_ref[r, :, pl.ds(s * PLANE + j, 128)], speeds[s], sums)
            for k in range(5):
                sums_ref[k, r, :, at] = sums[k]

    @pl.when(step == pl.num_programs(0) - 1)
    def _():
        finish_moments(sums_ref, rows_ref, table_ref, mom_ref)


def inner_kernel(
    count, order, codes, f_ref, rows_ref, pos_ref, radial_ref, axial_m_ref, rot_ref,
    out_ref, inverse_ref, pad_ref, lhs_ref,
):
    step = pl.program_id(0)
    row, place = places_of()

    @pl.when(step == 0)
    def _():
        pad_ref[:, :, 0:128] = jnp.zeros((count, NODE_COUNT, 128), BF16)
        pad_ref[:, :, 128 + PLANE :] = jnp.zeros((count, NODE_COUNT, 128), BF16)
        inverse_ref[...] = 1.0 / (ELEMENT_WIDTH * (row.astype(F32) + pos_ref[...]))
        minus = radial_ref[jnp.where(row == lax.axis_size("row") - 1, 2, 0)]
        for s in range(count):
            lhs_ref[s, 0, :, 0:NODE_COUNT] = minus
            lhs_ref[s, 1, :, 0:NODE_COUNT] = radial_ref[1]

    kind_out = jnp.where(jnp.logical_and(place == 1, codes[0, TOP] == 2), 2, 0)
    inverse = inverse_ref[...]
    for s in range(count):
        vz = slot_speed(order, step * count + s)
        axial = (vz * axial_m_ref[jnp.where(vz > 0, 1, kind_out)]).astype(BF16)
        lhs_ref[s, 0, :, NODE_COUNT:] = axial
        lhs_ref[s, 1, :, NODE_COUNT:] = axial
        for j in range(PLANE // 128):
            field = nodes_of(f_ref, s * PLANE + j * 128, 128)
            pad_ref[s, :, 128 + j * 128 : 256 + j * 128] = (field * inverse).astype(BF16)

    for tile in range(PLANE // TILE):
        start = tile * TILE
        turned = dot(pad_ref[:, :, start : start + WINDOW].reshape(count * NODE_COUNT, WINDOW), rot_ref[tile])
        for first, lanes, side in PIECES:
            if first // TILE != tile:
                continue
            vr = rows_ref[0:1, first : first + lanes]
            inside = first - start
            for s in range(count):
                here = s * PLANE + first
                field = nodes_of(f_ref, here, lanes)
                both = jnp.concatenate([(field * vr).astype(BF16), field.astype(BF16)], axis=0)
                change = turned[s * NODE_COUNT : (s + 1) * NODE_COUNT, inside : inside + lanes]
                change = change + dot(lhs_ref[s, side], both)
                out_ref[:, :, here : here + lanes] = change.astype(BF16).reshape(NODES, LOCAL_Z, lanes)


def total_of(parts):
    while len(parts) > 1:
        parts = [parts[k] + parts[k + 1] for k in range(0, len(parts), 2)]
    return parts[0]


def prepare_nodes(total, codes, place, rows_ref, edge_ref, table_ref, node_ref, wall_ref, plane_ref):
    wide = jnp.concatenate([total, jnp.zeros((128 - MOMENTS, 128), F32)], axis=0)
    table_ref[...] = jnp.transpose(wide)
    rho, ur, ut, uz, temp, qr, qt, qz = macroscopic_of(lambda k: table_ref[:, k : k + 1])
    inv_t = 1.0 / temp
    beta = ((1.0 - VISCOUS_RATIO) / 5.0) / (rho * temp * temp)
    kappa = rho * (TIME_STEP / KNUDSEN)
    peak = kappa * rho * inv_t * jnp.sqrt(inv_t)
    columns = [uz, -0.5 * inv_t, qz * beta, inv_t, peak, 1.0 - kappa, ur, ut, qr * beta, qt * beta]
    for k, column in enumerate(columns):
        node_ref[k] = jnp.broadcast_to(column, (NODE_COUNT, 128))
    net = table_ref[:, 3:4]
    gross = table_ref[:, 13:14]
    to_bottom = 0.5 * (gross - net)
    to_top = 0.5 * (gross + net)
    incident = jnp.sum(edge_ref[0] * to_bottom, axis=0, keepdims=True)
    upward = jnp.sum(edge_ref[1] * to_top, axis=0, keepdims=True)
    bottom = jnp.where(codes[0, BOTTOM] == 1, SAT_DENSITY, incident * (1.0 / HALF_FLUX))
    top = jnp.where(codes[0, TOP] == 2, 0.0, upward * (1.0 / HALF_FLUX))
    density = jnp.where(place == 0, bottom, top)
    wall_ref[...] = jnp.transpose(jnp.broadcast_to(density, (128, 128)))[0:NODES, :]

    def one_radius(r, carry):
        rows = pl.ds(pl.multiple_of(r * LOCAL_Z, LOCAL_Z), LOCAL_Z)
        n_half, n_inv = node_ref[1, rows, :], node_ref[3, rows, :]
        n_ur, n_ut = node_ref[6, rows, :], node_ref[7, rows, :]
        n_qr, n_qt = node_ref[8, rows, :], node_ref[9, rows, :]
        for j in range(PLANE // 128):
            at = pl.ds(j * 128, 128)
            cr = rows_ref[0:1, at] - n_ur
            ct = rows_ref[1:2, at] - n_ut
            square = cr * cr + ct * ct
            gauss = jnp.exp(square * n_half)
            along = cr * n_qr + ct * n_qt
            plane_ref[0, rows, at] = gauss
            plane_ref[1, rows, at] = along
            plane_ref[2, rows, at] = square * n_inv
        return carry

    lax.fori_loop(0, NODES, one_radius, 0)


def slot_factors(vz, node_ref):
    cz = vz - node_ref[0]
    square = cz * cz
    return node_ref[4] * jnp.exp(square * node_ref[1]), cz * node_ref[2], square * node_ref[3] - 5.0


def ghost_lifts(vz, ghost_r_ref, ghost_z_ref, lhs_ref):
    lean = jnp.abs(vz) * ghost_z_ref[jnp.where(vz > 0, 1, 0)]
    lhs_ref[0] = (ghost_r_ref[0] + lean).astype(BF16)
    lhs_ref[1] = (ghost_r_ref[1] + lean).astype(BF16)


def ghost_rows(s, vz, place, in_left_ref, in_turned_ref, in_right_ref, in_axial_ref, rows_ref, wall_ref, ghost_ref):
    own = (place == 0) == (vz > 0)
    strength = jnp.exp(-0.5 * vz * vz + jnp.zeros((NODES, 128), F32)) * wall_ref[...]
    for j in range(PLANE // 128):
        at = pl.ds(j * 128, 128)
        if j * 128 < HALF:
            radial = in_right_ref[s, :, at]
        else:
            back = pl.ds(j * 128 - HALF, 128)
            radial = in_left_ref[s, :, back] + in_turned_ref[s, :, back]
        axial = jnp.where(own, strength * rows_ref[2:3, at], in_axial_ref[s, :, at])
        rows = jnp.concatenate([rows_ref[0:1, at] * radial, axial, jnp.zeros((8, 128), F32)], axis=0)
        ghost_ref[:, at] = rows.astype(BF16)


def outer_kernel(count, part_count, order, codes, *refs):
    part_refs, refs = refs[:part_count], refs[part_count:]
    f_ref, inner_ref, in_left_ref, in_turned_ref, in_right_ref, in_axial_ref = refs[:6]
    rows_ref, edge_ref, ghost_r_ref, ghost_z_ref, out_ref = refs[6:11]
    plane_ref, node_ref, wall_ref, slot_ref, work_ref, lhs_ref, ghost_ref, table_ref = refs[11:]
    step = pl.program_id(0)
    row, place = places_of()

    @pl.when(step == 0)
    def _():
        total = total_of([p[...] for p in part_refs])
        prepare_nodes(total, codes, place, rows_ref, edge_ref, table_ref, node_ref, wall_ref, plane_ref)

    for s in range(count):
        vz = slot_speed(order, step * count + s)
        for k, value in enumerate(slot_factors(vz, node_ref)):
            slot_ref[s, k] = value
        ghost_lifts(vz, ghost_r_ref, ghost_z_ref, lhs_ref)
        ghost_rows(
            s, vz, place, in_left_ref, in_turned_ref, in_right_ref, in_axial_ref, rows_ref, wall_ref, ghost_ref
        )
        for first, lanes, side in PIECES:
            work_ref[s, :, first : first + lanes] = dot(
                lhs_ref[side, :, 0:GHOST_ROWS], ghost_ref[:, first : first + lanes]
            )

    def update(r, carry):
        rows = pl.ds(pl.multiple_of(r * LOCAL_Z, LOCAL_Z), LOCAL_Z)
        keep = node_ref[5, rows, :]
        factor = [[slot_ref[s, k, rows, :] for k in range(3)] for s in range(count)]
        for j in range(PLANE // 128):
            at = pl.ds(j * 128, 128)
            gauss, along, reach = (plane_ref[k, rows, at] for k in range(3))
            for s in range(count):
                here = pl.ds(s * PLANE + j * 128, 128)
                new = f_ref[r, :, here] * keep + work_ref[s, rows, at] + inner_ref[r, :, here].astype(F32)
                bend = (along + factor[s][1]) * (reach + factor[s][2]) + 1.0
                out_ref[r, :, here] = new + (gauss * factor[s][0]) * bend
        return carry

    lax.fori_loop(0, NODES, update, 0)


def last_kernel(part_count, codes, *refs):
    total_ref = total_of([p[...] for p in refs[:part_count]])
    edge_ref, macro_ref, flux_ref = refs[part_count:]
    row, place = places_of()
    values = macroscopic_of(lambda k: total_ref[k : k + 1, :])
    for k in range(8):
        for r in range(NODES):
            macro_ref[k, r : r + 1, :] = values[k][:, r * LOCAL_Z : (r + 1) * LOCAL_Z]
    net, gross = total_ref[3:4, :], total_ref[13:14, :]
    to_bottom = jnp.broadcast_to(0.5 * (gross - net), (8, 128))
    to_top = jnp.broadcast_to(0.5 * (gross + net), (8, 128))
    exact = lambda x, y: jnp.dot(x, y, precision=lax.Precision.HIGHEST, preferred_element_type=F32)
    incident = exact(to_bottom, edge_ref[0])
    upward = exact(to_top, edge_ref[1])
    downward = exact(to_bottom, edge_ref[1])
    bottom = jnp.where(codes[0, BOTTOM] == 1, SAT_DENSITY * HALF_FLUX - incident, 0.0)
    top = jnp.where(codes[0, TOP] == 2, upward - downward, 0.0)
    flux_ref[...] = jnp.where(place == 0, bottom, top)[0:1, 0:NODES]


def whole(shape):
    return pl.BlockSpec(shape, lambda *a: (0,) * len(shape), pipeline_mode=pl.Buffered(1))


def on_device(distribution, z_order, edge_codes):
    local_r, local_z, vdev = distribution.shape
    assert local_r == NODES and local_z == LOCAL_Z
    slots = vdev // PLANE
    group = math.gcd(slots, 3)
    rows_total = lax.axis_size("row")
    verts = lax.axis_size("vert")
    assert lax.axis_size("gz") == 2
    codes = edge_codes.T
    rows, pos, edge = jnp.asarray(ROWS), jnp.asarray(NODE_POS), jnp.asarray(EDGE)
    radial_m, axial_m = jnp.asarray(RADIAL_M), jnp.asarray(AXIAL_M)
    ghost_r, ghost_z = jnp.asarray(GHOST_R), jnp.asarray(GHOST_Z)
    trace_m, mirror_m, rot_m = jnp.asarray(TRACE_M), jnp.asarray(MIRROR_M), jnp.asarray(ROTATION_M)

    def slab(count):
        return pl.BlockSpec((NODES, LOCAL_Z, count * PLANE), lambda i, *n: (0, 0, i))

    def radial_spec(count):
        return pl.BlockSpec((count, LOCAL_Z, HALF), lambda i, *n: (i, 0, 0))

    def axial_spec(count):
        return pl.BlockSpec((count, NODES, PLANE), lambda i, *n: (i, 0, 0))

    def trace_specs(count):
        return [radial_spec(count), radial_spec(count), radial_spec(count), axial_spec(count)]

    mom_spec = whole((MOMENTS, 128))
    radial_shape = jax.ShapeDtypeStruct((slots, LOCAL_Z, HALF), F32)
    axial_shape = jax.ShapeDtypeStruct((slots, NODES, PLANE), F32)
    mom_shape = jax.ShapeDtypeStruct((MOMENTS, 128), F32)
    big_shape = jax.ShapeDtypeStruct(distribution.shape, F32)
    trace_shapes = [radial_shape, radial_shape, radial_shape, axial_shape]
    square = pltpu.VMEM((NODE_COUNT, 128), F32)

    def call(body, name, count, limit, in_specs, out_specs, out_shape, scratch, args):
        return pl.pallas_call(
            body,
            grid_spec=pltpu.PrefetchScalarGridSpec(
                num_scalar_prefetch=2,
                grid=(slots // count,),
                in_specs=in_specs,
                out_specs=out_specs,
                scratch_shapes=scratch,
            ),
            out_shape=out_shape,
            compiler_params=pltpu.CompilerParams(vmem_limit_bytes=limit * 1024 * 1024),
            name=name,
        )(z_order, codes, *args)

    def all_whole(tables):
        return [whole(x.shape) for x in tables]

    def traces_of(f, limit):
        return call(
            lambda *a: trace_kernel(group, *a), "traces", group, limit, [slab(group)] + all_whole([trace_m, mirror_m]),
            trace_specs(group), trace_shapes, [], [f, trace_m, mirror_m],
        )

    def moments_of(f, limit):
        return call(
            lambda *a: moment_kernel(group, *a), "moments", group, limit, [slab(group)] + all_whole([rows]),
            mom_spec, mom_shape, [pltpu.VMEM((5, NODES, LOCAL_Z, PLANE), F32), square], [f, rows],
        )

    def inner(f, limit):
        tables = [rows, pos, radial_m, axial_m, rot_m]
        scratch = [
            square,
            pltpu.VMEM((group, NODE_COUNT, PLANE + 256), BF16),
            pltpu.VMEM((group, 2, NODE_COUNT, 2 * NODE_COUNT), BF16),
        ]
        return call(
            lambda *a: inner_kernel(group, *a), "inner_increments", group, limit, [slab(group)] + all_whole(tables),
            slab(group), jax.ShapeDtypeStruct(f.shape, BF16), scratch, [f] + tables,
        )

    def outer(f, change, ghosts, parts, limit):
        count = math.gcd(slots, 2)
        tables = [rows, edge, ghost_r, ghost_z]
        scratch = [
            pltpu.VMEM((3, NODE_COUNT, PLANE), F32),
            pltpu.VMEM((10, NODE_COUNT, 128), F32),
            pltpu.VMEM((NODES, 128), F32),
            pltpu.VMEM((count, 3, NODE_COUNT, 128), F32),
            pltpu.VMEM((count, NODE_COUNT, PLANE), F32),
            pltpu.VMEM((2, NODE_COUNT, 128), BF16),
            pltpu.VMEM((GHOST_ROWS, PLANE), BF16),
            square,
        ]
        return call(
            lambda *a: outer_kernel(count, len(parts), *a), "update", count, limit,
            [mom_spec] * len(parts) + [slab(count), slab(count)] + trace_specs(count) + all_whole(tables),
            slab(count), big_shape, scratch, [*parts, f, change, *ghosts, *tables],
        )

    def spread(moments):
        parts = [moments]
        for shift in range(1, verts):
            parts.append(lax.ppermute(moments, "vert", [(i, i ^ shift) for i in range(verts)]))
        return parts

    def halo(right, left, turned, axial):
        from_axial = lax.ppermute(axial, "gz", [(0, 1), (1, 0)])
        from_left = lax.ppermute(right, "row", [(i, i + 1) for i in range(rows_total - 1)])
        from_right = lax.ppermute(left, "row", [(i + 1, i) for i in range(rows_total - 1)])
        return from_left, turned, from_right, from_axial

    current = distribution
    for number in range(STEPS):
        first, last = number == 0, number == STEPS - 1
        ghosts = halo(*traces_of(current, 56 if first else 12))
        parts = spread(moments_of(current, 56 if first else 18))
        change = inner(current, 44 if first else 20)
        current = outer(current, change, ghosts, parts, 32 if last else 20)
    parts = spread(moments_of(current, 56))
    macro, flux = pl.pallas_call(
        lambda *a: last_kernel(len(parts), *a),
        grid_spec=pltpu.PrefetchScalarGridSpec(
            num_scalar_prefetch=1,
            grid=(1,),
            in_specs=[mom_spec] * len(parts) + [whole(edge.shape)],
            out_specs=[whole((8, NODES, LOCAL_Z)), whole((1, NODES))],
        ),
        out_shape=[
            jax.ShapeDtypeStruct((8, NODES, LOCAL_Z), F32),
            jax.ShapeDtypeStruct((1, NODES), F32),
        ],
        name="macroscopic",
    )(codes, *parts, edge)
    return (current, macro, flux)


def solution(mesh):
    in_specs = (P("row", "gz", "vert"), P("vert"), P(None, "row"))
    out_specs = (P("row", "gz", "vert"), P(None, "row", "gz"), P("gz", "row"))
    return jax.shard_map(
        on_device, mesh=mesh, in_specs=in_specs, out_specs=out_specs, check_vma=False
    )
```

```python
import math

import jax
import jax.numpy as jnp
import ml_dtypes
import numpy as np
from jax import lax
from jax.experimental import pallas as pl
from jax.experimental.pallas import tpu as pltpu
from jax.sharding import PartitionSpec as P

NODES = 8
NVR = 48
NVT = 48
NVZ = 48
STEPS = 2

ELEMENT_WIDTH = 4.0
TIME_STEP = 0.001
KNUDSEN = 0.005
VISCOUS_RATIO = 2.0 / 3.0
SAT_DENSITY = 1.5
SPEED_LIMIT = 5.0

PLANE = NVR * NVT
HALF = PLANE // 2
THIRD = HALF // 3
BOTTOM, TOP = 0, 1
LOCAL_Z = 2 * NODES
NODE_COUNT = NODES * LOCAL_Z
TILE = 256
WINDOW = 512
GHOST_ROWS = 32
MOMENTS = 16
F32 = jnp.float32
BF16 = jnp.bfloat16
PIECES = [(t, TILE, 0) for t in range(0, 1024, TILE)] + [(1024, 128, 0), (1152, 128, 1)] + [
    (t, TILE, 1) for t in range(1280, PLANE, TILE)
]


def legendre_pair(position, point_count):
    previous = 1.0
    current = position
    for degree in range(2, point_count + 1):
        previous, current = (
            current,
            ((2 * degree - 1) * position * current - (degree - 1) * previous) / degree,
        )
    slope = point_count * (position * current - previous) / (position * position - 1.0)
    return (current, slope)


def dg_tables(point_count):
    point_list = []
    weight_list = []
    for number in range(point_count):
        position = math.cos(math.pi * (number + 0.75) / (point_count + 0.5))
        for sweep in range(60):
            value, slope = legendre_pair(position, point_count)
            position = position - value / slope
        value, slope = legendre_pair(position, point_count)
        point_list.append(position)
        weight_list.append(2.0 / ((1.0 - position * position) * slope * slope))
    point_list = point_list[::-1]
    weight_list = weight_list[::-1]
    points = np.array(point_list)
    derivative = np.zeros((point_count, point_count))
    right = np.zeros(point_count)
    left = np.zeros(point_count)
    products = [
        np.prod([points[i] - points[j] for j in range(point_count) if j != i])
        for i in range(point_count)
    ]
    for i in range(point_count):
        others = [j for j in range(point_count) if j != i]
        derivative[i, i] = sum(1.0 / (points[i] - points[j]) for j in others)
        for j in others:
            derivative[i, j] = products[i] / products[j] / (points[i] - points[j])
        right[i] = np.prod([1.0 - points[j] for j in others]) / products[i]
        left[i] = np.prod([-1.0 - points[j] for j in others]) / products[i]
    return points, np.array(weight_list), derivative, right, left


def speed_grid(point_count):
    return -SPEED_LIMIT + (np.arange(point_count) + 0.5) * (2.0 * SPEED_LIMIT / point_count)


POINTS, QUAD, DERIV, END_R, END_L = dg_tables(NODES)
LIFT_R = END_R / QUAD
LIFT_L = END_L / QUAD
GRID_R = speed_grid(NVR)
GRID_T = speed_grid(NVT)
GRID_Z = speed_grid(NVZ)
STEP_V = 2 * SPEED_LIMIT / NVR
WEIGHT = STEP_V**3 / (2 * math.pi) ** 1.5
HALF_FLUX = float(
    WEIGHT
    * np.sum(np.exp(-(GRID_R**2) / 2))
    * np.sum(np.exp(-(GRID_T**2) / 2))
    * np.sum(np.maximum(GRID_Z, 0.0) * np.exp(-(GRID_Z**2) / 2))
)
SCALE = TIME_STEP * 2.0 / ELEMENT_WIDTH


def transport_tables():
    ident = np.eye(NODES)
    up = DERIV + np.outer(LIFT_L, END_L)
    down = DERIV - np.outer(LIFT_R, END_R)
    zero = np.zeros((NODES, NODES))
    wide = np.eye(LOCAL_Z)
    radial = np.stack([np.kron(down, wide), np.kron(up, wide), np.kron(DERIV, wide)])
    zup = np.block([[up, zero], [-np.outer(LIFT_L, END_R), up]])
    zdown = np.block([[down, np.outer(LIFT_R, END_L)], [zero, down]])
    zout = np.block([[down, np.outer(LIFT_R, END_L)], [zero, DERIV]])
    axial = np.stack([np.kron(ident, zdown), np.kron(ident, zup), np.kron(ident, zout)])
    ghost_r = np.zeros((2, NODE_COUNT, 128))
    ghost_z = np.zeros((2, NODE_COUNT, 128))
    for r in range(NODES):
        for z in range(LOCAL_Z):
            n = r * LOCAL_Z + z
            ghost_r[0, n, z] = -LIFT_R[r]
            ghost_r[1, n, z] = LIFT_L[r]
            if z >= NODES:
                ghost_z[0, n, LOCAL_Z + r] = LIFT_R[z - NODES]
            else:
                ghost_z[1, n, LOCAL_Z + r] = LIFT_L[z]
    trace = np.zeros((2, 2, GHOST_ROWS, NODE_COUNT))
    for side in range(2):
        radial_row = END_R if side == 1 else END_L
        for place in range(2):
            for z in range(LOCAL_Z):
                for r in range(NODES):
                    trace[side, place, z, r * LOCAL_Z + z] = radial_row[r]
            for r in range(NODES):
                for k in range(NODES):
                    if place == 0:
                        trace[side, place, LOCAL_Z + r, r * LOCAL_Z + NODES + k] = END_R[k]
                    else:
                        trace[side, place, LOCAL_Z + r, r * LOCAL_Z + k] = END_L[k]
    return (
        (-SCALE * radial).astype(ml_dtypes.bfloat16),
        (-SCALE * axial).astype(np.float32),
        (SCALE * ghost_r).astype(np.float32),
        (SCALE * ghost_z).astype(np.float32),
        trace.astype(ml_dtypes.bfloat16),
    )


def rotation_table():
    full = np.zeros((PLANE + 2 * TILE, PLANE))
    factor = TIME_STEP / (2 * STEP_V)
    for a in range(NVR):
        for b in range(NVT):
            n = a * NVT + b
            first = factor * GRID_T[b] * GRID_T[b]
            second = factor * GRID_R[a] * GRID_T[b]
            if a + 1 < NVR:
                full[TILE + n + NVT, n] = -first
            if a > 0:
                full[TILE + n - NVT, n] = first
            if b + 1 < NVT:
                full[TILE + n + 1, n] = second
            if b > 0:
                full[TILE + n - 1, n] = -second
    tiles = [full[TILE + t - 128 : TILE + t - 128 + WINDOW, t : t + TILE] for t in range(0, PLANE, TILE)]
    return np.stack(tiles).astype(ml_dtypes.bfloat16)


def mirror_table():
    table = np.zeros((THIRD, THIRD))
    groups = THIRD // NVT
    for g in range(groups):
        for b in range(NVT):
            table[(groups - 1 - g) * NVT + b, g * NVT + b] = 1.0
    return table.astype(ml_dtypes.bfloat16)


def plane_rows():
    vr = np.repeat(GRID_R, NVT)
    vt = np.tile(GRID_T, NVR)
    rows = np.zeros((8, PLANE))
    rows[0] = vr
    rows[1] = vt
    rows[2] = np.exp(-(vr**2 + vt**2) / 2)
    return rows.astype(np.float32)


def edge_table():
    table = np.zeros((2, NODES, NODE_COUNT))
    for r in range(NODES):
        for k in range(NODES):
            table[0, r, r * LOCAL_Z + k] = END_L[k]
            table[1, r, r * LOCAL_Z + NODES + k] = END_R[k]
    return table.astype(np.float32)


def node_columns():
    table = np.zeros((NODE_COUNT, 128))
    for r in range(NODES):
        table[r * LOCAL_Z : (r + 1) * LOCAL_Z, :] = (1.0 + POINTS[r]) / 2
    return table.astype(np.float32)


RADIAL_M, AXIAL_M, GHOST_R, GHOST_Z, TRACE_M = transport_tables()
ROTATION_M = rotation_table()
MIRROR_M = mirror_table()
ROWS = plane_rows()
EDGE = edge_table()
NODE_POS = node_columns()


def slot_speed(order, slot):
    return (order[slot].astype(F32) + 0.5) * (2 * SPEED_LIMIT / NVZ) - SPEED_LIMIT


def dot(x, y):
    return jnp.dot(x, y, preferred_element_type=F32)


def macroscopic_of(m):
    rho = m(0)
    inv = 1.0 / rho
    ur, ut, uz = m(1) * inv, m(2) * inv, m(3) * inv
    rr, tt, rt, zz, rz, tz = (m(k) for k in range(4, 10))
    energy = rr + tt + zz
    speed = ur * ur + ut * ut + uz * uz
    temp = (energy * inv - speed) * (1.0 / 3.0)
    tail = 2.0 * rho * speed - energy
    qr = 0.5 * (m(10) - 2.0 * (ur * rr + ut * rt + uz * rz) + ur * tail)
    qt = 0.5 * (m(11) - 2.0 * (ur * rt + ut * tt + uz * tz) + ut * tail)
    qz = 0.5 * (m(12) - 2.0 * (ur * rz + ut * tz + uz * zz) + uz * tail)
    return rho, ur, ut, uz, temp, qr, qt, qz


def add_speed_sums(field, vz, sums):
    one = field * vz
    two = one * vz
    return [
        sums[0] + field,
        sums[1] + one,
        sums[2] + two,
        sums[3] + two * vz,
        sums[4] + field * jnp.abs(vz),
    ]


def finish_moments(sums_ref, rows_ref, table_ref, out_ref):
    lane = lax.broadcasted_iota(jnp.int32, (LOCAL_Z, 128), 1)

    def one_radius(r, carry):
        acc = [jnp.zeros((LOCAL_Z, 128), F32) for _ in range(14)]
        for j in range(PLANE // 128):
            at = pl.ds(j * 128, 128)
            vr = rows_ref[0:1, at]
            vt = rows_ref[1:2, at]
            g0, g1, g2, g3, g4 = (sums_ref[k, r, :, at] for k in range(5))
            a = vr * g0
            b = vt * g0
            aa = vr * a
            bb = vt * b
            c = vr * g1
            d = vt * g1
            perp = aa + bb + g2
            new = [g0, a, b, g1, aa, bb, vr * b, g2, c, d, vr * perp, vt * perp, vr * c + vt * d + g3, g4]
            acc = [x + y for x, y in zip(acc, new)]
        block = jnp.zeros((LOCAL_Z, 128), F32)
        for k in range(14):
            block = jnp.where(lane == k, WEIGHT * jnp.sum(acc[k], axis=1, keepdims=True), block)
        table_ref[pl.ds(pl.multiple_of(r * LOCAL_Z, LOCAL_Z), LOCAL_Z), :] = block
        return carry

    lax.fori_loop(0, NODES, one_radius, 0)
    out_ref[...] = jnp.transpose(table_ref[...])[0:MOMENTS, :]


def clear_sums(sums_ref):
    sums_ref[...] = jnp.zeros(sums_ref.shape, F32)


def places_of():
    return lax.axis_index("row"), lax.axis_index("gz")


def send_piece(s, first, lanes, side, place, narrow, trace_ref, right_ref, left_ref, axial_ref):
    got = dot(trace_ref[side, place], narrow)
    if side == 1:
        right_ref[s, :, first - HALF : first - HALF + lanes] = got[0:LOCAL_Z]
    else:
        left_ref[s, :, first : first + lanes] = got[0:LOCAL_Z]
    axial_ref[s, :, first : first + lanes] = got[LOCAL_Z : LOCAL_Z + NODES]


def turn_traces(count, row, mirror_ref, left_ref, turned_ref):
    @pl.when(row == 0)
    def _():
        for part in range(3):
            start = (2 - part) * THIRD
            flat = left_ref[:, :, start : start + THIRD].reshape(count * LOCAL_Z, THIRD).astype(BF16)
            got = dot(flat, mirror_ref[...])
            turned_ref[:, :, part * THIRD : (part + 1) * THIRD] = got.reshape(count, LOCAL_Z, THIRD)

    @pl.when(row != 0)
    def _():
        turned_ref[...] = jnp.zeros(turned_ref.shape, F32)


def nodes_of(ref, first, lanes):
    return ref[:, :, first : first + lanes].reshape(NODE_COUNT, lanes)


def trace_kernel(
    count, order, codes, f_ref, trace_ref, mirror_ref, right_ref, left_ref, turned_ref, axial_ref
):
    row, place = places_of()
    for s in range(count):
        for first, lanes, side in PIECES:
            narrow = nodes_of(f_ref, s * PLANE + first, lanes).astype(BF16)
            send_piece(s, first, lanes, side, place, narrow, trace_ref, right_ref, left_ref, axial_ref)
    turn_traces(count, row, mirror_ref, left_ref, turned_ref)


def moment_kernel(count, order, codes, f_ref, rows_ref, mom_ref, sums_ref, table_ref):
    step = pl.program_id(0)

    @pl.when(step == 0)
    def _():
        clear_sums(sums_ref)

    speeds = [slot_speed(order, step * count + s) for s in range(count)]
    for j in range(0, PLANE, 128):
        at = pl.ds(j, 128)
        for r in range(NODES):
            sums = [sums_ref[k, r, :, at] for k in range(5)]
            for s in range(count):
                sums = add_speed_sums(f_ref[r, :, pl.ds(s * PLANE + j, 128)], speeds[s], sums)
            for k in range(5):
                sums_ref[k, r, :, at] = sums[k]

    @pl.when(step == pl.num_programs(0) - 1)
    def _():
        finish_moments(sums_ref, rows_ref, table_ref, mom_ref)


def inner_kernel(
    count, order, codes, f_ref, rows_ref, pos_ref, radial_ref, axial_m_ref, rot_ref,
    out_ref, inverse_ref, pad_ref, lhs_ref,
):
    step = pl.program_id(0)
    row, place = places_of()

    @pl.when(step == 0)
    def _():
        pad_ref[:, :, 0:128] = jnp.zeros((count, NODE_COUNT, 128), BF16)
        pad_ref[:, :, 128 + PLANE :] = jnp.zeros((count, NODE_COUNT, 128), BF16)
        inverse_ref[...] = 1.0 / (ELEMENT_WIDTH * (row.astype(F32) + pos_ref[...]))
        minus = radial_ref[jnp.where(row == lax.axis_size("row") - 1, 2, 0)]
        for s in range(count):
            lhs_ref[s, 0, :, 0:NODE_COUNT] = minus
            lhs_ref[s, 1, :, 0:NODE_COUNT] = radial_ref[1]

    kind_out = jnp.where(jnp.logical_and(place == 1, codes[0, TOP] == 2), 2, 0)
    inverse = inverse_ref[...]
    for s in range(count):
        vz = slot_speed(order, step * count + s)
        axial = (vz * axial_m_ref[jnp.where(vz > 0, 1, kind_out)]).astype(BF16)
        lhs_ref[s, 0, :, NODE_COUNT:] = axial
        lhs_ref[s, 1, :, NODE_COUNT:] = axial
        for j in range(PLANE // 128):
            field = nodes_of(f_ref, s * PLANE + j * 128, 128)
            pad_ref[s, :, 128 + j * 128 : 256 + j * 128] = (field * inverse).astype(BF16)

    for tile in range(PLANE // TILE):
        start = tile * TILE
        turned = dot(pad_ref[:, :, start : start + WINDOW].reshape(count * NODE_COUNT, WINDOW), rot_ref[tile])
        for first, lanes, side in PIECES:
            if first // TILE != tile:
                continue
            vr = rows_ref[0:1, first : first + lanes]
            inside = first - start
            for s in range(count):
                here = s * PLANE + first
                field = nodes_of(f_ref, here, lanes)
                both = jnp.concatenate([(field * vr).astype(BF16), field.astype(BF16)], axis=0)
                change = turned[s * NODE_COUNT : (s + 1) * NODE_COUNT, inside : inside + lanes]
                change = change + dot(lhs_ref[s, side], both)
                out_ref[:, :, here : here + lanes] = change.astype(BF16).reshape(NODES, LOCAL_Z, lanes)


def total_of(parts):
    while len(parts) > 1:
        parts = [parts[k] + parts[k + 1] for k in range(0, len(parts), 2)]
    return parts[0]


def edge_sums(total, edge_ref):
    net, gross = total[3:4, :], total[13:14, :]
    down, up = 0.5 * (gross - net), 0.5 * (gross + net)
    pairs = ((0, down), (1, up), (1, down))
    return tuple(jnp.sum(edge_ref[k] * row, axis=1, keepdims=True) for k, row in pairs)


def prepare_nodes(total, codes, place, rows_ref, edge_ref, table_ref, node_ref, wall_ref, plane_ref):
    rho, ur, ut, uz, temp, qr, qt, qz = macroscopic_of(lambda k: total[k : k + 1, :])
    inv_t = 1.0 / temp
    beta = ((1.0 - VISCOUS_RATIO) / 5.0) / (rho * temp * temp)
    kappa = rho * (TIME_STEP / KNUDSEN)
    peak = kappa * rho * inv_t * jnp.sqrt(inv_t)
    values = [uz, -0.5 * inv_t, qz * beta, inv_t, peak, 1.0 - kappa, ur, ut, qr * beta, qt * beta]
    clear_sums(table_ref)
    for k, value in enumerate(values):
        table_ref[k : k + 1, :] = value
    table_ref[...] = jnp.transpose(table_ref[...])
    for k in range(len(values)):
        node_ref[k] = jnp.broadcast_to(table_ref[:, k : k + 1], (NODE_COUNT, 128))
    incident, upward, downward = edge_sums(total, edge_ref)
    bottom = jnp.where(codes[0, BOTTOM] == 1, SAT_DENSITY, incident * (1.0 / HALF_FLUX))
    top = jnp.where(codes[0, TOP] == 2, 0.0, upward * (1.0 / HALF_FLUX))
    wall_ref[...] = jnp.broadcast_to(jnp.where(place == 0, bottom, top), (NODES, 128))

    def one_radius(r, carry):
        rows = pl.ds(pl.multiple_of(r * LOCAL_Z, LOCAL_Z), LOCAL_Z)
        n_half, n_inv = node_ref[1, rows, :], node_ref[3, rows, :]
        n_ur, n_ut = node_ref[6, rows, :], node_ref[7, rows, :]
        n_qr, n_qt = node_ref[8, rows, :], node_ref[9, rows, :]
        for j in range(PLANE // 128):
            at = pl.ds(j * 128, 128)
            cr = rows_ref[0:1, at] - n_ur
            ct = rows_ref[1:2, at] - n_ut
            square = cr * cr + ct * ct
            gauss = jnp.exp(square * n_half)
            along = cr * n_qr + ct * n_qt
            plane_ref[0, rows, at] = gauss
            plane_ref[1, rows, at] = along
            plane_ref[2, rows, at] = square * n_inv
        return carry

    lax.fori_loop(0, NODES, one_radius, 0)


def slot_factors(vz, node_ref):
    cz = vz - node_ref[0]
    square = cz * cz
    return node_ref[4] * jnp.exp(square * node_ref[1]), cz * node_ref[2], square * node_ref[3] - 5.0


def ghost_lifts(vz, ghost_r_ref, ghost_z_ref, lhs_ref):
    lean = jnp.abs(vz) * ghost_z_ref[jnp.where(vz > 0, 1, 0)]
    lhs_ref[0] = (ghost_r_ref[0] + lean).astype(BF16)
    lhs_ref[1] = (ghost_r_ref[1] + lean).astype(BF16)


def ghost_rows(s, vz, place, in_left_ref, in_turned_ref, in_right_ref, in_axial_ref, rows_ref, wall_ref, ghost_ref):
    own = (place == 0) == (vz > 0)
    strength = jnp.exp(-0.5 * vz * vz + jnp.zeros((NODES, 128), F32)) * wall_ref[...]
    for j in range(PLANE // 128):
        at = pl.ds(j * 128, 128)
        if j * 128 < HALF:
            radial = in_right_ref[s, :, at]
        else:
            back = pl.ds(j * 128 - HALF, 128)
            radial = in_left_ref[s, :, back] + in_turned_ref[s, :, back]
        axial = jnp.where(own, strength * rows_ref[2:3, at], in_axial_ref[s, :, at])
        rows = jnp.concatenate([rows_ref[0:1, at] * radial, axial, jnp.zeros((8, 128), F32)], axis=0)
        ghost_ref[:, at] = rows.astype(BF16)


def outer_kernel(count, part_count, last, order, codes, *refs):
    part_refs, refs = refs[:part_count], refs[part_count:]
    f_ref, inner_ref, in_axial_ref, in_left_ref, in_turned_ref, in_right_ref = refs[:6]
    rows_ref, edge_ref, ghost_r_ref, ghost_z_ref, out_ref = refs[6:11]
    refs = refs[11:]
    if last:
        (mom_ref, sums_ref), refs = refs[:2], refs[2:]
    plane_ref, node_ref, wall_ref, slot_ref, work_ref, lhs_ref, ghost_ref, table_ref = refs
    step = pl.program_id(0)
    row, place = places_of()

    @pl.when(step == 0)
    def _():
        if last:
            clear_sums(sums_ref)
        total = total_of([p[...] for p in part_refs])
        prepare_nodes(total, codes, place, rows_ref, edge_ref, table_ref, node_ref, wall_ref, plane_ref)

    speeds = [slot_speed(order, step * count + s) for s in range(count)]
    for s in range(count):
        vz = speeds[s]
        for k, value in enumerate(slot_factors(vz, node_ref)):
            slot_ref[s, k] = value
        ghost_lifts(vz, ghost_r_ref, ghost_z_ref, lhs_ref)
        ghost_rows(
            s, vz, place, in_left_ref, in_turned_ref, in_right_ref, in_axial_ref, rows_ref, wall_ref, ghost_ref
        )
        for first, lanes, side in PIECES:
            work_ref[s, :, first : first + lanes] = dot(
                lhs_ref[side, :, 0:GHOST_ROWS], ghost_ref[:, first : first + lanes]
            )

    def update(r, carry):
        rows = pl.ds(pl.multiple_of(r * LOCAL_Z, LOCAL_Z), LOCAL_Z)
        keep = node_ref[5, rows, :]
        factor = [[slot_ref[s, k, rows, :] for k in range(3)] for s in range(count)]
        for j in range(PLANE // 128):
            at = pl.ds(j * 128, 128)
            gauss, along, reach = (plane_ref[k, rows, at] for k in range(3))
            if last:
                sums = [sums_ref[k, r, :, at] for k in range(5)]
            for s in range(count):
                here = pl.ds(s * PLANE + j * 128, 128)
                new = f_ref[r, :, here] * keep + work_ref[s, rows, at] + inner_ref[r, :, here].astype(F32)
                bend = (along + factor[s][1]) * (reach + factor[s][2]) + 1.0
                new = new + (gauss * factor[s][0]) * bend
                out_ref[r, :, here] = new
                if last:
                    sums = add_speed_sums(new, speeds[s], sums)
            if last:
                for k in range(5):
                    sums_ref[k, r, :, at] = sums[k]
        return carry

    lax.fori_loop(0, NODES, update, 0)
    if last:

        @pl.when(step == pl.num_programs(0) - 1)
        def _():
            finish_moments(sums_ref, rows_ref, table_ref, mom_ref)


def last_kernel(part_count, codes, *refs):
    total_ref = total_of([p[...] for p in refs[:part_count]])
    edge_ref, macro_ref, flux_ref = refs[part_count:]
    row, place = places_of()
    values = macroscopic_of(lambda k: total_ref[k : k + 1, :])
    for k in range(8):
        for r in range(NODES):
            macro_ref[k, r : r + 1, :] = values[k][:, r * LOCAL_Z : (r + 1) * LOCAL_Z]
    incident, upward, downward = edge_sums(total_ref, edge_ref)
    bottom = jnp.where(codes[0, BOTTOM] == 1, SAT_DENSITY * HALF_FLUX - incident, 0.0)
    top = jnp.where(codes[0, TOP] == 2, upward - downward, 0.0)
    square = jnp.broadcast_to(jnp.where(place == 0, bottom, top), (NODES, 128))
    same = lax.broadcasted_iota(jnp.int32, (NODES, 128), 0) == lax.broadcasted_iota(jnp.int32, (NODES, 128), 1)
    flux_ref[...] = jnp.sum(jnp.where(same, square, 0.0), axis=0, keepdims=True)[:, 0:NODES]


def whole(shape):
    return pl.BlockSpec(shape, lambda *a: (0,) * len(shape), pipeline_mode=pl.Buffered(1))


def on_device(distribution, z_order, edge_codes):
    local_r, local_z, vdev = distribution.shape
    assert local_r == NODES and local_z == LOCAL_Z
    slots = vdev // PLANE
    group = math.gcd(slots, 3)
    rows_total = lax.axis_size("row")
    verts = lax.axis_size("vert")
    assert lax.axis_size("gz") == 2
    codes = edge_codes.T
    rows, pos, edge = jnp.asarray(ROWS), jnp.asarray(NODE_POS), jnp.asarray(EDGE)
    radial_m, axial_m = jnp.asarray(RADIAL_M), jnp.asarray(AXIAL_M)
    ghost_r, ghost_z = jnp.asarray(GHOST_R), jnp.asarray(GHOST_Z)
    trace_m, mirror_m, rot_m = jnp.asarray(TRACE_M), jnp.asarray(MIRROR_M), jnp.asarray(ROTATION_M)

    def slab(count):
        return pl.BlockSpec((NODES, LOCAL_Z, count * PLANE), lambda i, *n: (0, 0, i))

    def radial_spec(count):
        return pl.BlockSpec((count, LOCAL_Z, HALF), lambda i, *n: (i, 0, 0))

    def axial_spec(count):
        return pl.BlockSpec((count, NODES, PLANE), lambda i, *n: (i, 0, 0))

    def trace_specs(count):
        return [radial_spec(count), radial_spec(count), radial_spec(count), axial_spec(count)]

    mom_spec = whole((MOMENTS, 128))
    radial_shape = jax.ShapeDtypeStruct((slots, LOCAL_Z, HALF), F32)
    axial_shape = jax.ShapeDtypeStruct((slots, NODES, PLANE), F32)
    mom_shape = jax.ShapeDtypeStruct((MOMENTS, 128), F32)
    big_shape = jax.ShapeDtypeStruct(distribution.shape, F32)
    trace_shapes = [radial_shape, radial_shape, radial_shape, axial_shape]
    square = pltpu.VMEM((NODE_COUNT, 128), F32)

    def call(body, name, count, limit, in_specs, out_specs, out_shape, scratch, args):
        return pl.pallas_call(
            body,
            grid_spec=pltpu.PrefetchScalarGridSpec(
                num_scalar_prefetch=2,
                grid=(slots // count,),
                in_specs=in_specs,
                out_specs=out_specs,
                scratch_shapes=scratch,
            ),
            out_shape=out_shape,
            compiler_params=pltpu.CompilerParams(vmem_limit_bytes=limit * 1024 * 1024),
            name=name,
        )(z_order, codes, *args)

    def all_whole(tables):
        return [whole(x.shape) for x in tables]

    def traces_of(f, limit):
        return call(
            lambda *a: trace_kernel(group, *a), "traces", group, limit, [slab(group)] + all_whole([trace_m, mirror_m]),
            trace_specs(group), trace_shapes, [], [f, trace_m, mirror_m],
        )

    def moments_of(f, limit):
        return call(
            lambda *a: moment_kernel(group, *a), "moments", group, limit, [slab(group)] + all_whole([rows]),
            mom_spec, mom_shape, [pltpu.VMEM((5, NODES, LOCAL_Z, PLANE), F32), square], [f, rows],
        )

    def inner(f, limit):
        tables = [rows, pos, radial_m, axial_m, rot_m]
        scratch = [
            square,
            pltpu.VMEM((group, NODE_COUNT, PLANE + 256), BF16),
            pltpu.VMEM((group, 2, NODE_COUNT, 2 * NODE_COUNT), BF16),
        ]
        return call(
            lambda *a: inner_kernel(group, *a), "inner_increments", group, limit, [slab(group)] + all_whole(tables),
            slab(group), jax.ShapeDtypeStruct(f.shape, BF16), scratch, [f] + tables,
        )

    def outer(f, change, ghosts, parts, last, limit):
        count = math.gcd(slots, 2)
        tables = [rows, edge, ghost_r, ghost_z]
        scratch = [
            pltpu.VMEM((3, NODE_COUNT, PLANE), F32),
            pltpu.VMEM((10, NODE_COUNT, 128), F32),
            pltpu.VMEM((NODES, 128), F32),
            pltpu.VMEM((count, 3, NODE_COUNT, 128), F32),
            pltpu.VMEM((count, NODE_COUNT, PLANE), F32),
            pltpu.VMEM((2, NODE_COUNT, 128), BF16),
            pltpu.VMEM((GHOST_ROWS, PLANE), BF16),
            square,
        ]
        return call(
            lambda *a: outer_kernel(count, len(parts), last, *a), "last_update" if last else "update", count, limit,
            [mom_spec] * len(parts) + [slab(count), slab(count), axial_spec(count)] + [radial_spec(count)] * 3
            + all_whole(tables),
            [slab(count)] + ([mom_spec] if last else []), [big_shape] + ([mom_shape] if last else []),
            ([pltpu.VMEM((5, NODES, LOCAL_Z, PLANE), F32)] if last else []) + scratch,
            [*parts, f, change, *ghosts, *tables],
        )

    def spread(moments):
        parts = [moments]
        for shift in range(1, verts):
            parts.append(lax.ppermute(moments, "vert", [(i, i ^ shift) for i in range(verts)]))
        return parts

    def halo(right, left, turned, axial):
        from_axial = lax.ppermute(axial, "gz", [(0, 1), (1, 0)])
        from_left = lax.ppermute(right, "row", [(i, i + 1) for i in range(rows_total - 1)])
        from_right = lax.ppermute(left, "row", [(i + 1, i) for i in range(rows_total - 1)])
        return from_axial, from_left, turned, from_right

    current = distribution
    for number in range(STEPS):
        last = number == STEPS - 1
        ghosts = halo(*traces_of(current, 12))
        parts = spread(moments_of(current, 18))
        change = inner(current, 20)
        current, *moments = outer(current, change, ghosts, parts, last, 28 if last else 20)
    parts = spread(moments[0])
    macro, flux = pl.pallas_call(
        lambda *a: last_kernel(len(parts), *a),
        grid_spec=pltpu.PrefetchScalarGridSpec(
            num_scalar_prefetch=1,
            grid=(1,),
            in_specs=[mom_spec] * len(parts) + [whole(edge.shape)],
            out_specs=[whole((8, NODES, LOCAL_Z)), whole((1, NODES))],
        ),
        out_shape=[
            jax.ShapeDtypeStruct((8, NODES, LOCAL_Z), F32),
            jax.ShapeDtypeStruct((1, NODES), F32),
        ],
        name="macroscopic",
    )(codes, *parts, edge)
    return (current, macro, flux)


def solution(mesh):
    in_specs = (P("row", "gz", "vert"), P("vert"), P(None, "row"))
    out_specs = (P("row", "gz", "vert"), P(None, "row", "gz"), P("gz", "row"))
    return jax.shard_map(
        on_device, mesh=mesh, in_specs=in_specs, out_specs=out_specs, check_vma=False
    )
```

```python
import math

import jax
import jax.numpy as jnp
import ml_dtypes
import numpy as np
from jax import lax
from jax.experimental import pallas as pl
from jax.experimental.pallas import tpu as pltpu
from jax.sharding import PartitionSpec as P

NODES = 8
NVR = 48
NVT = 48
NVZ = 48
STEPS = 2

ELEMENT_WIDTH = 4.0
TIME_STEP = 0.001
KNUDSEN = 0.005
VISCOUS_RATIO = 2.0 / 3.0
SAT_DENSITY = 1.5
SPEED_LIMIT = 5.0

PLANE = NVR * NVT
HALF = PLANE // 2
THIRD = HALF // 3
BOTTOM, TOP = 0, 1
LOCAL_Z = 2 * NODES
NODE_COUNT = NODES * LOCAL_Z
TILE = 256
WINDOW = 512
GHOST_ROWS = 32
MOMENTS = 16
F32 = jnp.float32
BF16 = jnp.bfloat16
PIECES = [(t, TILE, 0) for t in range(0, 1024, TILE)] + [(1024, 128, 0), (1152, 128, 1)] + [
    (t, TILE, 1) for t in range(1280, PLANE, TILE)
]


def legendre_pair(position, point_count):
    previous = 1.0
    current = position
    for degree in range(2, point_count + 1):
        previous, current = (
            current,
            ((2 * degree - 1) * position * current - (degree - 1) * previous) / degree,
        )
    slope = point_count * (position * current - previous) / (position * position - 1.0)
    return (current, slope)


def dg_tables(point_count):
    point_list = []
    weight_list = []
    for number in range(point_count):
        position = math.cos(math.pi * (number + 0.75) / (point_count + 0.5))
        for sweep in range(60):
            value, slope = legendre_pair(position, point_count)
            position = position - value / slope
        value, slope = legendre_pair(position, point_count)
        point_list.append(position)
        weight_list.append(2.0 / ((1.0 - position * position) * slope * slope))
    point_list = point_list[::-1]
    weight_list = weight_list[::-1]
    points = np.array(point_list)
    derivative = np.zeros((point_count, point_count))
    right = np.zeros(point_count)
    left = np.zeros(point_count)
    products = [
        np.prod([points[i] - points[j] for j in range(point_count) if j != i])
        for i in range(point_count)
    ]
    for i in range(point_count):
        others = [j for j in range(point_count) if j != i]
        derivative[i, i] = sum(1.0 / (points[i] - points[j]) for j in others)
        for j in others:
            derivative[i, j] = products[i] / products[j] / (points[i] - points[j])
        right[i] = np.prod([1.0 - points[j] for j in others]) / products[i]
        left[i] = np.prod([-1.0 - points[j] for j in others]) / products[i]
    return points, np.array(weight_list), derivative, right, left


def speed_grid(point_count):
    return -SPEED_LIMIT + (np.arange(point_count) + 0.5) * (2.0 * SPEED_LIMIT / point_count)


POINTS, QUAD, DERIV, END_R, END_L = dg_tables(NODES)
LIFT_R = END_R / QUAD
LIFT_L = END_L / QUAD
GRID_R = speed_grid(NVR)
GRID_T = speed_grid(NVT)
GRID_Z = speed_grid(NVZ)
STEP_V = 2 * SPEED_LIMIT / NVR
WEIGHT = STEP_V**3 / (2 * math.pi) ** 1.5
HALF_FLUX = float(
    WEIGHT
    * np.sum(np.exp(-(GRID_R**2) / 2))
    * np.sum(np.exp(-(GRID_T**2) / 2))
    * np.sum(np.maximum(GRID_Z, 0.0) * np.exp(-(GRID_Z**2) / 2))
)
SCALE = TIME_STEP * 2.0 / ELEMENT_WIDTH


def transport_tables():
    ident = np.eye(NODES)
    up = DERIV + np.outer(LIFT_L, END_L)
    down = DERIV - np.outer(LIFT_R, END_R)
    zero = np.zeros((NODES, NODES))
    wide = np.eye(LOCAL_Z)
    radial = np.stack([np.kron(down, wide), np.kron(up, wide), np.kron(DERIV, wide)])
    zup = np.block([[up, zero], [-np.outer(LIFT_L, END_R), up]])
    zdown = np.block([[down, np.outer(LIFT_R, END_L)], [zero, down]])
    zout = np.block([[down, np.outer(LIFT_R, END_L)], [zero, DERIV]])
    axial = np.stack([np.kron(ident, zdown), np.kron(ident, zup), np.kron(ident, zout)])
    ghost_r = np.zeros((2, NODE_COUNT, 128))
    ghost_z = np.zeros((2, LOCAL_Z, 128))
    for r in range(NODES):
        ghost_r[0, r * LOCAL_Z : (r + 1) * LOCAL_Z] = -LIFT_R[r]
        ghost_r[1, r * LOCAL_Z : (r + 1) * LOCAL_Z] = LIFT_L[r]
    for k in range(NODES):
        ghost_z[0, NODES + k] = LIFT_R[k]
        ghost_z[1, k] = LIFT_L[k]
    trace = np.zeros((2, 2, GHOST_ROWS, NODE_COUNT))
    for side in range(2):
        radial_row = END_R if side == 1 else END_L
        for place in range(2):
            for z in range(LOCAL_Z):
                for r in range(NODES):
                    trace[side, place, z, r * LOCAL_Z + z] = radial_row[r]
            for r in range(NODES):
                for k in range(NODES):
                    if place == 0:
                        trace[side, place, LOCAL_Z + r, r * LOCAL_Z + NODES + k] = END_R[k]
                    else:
                        trace[side, place, LOCAL_Z + r, r * LOCAL_Z + k] = END_L[k]
    return (
        (-SCALE * radial).astype(ml_dtypes.bfloat16),
        (-SCALE * axial).astype(np.float32),
        (SCALE * ghost_r).astype(np.float32),
        (SCALE * ghost_z).astype(np.float32),
        trace.astype(ml_dtypes.bfloat16),
    )


def rotation_table():
    full = np.zeros((PLANE + 2 * TILE, PLANE))
    factor = TIME_STEP / (2 * STEP_V)
    for a in range(NVR):
        for b in range(NVT):
            n = a * NVT + b
            first = factor * GRID_T[b] * GRID_T[b]
            second = factor * GRID_R[a] * GRID_T[b]
            if a + 1 < NVR:
                full[TILE + n + NVT, n] = -first
            if a > 0:
                full[TILE + n - NVT, n] = first
            if b + 1 < NVT:
                full[TILE + n + 1, n] = second
            if b > 0:
                full[TILE + n - 1, n] = -second
    tiles = [full[TILE + t - 128 : TILE + t - 128 + WINDOW, t : t + TILE] for t in range(0, PLANE, TILE)]
    return np.stack(tiles).astype(ml_dtypes.bfloat16)


def mirror_table():
    table = np.zeros((THIRD, THIRD))
    groups = THIRD // NVT
    for g in range(groups):
        for b in range(NVT):
            table[(groups - 1 - g) * NVT + b, g * NVT + b] = 1.0
    return table.astype(ml_dtypes.bfloat16)


def plane_rows():
    vr = np.repeat(GRID_R, NVT)
    vt = np.tile(GRID_T, NVR)
    rows = np.zeros((8, PLANE))
    rows[0] = vr
    rows[1] = vt
    rows[2] = np.exp(-(vr**2 + vt**2) / 2)
    return rows.astype(np.float32)


def edge_table():
    table = np.zeros((2, NODES, NODE_COUNT))
    for r in range(NODES):
        for k in range(NODES):
            table[0, r, r * LOCAL_Z + k] = END_L[k]
            table[1, r, r * LOCAL_Z + NODES + k] = END_R[k]
    return table.astype(np.float32)


def node_columns():
    table = np.zeros((NODE_COUNT, 128))
    for r in range(NODES):
        table[r * LOCAL_Z : (r + 1) * LOCAL_Z, :] = (1.0 + POINTS[r]) / 2
    return table.astype(np.float32)


RADIAL_M, AXIAL_M, GHOST_R, GHOST_Z, TRACE_M = transport_tables()
ROTATION_M = rotation_table()
MIRROR_M = mirror_table()
ROWS = plane_rows()
EDGE = edge_table()
NODE_POS = node_columns()


def slot_speed(order, slot):
    return (order[slot].astype(F32) + 0.5) * (2 * SPEED_LIMIT / NVZ) - SPEED_LIMIT


def dot(x, y):
    return jnp.dot(x, y, preferred_element_type=F32)


def macroscopic_of(m):
    rho = m(0)
    inv = 1.0 / rho
    ur, ut, uz = m(1) * inv, m(2) * inv, m(3) * inv
    rr, tt, rt, zz, rz, tz = (m(k) for k in range(4, 10))
    energy = rr + tt + zz
    speed = ur * ur + ut * ut + uz * uz
    temp = (energy * inv - speed) * (1.0 / 3.0)
    tail = 2.0 * rho * speed - energy
    qr = 0.5 * (m(10) - 2.0 * (ur * rr + ut * rt + uz * rz) + ur * tail)
    qt = 0.5 * (m(11) - 2.0 * (ur * rt + ut * tt + uz * tz) + ut * tail)
    qz = 0.5 * (m(12) - 2.0 * (ur * rz + ut * tz + uz * zz) + uz * tail)
    return rho, ur, ut, uz, temp, qr, qt, qz


def add_speed_sums(field, vz, sums):
    one = field * vz
    two = one * vz
    return [
        sums[0] + field,
        sums[1] + one,
        sums[2] + two,
        sums[3] + two * vz,
        sums[4] + field * jnp.abs(vz),
    ]


def finish_moments(sums_ref, rows_ref, table_ref, out_ref):
    lane = lax.broadcasted_iota(jnp.int32, (LOCAL_Z, 128), 1)

    def one_radius(r, carry):
        acc = [jnp.zeros((LOCAL_Z, 128), F32) for _ in range(14)]
        for j in range(PLANE // 128):
            at = pl.ds(j * 128, 128)
            vr = rows_ref[0:1, at]
            vt = rows_ref[1:2, at]
            g0, g1, g2, g3, g4 = (sums_ref[k, r, :, at] for k in range(5))
            a = vr * g0
            b = vt * g0
            aa = vr * a
            bb = vt * b
            c = vr * g1
            d = vt * g1
            perp = aa + bb + g2
            new = [g0, a, b, g1, aa, bb, vr * b, g2, c, d, vr * perp, vt * perp, vr * c + vt * d + g3, g4]
            acc = [x + y for x, y in zip(acc, new)]
        block = jnp.zeros((LOCAL_Z, 128), F32)
        for k in range(14):
            block = jnp.where(lane == k, WEIGHT * jnp.sum(acc[k], axis=1, keepdims=True), block)
        table_ref[pl.ds(pl.multiple_of(r * LOCAL_Z, LOCAL_Z), LOCAL_Z), :] = block
        return carry

    lax.fori_loop(0, NODES, one_radius, 0)
    out_ref[...] = jnp.transpose(table_ref[...])[0:MOMENTS, :]


def clear_sums(sums_ref):
    sums_ref[...] = jnp.zeros(sums_ref.shape, F32)


def places_of():
    return lax.axis_index("row"), lax.axis_index("gz")


def send_piece(s, first, lanes, side, place, narrow, trace_ref, right_ref, left_ref, axial_ref):
    got = dot(trace_ref[side, place], narrow)
    if side == 1:
        right_ref[s, :, first - HALF : first - HALF + lanes] = got[0:LOCAL_Z]
    else:
        left_ref[s, :, first : first + lanes] = got[0:LOCAL_Z]
    axial_ref[s, :, first : first + lanes] = got[LOCAL_Z : LOCAL_Z + NODES]


def turn_traces(count, row, mirror_ref, left_ref, turned_ref):
    @pl.when(row == 0)
    def _():
        for part in range(3):
            start = (2 - part) * THIRD
            flat = left_ref[:, :, start : start + THIRD].reshape(count * LOCAL_Z, THIRD).astype(BF16)
            got = dot(flat, mirror_ref[...])
            turned_ref[:, :, part * THIRD : (part + 1) * THIRD] = got.reshape(count, LOCAL_Z, THIRD)

    @pl.when(row != 0)
    def _():
        turned_ref[...] = jnp.zeros(turned_ref.shape, F32)


def nodes_of(ref, first, lanes):
    return ref[:, :, first : first + lanes].reshape(NODE_COUNT, lanes)


def trace_kernel(
    count, order, codes, f_ref, trace_ref, mirror_ref, right_ref, left_ref, turned_ref, axial_ref
):
    row, place = places_of()
    for s in range(count):
        for first, lanes, side in PIECES:
            narrow = nodes_of(f_ref, s * PLANE + first, lanes).astype(BF16)
            send_piece(s, first, lanes, side, place, narrow, trace_ref, right_ref, left_ref, axial_ref)
    turn_traces(count, row, mirror_ref, left_ref, turned_ref)


def inner_kernel(
    count, order, codes, f_ref, rows_ref, pos_ref, radial_ref, axial_m_ref, rot_ref,
    out_ref, mom_ref, sums_ref, table_ref, inverse_ref, pad_ref, lhs_ref,
):
    step = pl.program_id(0)
    row, place = places_of()

    @pl.when(step == 0)
    def _():
        clear_sums(sums_ref)
        pad_ref[:, :, 0:128] = jnp.zeros((count, NODE_COUNT, 128), BF16)
        pad_ref[:, :, 128 + PLANE :] = jnp.zeros((count, NODE_COUNT, 128), BF16)
        inverse_ref[...] = 1.0 / (ELEMENT_WIDTH * (row.astype(F32) + pos_ref[...]))
        minus = radial_ref[jnp.where(row == lax.axis_size("row") - 1, 2, 0)]
        for s in range(count):
            lhs_ref[s, 0, :, 0:NODE_COUNT] = minus
            lhs_ref[s, 1, :, 0:NODE_COUNT] = radial_ref[1]

    kind_out = jnp.where(jnp.logical_and(place == 1, codes[0, TOP] == 2), 2, 0)
    inverse = inverse_ref[...]
    speeds = [slot_speed(order, step * count + s) for s in range(count)]
    for s in range(count):
        vz = speeds[s]
        axial = (vz * axial_m_ref[jnp.where(vz > 0, 1, kind_out)]).astype(BF16)
        lhs_ref[s, 0, :, NODE_COUNT:] = axial
        lhs_ref[s, 1, :, NODE_COUNT:] = axial
        for j in range(PLANE // 128):
            field = nodes_of(f_ref, s * PLANE + j * 128, 128)
            pad_ref[s, :, 128 + j * 128 : 256 + j * 128] = (field * inverse).astype(BF16)

    for tile in range(PLANE // TILE):
        start = tile * TILE
        turned = dot(pad_ref[:, :, start : start + WINDOW].reshape(count * NODE_COUNT, WINDOW), rot_ref[tile])
        for first, lanes, side in PIECES:
            if first // TILE != tile:
                continue
            vr = rows_ref[0:1, first : first + lanes]
            inside = first - start
            for s in range(count):
                here = s * PLANE + first
                field = nodes_of(f_ref, here, lanes)
                both = jnp.concatenate([(field * vr).astype(BF16), field.astype(BF16)], axis=0)
                change = turned[s * NODE_COUNT : (s + 1) * NODE_COUNT, inside : inside + lanes]
                change = change + dot(lhs_ref[s, side], both)
                out_ref[:, :, here : here + lanes] = change.astype(BF16).reshape(NODES, LOCAL_Z, lanes)
            for j in range(first, first + lanes, 128):
                at = pl.ds(j, 128)
                for r in range(NODES):
                    sums = [sums_ref[k, r, :, at] for k in range(5)]
                    for s in range(count):
                        sums = add_speed_sums(f_ref[r, :, pl.ds(s * PLANE + j, 128)], speeds[s], sums)
                    for k in range(5):
                        sums_ref[k, r, :, at] = sums[k]

    @pl.when(step == pl.num_programs(0) - 1)
    def _():
        finish_moments(sums_ref, rows_ref, table_ref, mom_ref)


def total_of(parts):
    while len(parts) > 1:
        parts = [parts[k] + parts[k + 1] for k in range(0, len(parts), 2)]
    return parts[0]


def edge_sums(total, edge_ref):
    net, gross = total[3:4, :], total[13:14, :]
    down, up = 0.5 * (gross - net), 0.5 * (gross + net)
    pairs = ((0, down), (1, up), (1, down))
    return tuple(jnp.sum(edge_ref[k] * row, axis=1, keepdims=True) for k, row in pairs)


def prepare_nodes(total, codes, place, rows_ref, edge_ref, table_ref, node_ref, wall_ref, plane_ref):
    rho, ur, ut, uz, temp, qr, qt, qz = macroscopic_of(lambda k: total[k : k + 1, :])
    inv_t = 1.0 / temp
    beta = ((1.0 - VISCOUS_RATIO) / 5.0) / (rho * temp * temp)
    kappa = rho * (TIME_STEP / KNUDSEN)
    peak = kappa * rho * inv_t * jnp.sqrt(inv_t)
    values = [uz, -0.5 * inv_t, qz * beta, inv_t, peak, 1.0 - kappa, ur, ut, qr * beta, qt * beta]
    clear_sums(table_ref)
    for k, value in enumerate(values):
        table_ref[k : k + 1, :] = value
    table_ref[...] = jnp.transpose(table_ref[...])
    for k in range(len(values)):
        node_ref[k] = jnp.broadcast_to(table_ref[:, k : k + 1], (NODE_COUNT, 128))
    incident, upward, downward = edge_sums(total, edge_ref)
    bottom = jnp.where(codes[0, BOTTOM] == 1, SAT_DENSITY, incident * (1.0 / HALF_FLUX))
    top = jnp.where(codes[0, TOP] == 2, 0.0, upward * (1.0 / HALF_FLUX))
    wall_ref[...] = jnp.broadcast_to(jnp.where(place == 0, bottom, top), (NODES, 128))

    def one_radius(r, carry):
        rows = pl.ds(pl.multiple_of(r * LOCAL_Z, LOCAL_Z), LOCAL_Z)
        n_half, n_inv = node_ref[1, rows, :], node_ref[3, rows, :]
        n_ur, n_ut = node_ref[6, rows, :], node_ref[7, rows, :]
        n_qr, n_qt = node_ref[8, rows, :], node_ref[9, rows, :]
        for j in range(PLANE // 128):
            at = pl.ds(j * 128, 128)
            cr = rows_ref[0:1, at] - n_ur
            ct = rows_ref[1:2, at] - n_ut
            square = cr * cr + ct * ct
            gauss = jnp.exp(square * n_half)
            along = cr * n_qr + ct * n_qt
            plane_ref[0, rows, at] = gauss
            plane_ref[1, rows, at] = along
            plane_ref[2, rows, at] = square * n_inv
        return carry

    lax.fori_loop(0, NODES, one_radius, 0)


def slot_factors(vz, node_ref):
    cz = vz - node_ref[0]
    square = cz * cz
    return node_ref[4] * jnp.exp(square * node_ref[1]), cz * node_ref[2], square * node_ref[3] - 5.0


def ghost_rows(
    s, vz, place, in_axial_ref, in_left_ref, in_turned_ref, in_right_ref, rows_ref, wall_ref, radial_ref, axial_ref
):
    own = (place == 0) == (vz > 0)
    strength = jnp.exp(-0.5 * vz * vz + jnp.zeros((NODES, 128), F32)) * wall_ref[...]
    for j in range(PLANE // 128):
        at = pl.ds(j * 128, 128)
        if j * 128 < HALF:
            radial = in_right_ref[s, :, at]
        else:
            back = pl.ds(j * 128 - HALF, 128)
            radial = in_left_ref[s, :, back] + in_turned_ref[s, :, back]
        radial_ref[s, :, at] = rows_ref[0:1, at] * radial
        axial = jnp.where(own, strength * rows_ref[2:3, at], in_axial_ref[s, :, at])
        for r in range(NODES):
            axial_ref[s, r, :, at] = jnp.broadcast_to(axial[r : r + 1], (NODES, 128))


def outer_kernel(count, part_count, last, order, codes, *refs):
    part_refs, refs = refs[:part_count], refs[part_count:]
    f_ref, inner_ref, in_axial_ref, in_left_ref, in_turned_ref, in_right_ref = refs[:6]
    rows_ref, edge_ref, ghost_r_ref, ghost_z_ref, out_ref = refs[6:11]
    refs = refs[11:]
    if last:
        (mom_ref, sums_ref), refs = refs[:2], refs[2:]
    plane_ref, node_ref, wall_ref, slot_ref, lean_ref, radial_ref, axial_ref, table_ref = refs
    step = pl.program_id(0)
    row, place = places_of()

    @pl.when(step == 0)
    def _():
        if last:
            clear_sums(sums_ref)
        total = total_of([p[...] for p in part_refs])
        prepare_nodes(total, codes, place, rows_ref, edge_ref, table_ref, node_ref, wall_ref, plane_ref)

    speeds = [slot_speed(order, step * count + s) for s in range(count)]
    for s in range(count):
        vz = speeds[s]
        for k, value in enumerate(slot_factors(vz, node_ref)):
            slot_ref[s, k] = value
        lean_ref[s] = jnp.abs(vz) * ghost_z_ref[jnp.where(vz > 0, 1, 0)]
        ghost_rows(
            s, vz, place, in_axial_ref, in_left_ref, in_turned_ref, in_right_ref, rows_ref, wall_ref,
            radial_ref, axial_ref,
        )

    def update(r, carry):
        rows = pl.ds(pl.multiple_of(r * LOCAL_Z, LOCAL_Z), LOCAL_Z)
        keep = node_ref[5, rows, :]
        lifts = [ghost_r_ref[side, rows, :] for side in range(2)]
        factor = [[slot_ref[s, k, rows, :] for k in range(3)] for s in range(count)]
        lean = [lean_ref[s] for s in range(count)]
        for j in range(PLANE // 128):
            at = pl.ds(j * 128, 128)
            gauss, along, reach = (plane_ref[k, rows, at] for k in range(3))
            if last:
                sums = [sums_ref[k, r, :, at] for k in range(5)]
            for s in range(count):
                here = pl.ds(s * PLANE + j * 128, 128)
                new = f_ref[r, :, here] * keep + inner_ref[r, :, here].astype(F32)
                new = new + radial_ref[s, :, at] * lifts[1 if j * 128 >= HALF else 0]
                across = axial_ref[s, r, :, at]
                new = new + jnp.concatenate([across, across], axis=0) * lean[s]
                bend = (along + factor[s][1]) * (reach + factor[s][2]) + 1.0
                new = new + (gauss * factor[s][0]) * bend
                out_ref[r, :, here] = new
                if last:
                    sums = add_speed_sums(new, speeds[s], sums)
            if last:
                for k in range(5):
                    sums_ref[k, r, :, at] = sums[k]
        return carry

    lax.fori_loop(0, NODES, update, 0)
    if last:

        @pl.when(step == pl.num_programs(0) - 1)
        def _():
            finish_moments(sums_ref, rows_ref, table_ref, mom_ref)


def last_kernel(part_count, codes, *refs):
    total_ref = total_of([p[...] for p in refs[:part_count]])
    edge_ref, macro_ref, flux_ref = refs[part_count:]
    row, place = places_of()
    values = macroscopic_of(lambda k: total_ref[k : k + 1, :])
    for k in range(8):
        for r in range(NODES):
            macro_ref[k, r : r + 1, :] = values[k][:, r * LOCAL_Z : (r + 1) * LOCAL_Z]
    incident, upward, downward = edge_sums(total_ref, edge_ref)
    bottom = jnp.where(codes[0, BOTTOM] == 1, SAT_DENSITY * HALF_FLUX - incident, 0.0)
    top = jnp.where(codes[0, TOP] == 2, upward - downward, 0.0)
    square = jnp.broadcast_to(jnp.where(place == 0, bottom, top), (NODES, 128))
    same = lax.broadcasted_iota(jnp.int32, (NODES, 128), 0) == lax.broadcasted_iota(jnp.int32, (NODES, 128), 1)
    flux_ref[...] = jnp.sum(jnp.where(same, square, 0.0), axis=0, keepdims=True)[:, 0:NODES]


def whole(shape):
    return pl.BlockSpec(shape, lambda *a: (0,) * len(shape), pipeline_mode=pl.Buffered(1))


def on_device(distribution, z_order, edge_codes):
    local_r, local_z, vdev = distribution.shape
    assert local_r == NODES and local_z == LOCAL_Z
    slots = vdev // PLANE
    group = math.gcd(slots, 3)
    rows_total = lax.axis_size("row")
    verts = lax.axis_size("vert")
    assert lax.axis_size("gz") == 2
    codes = edge_codes.T
    rows, pos, edge = jnp.asarray(ROWS), jnp.asarray(NODE_POS), jnp.asarray(EDGE)
    radial_m, axial_m = jnp.asarray(RADIAL_M), jnp.asarray(AXIAL_M)
    ghost_r, ghost_z = jnp.asarray(GHOST_R), jnp.asarray(GHOST_Z)
    trace_m, mirror_m, rot_m = jnp.asarray(TRACE_M), jnp.asarray(MIRROR_M), jnp.asarray(ROTATION_M)

    def slab(count):
        return pl.BlockSpec((NODES, LOCAL_Z, count * PLANE), lambda i, *n: (0, 0, i))

    def radial_spec(count):
        return pl.BlockSpec((count, LOCAL_Z, HALF), lambda i, *n: (i, 0, 0))

    def axial_spec(count):
        return pl.BlockSpec((count, NODES, PLANE), lambda i, *n: (i, 0, 0))

    def trace_specs(count):
        return [radial_spec(count), radial_spec(count), radial_spec(count), axial_spec(count)]

    mom_spec = whole((MOMENTS, 128))
    radial_shape = jax.ShapeDtypeStruct((slots, LOCAL_Z, HALF), F32)
    axial_shape = jax.ShapeDtypeStruct((slots, NODES, PLANE), F32)
    mom_shape = jax.ShapeDtypeStruct((MOMENTS, 128), F32)
    big_shape = jax.ShapeDtypeStruct(distribution.shape, F32)
    trace_shapes = [radial_shape, radial_shape, radial_shape, axial_shape]
    square = pltpu.VMEM((NODE_COUNT, 128), F32)

    def call(body, name, count, limit, in_specs, out_specs, out_shape, scratch, args):
        return pl.pallas_call(
            body,
            grid_spec=pltpu.PrefetchScalarGridSpec(
                num_scalar_prefetch=2,
                grid=(slots // count,),
                in_specs=in_specs,
                out_specs=out_specs,
                scratch_shapes=scratch,
            ),
            out_shape=out_shape,
            compiler_params=pltpu.CompilerParams(vmem_limit_bytes=limit * 1024 * 1024),
            name=name,
        )(z_order, codes, *args)

    def all_whole(tables):
        return [whole(x.shape) for x in tables]

    def traces_of(f, limit):
        return call(
            lambda *a: trace_kernel(group, *a), "traces", group, limit, [slab(group)] + all_whole([trace_m, mirror_m]),
            trace_specs(group), trace_shapes, [], [f, trace_m, mirror_m],
        )

    def inner(f, limit):
        group = math.gcd(slots, 2)
        tables = [rows, pos, radial_m, axial_m, rot_m]
        scratch = [
            pltpu.VMEM((5, NODES, LOCAL_Z, PLANE), F32),
            square,
            square,
            pltpu.VMEM((group, NODE_COUNT, PLANE + 256), BF16),
            pltpu.VMEM((group, 2, NODE_COUNT, 2 * NODE_COUNT), BF16),
        ]
        return call(
            lambda *a: inner_kernel(group, *a), "inner_increments", group, limit, [slab(group)] + all_whole(tables),
            [slab(group), mom_spec], [jax.ShapeDtypeStruct(f.shape, BF16), mom_shape], scratch, [f] + tables,
        )

    def outer(f, change, ghosts, parts, last, limit):
        count = 1 if last else math.gcd(slots, 2)
        tables = [rows, edge, ghost_r, ghost_z]
        scratch = [
            pltpu.VMEM((3, NODE_COUNT, PLANE), F32),
            pltpu.VMEM((10, NODE_COUNT, 128), F32),
            pltpu.VMEM((NODES, 128), F32),
            pltpu.VMEM((count, 3, NODE_COUNT, 128), F32),
            pltpu.VMEM((count, LOCAL_Z, 128), F32),
            pltpu.VMEM((count, LOCAL_Z, PLANE), F32),
            pltpu.VMEM((count, NODES, NODES, PLANE), F32),
            square,
        ]
        return call(
            lambda *a: outer_kernel(count, len(parts), last, *a), "last_update" if last else "update", count, limit,
            [mom_spec] * len(parts) + [slab(count), slab(count), axial_spec(count)] + [radial_spec(count)] * 3
            + all_whole(tables),
            [slab(count)] + ([mom_spec] if last else []), [big_shape] + ([mom_shape] if last else []),
            ([pltpu.VMEM((5, NODES, LOCAL_Z, PLANE), F32)] if last else []) + scratch,
            [*parts, f, change, *ghosts, *tables],
        )

    def spread(moments):
        parts = [moments]
        for shift in range(1, verts):
            parts.append(lax.ppermute(moments, "vert", [(i, i ^ shift) for i in range(verts)]))
        return parts

    def halo(right, left, turned, axial):
        from_axial = lax.ppermute(axial, "gz", [(0, 1), (1, 0)])
        from_left = lax.ppermute(right, "row", [(i, i + 1) for i in range(rows_total - 1)])
        from_right = lax.ppermute(left, "row", [(i + 1, i) for i in range(rows_total - 1)])
        return from_axial, from_left, turned, from_right

    current = distribution
    for number in range(STEPS):
        last = number == STEPS - 1
        ghosts = halo(*traces_of(current, 20))
        change, moments = inner(current, 21)
        parts = spread(moments)
        current, *final = outer(current, change, ghosts, parts, last, 20)
    parts = spread(final[0])
    macro, flux = pl.pallas_call(
        lambda *a: last_kernel(len(parts), *a),
        grid_spec=pltpu.PrefetchScalarGridSpec(
            num_scalar_prefetch=1,
            grid=(1,),
            in_specs=[mom_spec] * len(parts) + [whole(edge.shape)],
            out_specs=[whole((8, NODES, LOCAL_Z)), whole((1, NODES))],
        ),
        out_shape=[
            jax.ShapeDtypeStruct((8, NODES, LOCAL_Z), F32),
            jax.ShapeDtypeStruct((1, NODES), F32),
        ],
        name="macroscopic",
    )(codes, *parts, edge)
    return (current, macro, flux)


def solution(mesh):
    in_specs = (P("row", "gz", "vert"), P("vert"), P(None, "row"))
    out_specs = (P("row", "gz", "vert"), P(None, "row", "gz"), P("gz", "row"))
    return jax.shard_map(
        on_device, mesh=mesh, in_specs=in_specs, out_specs=out_specs, check_vma=False
    )
```

```python
import math

import jax
import jax.numpy as jnp
import ml_dtypes
import numpy as np
from jax import lax
from jax.experimental import pallas as pl
from jax.experimental.pallas import tpu as pltpu
from jax.sharding import PartitionSpec as P

NODES = 8
NVR = 48
NVT = 48
NVZ = 48
STEPS = 2

ELEMENT_WIDTH = 4.0
TIME_STEP = 0.001
KNUDSEN = 0.005
VISCOUS_RATIO = 2.0 / 3.0
SAT_DENSITY = 1.5
SPEED_LIMIT = 5.0

PLANE = NVR * NVT
HALF = PLANE // 2
THIRD = HALF // 3
BOTTOM, TOP = 0, 1
LOCAL_Z = 2 * NODES
NODE_COUNT = NODES * LOCAL_Z
TILE = 256
WINDOW = 512
GHOST_ROWS = 32
MOMENTS = 16
F32 = jnp.float32
BF16 = jnp.bfloat16
PIECES = [(t, TILE, 0) for t in range(0, 1024, TILE)] + [(1024, 128, 0), (1152, 128, 1)] + [
    (t, TILE, 1) for t in range(1280, PLANE, TILE)
]


def legendre_pair(position, point_count):
    previous = 1.0
    current = position
    for degree in range(2, point_count + 1):
        previous, current = (
            current,
            ((2 * degree - 1) * position * current - (degree - 1) * previous) / degree,
        )
    slope = point_count * (position * current - previous) / (position * position - 1.0)
    return (current, slope)


def dg_tables(point_count):
    point_list = []
    weight_list = []
    for number in range(point_count):
        position = math.cos(math.pi * (number + 0.75) / (point_count + 0.5))
        for sweep in range(60):
            value, slope = legendre_pair(position, point_count)
            position = position - value / slope
        value, slope = legendre_pair(position, point_count)
        point_list.append(position)
        weight_list.append(2.0 / ((1.0 - position * position) * slope * slope))
    point_list = point_list[::-1]
    weight_list = weight_list[::-1]
    points = np.array(point_list)
    derivative = np.zeros((point_count, point_count))
    right = np.zeros(point_count)
    left = np.zeros(point_count)
    products = [
        np.prod([points[i] - points[j] for j in range(point_count) if j != i])
        for i in range(point_count)
    ]
    for i in range(point_count):
        others = [j for j in range(point_count) if j != i]
        derivative[i, i] = sum(1.0 / (points[i] - points[j]) for j in others)
        for j in others:
            derivative[i, j] = products[i] / products[j] / (points[i] - points[j])
        right[i] = np.prod([1.0 - points[j] for j in others]) / products[i]
        left[i] = np.prod([-1.0 - points[j] for j in others]) / products[i]
    return points, np.array(weight_list), derivative, right, left


def speed_grid(point_count):
    return -SPEED_LIMIT + (np.arange(point_count) + 0.5) * (2.0 * SPEED_LIMIT / point_count)


POINTS, QUAD, DERIV, END_R, END_L = dg_tables(NODES)
LIFT_R = END_R / QUAD
LIFT_L = END_L / QUAD
GRID_R = speed_grid(NVR)
GRID_T = speed_grid(NVT)
GRID_Z = speed_grid(NVZ)
STEP_V = 2 * SPEED_LIMIT / NVR
WEIGHT = STEP_V**3 / (2 * math.pi) ** 1.5
HALF_FLUX = float(
    WEIGHT
    * np.sum(np.exp(-(GRID_R**2) / 2))
    * np.sum(np.exp(-(GRID_T**2) / 2))
    * np.sum(np.maximum(GRID_Z, 0.0) * np.exp(-(GRID_Z**2) / 2))
)
SCALE = TIME_STEP * 2.0 / ELEMENT_WIDTH


def transport_tables():
    ident = np.eye(NODES)
    up = DERIV + np.outer(LIFT_L, END_L)
    down = DERIV - np.outer(LIFT_R, END_R)
    zero = np.zeros((NODES, NODES))
    wide = np.eye(LOCAL_Z)
    radial = np.stack([np.kron(down, wide), np.kron(up, wide), np.kron(DERIV, wide)])
    zup = np.block([[up, zero], [-np.outer(LIFT_L, END_R), up]])
    zdown = np.block([[down, np.outer(LIFT_R, END_L)], [zero, down]])
    zout = np.block([[down, np.outer(LIFT_R, END_L)], [zero, DERIV]])
    axial = np.stack([np.kron(ident, zdown), np.kron(ident, zup), np.kron(ident, zout)])
    ghost_r = np.zeros((2, NODE_COUNT, 128))
    ghost_z = np.zeros((2, LOCAL_Z, 128))
    for r in range(NODES):
        ghost_r[0, r * LOCAL_Z : (r + 1) * LOCAL_Z] = -LIFT_R[r]
        ghost_r[1, r * LOCAL_Z : (r + 1) * LOCAL_Z] = LIFT_L[r]
    for k in range(NODES):
        ghost_z[0, NODES + k] = LIFT_R[k]
        ghost_z[1, k] = LIFT_L[k]
    trace = np.zeros((2, 2, GHOST_ROWS, NODE_COUNT))
    for side in range(2):
        radial_row = END_R if side == 1 else END_L
        for place in range(2):
            for z in range(LOCAL_Z):
                for r in range(NODES):
                    trace[side, place, z, r * LOCAL_Z + z] = radial_row[r]
            for r in range(NODES):
                for k in range(NODES):
                    if place == 0:
                        trace[side, place, LOCAL_Z + r, r * LOCAL_Z + NODES + k] = END_R[k]
                    else:
                        trace[side, place, LOCAL_Z + r, r * LOCAL_Z + k] = END_L[k]
    return (
        (-SCALE * radial).astype(ml_dtypes.bfloat16),
        (-SCALE * axial).astype(np.float32),
        (SCALE * ghost_r).astype(np.float32),
        (SCALE * ghost_z).astype(np.float32),
        trace.astype(ml_dtypes.bfloat16),
    )


def rotation_table():
    full = np.zeros((PLANE + 2 * TILE, PLANE))
    factor = TIME_STEP / (2 * STEP_V)
    for a in range(NVR):
        for b in range(NVT):
            n = a * NVT + b
            first = factor * GRID_T[b] * GRID_T[b]
            second = factor * GRID_R[a] * GRID_T[b]
            if a + 1 < NVR:
                full[TILE + n + NVT, n] = -first
            if a > 0:
                full[TILE + n - NVT, n] = first
            if b + 1 < NVT:
                full[TILE + n + 1, n] = second
            if b > 0:
                full[TILE + n - 1, n] = -second
    tiles = [full[TILE + t - 128 : TILE + t - 128 + WINDOW, t : t + TILE] for t in range(0, PLANE, TILE)]
    return np.stack(tiles).astype(ml_dtypes.bfloat16)


def mirror_table():
    table = np.zeros((THIRD, THIRD))
    groups = THIRD // NVT
    for g in range(groups):
        for b in range(NVT):
            table[(groups - 1 - g) * NVT + b, g * NVT + b] = 1.0
    return table.astype(ml_dtypes.bfloat16)


def plane_rows():
    vr = np.repeat(GRID_R, NVT)
    vt = np.tile(GRID_T, NVR)
    rows = np.zeros((8, PLANE))
    rows[0] = vr
    rows[1] = vt
    rows[2] = np.exp(-(vr**2 + vt**2) / 2)
    return rows.astype(np.float32)


def edge_table():
    table = np.zeros((2, NODES, NODE_COUNT))
    for r in range(NODES):
        for k in range(NODES):
            table[0, r, r * LOCAL_Z + k] = END_L[k]
            table[1, r, r * LOCAL_Z + NODES + k] = END_R[k]
    return table.astype(np.float32)


def node_columns():
    table = np.zeros((NODE_COUNT, 128))
    for r in range(NODES):
        table[r * LOCAL_Z : (r + 1) * LOCAL_Z, :] = (1.0 + POINTS[r]) / 2
    return table.astype(np.float32)


RADIAL_M, AXIAL_M, GHOST_R, GHOST_Z, TRACE_M = transport_tables()
ROTATION_M = rotation_table()
MIRROR_M = mirror_table()
ROWS = plane_rows()
EDGE = edge_table()
NODE_POS = node_columns()


def slot_speed(order, slot):
    return (order[slot].astype(F32) + 0.5) * (2 * SPEED_LIMIT / NVZ) - SPEED_LIMIT


def dot(x, y):
    return jnp.dot(x, y, preferred_element_type=F32)


def macroscopic_of(m):
    rho = m(0)
    inv = 1.0 / rho
    ur, ut, uz = m(1) * inv, m(2) * inv, m(3) * inv
    rr, tt, rt, zz, rz, tz = (m(k) for k in range(4, 10))
    energy = rr + tt + zz
    speed = ur * ur + ut * ut + uz * uz
    temp = (energy * inv - speed) * (1.0 / 3.0)
    tail = 2.0 * rho * speed - energy
    qr = 0.5 * (m(10) - 2.0 * (ur * rr + ut * rt + uz * rz) + ur * tail)
    qt = 0.5 * (m(11) - 2.0 * (ur * rt + ut * tt + uz * tz) + ut * tail)
    qz = 0.5 * (m(12) - 2.0 * (ur * rz + ut * tz + uz * zz) + uz * tail)
    return rho, ur, ut, uz, temp, qr, qt, qz


def add_speed_sums(field, vz, sums):
    one = field * vz
    two = one * vz
    return [
        sums[0] + field,
        sums[1] + one,
        sums[2] + two,
        sums[3] + two * vz,
        sums[4] + field * jnp.abs(vz),
    ]


def finish_moments(sums_ref, rows_ref, table_ref, out_ref):
    lane = lax.broadcasted_iota(jnp.int32, (LOCAL_Z, 128), 1)

    def one_radius(r, carry):
        acc = [jnp.zeros((LOCAL_Z, 128), F32) for _ in range(14)]
        for j in range(PLANE // 128):
            at = pl.ds(j * 128, 128)
            vr = rows_ref[0:1, at]
            vt = rows_ref[1:2, at]
            g0, g1, g2, g3, g4 = (sums_ref[k, r, :, at] for k in range(5))
            a = vr * g0
            b = vt * g0
            aa = vr * a
            bb = vt * b
            c = vr * g1
            d = vt * g1
            perp = aa + bb + g2
            new = [g0, a, b, g1, aa, bb, vr * b, g2, c, d, vr * perp, vt * perp, vr * c + vt * d + g3, g4]
            acc = [x + y for x, y in zip(acc, new)]
        block = jnp.zeros((LOCAL_Z, 128), F32)
        for k in range(14):
            block = jnp.where(lane == k, WEIGHT * jnp.sum(acc[k], axis=1, keepdims=True), block)
        table_ref[pl.ds(pl.multiple_of(r * LOCAL_Z, LOCAL_Z), LOCAL_Z), :] = block
        return carry

    lax.fori_loop(0, NODES, one_radius, 0)
    out_ref[...] = jnp.transpose(table_ref[...])[0:MOMENTS, :]


def clear_sums(sums_ref):
    sums_ref[...] = jnp.zeros(sums_ref.shape, F32)


def places_of():
    return lax.axis_index("row"), lax.axis_index("gz")


def send_piece(s, first, lanes, side, place, narrow, trace_ref, right_ref, left_ref, axial_ref):
    got = dot(trace_ref[side, place], narrow)
    if side == 1:
        right_ref[s, :, first - HALF : first - HALF + lanes] = got[0:LOCAL_Z]
    else:
        left_ref[s, :, first : first + lanes] = got[0:LOCAL_Z]
    axial_ref[s, :, first : first + lanes] = got[LOCAL_Z : LOCAL_Z + NODES]


def turn_traces(count, row, mirror_ref, left_ref, turned_ref):
    @pl.when(row == 0)
    def _():
        for part in range(3):
            start = (2 - part) * THIRD
            flat = left_ref[:, :, start : start + THIRD].reshape(count * LOCAL_Z, THIRD).astype(BF16)
            got = dot(flat, mirror_ref[...])
            turned_ref[:, :, part * THIRD : (part + 1) * THIRD] = got.reshape(count, LOCAL_Z, THIRD)

    @pl.when(row != 0)
    def _():
        turned_ref[...] = jnp.zeros(turned_ref.shape, F32)


def nodes_of(ref, first, lanes):
    return ref[:, :, first : first + lanes].reshape(NODE_COUNT, lanes)


def trace_kernel(count, order, codes, f_ref, trace_ref, right_ref, left_ref, axial_ref):
    row, place = places_of()
    for s in range(count):
        for first, lanes, side in PIECES:
            narrow = nodes_of(f_ref, s * PLANE + first, lanes).astype(BF16)
            send_piece(s, first, lanes, side, place, narrow, trace_ref, right_ref, left_ref, axial_ref)


def moment_kernel(
    count, order, codes, f_ref, left_ref, rows_ref, mirror_ref, mom_ref, turned_ref, sums_ref, table_ref
):
    step = pl.program_id(0)
    row, place = places_of()

    @pl.when(step == 0)
    def _():
        clear_sums(sums_ref)

    turn_traces(count, row, mirror_ref, left_ref, turned_ref)
    speeds = [slot_speed(order, step * count + s) for s in range(count)]
    for j in range(0, PLANE, 128):
        at = pl.ds(j, 128)
        for r in range(NODES):
            sums = [sums_ref[k, r, :, at] for k in range(5)]
            for s in range(count):
                sums = add_speed_sums(f_ref[r, :, pl.ds(s * PLANE + j, 128)], speeds[s], sums)
            for k in range(5):
                sums_ref[k, r, :, at] = sums[k]

    @pl.when(step == pl.num_programs(0) - 1)
    def _():
        finish_moments(sums_ref, rows_ref, table_ref, mom_ref)


def inner_kernel(
    count, order, codes, f_ref, rows_ref, pos_ref, radial_ref, axial_m_ref, rot_ref,
    out_ref, inverse_ref, pad_ref, lhs_ref,
):
    step = pl.program_id(0)
    row, place = places_of()

    @pl.when(step == 0)
    def _():
        pad_ref[:, :, 0:128] = jnp.zeros((count, NODE_COUNT, 128), BF16)
        pad_ref[:, :, 128 + PLANE :] = jnp.zeros((count, NODE_COUNT, 128), BF16)
        inverse_ref[...] = 1.0 / (ELEMENT_WIDTH * (row.astype(F32) + pos_ref[...]))
        minus = radial_ref[jnp.where(row == lax.axis_size("row") - 1, 2, 0)]
        for s in range(count):
            lhs_ref[s, 0, :, 0:NODE_COUNT] = minus
            lhs_ref[s, 1, :, 0:NODE_COUNT] = radial_ref[1]

    kind_out = jnp.where(jnp.logical_and(place == 1, codes[0, TOP] == 2), 2, 0)
    inverse = inverse_ref[...]
    speeds = [slot_speed(order, step * count + s) for s in range(count)]
    for s in range(count):
        vz = speeds[s]
        axial = (vz * axial_m_ref[jnp.where(vz > 0, 1, kind_out)]).astype(BF16)
        lhs_ref[s, 0, :, NODE_COUNT:] = axial
        lhs_ref[s, 1, :, NODE_COUNT:] = axial
        for j in range(PLANE // 128):
            field = nodes_of(f_ref, s * PLANE + j * 128, 128)
            pad_ref[s, :, 128 + j * 128 : 256 + j * 128] = (field * inverse).astype(BF16)

    for tile in range(PLANE // TILE):
        start = tile * TILE
        turned = dot(pad_ref[:, :, start : start + WINDOW].reshape(count * NODE_COUNT, WINDOW), rot_ref[tile])
        for first, lanes, side in PIECES:
            if first // TILE != tile:
                continue
            vr = rows_ref[0:1, first : first + lanes]
            inside = first - start
            for s in range(count):
                here = s * PLANE + first
                field = nodes_of(f_ref, here, lanes)
                both = jnp.concatenate([(field * vr).astype(BF16), field.astype(BF16)], axis=0)
                change = turned[s * NODE_COUNT : (s + 1) * NODE_COUNT, inside : inside + lanes]
                change = change + dot(lhs_ref[s, side], both)
                out_ref[:, :, here : here + lanes] = change.astype(BF16).reshape(NODES, LOCAL_Z, lanes)


def total_of(parts):
    while len(parts) > 1:
        parts = [parts[k] + parts[k + 1] for k in range(0, len(parts), 2)]
    return parts[0]


def edge_sums(total, edge_ref):
    net, gross = total[3:4, :], total[13:14, :]
    down, up = 0.5 * (gross - net), 0.5 * (gross + net)
    pairs = ((0, down), (1, up), (1, down))
    return tuple(jnp.sum(edge_ref[k] * row, axis=1, keepdims=True) for k, row in pairs)


def prepare_nodes(total, codes, place, rows_ref, edge_ref, table_ref, node_ref, wall_ref, plane_ref):
    rho, ur, ut, uz, temp, qr, qt, qz = macroscopic_of(lambda k: total[k : k + 1, :])
    inv_t = 1.0 / temp
    beta = ((1.0 - VISCOUS_RATIO) / 5.0) / (rho * temp * temp)
    kappa = rho * (TIME_STEP / KNUDSEN)
    peak = kappa * rho * inv_t * jnp.sqrt(inv_t)
    values = [uz, -0.5 * inv_t, qz * beta, inv_t, peak, 1.0 - kappa, ur, ut, qr * beta, qt * beta]
    clear_sums(table_ref)
    for k, value in enumerate(values):
        table_ref[k : k + 1, :] = value
    table_ref[...] = jnp.transpose(table_ref[...])
    for k in range(len(values)):
        node_ref[k] = jnp.broadcast_to(table_ref[:, k : k + 1], (NODE_COUNT, 128))
    incident, upward, downward = edge_sums(total, edge_ref)
    bottom = jnp.where(codes[0, BOTTOM] == 1, SAT_DENSITY, incident * (1.0 / HALF_FLUX))
    top = jnp.where(codes[0, TOP] == 2, 0.0, upward * (1.0 / HALF_FLUX))
    wall_ref[...] = jnp.broadcast_to(jnp.where(place == 0, bottom, top), (NODES, 128))

    def one_radius(r, carry):
        rows = pl.ds(pl.multiple_of(r * LOCAL_Z, LOCAL_Z), LOCAL_Z)
        n_half, n_inv = node_ref[1, rows, :], node_ref[3, rows, :]
        n_ur, n_ut = node_ref[6, rows, :], node_ref[7, rows, :]
        n_qr, n_qt = node_ref[8, rows, :], node_ref[9, rows, :]
        for j in range(PLANE // 128):
            at = pl.ds(j * 128, 128)
            cr = rows_ref[0:1, at] - n_ur
            ct = rows_ref[1:2, at] - n_ut
            square = cr * cr + ct * ct
            gauss = jnp.exp(square * n_half)
            along = cr * n_qr + ct * n_qt
            plane_ref[0, rows, at] = gauss
            plane_ref[1, rows, at] = along
            plane_ref[2, rows, at] = square * n_inv
        return carry

    lax.fori_loop(0, NODES, one_radius, 0)


def slot_factors(vz, node_ref):
    cz = vz - node_ref[0]
    square = cz * cz
    return node_ref[4] * jnp.exp(square * node_ref[1]), cz * node_ref[2], square * node_ref[3] - 5.0


def ghost_rows(
    s, vz, place, in_axial_ref, in_left_ref, in_turned_ref, in_right_ref, rows_ref, wall_ref, radial_ref, axial_ref
):
    own = (place == 0) == (vz > 0)
    strength = jnp.exp(-0.5 * vz * vz + jnp.zeros((NODES, 128), F32)) * wall_ref[...]
    for j in range(PLANE // 128):
        at = pl.ds(j * 128, 128)
        if j * 128 < HALF:
            radial = in_right_ref[s, :, at]
        else:
            back = pl.ds(j * 128 - HALF, 128)
            radial = in_left_ref[s, :, back] + in_turned_ref[s, :, back]
        radial_ref[s, :, at] = rows_ref[0:1, at] * radial
        axial = jnp.where(own, strength * rows_ref[2:3, at], in_axial_ref[s, :, at])
        for r in range(NODES):
            axial_ref[s, r, :, at] = jnp.broadcast_to(axial[r : r + 1], (NODES, 128))


def outer_kernel(count, part_count, last, order, codes, *refs):
    part_refs, refs = refs[:part_count], refs[part_count:]
    f_ref, inner_ref, in_axial_ref, in_left_ref, in_turned_ref, in_right_ref = refs[:6]
    rows_ref, edge_ref, ghost_r_ref, ghost_z_ref, out_ref = refs[6:11]
    refs = refs[11:]
    if last:
        (mom_ref, sums_ref), refs = refs[:2], refs[2:]
    plane_ref, node_ref, wall_ref, slot_ref, lean_ref, radial_ref, axial_ref, table_ref = refs
    step = pl.program_id(0)
    row, place = places_of()

    @pl.when(step == 0)
    def _():
        if last:
            clear_sums(sums_ref)
        total = total_of([p[...] for p in part_refs])
        prepare_nodes(total, codes, place, rows_ref, edge_ref, table_ref, node_ref, wall_ref, plane_ref)

    speeds = [slot_speed(order, step * count + s) for s in range(count)]
    for s in range(count):
        vz = speeds[s]
        for k, value in enumerate(slot_factors(vz, node_ref)):
            slot_ref[s, k] = value
        lean_ref[s] = jnp.abs(vz) * ghost_z_ref[jnp.where(vz > 0, 1, 0)]
        ghost_rows(
            s, vz, place, in_axial_ref, in_left_ref, in_turned_ref, in_right_ref, rows_ref, wall_ref,
            radial_ref, axial_ref,
        )

    def update(r, carry):
        rows = pl.ds(pl.multiple_of(r * LOCAL_Z, LOCAL_Z), LOCAL_Z)
        keep = node_ref[5, rows, :]
        lifts = [ghost_r_ref[side, rows, :] for side in range(2)]
        factor = [[slot_ref[s, k, rows, :] for k in range(3)] for s in range(count)]
        lean = [lean_ref[s] for s in range(count)]
        for j in range(PLANE // 128):
            at = pl.ds(j * 128, 128)
            gauss, along, reach = (plane_ref[k, rows, at] for k in range(3))
            if last:
                sums = [sums_ref[k, r, :, at] for k in range(5)]
            for s in range(count):
                here = pl.ds(s * PLANE + j * 128, 128)
                new = f_ref[r, :, here] * keep + inner_ref[r, :, here].astype(F32)
                new = new + radial_ref[s, :, at] * lifts[1 if j * 128 >= HALF else 0]
                across = axial_ref[s, r, :, at]
                new = new + jnp.concatenate([across, across], axis=0) * lean[s]
                bend = (along + factor[s][1]) * (reach + factor[s][2]) + 1.0
                new = new + (gauss * factor[s][0]) * bend
                out_ref[r, :, here] = new
                if last:
                    sums = add_speed_sums(new, speeds[s], sums)
            if last:
                for k in range(5):
                    sums_ref[k, r, :, at] = sums[k]
        return carry

    lax.fori_loop(0, NODES, update, 0)
    if last:

        @pl.when(step == pl.num_programs(0) - 1)
        def _():
            finish_moments(sums_ref, rows_ref, table_ref, mom_ref)


def last_kernel(part_count, codes, *refs):
    total_ref = total_of([p[...] for p in refs[:part_count]])
    edge_ref, macro_ref, flux_ref = refs[part_count:]
    row, place = places_of()
    values = macroscopic_of(lambda k: total_ref[k : k + 1, :])
    for k in range(8):
        for r in range(NODES):
            macro_ref[k, r : r + 1, :] = values[k][:, r * LOCAL_Z : (r + 1) * LOCAL_Z]
    incident, upward, downward = edge_sums(total_ref, edge_ref)
    bottom = jnp.where(codes[0, BOTTOM] == 1, SAT_DENSITY * HALF_FLUX - incident, 0.0)
    top = jnp.where(codes[0, TOP] == 2, upward - downward, 0.0)
    square = jnp.broadcast_to(jnp.where(place == 0, bottom, top), (NODES, 128))
    same = lax.broadcasted_iota(jnp.int32, (NODES, 128), 0) == lax.broadcasted_iota(jnp.int32, (NODES, 128), 1)
    flux_ref[...] = jnp.sum(jnp.where(same, square, 0.0), axis=0, keepdims=True)[:, 0:NODES]


def whole(shape):
    return pl.BlockSpec(shape, lambda *a: (0,) * len(shape), pipeline_mode=pl.Buffered(1))


def on_device(distribution, z_order, edge_codes):
    local_r, local_z, vdev = distribution.shape
    assert local_r == NODES and local_z == LOCAL_Z
    slots = vdev // PLANE
    group = math.gcd(slots, 3)
    rows_total = lax.axis_size("row")
    verts = lax.axis_size("vert")
    assert lax.axis_size("gz") == 2
    codes = edge_codes.T
    fixed = lambda x: pltpu.with_memory_space_constraint(jnp.asarray(x), pltpu.HBM)
    codes, z_order = fixed(codes), fixed(z_order)
    rows, pos, edge = fixed(ROWS), fixed(NODE_POS), fixed(EDGE)
    radial_m, axial_m = fixed(RADIAL_M), fixed(AXIAL_M)
    ghost_r, ghost_z = fixed(GHOST_R), fixed(GHOST_Z)
    trace_m, mirror_m, rot_m = fixed(TRACE_M), fixed(MIRROR_M), fixed(ROTATION_M)

    def slab(count):
        return pl.BlockSpec((NODES, LOCAL_Z, count * PLANE), lambda i, *n: (0, 0, i))

    def radial_spec(count):
        return pl.BlockSpec((count, LOCAL_Z, HALF), lambda i, *n: (i, 0, 0))

    def axial_spec(count):
        return pl.BlockSpec((count, NODES, PLANE), lambda i, *n: (i, 0, 0))

    def trace_specs(count):
        return [radial_spec(count), radial_spec(count), radial_spec(count), axial_spec(count)]

    mom_spec = whole((MOMENTS, 128))
    radial_shape = jax.ShapeDtypeStruct((slots, LOCAL_Z, HALF), F32)
    axial_shape = jax.ShapeDtypeStruct((slots, NODES, PLANE), F32)
    mom_shape = jax.ShapeDtypeStruct((MOMENTS, 128), F32)
    big_shape = jax.ShapeDtypeStruct(distribution.shape, F32)
    trace_shapes = [radial_shape, radial_shape, radial_shape, axial_shape]
    square = pltpu.VMEM((NODE_COUNT, 128), F32)

    def call(body, name, count, limit, in_specs, out_specs, out_shape, scratch, args):
        return pl.pallas_call(
            body,
            grid_spec=pltpu.PrefetchScalarGridSpec(
                num_scalar_prefetch=2,
                grid=(slots // count,),
                in_specs=in_specs,
                out_specs=out_specs,
                scratch_shapes=scratch,
            ),
            out_shape=out_shape,
            compiler_params=pltpu.CompilerParams(vmem_limit_bytes=limit * 1024 * 1024),
            name=name,
        )(z_order, codes, *args)

    def all_whole(tables):
        return [whole(x.shape) for x in tables]

    def traces_of(f):
        return call(
            lambda *a: trace_kernel(group, *a), "traces", group, 20, [slab(group)] + all_whole([trace_m]),
            [radial_spec(group), radial_spec(group), axial_spec(group)], [radial_shape, radial_shape, axial_shape],
            [], [f, trace_m],
        )

    def moments_of(f, left):
        return call(
            lambda *a: moment_kernel(group, *a), "moments", group, 20,
            [slab(group), radial_spec(group)] + all_whole([rows, mirror_m]),
            [mom_spec, radial_spec(group)], [mom_shape, radial_shape],
            [pltpu.VMEM((5, NODES, LOCAL_Z, PLANE), F32), square], [f, left, rows, mirror_m],
        )

    def inner(f):
        tables = [rows, pos, radial_m, axial_m, rot_m]
        scratch = [
            square,
            pltpu.VMEM((group, NODE_COUNT, PLANE + 256), BF16),
            pltpu.VMEM((group, 2, NODE_COUNT, 2 * NODE_COUNT), BF16),
        ]
        return call(
            lambda *a: inner_kernel(group, *a), "inner_increments", group, 20, [slab(group)] + all_whole(tables),
            slab(group), jax.ShapeDtypeStruct(f.shape, BF16), scratch, [f] + tables,
        )

    def outer(f, change, ghosts, parts, last):
        count = 1 if last else math.gcd(slots, 2)
        tables = [rows, edge, ghost_r, ghost_z]
        scratch = [
            pltpu.VMEM((3, NODE_COUNT, PLANE), F32),
            pltpu.VMEM((10, NODE_COUNT, 128), F32),
            pltpu.VMEM((NODES, 128), F32),
            pltpu.VMEM((count, 3, NODE_COUNT, 128), F32),
            pltpu.VMEM((count, LOCAL_Z, 128), F32),
            pltpu.VMEM((count, LOCAL_Z, PLANE), F32),
            pltpu.VMEM((count, NODES, NODES, PLANE), F32),
            square,
        ]
        return call(
            lambda *a: outer_kernel(count, len(parts), last, *a), "last_update" if last else "update", count, 20,
            [mom_spec] * len(parts) + [slab(count), slab(count), axial_spec(count)] + [radial_spec(count)] * 3
            + all_whole(tables),
            [slab(count)] + ([mom_spec] if last else []), [big_shape] + ([mom_shape] if last else []),
            ([pltpu.VMEM((5, NODES, LOCAL_Z, PLANE), F32)] if last else []) + scratch,
            [*parts, f, change, *ghosts, *tables],
        )

    def spread(moments):
        parts = [moments]
        for shift in range(1, verts):
            parts.append(lax.ppermute(moments, "vert", [(i, i ^ shift) for i in range(verts)]))
        return parts

    def halo(right, left, axial):
        from_axial = lax.ppermute(axial, "gz", [(0, 1), (1, 0)])
        from_left = lax.ppermute(right, "row", [(i, i + 1) for i in range(rows_total - 1)])
        from_right = lax.ppermute(left, "row", [(i + 1, i) for i in range(rows_total - 1)])
        return from_axial, from_left, from_right

    current = distribution
    for number in range(STEPS):
        last = number == STEPS - 1
        traces = traces_of(current)
        from_axial, from_left, from_right = halo(*traces)
        moments, turned = moments_of(current, traces[1])
        parts = spread(moments)
        change = inner(current)
        ghosts = [from_axial, from_left, turned, from_right]
        current, *final = outer(current, change, ghosts, parts, last)
    parts = spread(final[0])
    macro, flux = pl.pallas_call(
        lambda *a: last_kernel(len(parts), *a),
        grid_spec=pltpu.PrefetchScalarGridSpec(
            num_scalar_prefetch=1,
            grid=(1,),
            in_specs=[mom_spec] * len(parts) + [whole(edge.shape)],
            out_specs=[whole((8, NODES, LOCAL_Z)), whole((1, NODES))],
        ),
        out_shape=[
            jax.ShapeDtypeStruct((8, NODES, LOCAL_Z), F32),
            jax.ShapeDtypeStruct((1, NODES), F32),
        ],
        name="macroscopic",
    )(codes, *parts, edge)
    return (current, macro, flux)


def solution(mesh):
    in_specs = (P("row", "gz", "vert"), P("vert"), P(None, "row"))
    out_specs = (P("row", "gz", "vert"), P(None, "row", "gz"), P("gz", "row"))
    return jax.shard_map(
        on_device, mesh=mesh, in_specs=in_specs, out_specs=out_specs, check_vma=False
    )
```

```python
import math

import jax
import jax.numpy as jnp
import ml_dtypes
import numpy as np
from jax import lax
from jax.experimental import pallas as pl
from jax.experimental.pallas import tpu as pltpu
from jax.sharding import PartitionSpec as P

NODES = 8
NVR = 48
NVT = 48
NVZ = 48
STEPS = 2

ELEMENT_WIDTH = 4.0
TIME_STEP = 0.001
KNUDSEN = 0.005
VISCOUS_RATIO = 2.0 / 3.0
SAT_DENSITY = 1.5
SPEED_LIMIT = 5.0

PLANE = NVR * NVT
HALF = PLANE // 2
THIRD = HALF // 3
BOTTOM, TOP = 0, 1
LOCAL_Z = 2 * NODES
NODE_COUNT = NODES * LOCAL_Z
TILE = 256
WINDOW = 512
GHOST_ROWS = 32
MOMENTS = 16
F32 = jnp.float32
BF16 = jnp.bfloat16
PIECES = [(t, TILE, 0) for t in range(0, 1024, TILE)] + [(1024, 128, 0), (1152, 128, 1)] + [
    (t, TILE, 1) for t in range(1280, PLANE, TILE)
]
HALF_PIECES = [(t, TILE) for t in range(0, 1024, TILE)] + [(1024, 128)]


def legendre_pair(position, point_count):
    previous = 1.0
    current = position
    for degree in range(2, point_count + 1):
        previous, current = (
            current,
            ((2 * degree - 1) * position * current - (degree - 1) * previous) / degree,
        )
    slope = point_count * (position * current - previous) / (position * position - 1.0)
    return (current, slope)


def dg_tables(point_count):
    point_list = []
    weight_list = []
    for number in range(point_count):
        position = math.cos(math.pi * (number + 0.75) / (point_count + 0.5))
        for sweep in range(60):
            value, slope = legendre_pair(position, point_count)
            position = position - value / slope
        value, slope = legendre_pair(position, point_count)
        point_list.append(position)
        weight_list.append(2.0 / ((1.0 - position * position) * slope * slope))
    point_list = point_list[::-1]
    weight_list = weight_list[::-1]
    points = np.array(point_list)
    derivative = np.zeros((point_count, point_count))
    right = np.zeros(point_count)
    left = np.zeros(point_count)
    products = [
        np.prod([points[i] - points[j] for j in range(point_count) if j != i])
        for i in range(point_count)
    ]
    for i in range(point_count):
        others = [j for j in range(point_count) if j != i]
        derivative[i, i] = sum(1.0 / (points[i] - points[j]) for j in others)
        for j in others:
            derivative[i, j] = products[i] / products[j] / (points[i] - points[j])
        right[i] = np.prod([1.0 - points[j] for j in others]) / products[i]
        left[i] = np.prod([-1.0 - points[j] for j in others]) / products[i]
    return points, np.array(weight_list), derivative, right, left


def speed_grid(point_count):
    return -SPEED_LIMIT + (np.arange(point_count) + 0.5) * (2.0 * SPEED_LIMIT / point_count)


POINTS, QUAD, DERIV, END_R, END_L = dg_tables(NODES)
LIFT_R = END_R / QUAD
LIFT_L = END_L / QUAD
GRID_R = speed_grid(NVR)
GRID_T = speed_grid(NVT)
GRID_Z = speed_grid(NVZ)
STEP_V = 2 * SPEED_LIMIT / NVR
WEIGHT = STEP_V**3 / (2 * math.pi) ** 1.5
HALF_FLUX = float(
    WEIGHT
    * np.sum(np.exp(-(GRID_R**2) / 2))
    * np.sum(np.exp(-(GRID_T**2) / 2))
    * np.sum(np.maximum(GRID_Z, 0.0) * np.exp(-(GRID_Z**2) / 2))
)
SCALE = TIME_STEP * 2.0 / ELEMENT_WIDTH


def transport_tables():
    ident = np.eye(NODES)
    up = DERIV + np.outer(LIFT_L, END_L)
    down = DERIV - np.outer(LIFT_R, END_R)
    zero = np.zeros((NODES, NODES))
    wide = np.eye(LOCAL_Z)
    radial = np.stack([np.kron(down, wide), np.kron(up, wide), np.kron(DERIV, wide)])
    zup = np.block([[up, zero], [-np.outer(LIFT_L, END_R), up]])
    zdown = np.block([[down, np.outer(LIFT_R, END_L)], [zero, down]])
    zout = np.block([[down, np.outer(LIFT_R, END_L)], [zero, DERIV]])
    axial = np.stack([np.kron(ident, zdown), np.kron(ident, zup), np.kron(ident, zout)])
    ghost_r = np.zeros((2, NODE_COUNT, 128))
    ghost_z = np.zeros((2, LOCAL_Z, 128))
    for r in range(NODES):
        ghost_r[0, r * LOCAL_Z : (r + 1) * LOCAL_Z] = -LIFT_R[r]
        ghost_r[1, r * LOCAL_Z : (r + 1) * LOCAL_Z] = LIFT_L[r]
    for k in range(NODES):
        ghost_z[0, NODES + k] = LIFT_R[k]
        ghost_z[1, k] = LIFT_L[k]
    trace = np.zeros((2, 2, GHOST_ROWS, NODE_COUNT))
    for side in range(2):
        radial_row = END_R if side == 1 else END_L
        for place in range(2):
            for z in range(LOCAL_Z):
                for r in range(NODES):
                    trace[side, place, z, r * LOCAL_Z + z] = radial_row[r]
            for r in range(NODES):
                for k in range(NODES):
                    if place == 0:
                        trace[side, place, LOCAL_Z + r, r * LOCAL_Z + NODES + k] = END_R[k]
                    else:
                        trace[side, place, LOCAL_Z + r, r * LOCAL_Z + k] = END_L[k]
    return (
        (-SCALE * radial).astype(ml_dtypes.bfloat16),
        (-SCALE * axial).astype(np.float32),
        (SCALE * ghost_r).astype(ml_dtypes.bfloat16),
        (SCALE * ghost_z).astype(np.float32),
        trace.astype(ml_dtypes.bfloat16),
    )


def rotation_table():
    full = np.zeros((PLANE + 2 * TILE, PLANE))
    factor = TIME_STEP / (2 * STEP_V)
    for a in range(NVR):
        for b in range(NVT):
            n = a * NVT + b
            first = factor * GRID_T[b] * GRID_T[b]
            second = factor * GRID_R[a] * GRID_T[b]
            if a + 1 < NVR:
                full[TILE + n + NVT, n] = -first
            if a > 0:
                full[TILE + n - NVT, n] = first
            if b + 1 < NVT:
                full[TILE + n + 1, n] = second
            if b > 0:
                full[TILE + n - 1, n] = -second
    tiles = [full[TILE + t - 128 : TILE + t - 128 + WINDOW, t : t + TILE] for t in range(0, PLANE, TILE)]
    return np.stack(tiles).astype(ml_dtypes.bfloat16)


def mirror_table():
    table = np.zeros((THIRD, THIRD))
    groups = THIRD // NVT
    for g in range(groups):
        for b in range(NVT):
            table[(groups - 1 - g) * NVT + b, g * NVT + b] = 1.0
    return table.astype(ml_dtypes.bfloat16)


def plane_rows():
    vr = np.repeat(GRID_R, NVT)
    vt = np.tile(GRID_T, NVR)
    rows = np.zeros((8, PLANE))
    rows[0] = vr
    rows[1] = vt
    rows[2] = np.exp(-(vr**2 + vt**2) / 2)
    return rows.astype(np.float32)


def edge_table():
    table = np.zeros((2, NODES, NODE_COUNT))
    for r in range(NODES):
        for k in range(NODES):
            table[0, r, r * LOCAL_Z + k] = END_L[k]
            table[1, r, r * LOCAL_Z + NODES + k] = END_R[k]
    return table.astype(np.float32)


def node_columns():
    table = np.zeros((NODE_COUNT, 128))
    for r in range(NODES):
        table[r * LOCAL_Z : (r + 1) * LOCAL_Z, :] = (1.0 + POINTS[r]) / 2
    return table.astype(np.float32)


RADIAL_M, AXIAL_M, GHOST_R, GHOST_Z, TRACE_M = transport_tables()
ROTATION_M = rotation_table()
MIRROR_M = mirror_table()
ROWS = plane_rows()
EDGE = edge_table()
NODE_POS = node_columns()


def slot_speed(order, slot):
    return (order[slot].astype(F32) + 0.5) * (2 * SPEED_LIMIT / NVZ) - SPEED_LIMIT


def dot(x, y):
    return jnp.dot(x, y, preferred_element_type=F32)


def macroscopic_of(m):
    rho = m(0)
    inv = 1.0 / rho
    ur, ut, uz = m(1) * inv, m(2) * inv, m(3) * inv
    rr, tt, rt, zz, rz, tz = (m(k) for k in range(4, 10))
    energy = rr + tt + zz
    speed = ur * ur + ut * ut + uz * uz
    temp = (energy * inv - speed) * (1.0 / 3.0)
    tail = 2.0 * rho * speed - energy
    qr = 0.5 * (m(10) - 2.0 * (ur * rr + ut * rt + uz * rz) + ur * tail)
    qt = 0.5 * (m(11) - 2.0 * (ur * rt + ut * tt + uz * tz) + ut * tail)
    qz = 0.5 * (m(12) - 2.0 * (ur * rz + ut * tz + uz * zz) + uz * tail)
    return rho, ur, ut, uz, temp, qr, qt, qz


def add_speed_sums(field, vz, sums):
    one = field * vz
    two = one * vz
    return [sums[0] + field, sums[1] + one, sums[2] + two, sums[3] + two * vz]


def finish_moments(sums_ref, rows_ref, table_ref, out_ref):
    lane = lax.broadcasted_iota(jnp.int32, (LOCAL_Z, 128), 1)

    def one_radius(r, carry):
        acc = [jnp.zeros((LOCAL_Z, 128), F32) for _ in range(14)]
        for j in range(PLANE // 128):
            at = pl.ds(j * 128, 128)
            vr = rows_ref[0:1, at]
            vt = rows_ref[1:2, at]
            g0, g1, g2, g3, g4 = (sums_ref[k, r, :, at] for k in range(5))
            a = vr * g0
            b = vt * g0
            aa = vr * a
            bb = vt * b
            c = vr * g1
            d = vt * g1
            perp = aa + bb + g2
            new = [g0, a, b, g1, aa, bb, vr * b, g2, c, d, vr * perp, vt * perp, vr * c + vt * d + g3, g4]
            acc = [x + y for x, y in zip(acc, new)]
        block = jnp.zeros((LOCAL_Z, 128), F32)
        for k in range(14):
            block = jnp.where(lane == k, WEIGHT * jnp.sum(acc[k], axis=1, keepdims=True), block)
        table_ref[pl.ds(pl.multiple_of(r * LOCAL_Z, LOCAL_Z), LOCAL_Z), :] = block
        return carry

    lax.fori_loop(0, NODES, one_radius, 0)
    out_ref[...] = jnp.transpose(table_ref[...])[0:MOMENTS, :]


def clear_sums(sums_ref):
    sums_ref[...] = jnp.zeros(sums_ref.shape, F32)


def places_of():
    return lax.axis_index("row"), lax.axis_index("gz")


def turn_traces(count, row, mirror_ref, left_ref, turned_ref):
    @pl.when(row == 0)
    def _():
        for part in range(3):
            start = (2 - part) * THIRD
            flat = left_ref[:, :, start : start + THIRD].reshape(count * LOCAL_Z, THIRD).astype(BF16)
            got = dot(flat, mirror_ref[...])
            turned_ref[:, :, part * THIRD : (part + 1) * THIRD] = got.reshape(count, LOCAL_Z, THIRD)

    @pl.when(row != 0)
    def _():
        turned_ref[...] = jnp.zeros(turned_ref.shape, F32)


def nodes_of(ref, first, lanes):
    return ref[:, :, first : first + lanes].reshape(NODE_COUNT, lanes)


def trace_kernel(count, order, codes, f_ref, trace_ref, near_ref, far_ref, axial_ref):
    row, place = places_of()
    even = lax.rem(row, 2) == 0
    for s in range(count):
        for first, lanes in HALF_PIECES:
            got = []
            for side in range(2):
                here = side * HALF + first
                narrow = nodes_of(f_ref, s * PLANE + here, lanes).astype(BF16)
                got.append(dot(trace_ref[side, place], narrow))
                axial_ref[s, :, here : here + lanes] = got[side][LOCAL_Z : LOCAL_Z + NODES]
            left, right = got[0][0:LOCAL_Z], got[1][0:LOCAL_Z]
            near_ref[s, :, first : first + lanes] = jnp.where(even, right, left)
            far_ref[s, :, first : first + lanes] = jnp.where(even, left, right)


def moment_kernel(
    count, order, codes, f_ref, left_ref, rows_ref, mirror_ref, mom_ref, turned_ref, sums_ref, table_ref
):
    step = pl.program_id(0)
    row, place = places_of()

    @pl.when(step == 0)
    def _():
        clear_sums(sums_ref)

    turn_traces(count, row, mirror_ref, left_ref, turned_ref)
    edge = pl.ds(pl.multiple_of(place * NODES, NODES), NODES)
    speeds = [slot_speed(order, step * count + s) for s in range(count)]
    for j in range(0, PLANE, 128):
        at = pl.ds(j, 128)
        for r in range(NODES):
            sums = [sums_ref[k, r, :, at] for k in range(4)]
            gross = sums_ref[4, r, edge, at]
            for s in range(count):
                here = pl.ds(s * PLANE + j, 128)
                sums = add_speed_sums(f_ref[r, :, here], speeds[s], sums)
                gross = gross + f_ref[r, edge, here] * jnp.abs(speeds[s])
            for k in range(4):
                sums_ref[k, r, :, at] = sums[k]
            sums_ref[4, r, edge, at] = gross

    @pl.when(step == pl.num_programs(0) - 1)
    def _():
        finish_moments(sums_ref, rows_ref, table_ref, mom_ref)


def inner_kernel(
    count, order, codes, f_ref, rows_ref, pos_ref, radial_ref, axial_m_ref, rot_ref,
    out_ref, inverse_ref, pad_ref, lhs_ref,
):
    step = pl.program_id(0)
    row, place = places_of()

    @pl.when(step == 0)
    def _():
        pad_ref[:, :, 0:128] = jnp.zeros((count, NODE_COUNT, 128), BF16)
        pad_ref[:, :, 128 + PLANE :] = jnp.zeros((count, NODE_COUNT, 128), BF16)
        inverse_ref[...] = 1.0 / (ELEMENT_WIDTH * (row.astype(F32) + pos_ref[...]))
        minus = radial_ref[jnp.where(row == lax.axis_size("row") - 1, 2, 0)]
        for s in range(count):
            lhs_ref[s, 0, :, 0:NODE_COUNT] = minus
            lhs_ref[s, 1, :, 0:NODE_COUNT] = radial_ref[1]

    kind_out = jnp.where(jnp.logical_and(place == 1, codes[0, TOP] == 2), 2, 0)
    inverse = inverse_ref[...]
    speeds = [slot_speed(order, step * count + s) for s in range(count)]
    for s in range(count):
        vz = speeds[s]
        axial = (vz * axial_m_ref[jnp.where(vz > 0, 1, kind_out)]).astype(BF16)
        lhs_ref[s, 0, :, NODE_COUNT:] = axial
        lhs_ref[s, 1, :, NODE_COUNT:] = axial
        for j in range(PLANE // 128):
            field = nodes_of(f_ref, s * PLANE + j * 128, 128)
            pad_ref[s, :, 128 + j * 128 : 256 + j * 128] = (field * inverse).astype(BF16)

    for tile in range(PLANE // TILE):
        start = tile * TILE
        turned = dot(pad_ref[:, :, start : start + WINDOW].reshape(count * NODE_COUNT, WINDOW), rot_ref[tile])
        for first, lanes, side in PIECES:
            if first // TILE != tile:
                continue
            vr = rows_ref[0:1, first : first + lanes]
            inside = first - start
            for s in range(count):
                here = s * PLANE + first
                field = nodes_of(f_ref, here, lanes)
                both = jnp.concatenate([(field * vr).astype(BF16), field.astype(BF16)], axis=0)
                change = turned[s * NODE_COUNT : (s + 1) * NODE_COUNT, inside : inside + lanes]
                change = change + dot(lhs_ref[s, side], both)
                out_ref[:, :, here : here + lanes] = change.astype(BF16).reshape(NODES, LOCAL_Z, lanes)


def total_of(parts):
    while len(parts) > 1:
        parts = [parts[k] + parts[k + 1] for k in range(0, len(parts), 2)]
    return parts[0]


def edge_sums(total, edge_ref):
    net, gross = total[3:4, :], total[13:14, :]
    down, up = 0.5 * (gross - net), 0.5 * (gross + net)
    pairs = ((0, down), (1, up), (1, down))
    return tuple(jnp.sum(edge_ref[k] * row, axis=1, keepdims=True) for k, row in pairs)


def prepare_nodes(total, codes, place, rows_ref, edge_ref, table_ref, node_ref, wall_ref, plane_ref):
    rho, ur, ut, uz, temp, qr, qt, qz = macroscopic_of(lambda k: total[k : k + 1, :])
    inv_t = 1.0 / temp
    beta = ((1.0 - VISCOUS_RATIO) / 5.0) / (rho * temp * temp)
    kappa = rho * (TIME_STEP / KNUDSEN)
    peak = kappa * rho * inv_t * jnp.sqrt(inv_t)
    values = [uz, -0.5 * inv_t, qz * beta, inv_t, peak, 1.0 - kappa, ur, ut, qr * beta, qt * beta]
    clear_sums(table_ref)
    for k, value in enumerate(values):
        table_ref[k : k + 1, :] = value
    table_ref[...] = jnp.transpose(table_ref[...])
    for k in range(len(values)):
        node_ref[k] = jnp.broadcast_to(table_ref[:, k : k + 1], (NODE_COUNT, 128))
    incident, upward, downward = edge_sums(total, edge_ref)
    bottom = jnp.where(codes[0, BOTTOM] == 1, SAT_DENSITY, incident * (1.0 / HALF_FLUX))
    top = jnp.where(codes[0, TOP] == 2, 0.0, upward * (1.0 / HALF_FLUX))
    wall_ref[...] = jnp.broadcast_to(jnp.where(place == 0, bottom, top), (NODES, 128))

    def one_radius(r, carry):
        rows = pl.ds(pl.multiple_of(r * LOCAL_Z, LOCAL_Z), LOCAL_Z)
        n_half, n_inv = node_ref[1, rows, :], node_ref[3, rows, :]
        n_ur, n_ut = node_ref[6, rows, :], node_ref[7, rows, :]
        n_qr, n_qt = node_ref[8, rows, :], node_ref[9, rows, :]
        for j in range(PLANE // 128):
            at = pl.ds(j * 128, 128)
            cr = rows_ref[0:1, at] - n_ur
            ct = rows_ref[1:2, at] - n_ut
            square = cr * cr + ct * ct
            gauss = jnp.exp(square * n_half)
            along = cr * n_qr + ct * n_qt
            plane_ref[0, rows, at] = gauss
            plane_ref[1, rows, at] = along
            plane_ref[2, rows, at] = square * n_inv
        return carry

    lax.fori_loop(0, NODES, one_radius, 0)


def slot_factors(vz, node_ref):
    cz = vz - node_ref[0]
    square = cz * cz
    return node_ref[4] * jnp.exp(square * node_ref[1]), cz * node_ref[2], square * node_ref[3] - 5.0


def ghost_rows(
    s, vz, row, place, in_axial_ref, in_near_ref, in_turned_ref, in_far_ref, rows_ref, wall_ref, radial_ref, axial_ref
):
    own = (place == 0) == (vz > 0)
    even = lax.rem(row, 2) == 0
    strength = jnp.exp(-0.5 * vz * vz + jnp.zeros((NODES, 128), F32)) * wall_ref[...]
    for j in range(PLANE // 128):
        at = pl.ds(j * 128, 128)
        if j * 128 < HALF:
            radial = jnp.where(even, in_near_ref[s, :, at], in_far_ref[s, :, at])
        else:
            back = pl.ds(j * 128 - HALF, 128)
            radial = jnp.where(even, in_far_ref[s, :, back], in_near_ref[s, :, back]) + in_turned_ref[s, :, back]
        radial_ref[s, :, at] = (rows_ref[0:1, at] * radial).astype(BF16)
        axial = jnp.where(own, strength * rows_ref[2:3, at], in_axial_ref[s, :, at])
        for r in range(NODES):
            axial_ref[s, r, :, at] = jnp.broadcast_to(axial[r : r + 1], (LOCAL_Z, 128)).astype(BF16)


def outer_kernel(count, part_count, last, order, codes, *refs):
    part_refs, refs = refs[:part_count], refs[part_count:]
    f_ref, inner_ref, in_axial_ref, in_near_ref, in_turned_ref, in_far_ref = refs[:6]
    rows_ref, edge_ref, ghost_r_ref, ghost_z_ref, out_ref = refs[6:11]
    refs = refs[11:]
    if last:
        (mom_ref, sums_ref), refs = refs[:2], refs[2:]
    plane_ref, node_ref, wall_ref, slot_ref, lean_ref, radial_ref, axial_ref, table_ref = refs
    step = pl.program_id(0)
    row, place = places_of()

    @pl.when(step == 0)
    def _():
        if last:
            clear_sums(sums_ref)
        total = total_of([p[...] for p in part_refs])
        prepare_nodes(total, codes, place, rows_ref, edge_ref, table_ref, node_ref, wall_ref, plane_ref)

    edge = pl.ds(pl.multiple_of(place * NODES, NODES), NODES)
    speeds = [slot_speed(order, step * count + s) for s in range(count)]
    for s in range(count):
        vz = speeds[s]
        for k, value in enumerate(slot_factors(vz, node_ref)):
            slot_ref[s, k] = value
        lean_ref[s] = (jnp.abs(vz) * ghost_z_ref[jnp.where(vz > 0, 1, 0)]).astype(BF16)
        ghost_rows(
            s, vz, row, place, in_axial_ref, in_near_ref, in_turned_ref, in_far_ref, rows_ref, wall_ref,
            radial_ref, axial_ref,
        )

    def update(r, carry):
        rows = pl.ds(pl.multiple_of(r * LOCAL_Z, LOCAL_Z), LOCAL_Z)
        keep = node_ref[5, rows, :]
        lifts = [ghost_r_ref[side, rows, :] for side in range(2)]
        factor = [[slot_ref[s, k, rows, :] for k in range(3)] for s in range(count)]
        lean = [lean_ref[s] for s in range(count)]
        for j in range(PLANE // 128):
            at = pl.ds(j * 128, 128)
            gauss, along, reach = (plane_ref[k, rows, at] for k in range(3))
            if last:
                sums = [sums_ref[k, r, :, at] for k in range(4)]
                gross = sums_ref[4, r, edge, at]
            for s in range(count):
                here = pl.ds(s * PLANE + j * 128, 128)
                change = inner_ref[r, :, here] + radial_ref[s, :, at] * lifts[1 if j * 128 >= HALF else 0]
                change = change + axial_ref[s, r, :, at] * lean[s]
                new = f_ref[r, :, here] * keep + change.astype(F32)
                bend = (along + factor[s][1]) * (reach + factor[s][2]) + 1.0
                new = new + (gauss * factor[s][0]) * bend
                out_ref[r, :, here] = new
                if last:
                    sums = add_speed_sums(new, speeds[s], sums)
                    gross = gross + jnp.where(place == 0, new[0:NODES], new[NODES:]) * jnp.abs(speeds[s])
            if last:
                for k in range(4):
                    sums_ref[k, r, :, at] = sums[k]
                sums_ref[4, r, edge, at] = gross
        return carry

    lax.fori_loop(0, NODES, update, 0)
    if last:

        @pl.when(step == pl.num_programs(0) - 1)
        def _():
            finish_moments(sums_ref, rows_ref, table_ref, mom_ref)


def last_kernel(part_count, codes, *refs):
    total_ref = total_of([p[...] for p in refs[:part_count]])
    edge_ref, macro_ref, flux_ref = refs[part_count:]
    row, place = places_of()
    values = macroscopic_of(lambda k: total_ref[k : k + 1, :])
    for k in range(8):
        for r in range(NODES):
            macro_ref[k, r : r + 1, :] = values[k][:, r * LOCAL_Z : (r + 1) * LOCAL_Z]
    incident, upward, downward = edge_sums(total_ref, edge_ref)
    bottom = jnp.where(codes[0, BOTTOM] == 1, SAT_DENSITY * HALF_FLUX - incident, 0.0)
    top = jnp.where(codes[0, TOP] == 2, upward - downward, 0.0)
    square = jnp.broadcast_to(jnp.where(place == 0, bottom, top), (NODES, 128))
    same = lax.broadcasted_iota(jnp.int32, (NODES, 128), 0) == lax.broadcasted_iota(jnp.int32, (NODES, 128), 1)
    flux_ref[...] = jnp.sum(jnp.where(same, square, 0.0), axis=0, keepdims=True)[:, 0:NODES]


def whole(shape):
    return pl.BlockSpec(shape, lambda *a: (0,) * len(shape), pipeline_mode=pl.Buffered(1))


def on_device(distribution, z_order, edge_codes):
    local_r, local_z, vdev = distribution.shape
    assert local_r == NODES and local_z == LOCAL_Z
    slots = vdev // PLANE
    group = math.gcd(slots, 3)
    rows_total = lax.axis_size("row")
    verts = lax.axis_size("vert")
    assert lax.axis_size("gz") == 2 and rows_total % 2 == 0
    codes = edge_codes.T
    fixed = lambda x: pltpu.with_memory_space_constraint(jnp.asarray(x), pltpu.HBM)
    codes, z_order = fixed(codes), fixed(z_order)
    rows, pos, edge = fixed(ROWS), fixed(NODE_POS), fixed(EDGE)
    radial_m, axial_m = fixed(RADIAL_M), fixed(AXIAL_M)
    ghost_r, ghost_z = fixed(GHOST_R), fixed(GHOST_Z)
    trace_m, mirror_m, rot_m = fixed(TRACE_M), fixed(MIRROR_M), jnp.asarray(ROTATION_M)

    def slab(count):
        return pl.BlockSpec((NODES, LOCAL_Z, count * PLANE), lambda i, *n: (0, 0, i))

    def radial_spec(count):
        return pl.BlockSpec((count, LOCAL_Z, HALF), lambda i, *n: (i, 0, 0))

    def axial_spec(count):
        return pl.BlockSpec((count, NODES, PLANE), lambda i, *n: (i, 0, 0))

    def trace_specs(count):
        return [radial_spec(count), radial_spec(count), radial_spec(count), axial_spec(count)]

    mom_spec = whole((MOMENTS, 128))
    radial_shape = jax.ShapeDtypeStruct((slots, LOCAL_Z, HALF), F32)
    axial_shape = jax.ShapeDtypeStruct((slots, NODES, PLANE), F32)
    mom_shape = jax.ShapeDtypeStruct((MOMENTS, 128), F32)
    big_shape = jax.ShapeDtypeStruct(distribution.shape, F32)
    trace_shapes = [radial_shape, radial_shape, radial_shape, axial_shape]
    square = pltpu.VMEM((NODE_COUNT, 128), F32)

    def call(body, name, count, limit, in_specs, out_specs, out_shape, scratch, args):
        return pl.pallas_call(
            body,
            grid_spec=pltpu.PrefetchScalarGridSpec(
                num_scalar_prefetch=2,
                grid=(slots // count,),
                in_specs=in_specs,
                out_specs=out_specs,
                scratch_shapes=scratch,
            ),
            out_shape=out_shape,
            compiler_params=pltpu.CompilerParams(vmem_limit_bytes=limit * 1024 * 1024),
            name=name,
        )(z_order, codes, *args)

    def all_whole(tables):
        return [whole(x.shape) for x in tables]

    def traces_of(f):
        return call(
            lambda *a: trace_kernel(group, *a), "traces", group, 20, [slab(group)] + all_whole([trace_m]),
            [radial_spec(group), radial_spec(group), axial_spec(group)], [radial_shape, radial_shape, axial_shape],
            [], [f, trace_m],
        )

    def moments_of(f, left):
        return call(
            lambda *a: moment_kernel(group, *a), "moments", group, 20,
            [slab(group), radial_spec(group)] + all_whole([rows, mirror_m]),
            [mom_spec, radial_spec(group)], [mom_shape, radial_shape],
            [pltpu.VMEM((5, NODES, LOCAL_Z, PLANE), F32), square], [f, left, rows, mirror_m],
        )

    def inner(f):
        tables = [rows, pos, radial_m, axial_m, rot_m]
        scratch = [
            square,
            pltpu.VMEM((group, NODE_COUNT, PLANE + 256), BF16),
            pltpu.VMEM((group, 2, NODE_COUNT, 2 * NODE_COUNT), BF16),
        ]
        return call(
            lambda *a: inner_kernel(group, *a), "inner_increments", group, 20, [slab(group)] + all_whole(tables),
            slab(group), jax.ShapeDtypeStruct(f.shape, BF16), scratch, [f] + tables,
        )

    def outer(f, change, ghosts, parts, last):
        count = 1 if last else math.gcd(slots, 2)
        tables = [rows, edge, ghost_r, ghost_z]
        scratch = [
            pltpu.VMEM((3, NODE_COUNT, PLANE), F32),
            pltpu.VMEM((10, NODE_COUNT, 128), F32),
            pltpu.VMEM((NODES, 128), F32),
            pltpu.VMEM((count, 3, NODE_COUNT, 128), F32),
            pltpu.VMEM((count, LOCAL_Z, 128), BF16),
            pltpu.VMEM((count, LOCAL_Z, PLANE), BF16),
            pltpu.VMEM((count, NODES, LOCAL_Z, PLANE), BF16),
            square,
        ]
        return call(
            lambda *a: outer_kernel(count, len(parts), last, *a), "last_update" if last else "update", count, 20,
            [mom_spec] * len(parts) + [slab(count), slab(count), axial_spec(count)] + [radial_spec(count)] * 3
            + all_whole(tables),
            [slab(count)] + ([mom_spec] if last else []), [big_shape] + ([mom_shape] if last else []),
            ([pltpu.VMEM((5, NODES, LOCAL_Z, PLANE), F32)] if last else []) + scratch,
            [*parts, f, change, *ghosts, *tables],
        )

    def spread(moments):
        parts = [moments]
        for shift in range(1, verts):
            parts.append(lax.ppermute(moments, "vert", [(i, i ^ shift) for i in range(verts)]))
        return parts

    def halo(near, far, axial):
        from_axial = lax.ppermute(axial, "gz", [(0, 1), (1, 0)])
        pairs = [(i, i ^ 1) for i in range(rows_total)]
        from_near = lax.ppermute(near, "row", pairs)
        between = [(i, i + 1) for i in range(1, rows_total - 1, 2)]
        from_far = lax.ppermute(far, "row", between + [(b, a) for a, b in between])
        return from_axial, from_near, from_far

    current = distribution
    for number in range(STEPS):
        last = number == STEPS - 1
        traces = traces_of(current)
        from_axial, from_near, from_far = halo(*traces)
        moments, turned = moments_of(current, traces[1])
        parts = spread(moments)
        change = inner(current)
        ghosts = [from_axial, from_near, turned, from_far]
        current, *final = outer(current, change, ghosts, parts, last)
    parts = spread(final[0])
    macro, flux = pl.pallas_call(
        lambda *a: last_kernel(len(parts), *a),
        grid_spec=pltpu.PrefetchScalarGridSpec(
            num_scalar_prefetch=1,
            grid=(1,),
            in_specs=[mom_spec] * len(parts) + [whole(edge.shape)],
            out_specs=[whole((8, NODES, LOCAL_Z)), whole((1, NODES))],
        ),
        out_shape=[
            jax.ShapeDtypeStruct((8, NODES, LOCAL_Z), F32),
            jax.ShapeDtypeStruct((1, NODES), F32),
        ],
        compiler_params=pltpu.CompilerParams(vmem_limit_bytes=4 * 1024 * 1024),
        name="macroscopic",
    )(codes, *parts, edge)
    return (current, macro, flux)


def solution(mesh):
    in_specs = (P("row", "gz", "vert"), P("vert"), P(None, "row"))
    out_specs = (P("row", "gz", "vert"), P(None, "row", "gz"), P("gz", "row"))
    return jax.shard_map(
        on_device, mesh=mesh, in_specs=in_specs, out_specs=out_specs, check_vma=False
    )
```

```python
import math

import jax
import jax.numpy as jnp
import ml_dtypes
import numpy as np
from jax import lax
from jax.experimental import pallas as pl
from jax.experimental.pallas import tpu as pltpu
from jax.sharding import PartitionSpec as P

NODES = 8
NVR = 48
NVT = 48
NVZ = 48
STEPS = 2

ELEMENT_WIDTH = 4.0
TIME_STEP = 0.001
KNUDSEN = 0.005
VISCOUS_RATIO = 2.0 / 3.0
SAT_DENSITY = 1.5
SPEED_LIMIT = 5.0

PLANE = NVR * NVT
HALF = PLANE // 2
THIRD = HALF // 3
BOTTOM, TOP = 0, 1
LOCAL_Z = 2 * NODES
NODE_COUNT = NODES * LOCAL_Z
TILE = 256
WINDOW = 512
GHOST_ROWS = 32
MOMENTS = 16
F32 = jnp.float32
BF16 = jnp.bfloat16
PIECES = [(t, TILE, 0) for t in range(0, 1024, TILE)] + [(1024, 128, 0), (1152, 128, 1)] + [
    (t, TILE, 1) for t in range(1280, PLANE, TILE)
]
HALF_PIECES = [(t, TILE) for t in range(0, 1024, TILE)] + [(1024, 128)]


def legendre_pair(position, point_count):
    previous = 1.0
    current = position
    for degree in range(2, point_count + 1):
        previous, current = (
            current,
            ((2 * degree - 1) * position * current - (degree - 1) * previous) / degree,
        )
    slope = point_count * (position * current - previous) / (position * position - 1.0)
    return (current, slope)


def dg_tables(point_count):
    point_list = []
    weight_list = []
    for number in range(point_count):
        position = math.cos(math.pi * (number + 0.75) / (point_count + 0.5))
        for sweep in range(60):
            value, slope = legendre_pair(position, point_count)
            position = position - value / slope
        value, slope = legendre_pair(position, point_count)
        point_list.append(position)
        weight_list.append(2.0 / ((1.0 - position * position) * slope * slope))
    point_list = point_list[::-1]
    weight_list = weight_list[::-1]
    points = np.array(point_list)
    derivative = np.zeros((point_count, point_count))
    right = np.zeros(point_count)
    left = np.zeros(point_count)
    products = [
        np.prod([points[i] - points[j] for j in range(point_count) if j != i])
        for i in range(point_count)
    ]
    for i in range(point_count):
        others = [j for j in range(point_count) if j != i]
        derivative[i, i] = sum(1.0 / (points[i] - points[j]) for j in others)
        for j in others:
            derivative[i, j] = products[i] / products[j] / (points[i] - points[j])
        right[i] = np.prod([1.0 - points[j] for j in others]) / products[i]
        left[i] = np.prod([-1.0 - points[j] for j in others]) / products[i]
    return points, np.array(weight_list), derivative, right, left


def speed_grid(point_count):
    return -SPEED_LIMIT + (np.arange(point_count) + 0.5) * (2.0 * SPEED_LIMIT / point_count)


POINTS, QUAD, DERIV, END_R, END_L = dg_tables(NODES)
LIFT_R = END_R / QUAD
LIFT_L = END_L / QUAD
GRID_R = speed_grid(NVR)
GRID_T = speed_grid(NVT)
GRID_Z = speed_grid(NVZ)
STEP_V = 2 * SPEED_LIMIT / NVR
WEIGHT = STEP_V**3 / (2 * math.pi) ** 1.5
HALF_FLUX = float(
    WEIGHT
    * np.sum(np.exp(-(GRID_R**2) / 2))
    * np.sum(np.exp(-(GRID_T**2) / 2))
    * np.sum(np.maximum(GRID_Z, 0.0) * np.exp(-(GRID_Z**2) / 2))
)
SCALE = TIME_STEP * 2.0 / ELEMENT_WIDTH


def transport_tables():
    ident = np.eye(NODES)
    up = DERIV + np.outer(LIFT_L, END_L)
    down = DERIV - np.outer(LIFT_R, END_R)
    zero = np.zeros((NODES, NODES))
    wide = np.eye(LOCAL_Z)
    radial = np.stack([np.kron(down, wide), np.kron(up, wide), np.kron(DERIV, wide)])
    zup = np.block([[up, zero], [-np.outer(LIFT_L, END_R), up]])
    zdown = np.block([[down, np.outer(LIFT_R, END_L)], [zero, down]])
    zout = np.block([[down, np.outer(LIFT_R, END_L)], [zero, DERIV]])
    axial = np.stack([np.kron(ident, zdown), np.kron(ident, zup), np.kron(ident, zout)])
    ghost_r = np.zeros((2, NODE_COUNT, 128))
    ghost_z = np.zeros((2, LOCAL_Z, 128))
    for r in range(NODES):
        ghost_r[0, r * LOCAL_Z : (r + 1) * LOCAL_Z] = -LIFT_R[r]
        ghost_r[1, r * LOCAL_Z : (r + 1) * LOCAL_Z] = LIFT_L[r]
    for k in range(NODES):
        ghost_z[0, NODES + k] = LIFT_R[k]
        ghost_z[1, k] = LIFT_L[k]
    trace = np.zeros((2, 2, GHOST_ROWS, NODE_COUNT))
    for side in range(2):
        radial_row = END_R if side == 1 else END_L
        for place in range(2):
            for z in range(LOCAL_Z):
                for r in range(NODES):
                    trace[side, place, z, r * LOCAL_Z + z] = radial_row[r]
            for r in range(NODES):
                for k in range(NODES):
                    if place == 0:
                        trace[side, place, LOCAL_Z + r, r * LOCAL_Z + NODES + k] = END_R[k]
                    else:
                        trace[side, place, LOCAL_Z + r, r * LOCAL_Z + k] = END_L[k]
    return (
        (-SCALE * radial).astype(ml_dtypes.bfloat16),
        (-SCALE * axial).astype(np.float32),
        (SCALE * ghost_r).astype(np.float32),
        (SCALE * ghost_z).astype(np.float32),
        trace.astype(ml_dtypes.bfloat16),
    )


def rotation_table():
    full = np.zeros((PLANE + 2 * TILE, PLANE))
    factor = TIME_STEP / (2 * STEP_V)
    for a in range(NVR):
        for b in range(NVT):
            n = a * NVT + b
            first = factor * GRID_T[b] * GRID_T[b]
            second = factor * GRID_R[a] * GRID_T[b]
            if a + 1 < NVR:
                full[TILE + n + NVT, n] = -first
            if a > 0:
                full[TILE + n - NVT, n] = first
            if b + 1 < NVT:
                full[TILE + n + 1, n] = second
            if b > 0:
                full[TILE + n - 1, n] = -second
    tiles = [full[TILE + t - 128 : TILE + t - 128 + WINDOW, t : t + TILE] for t in range(0, PLANE, TILE)]
    return np.stack(tiles).astype(ml_dtypes.bfloat16)


def mirror_table():
    table = np.zeros((THIRD, THIRD))
    groups = THIRD // NVT
    for g in range(groups):
        for b in range(NVT):
            table[(groups - 1 - g) * NVT + b, g * NVT + b] = 1.0
    return table.astype(ml_dtypes.bfloat16)


def plane_rows():
    vr = np.repeat(GRID_R, NVT)
    vt = np.tile(GRID_T, NVR)
    rows = np.zeros((8, PLANE))
    rows[0] = vr
    rows[1] = vt
    rows[2] = np.exp(-(vr**2 + vt**2) / 2)
    return rows.astype(np.float32)


def edge_table():
    table = np.zeros((2, NODES, NODE_COUNT))
    for r in range(NODES):
        for k in range(NODES):
            table[0, r, r * LOCAL_Z + k] = END_L[k]
            table[1, r, r * LOCAL_Z + NODES + k] = END_R[k]
    return table.astype(np.float32)


def node_columns():
    table = np.zeros((NODE_COUNT, 128))
    for r in range(NODES):
        table[r * LOCAL_Z : (r + 1) * LOCAL_Z, :] = (1.0 + POINTS[r]) / 2
    return table.astype(np.float32)


RADIAL_M, AXIAL_M, GHOST_R, GHOST_Z, TRACE_M = transport_tables()
ROTATION_M = rotation_table()
MIRROR_M = mirror_table()
ROWS = plane_rows()
EDGE = edge_table()
NODE_POS = node_columns()


def slot_speed(order, slot):
    return (order[slot].astype(F32) + 0.5) * (2 * SPEED_LIMIT / NVZ) - SPEED_LIMIT


def dot(x, y):
    return jnp.dot(x, y, preferred_element_type=F32)


def macroscopic_of(m):
    rho = m(0)
    inv = 1.0 / rho
    ur, ut, uz = m(1) * inv, m(2) * inv, m(3) * inv
    rr, tt, rt, zz, rz, tz = (m(k) for k in range(4, 10))
    energy = rr + tt + zz
    speed = ur * ur + ut * ut + uz * uz
    temp = (energy * inv - speed) * (1.0 / 3.0)
    tail = 2.0 * rho * speed - energy
    qr = 0.5 * (m(10) - 2.0 * (ur * rr + ut * rt + uz * rz) + ur * tail)
    qt = 0.5 * (m(11) - 2.0 * (ur * rt + ut * tt + uz * tz) + ut * tail)
    qz = 0.5 * (m(12) - 2.0 * (ur * rz + ut * tz + uz * zz) + uz * tail)
    return rho, ur, ut, uz, temp, qr, qt, qz


def add_speed_sums(field, vz, sums):
    one = field * vz
    two = one * vz
    return [
        sums[0] + field,
        sums[1] + one,
        sums[2] + two,
        sums[3] + two * vz,
        sums[4] + field * jnp.abs(vz),
    ]


def finish_moments(sums_ref, rows_ref, table_ref, out_ref):
    lane = lax.broadcasted_iota(jnp.int32, (LOCAL_Z, 128), 1)

    def one_radius(r, carry):
        acc = [jnp.zeros((LOCAL_Z, 128), F32) for _ in range(14)]
        for j in range(PLANE // 128):
            at = pl.ds(j * 128, 128)
            vr = rows_ref[0:1, at]
            vt = rows_ref[1:2, at]
            g0, g1, g2, g3, g4 = (sums_ref[k, r, :, at] for k in range(5))
            a = vr * g0
            b = vt * g0
            aa = vr * a
            bb = vt * b
            c = vr * g1
            d = vt * g1
            perp = aa + bb + g2
            new = [g0, a, b, g1, aa, bb, vr * b, g2, c, d, vr * perp, vt * perp, vr * c + vt * d + g3, g4]
            acc = [x + y for x, y in zip(acc, new)]
        block = jnp.zeros((LOCAL_Z, 128), F32)
        for k in range(14):
            block = jnp.where(lane == k, WEIGHT * jnp.sum(acc[k], axis=1, keepdims=True), block)
        table_ref[pl.ds(pl.multiple_of(r * LOCAL_Z, LOCAL_Z), LOCAL_Z), :] = block
        return carry

    lax.fori_loop(0, NODES, one_radius, 0)
    out_ref[...] = jnp.transpose(table_ref[...])[0:MOMENTS, :]


def clear_sums(sums_ref):
    sums_ref[...] = jnp.zeros(sums_ref.shape, F32)


def places_of():
    return lax.axis_index("row"), lax.axis_index("gz")


def turn_traces(count, row, mirror_ref, left_ref, turned_ref):
    @pl.when(row == 0)
    def _():
        for part in range(3):
            start = (2 - part) * THIRD
            flat = left_ref[:, :, start : start + THIRD].reshape(count * LOCAL_Z, THIRD).astype(BF16)
            got = dot(flat, mirror_ref[...])
            turned_ref[:, :, part * THIRD : (part + 1) * THIRD] = got.reshape(count, LOCAL_Z, THIRD)

    @pl.when(row != 0)
    def _():
        turned_ref[...] = jnp.zeros(turned_ref.shape, F32)


def nodes_of(ref, first, lanes):
    return ref[:, :, first : first + lanes].reshape(NODE_COUNT, lanes)


def trace_kernel(count, order, codes, f_ref, trace_ref, near_ref, far_ref, axial_ref):
    row, place = places_of()
    even = lax.rem(row, 2) == 0
    for s in range(count):
        for first, lanes in HALF_PIECES:
            got = []
            for side in range(2):
                here = side * HALF + first
                narrow = nodes_of(f_ref, s * PLANE + here, lanes).astype(BF16)
                got.append(dot(trace_ref[side, place], narrow))
                axial_ref[s, :, here : here + lanes] = got[side][LOCAL_Z : LOCAL_Z + NODES]
            left, right = got[0][0:LOCAL_Z], got[1][0:LOCAL_Z]
            near_ref[s, :, first : first + lanes] = jnp.where(even, right, left)
            far_ref[s, :, first : first + lanes] = jnp.where(even, left, right)


def moment_kernel(
    count, order, codes, f_ref, left_ref, rows_ref, mirror_ref, mom_ref, turned_ref, sums_ref, table_ref
):
    step = pl.program_id(0)
    row, place = places_of()

    @pl.when(step == 0)
    def _():
        clear_sums(sums_ref)

    turn_traces(count, row, mirror_ref, left_ref, turned_ref)
    speeds = [slot_speed(order, step * count + s) for s in range(count)]
    for j in range(0, PLANE, 128):
        at = pl.ds(j, 128)
        for r in range(NODES):
            sums = [sums_ref[k, r, :, at] for k in range(5)]
            for s in range(count):
                sums = add_speed_sums(f_ref[r, :, pl.ds(s * PLANE + j, 128)], speeds[s], sums)
            for k in range(5):
                sums_ref[k, r, :, at] = sums[k]

    @pl.when(step == pl.num_programs(0) - 1)
    def _():
        finish_moments(sums_ref, rows_ref, table_ref, mom_ref)


def total_of(parts):
    while len(parts) > 1:
        parts = [parts[k] + parts[k + 1] for k in range(0, len(parts), 2)]
    return parts[0]


def edge_sums(total, edge_ref):
    net, gross = total[3:4, :], total[13:14, :]
    down, up = 0.5 * (gross - net), 0.5 * (gross + net)
    pairs = ((0, down), (1, up), (1, down))
    return tuple(jnp.sum(edge_ref[k] * row, axis=1, keepdims=True) for k, row in pairs)


def prepare_nodes(total, codes, place, rows_ref, edge_ref, table_ref, node_ref, wall_ref, plane_ref):
    rho, ur, ut, uz, temp, qr, qt, qz = macroscopic_of(lambda k: total[k : k + 1, :])
    inv_t = 1.0 / temp
    beta = ((1.0 - VISCOUS_RATIO) / 5.0) / (rho * temp * temp)
    kappa = rho * (TIME_STEP / KNUDSEN)
    peak = kappa * rho * inv_t * jnp.sqrt(inv_t)
    values = [uz, -0.5 * inv_t, qz * beta, inv_t, peak, 1.0 - kappa, ur, ut, qr * beta, qt * beta]
    clear_sums(table_ref)
    for k, value in enumerate(values):
        table_ref[k : k + 1, :] = value
    table_ref[...] = jnp.transpose(table_ref[...])
    for k in range(len(values)):
        node_ref[k] = jnp.broadcast_to(table_ref[:, k : k + 1], (NODE_COUNT, 128))
    incident, upward, downward = edge_sums(total, edge_ref)
    bottom = jnp.where(codes[0, BOTTOM] == 1, SAT_DENSITY, incident * (1.0 / HALF_FLUX))
    top = jnp.where(codes[0, TOP] == 2, 0.0, upward * (1.0 / HALF_FLUX))
    wall_ref[...] = jnp.broadcast_to(jnp.where(place == 0, bottom, top), (NODES, 128))

    def one_radius(r, carry):
        rows = pl.ds(pl.multiple_of(r * LOCAL_Z, LOCAL_Z), LOCAL_Z)
        n_half, n_inv = node_ref[1, rows, :], node_ref[3, rows, :]
        n_ur, n_ut = node_ref[6, rows, :], node_ref[7, rows, :]
        n_qr, n_qt = node_ref[8, rows, :], node_ref[9, rows, :]
        for j in range(PLANE // 128):
            at = pl.ds(j * 128, 128)
            cr = rows_ref[0:1, at] - n_ur
            ct = rows_ref[1:2, at] - n_ut
            square = cr * cr + ct * ct
            gauss = jnp.exp(square * n_half)
            along = cr * n_qr + ct * n_qt
            plane_ref[0, rows, at] = gauss
            plane_ref[1, rows, at] = along
            plane_ref[2, rows, at] = square * n_inv
        return carry

    lax.fori_loop(0, NODES, one_radius, 0)


def slot_factors(vz, node_ref):
    cz = vz - node_ref[0]
    square = cz * cz
    return node_ref[4] * jnp.exp(square * node_ref[1]), cz * node_ref[2], square * node_ref[3] - 5.0


def ghost_rows(
    s, vz, row, place, in_axial_ref, in_near_ref, in_turned_ref, in_far_ref, rows_ref, wall_ref, radial_ref, axial_ref
):
    own = (place == 0) == (vz > 0)
    even = lax.rem(row, 2) == 0
    strength = jnp.exp(-0.5 * vz * vz + jnp.zeros((NODES, 128), F32)) * wall_ref[...]
    for j in range(PLANE // 128):
        at = pl.ds(j * 128, 128)
        if j * 128 < HALF:
            radial = jnp.where(even, in_near_ref[s, :, at], in_far_ref[s, :, at])
        else:
            back = pl.ds(j * 128 - HALF, 128)
            radial = jnp.where(even, in_far_ref[s, :, back], in_near_ref[s, :, back]) + in_turned_ref[s, :, back]
        radial_ref[s, :, at] = rows_ref[0:1, at] * radial
        axial = jnp.where(own, strength * rows_ref[2:3, at], in_axial_ref[s, :, at])
        for r in range(NODES):
            axial_ref[s, r, :, at] = jnp.broadcast_to(axial[r : r + 1], (NODES, 128))


def outer_kernel(count, part_count, last, order, codes, *refs):
    part_refs, refs = refs[:part_count], refs[part_count:]
    f_ref, in_axial_ref, in_near_ref, in_turned_ref, in_far_ref = refs[:5]
    rows_ref, edge_ref, ghost_r_ref, ghost_z_ref, pos_ref, radial_m_ref, axial_m_ref, rot_ref, out_ref = refs[5:14]
    refs = refs[14:]
    if last:
        (mom_ref, sums_ref), refs = refs[:2], refs[2:]
    plane_ref, node_ref, wall_ref, slot_ref, lean_ref, radial_ref, axial_ref, table_ref = refs[:8]
    inverse_ref, pad_ref, lhs_ref, work_ref = refs[8:]
    step = pl.program_id(0)
    row, place = places_of()

    @pl.when(step == 0)
    def _():
        if last:
            clear_sums(sums_ref)
        total = total_of([p[...] for p in part_refs])
        prepare_nodes(total, codes, place, rows_ref, edge_ref, table_ref, node_ref, wall_ref, plane_ref)
        pad_ref[:, :, 0:128] = jnp.zeros((count, NODE_COUNT, 128), BF16)
        pad_ref[:, :, 128 + PLANE :] = jnp.zeros((count, NODE_COUNT, 128), BF16)
        inverse_ref[...] = 1.0 / (ELEMENT_WIDTH * (row.astype(F32) + pos_ref[...]))
        minus = radial_m_ref[jnp.where(row == lax.axis_size("row") - 1, 2, 0)]
        for s in range(count):
            lhs_ref[s, 0, :, 0:NODE_COUNT] = minus
            lhs_ref[s, 1, :, 0:NODE_COUNT] = radial_m_ref[1]

    speeds = [slot_speed(order, step * count + s) for s in range(count)]
    for s in range(count):
        vz = speeds[s]
        for k, value in enumerate(slot_factors(vz, node_ref)):
            slot_ref[s, k] = value
        lean_ref[s] = jnp.abs(vz) * ghost_z_ref[jnp.where(vz > 0, 1, 0)]
        ghost_rows(
            s, vz, row, place, in_axial_ref, in_near_ref, in_turned_ref, in_far_ref, rows_ref, wall_ref,
            radial_ref, axial_ref,
        )

    kind_out = jnp.where(jnp.logical_and(place == 1, codes[0, TOP] == 2), 2, 0)
    inverse = inverse_ref[...]
    for s in range(count):
        axial = (speeds[s] * axial_m_ref[jnp.where(speeds[s] > 0, 1, kind_out)]).astype(BF16)
        lhs_ref[s, 0, :, NODE_COUNT:] = axial
        lhs_ref[s, 1, :, NODE_COUNT:] = axial
        for j in range(PLANE // 128):
            field = nodes_of(f_ref, s * PLANE + j * 128, 128)
            pad_ref[s, :, 128 + j * 128 : 256 + j * 128] = (field * inverse).astype(BF16)

    for tile in range(PLANE // TILE):
        start = tile * TILE
        turned = dot(pad_ref[:, :, start : start + WINDOW].reshape(count * NODE_COUNT, WINDOW), rot_ref[tile])
        for first, lanes, side in PIECES:
            if first // TILE != tile:
                continue
            vr = rows_ref[0:1, first : first + lanes]
            inside = first - start
            for s in range(count):
                field = nodes_of(f_ref, s * PLANE + first, lanes)
                both = jnp.concatenate([(field * vr).astype(BF16), field.astype(BF16)], axis=0)
                change = turned[s * NODE_COUNT : (s + 1) * NODE_COUNT, inside : inside + lanes]
                work_ref[s, :, first : first + lanes] = change + dot(lhs_ref[s, side], both)

    def update(r, carry):
        rows = pl.ds(pl.multiple_of(r * LOCAL_Z, LOCAL_Z), LOCAL_Z)
        keep = node_ref[5, rows, :]
        lifts = [ghost_r_ref[side, rows, :] for side in range(2)]
        factor = [[slot_ref[s, k, rows, :] for k in range(3)] for s in range(count)]
        lean = [lean_ref[s] for s in range(count)]
        for j in range(PLANE // 128):
            at = pl.ds(j * 128, 128)
            gauss, along, reach = (plane_ref[k, rows, at] for k in range(3))
            if last:
                sums = [sums_ref[k, r, :, at] for k in range(5)]
            for s in range(count):
                here = pl.ds(s * PLANE + j * 128, 128)
                across = axial_ref[s, r, :, at]
                new = f_ref[r, :, here] * keep + work_ref[s, rows, at]
                new = new + radial_ref[s, :, at] * lifts[1 if j * 128 >= HALF else 0]
                new = new + jnp.concatenate([across, across], axis=0) * lean[s]
                bend = (along + factor[s][1]) * (reach + factor[s][2]) + 1.0
                new = new + (gauss * factor[s][0]) * bend
                out_ref[r, :, here] = new
                if last:
                    sums = add_speed_sums(new, speeds[s], sums)
            if last:
                for k in range(5):
                    sums_ref[k, r, :, at] = sums[k]
        return carry

    lax.fori_loop(0, NODES, update, 0)
    if last:

        @pl.when(step == pl.num_programs(0) - 1)
        def _():
            finish_moments(sums_ref, rows_ref, table_ref, mom_ref)


def last_kernel(part_count, codes, *refs):
    total_ref = total_of([p[...] for p in refs[:part_count]])
    edge_ref, macro_ref, flux_ref = refs[part_count:]
    row, place = places_of()
    values = macroscopic_of(lambda k: total_ref[k : k + 1, :])
    for k in range(8):
        for r in range(NODES):
            macro_ref[k, r : r + 1, :] = values[k][:, r * LOCAL_Z : (r + 1) * LOCAL_Z]
    incident, upward, downward = edge_sums(total_ref, edge_ref)
    bottom = jnp.where(codes[0, BOTTOM] == 1, SAT_DENSITY * HALF_FLUX - incident, 0.0)
    top = jnp.where(codes[0, TOP] == 2, upward - downward, 0.0)
    square = jnp.broadcast_to(jnp.where(place == 0, bottom, top), (NODES, 128))
    same = lax.broadcasted_iota(jnp.int32, (NODES, 128), 0) == lax.broadcasted_iota(jnp.int32, (NODES, 128), 1)
    flux_ref[...] = jnp.sum(jnp.where(same, square, 0.0), axis=0, keepdims=True)[:, 0:NODES]


def whole(shape):
    return pl.BlockSpec(shape, lambda *a: (0,) * len(shape), pipeline_mode=pl.Buffered(1))


def on_device(distribution, z_order, edge_codes):
    local_r, local_z, vdev = distribution.shape
    assert local_r == NODES and local_z == LOCAL_Z
    slots = vdev // PLANE
    group = math.gcd(slots, 3)
    rows_total = lax.axis_size("row")
    verts = lax.axis_size("vert")
    assert lax.axis_size("gz") == 2 and rows_total % 2 == 0
    codes = edge_codes.T
    fixed = lambda x: pltpu.with_memory_space_constraint(jnp.asarray(x), pltpu.HBM)
    codes, z_order = fixed(codes), fixed(z_order)
    rows, pos, edge = fixed(ROWS), fixed(NODE_POS), fixed(EDGE)
    radial_m, axial_m = fixed(RADIAL_M), fixed(AXIAL_M)
    ghost_r, ghost_z = fixed(GHOST_R), fixed(GHOST_Z)
    trace_m, mirror_m, rot_m = fixed(TRACE_M), fixed(MIRROR_M), jnp.asarray(ROTATION_M)

    def slab(count):
        return pl.BlockSpec((NODES, LOCAL_Z, count * PLANE), lambda i, *n: (0, 0, i))

    def radial_spec(count):
        return pl.BlockSpec((count, LOCAL_Z, HALF), lambda i, *n: (i, 0, 0))

    def axial_spec(count):
        return pl.BlockSpec((count, NODES, PLANE), lambda i, *n: (i, 0, 0))

    def trace_specs(count):
        return [radial_spec(count), radial_spec(count), radial_spec(count), axial_spec(count)]

    mom_spec = whole((MOMENTS, 128))
    radial_shape = jax.ShapeDtypeStruct((slots, LOCAL_Z, HALF), F32)
    axial_shape = jax.ShapeDtypeStruct((slots, NODES, PLANE), F32)
    mom_shape = jax.ShapeDtypeStruct((MOMENTS, 128), F32)
    big_shape = jax.ShapeDtypeStruct(distribution.shape, F32)
    trace_shapes = [radial_shape, radial_shape, radial_shape, axial_shape]
    square = pltpu.VMEM((NODE_COUNT, 128), F32)

    def call(body, name, count, limit, in_specs, out_specs, out_shape, scratch, args):
        return pl.pallas_call(
            body,
            grid_spec=pltpu.PrefetchScalarGridSpec(
                num_scalar_prefetch=2,
                grid=(slots // count,),
                in_specs=in_specs,
                out_specs=out_specs,
                scratch_shapes=scratch,
            ),
            out_shape=out_shape,
            compiler_params=pltpu.CompilerParams(vmem_limit_bytes=limit * 1024 * 1024),
            name=name,
        )(z_order, codes, *args)

    def all_whole(tables):
        return [whole(x.shape) for x in tables]

    def traces_of(f):
        return call(
            lambda *a: trace_kernel(group, *a), "traces", group, 20, [slab(group)] + all_whole([trace_m]),
            [radial_spec(group), radial_spec(group), axial_spec(group)], [radial_shape, radial_shape, axial_shape],
            [], [f, trace_m],
        )

    def moments_of(f, left):
        return call(
            lambda *a: moment_kernel(group, *a), "moments", group, 20,
            [slab(group), radial_spec(group)] + all_whole([rows, mirror_m]),
            [mom_spec, radial_spec(group)], [mom_shape, radial_shape],
            [pltpu.VMEM((5, NODES, LOCAL_Z, PLANE), F32), square], [f, left, rows, mirror_m],
        )

    def outer(f, ghosts, parts, last):
        count = math.gcd(slots, 2)
        if last:
            f = pltpu.with_memory_space_constraint(f, pltpu.HBM)
        tables = [rows, edge, ghost_r, ghost_z, pos, radial_m, axial_m, rot_m]
        scratch = [
            pltpu.VMEM((3, NODE_COUNT, PLANE), F32),
            pltpu.VMEM((10, NODE_COUNT, 128), F32),
            pltpu.VMEM((NODES, 128), F32),
            pltpu.VMEM((count, 3, NODE_COUNT, 128), F32),
            pltpu.VMEM((count, LOCAL_Z, 128), F32),
            pltpu.VMEM((count, LOCAL_Z, PLANE), F32),
            pltpu.VMEM((count, NODES, NODES, PLANE), F32),
            square,
            square,
            pltpu.VMEM((count, NODE_COUNT, PLANE + 256), BF16),
            pltpu.VMEM((count, 2, NODE_COUNT, 2 * NODE_COUNT), BF16),
            pltpu.VMEM((count, NODE_COUNT, PLANE), F32),
        ]
        return call(
            lambda *a: outer_kernel(count, len(parts), last, *a), "last_update" if last else "update", count, 32 if last else 26,
            [mom_spec] * len(parts) + [slab(count), axial_spec(count)] + [radial_spec(count)] * 3
            + all_whole(tables),
            [slab(count)] + ([mom_spec] if last else []), [big_shape] + ([mom_shape] if last else []),
            ([pltpu.VMEM((5, NODES, LOCAL_Z, PLANE), F32)] if last else []) + scratch,
            [*parts, f, *ghosts, *tables],
        )

    def spread(moments):
        parts = [moments]
        for shift in range(1, verts):
            parts.append(lax.ppermute(moments, "vert", [(i, i ^ shift) for i in range(verts)]))
        return parts

    def halo(near, far, axial):
        from_axial = lax.ppermute(axial, "gz", [(0, 1), (1, 0)])
        pairs = [(i, i ^ 1) for i in range(rows_total)]
        from_near = lax.ppermute(near, "row", pairs)
        between = [(i, i + 1) for i in range(1, rows_total - 1, 2)]
        from_far = lax.ppermute(far, "row", between + [(b, a) for a, b in between])
        return from_axial, from_near, from_far

    current = distribution
    for number in range(STEPS):
        last = number == STEPS - 1
        traces = traces_of(current)
        from_axial, from_near, from_far = halo(*traces)
        moments, turned = moments_of(current, traces[1])
        parts = spread(moments)
        ghosts = [from_axial, from_near, turned, from_far]
        current, *final = outer(current, ghosts, parts, last)
    parts = spread(final[0])
    macro, flux = pl.pallas_call(
        lambda *a: last_kernel(len(parts), *a),
        grid_spec=pltpu.PrefetchScalarGridSpec(
            num_scalar_prefetch=1,
            grid=(1,),
            in_specs=[mom_spec] * len(parts) + [whole(edge.shape)],
            out_specs=[whole((8, NODES, LOCAL_Z)), whole((1, NODES))],
        ),
        out_shape=[
            jax.ShapeDtypeStruct((8, NODES, LOCAL_Z), F32),
            jax.ShapeDtypeStruct((1, NODES), F32),
        ],
        compiler_params=pltpu.CompilerParams(vmem_limit_bytes=4 * 1024 * 1024),
        name="macroscopic",
    )(codes, *parts, edge)
    return (current, macro, flux)


def solution(mesh):
    in_specs = (P("row", "gz", "vert"), P("vert"), P(None, "row"))
    out_specs = (P("row", "gz", "vert"), P(None, "row", "gz"), P("gz", "row"))
    return jax.shard_map(
        on_device, mesh=mesh, in_specs=in_specs, out_specs=out_specs, check_vma=False
    )
```

```python
import math

import jax
import jax.numpy as jnp
import ml_dtypes
import numpy as np
from jax import lax
from jax.experimental import pallas as pl
from jax.experimental.pallas import tpu as pltpu
from jax.sharding import PartitionSpec as P

NODES = 8
NVR = 48
NVT = 48
NVZ = 48
STEPS = 2

ELEMENT_WIDTH = 4.0
TIME_STEP = 0.001
KNUDSEN = 0.005
VISCOUS_RATIO = 2.0 / 3.0
SAT_DENSITY = 1.5
SPEED_LIMIT = 5.0

PLANE = NVR * NVT
HALF = PLANE // 2
THIRD = HALF // 3
BOTTOM, TOP = 0, 1
LOCAL_Z = 2 * NODES
NODE_COUNT = NODES * LOCAL_Z
TILE = 256
WINDOW = 512
GHOST_ROWS = 32
MOMENTS = 16
F32 = jnp.float32
BF16 = jnp.bfloat16
PIECES = [(t, TILE, 0) for t in range(0, 1024, TILE)] + [(1024, 128, 0), (1152, 128, 1)] + [
    (t, TILE, 1) for t in range(1280, PLANE, TILE)
]
HALF_PIECES = [(t, TILE) for t in range(0, 1024, TILE)] + [(1024, 128)]


def legendre_pair(position, point_count):
    previous = 1.0
    current = position
    for degree in range(2, point_count + 1):
        previous, current = (
            current,
            ((2 * degree - 1) * position * current - (degree - 1) * previous) / degree,
        )
    slope = point_count * (position * current - previous) / (position * position - 1.0)
    return (current, slope)


def dg_tables(point_count):
    point_list = []
    weight_list = []
    for number in range(point_count):
        position = math.cos(math.pi * (number + 0.75) / (point_count + 0.5))
        for sweep in range(60):
            value, slope = legendre_pair(position, point_count)
            position = position - value / slope
        value, slope = legendre_pair(position, point_count)
        point_list.append(position)
        weight_list.append(2.0 / ((1.0 - position * position) * slope * slope))
    point_list = point_list[::-1]
    weight_list = weight_list[::-1]
    points = np.array(point_list)
    derivative = np.zeros((point_count, point_count))
    right = np.zeros(point_count)
    left = np.zeros(point_count)
    products = [
        np.prod([points[i] - points[j] for j in range(point_count) if j != i])
        for i in range(point_count)
    ]
    for i in range(point_count):
        others = [j for j in range(point_count) if j != i]
        derivative[i, i] = sum(1.0 / (points[i] - points[j]) for j in others)
        for j in others:
            derivative[i, j] = products[i] / products[j] / (points[i] - points[j])
        right[i] = np.prod([1.0 - points[j] for j in others]) / products[i]
        left[i] = np.prod([-1.0 - points[j] for j in others]) / products[i]
    return points, np.array(weight_list), derivative, right, left


def speed_grid(point_count):
    return -SPEED_LIMIT + (np.arange(point_count) + 0.5) * (2.0 * SPEED_LIMIT / point_count)


POINTS, QUAD, DERIV, END_R, END_L = dg_tables(NODES)
LIFT_R = END_R / QUAD
LIFT_L = END_L / QUAD
GRID_R = speed_grid(NVR)
GRID_T = speed_grid(NVT)
GRID_Z = speed_grid(NVZ)
STEP_V = 2 * SPEED_LIMIT / NVR
WEIGHT = STEP_V**3 / (2 * math.pi) ** 1.5
HALF_FLUX = float(
    WEIGHT
    * np.sum(np.exp(-(GRID_R**2) / 2))
    * np.sum(np.exp(-(GRID_T**2) / 2))
    * np.sum(np.maximum(GRID_Z, 0.0) * np.exp(-(GRID_Z**2) / 2))
)
SCALE = TIME_STEP * 2.0 / ELEMENT_WIDTH


def transport_tables():
    ident = np.eye(NODES)
    up = DERIV + np.outer(LIFT_L, END_L)
    down = DERIV - np.outer(LIFT_R, END_R)
    zero = np.zeros((NODES, NODES))
    wide = np.eye(LOCAL_Z)
    radial = np.stack([np.kron(down, wide), np.kron(up, wide), np.kron(DERIV, wide)])
    zup = np.block([[up, zero], [-np.outer(LIFT_L, END_R), up]])
    zdown = np.block([[down, np.outer(LIFT_R, END_L)], [zero, down]])
    zout = np.block([[down, np.outer(LIFT_R, END_L)], [zero, DERIV]])
    axial = np.stack([np.kron(ident, zdown), np.kron(ident, zup), np.kron(ident, zout)])
    ghost_r = np.zeros((2, NODE_COUNT, 128))
    ghost_z = np.zeros((2, NODE_COUNT, 128))
    for r in range(NODES):
        for z in range(LOCAL_Z):
            n = r * LOCAL_Z + z
            ghost_r[0, n, z] = -LIFT_R[r]
            ghost_r[1, n, z] = LIFT_L[r]
            if z >= NODES:
                ghost_z[0, n, LOCAL_Z + r] = LIFT_R[z - NODES]
            else:
                ghost_z[1, n, LOCAL_Z + r] = LIFT_L[z]
    trace = np.zeros((2, 2, GHOST_ROWS, NODE_COUNT))
    for side in range(2):
        radial_row = END_R if side == 1 else END_L
        for place in range(2):
            for z in range(LOCAL_Z):
                for r in range(NODES):
                    trace[side, place, z, r * LOCAL_Z + z] = radial_row[r]
            for r in range(NODES):
                for k in range(NODES):
                    if place == 0:
                        trace[side, place, LOCAL_Z + r, r * LOCAL_Z + NODES + k] = END_R[k]
                    else:
                        trace[side, place, LOCAL_Z + r, r * LOCAL_Z + k] = END_L[k]
    return (
        (-SCALE * radial).astype(ml_dtypes.bfloat16),
        (-SCALE * axial).astype(np.float32),
        (SCALE * ghost_r).astype(np.float32),
        (SCALE * ghost_z).astype(np.float32),
        trace.astype(ml_dtypes.bfloat16),
    )


def rotation_table():
    full = np.zeros((PLANE + 2 * TILE, PLANE))
    factor = TIME_STEP / (2 * STEP_V)
    for a in range(NVR):
        for b in range(NVT):
            n = a * NVT + b
            first = factor * GRID_T[b] * GRID_T[b]
            second = factor * GRID_R[a] * GRID_T[b]
            if a + 1 < NVR:
                full[TILE + n + NVT, n] = -first
            if a > 0:
                full[TILE + n - NVT, n] = first
            if b + 1 < NVT:
                full[TILE + n + 1, n] = second
            if b > 0:
                full[TILE + n - 1, n] = -second
    tiles = [full[TILE + t - 128 : TILE + t - 128 + WINDOW, t : t + TILE] for t in range(0, PLANE, TILE)]
    return np.stack(tiles).astype(ml_dtypes.bfloat16)


def mirror_table():
    table = np.zeros((THIRD, THIRD))
    groups = THIRD // NVT
    for g in range(groups):
        for b in range(NVT):
            table[(groups - 1 - g) * NVT + b, g * NVT + b] = 1.0
    return table.astype(ml_dtypes.bfloat16)


def plane_rows():
    vr = np.repeat(GRID_R, NVT)
    vt = np.tile(GRID_T, NVR)
    rows = np.zeros((8, PLANE))
    rows[0] = vr
    rows[1] = vt
    rows[2] = np.exp(-(vr**2 + vt**2) / 2)
    return rows.astype(np.float32)


def edge_table():
    table = np.zeros((2, NODES, NODE_COUNT))
    for r in range(NODES):
        for k in range(NODES):
            table[0, r, r * LOCAL_Z + k] = END_L[k]
            table[1, r, r * LOCAL_Z + NODES + k] = END_R[k]
    return table.astype(np.float32)


def node_columns():
    table = np.zeros((NODE_COUNT, 128))
    for r in range(NODES):
        table[r * LOCAL_Z : (r + 1) * LOCAL_Z, :] = (1.0 + POINTS[r]) / 2
    return table.astype(np.float32)


RADIAL_M, AXIAL_M, GHOST_R, GHOST_Z, TRACE_M = transport_tables()
ROTATION_M = rotation_table()
MIRROR_M = mirror_table()
ROWS = plane_rows()
EDGE = edge_table()
NODE_POS = node_columns()


def slot_speed(order, slot):
    return (order[slot].astype(F32) + 0.5) * (2 * SPEED_LIMIT / NVZ) - SPEED_LIMIT


def dot(x, y):
    return jnp.dot(x, y, preferred_element_type=F32)


def macroscopic_of(m):
    rho = m(0)
    inv = 1.0 / rho
    ur, ut, uz = m(1) * inv, m(2) * inv, m(3) * inv
    rr, tt, rt, zz, rz, tz = (m(k) for k in range(4, 10))
    energy = rr + tt + zz
    speed = ur * ur + ut * ut + uz * uz
    temp = (energy * inv - speed) * (1.0 / 3.0)
    tail = 2.0 * rho * speed - energy
    qr = 0.5 * (m(10) - 2.0 * (ur * rr + ut * rt + uz * rz) + ur * tail)
    qt = 0.5 * (m(11) - 2.0 * (ur * rt + ut * tt + uz * tz) + ut * tail)
    qz = 0.5 * (m(12) - 2.0 * (ur * rz + ut * tz + uz * zz) + uz * tail)
    return rho, ur, ut, uz, temp, qr, qt, qz


def add_speed_sums(field, vz, sums):
    one = field * vz
    two = one * vz
    return [
        sums[0] + field,
        sums[1] + one,
        sums[2] + two,
        sums[3] + two * vz,
        sums[4] + field * jnp.abs(vz),
    ]


def finish_moments(sums_ref, rows_ref, table_ref, out_ref):
    lane = lax.broadcasted_iota(jnp.int32, (LOCAL_Z, 128), 1)

    def one_radius(r, carry):
        acc = [jnp.zeros((LOCAL_Z, 128), F32) for _ in range(14)]
        for j in range(PLANE // 128):
            at = pl.ds(j * 128, 128)
            vr = rows_ref[0:1, at]
            vt = rows_ref[1:2, at]
            g0, g1, g2, g3, g4 = (sums_ref[k, r, :, at] for k in range(5))
            a = vr * g0
            b = vt * g0
            aa = vr * a
            bb = vt * b
            c = vr * g1
            d = vt * g1
            perp = aa + bb + g2
            new = [g0, a, b, g1, aa, bb, vr * b, g2, c, d, vr * perp, vt * perp, vr * c + vt * d + g3, g4]
            acc = [x + y for x, y in zip(acc, new)]
        block = jnp.zeros((LOCAL_Z, 128), F32)
        for k in range(14):
            block = jnp.where(lane == k, WEIGHT * jnp.sum(acc[k], axis=1, keepdims=True), block)
        table_ref[pl.ds(pl.multiple_of(r * LOCAL_Z, LOCAL_Z), LOCAL_Z), :] = block
        return carry

    lax.fori_loop(0, NODES, one_radius, 0)
    out_ref[...] = jnp.transpose(table_ref[...])[0:MOMENTS, :]


def clear_sums(sums_ref):
    sums_ref[...] = jnp.zeros(sums_ref.shape, F32)


def places_of():
    return lax.axis_index("row"), lax.axis_index("gz")


def turn_traces(count, row, mirror_ref, left_ref, turned_ref):
    @pl.when(row == 0)
    def _():
        for part in range(3):
            start = (2 - part) * THIRD
            flat = left_ref[:, :, start : start + THIRD].reshape(count * LOCAL_Z, THIRD).astype(BF16)
            got = dot(flat, mirror_ref[...])
            turned_ref[:, :, part * THIRD : (part + 1) * THIRD] = got.reshape(count, LOCAL_Z, THIRD)

    @pl.when(row != 0)
    def _():
        turned_ref[...] = jnp.zeros(turned_ref.shape, F32)


def nodes_of(ref, first, lanes):
    return ref[:, :, first : first + lanes].reshape(NODE_COUNT, lanes)


def trace_kernel(count, order, codes, f_ref, trace_ref, near_ref, far_ref, axial_ref):
    row, place = places_of()
    even = lax.rem(row, 2) == 0
    for s in range(count):
        for first, lanes in HALF_PIECES:
            got = []
            for side in range(2):
                here = side * HALF + first
                narrow = nodes_of(f_ref, s * PLANE + here, lanes).astype(BF16)
                got.append(dot(trace_ref[side, place], narrow))
                axial_ref[s, :, here : here + lanes] = got[side][LOCAL_Z : LOCAL_Z + NODES]
            left, right = got[0][0:LOCAL_Z], got[1][0:LOCAL_Z]
            near_ref[s, :, first : first + lanes] = jnp.where(even, right, left)
            far_ref[s, :, first : first + lanes] = jnp.where(even, left, right)


def moment_kernel(
    count, order, codes, f_ref, left_ref, rows_ref, mirror_ref, mom_ref, turned_ref, sums_ref, table_ref
):
    step = pl.program_id(0)
    row, place = places_of()

    @pl.when(step == 0)
    def _():
        clear_sums(sums_ref)

    turn_traces(count, row, mirror_ref, left_ref, turned_ref)
    speeds = [slot_speed(order, step * count + s) for s in range(count)]
    for j in range(0, PLANE, 128):
        at = pl.ds(j, 128)
        for r in range(NODES):
            sums = [sums_ref[k, r, :, at] for k in range(5)]
            for s in range(count):
                sums = add_speed_sums(f_ref[r, :, pl.ds(s * PLANE + j, 128)], speeds[s], sums)
            for k in range(5):
                sums_ref[k, r, :, at] = sums[k]

    @pl.when(step == pl.num_programs(0) - 1)
    def _():
        finish_moments(sums_ref, rows_ref, table_ref, mom_ref)


def total_of(parts):
    while len(parts) > 1:
        parts = [parts[k] + parts[k + 1] for k in range(0, len(parts), 2)]
    return parts[0]


def edge_sums(total, edge_ref):
    net, gross = total[3:4, :], total[13:14, :]
    down, up = 0.5 * (gross - net), 0.5 * (gross + net)
    pairs = ((0, down), (1, up), (1, down))
    return tuple(jnp.sum(edge_ref[k] * row, axis=1, keepdims=True) for k, row in pairs)


def prepare_nodes(total, codes, place, rows_ref, edge_ref, table_ref, node_ref, wall_ref, plane_ref):
    rho, ur, ut, uz, temp, qr, qt, qz = macroscopic_of(lambda k: total[k : k + 1, :])
    inv_t = 1.0 / temp
    beta = ((1.0 - VISCOUS_RATIO) / 5.0) / (rho * temp * temp)
    kappa = rho * (TIME_STEP / KNUDSEN)
    peak = kappa * rho * inv_t * jnp.sqrt(inv_t)
    values = [uz, -0.5 * inv_t, qz * beta, inv_t, peak, 1.0 - kappa, ur, ut, qr * beta, qt * beta]
    clear_sums(table_ref)
    for k, value in enumerate(values):
        table_ref[k : k + 1, :] = value
    table_ref[...] = jnp.transpose(table_ref[...])
    for k in range(len(values)):
        node_ref[k] = jnp.broadcast_to(table_ref[:, k : k + 1], (NODE_COUNT, 128))
    incident, upward, downward = edge_sums(total, edge_ref)
    bottom = jnp.where(codes[0, BOTTOM] == 1, SAT_DENSITY, incident * (1.0 / HALF_FLUX))
    top = jnp.where(codes[0, TOP] == 2, 0.0, upward * (1.0 / HALF_FLUX))
    wall_ref[...] = jnp.broadcast_to(jnp.where(place == 0, bottom, top), (NODES, 128))

    def one_radius(r, carry):
        rows = pl.ds(pl.multiple_of(r * LOCAL_Z, LOCAL_Z), LOCAL_Z)
        n_half, n_inv = node_ref[1, rows, :], node_ref[3, rows, :]
        n_ur, n_ut = node_ref[6, rows, :], node_ref[7, rows, :]
        n_qr, n_qt = node_ref[8, rows, :], node_ref[9, rows, :]
        for j in range(PLANE // 128):
            at = pl.ds(j * 128, 128)
            cr = rows_ref[0:1, at] - n_ur
            ct = rows_ref[1:2, at] - n_ut
            square = cr * cr + ct * ct
            gauss = jnp.exp(square * n_half)
            along = cr * n_qr + ct * n_qt
            plane_ref[0, rows, at] = gauss
            plane_ref[1, rows, at] = along
            plane_ref[2, rows, at] = square * n_inv
        return carry

    lax.fori_loop(0, NODES, one_radius, 0)


def slot_factors(vz, node_ref):
    cz = vz - node_ref[0]
    square = cz * cz
    return node_ref[4] * jnp.exp(square * node_ref[1]), cz * node_ref[2], square * node_ref[3] - 5.0


def ghost_rows(
    s, vz, row, place, in_axial_ref, in_near_ref, in_turned_ref, in_far_ref, rows_ref, wall_ref, ghost_ref
):
    own = (place == 0) == (vz > 0)
    even = lax.rem(row, 2) == 0
    strength = jnp.exp(-0.5 * vz * vz + jnp.zeros((NODES, 128), F32)) * wall_ref[...]
    for j in range(PLANE // 128):
        at = pl.ds(j * 128, 128)
        if j * 128 < HALF:
            radial = jnp.where(even, in_near_ref[s, :, at], in_far_ref[s, :, at])
        else:
            back = pl.ds(j * 128 - HALF, 128)
            radial = jnp.where(even, in_far_ref[s, :, back], in_near_ref[s, :, back]) + in_turned_ref[s, :, back]
        axial = jnp.where(own, strength * rows_ref[2:3, at], in_axial_ref[s, :, at])
        rows = jnp.concatenate([rows_ref[0:1, at] * radial, axial, jnp.zeros((8, 128), F32)], axis=0)
        ghost_ref[s * GHOST_ROWS : (s + 1) * GHOST_ROWS, at] = rows.astype(BF16)


def outer_kernel(count, part_count, last, order, codes, *refs):
    part_refs, refs = refs[:part_count], refs[part_count:]
    f_ref, in_axial_ref, in_near_ref, in_turned_ref, in_far_ref = refs[:5]
    rows_ref, edge_ref, ghost_r_ref, ghost_z_ref, pos_ref, radial_m_ref, axial_m_ref, rot_ref, out_ref = refs[5:14]
    refs = refs[14:]
    if last:
        (mom_ref, sums_ref), refs = refs[:2], refs[2:]
    plane_ref, node_ref, wall_ref, slot_ref, lift_ref, ghost_ref, table_ref = refs[:7]
    inverse_ref, pad_ref, lhs_ref, work_ref = refs[7:]
    step = pl.program_id(0)
    row, place = places_of()

    @pl.when(step == 0)
    def _():
        if last:
            clear_sums(sums_ref)
        total = total_of([p[...] for p in part_refs])
        prepare_nodes(total, codes, place, rows_ref, edge_ref, table_ref, node_ref, wall_ref, plane_ref)
        pad_ref[:, :, 0:128] = jnp.zeros((count, NODE_COUNT, 128), BF16)
        pad_ref[:, :, 128 + PLANE :] = jnp.zeros((count, NODE_COUNT, 128), BF16)
        inverse_ref[...] = 1.0 / (ELEMENT_WIDTH * (row.astype(F32) + pos_ref[...]))
        minus = radial_m_ref[jnp.where(row == lax.axis_size("row") - 1, 2, 0)]
        for s in range(count):
            lhs_ref[s, 0, :, 0:NODE_COUNT] = minus
            lhs_ref[s, 1, :, 0:NODE_COUNT] = radial_m_ref[1]

    speeds = [slot_speed(order, step * count + s) for s in range(count)]
    for s in range(count):
        vz = speeds[s]
        for k, value in enumerate(slot_factors(vz, node_ref)):
            slot_ref[s, k] = value
        lean = jnp.abs(vz) * ghost_z_ref[jnp.where(vz > 0, 1, 0)]
        for side in range(2):
            lift = ghost_r_ref[side] + lean
            lift_ref[s, side] = (pltpu.roll(lift, s * GHOST_ROWS, 1) if s else lift).astype(BF16)
        ghost_rows(
            s, vz, row, place, in_axial_ref, in_near_ref, in_turned_ref, in_far_ref, rows_ref, wall_ref, ghost_ref
        )

    kind_out = jnp.where(jnp.logical_and(place == 1, codes[0, TOP] == 2), 2, 0)
    inverse = inverse_ref[...]
    for s in range(count):
        axial = (speeds[s] * axial_m_ref[jnp.where(speeds[s] > 0, 1, kind_out)]).astype(BF16)
        lhs_ref[s, 0, :, NODE_COUNT:] = axial
        lhs_ref[s, 1, :, NODE_COUNT:] = axial
        for j in range(PLANE // 128):
            field = nodes_of(f_ref, s * PLANE + j * 128, 128)
            pad_ref[s, :, 128 + j * 128 : 256 + j * 128] = (field * inverse).astype(BF16)

    held = count * GHOST_ROWS
    lane = lax.broadcasted_iota(jnp.int32, (count * NODE_COUNT, 128), 1)
    for first, lanes, side in PIECES:
        tile = first // TILE
        start = tile * TILE
        inside = first - start
        lifts = lift_ref[:, side].reshape(count * NODE_COUNT, 128)
        window = pad_ref[:, :, start : start + WINDOW].reshape(count * NODE_COUNT, WINDOW)
        window = jnp.concatenate([jnp.where(lane < held, lifts, window[:, 0:128]), window[:, 128:]], axis=1)
        turning = jnp.concatenate(
            [ghost_ref[:, first : first + lanes], rot_ref[tile, held:, inside : inside + lanes]], axis=0
        )
        turned = dot(window, turning)
        vr = rows_ref[0:1, first : first + lanes]
        for s in range(count):
            field = nodes_of(f_ref, s * PLANE + first, lanes)
            both = jnp.concatenate([(field * vr).astype(BF16), field.astype(BF16)], axis=0)
            work_ref[s, :, first : first + lanes] = turned[s * NODE_COUNT : (s + 1) * NODE_COUNT] + dot(
                lhs_ref[s, side], both
            )

    def update(r, carry):
        rows = pl.ds(pl.multiple_of(r * LOCAL_Z, LOCAL_Z), LOCAL_Z)
        keep = node_ref[5, rows, :]
        factor = [[slot_ref[s, k, rows, :] for k in range(3)] for s in range(count)]
        for j in range(PLANE // 128):
            at = pl.ds(j * 128, 128)
            gauss, along, reach = (plane_ref[k, rows, at] for k in range(3))
            if last:
                sums = [sums_ref[k, r, :, at] for k in range(5)]
            for s in range(count):
                here = pl.ds(s * PLANE + j * 128, 128)
                new = f_ref[r, :, here] * keep + work_ref[s, rows, at]
                bend = (along + factor[s][1]) * (reach + factor[s][2]) + 1.0
                new = new + (gauss * factor[s][0]) * bend
                out_ref[r, :, here] = new
                if last:
                    sums = add_speed_sums(new, speeds[s], sums)
            if last:
                for k in range(5):
                    sums_ref[k, r, :, at] = sums[k]
        return carry

    lax.fori_loop(0, NODES, update, 0)
    if last:

        @pl.when(step == pl.num_programs(0) - 1)
        def _():
            finish_moments(sums_ref, rows_ref, table_ref, mom_ref)


def last_kernel(part_count, codes, *refs):
    total_ref = total_of([p[...] for p in refs[:part_count]])
    edge_ref, macro_ref, flux_ref = refs[part_count:]
    row, place = places_of()
    values = macroscopic_of(lambda k: total_ref[k : k + 1, :])
    for k in range(8):
        for r in range(NODES):
            macro_ref[k, r : r + 1, :] = values[k][:, r * LOCAL_Z : (r + 1) * LOCAL_Z]
    incident, upward, downward = edge_sums(total_ref, edge_ref)
    bottom = jnp.where(codes[0, BOTTOM] == 1, SAT_DENSITY * HALF_FLUX - incident, 0.0)
    top = jnp.where(codes[0, TOP] == 2, upward - downward, 0.0)
    square = jnp.broadcast_to(jnp.where(place == 0, bottom, top), (NODES, 128))
    same = lax.broadcasted_iota(jnp.int32, (NODES, 128), 0) == lax.broadcasted_iota(jnp.int32, (NODES, 128), 1)
    flux_ref[...] = jnp.sum(jnp.where(same, square, 0.0), axis=0, keepdims=True)[:, 0:NODES]


def whole(shape):
    return pl.BlockSpec(shape, lambda *a: (0,) * len(shape), pipeline_mode=pl.Buffered(1))


def on_device(distribution, z_order, edge_codes):
    local_r, local_z, vdev = distribution.shape
    assert local_r == NODES and local_z == LOCAL_Z
    slots = vdev // PLANE
    group = math.gcd(slots, 3)
    rows_total = lax.axis_size("row")
    verts = lax.axis_size("vert")
    assert lax.axis_size("gz") == 2 and rows_total % 2 == 0
    codes = edge_codes.T
    fixed = lambda x: pltpu.with_memory_space_constraint(jnp.asarray(x), pltpu.HBM)
    codes, z_order = fixed(codes), fixed(z_order)
    rows, pos, edge = fixed(ROWS), fixed(NODE_POS), fixed(EDGE)
    radial_m, axial_m = fixed(RADIAL_M), fixed(AXIAL_M)
    ghost_r, ghost_z = fixed(GHOST_R), fixed(GHOST_Z)
    trace_m, mirror_m, rot_m = fixed(TRACE_M), fixed(MIRROR_M), jnp.asarray(ROTATION_M)

    def slab(count):
        return pl.BlockSpec((NODES, LOCAL_Z, count * PLANE), lambda i, *n: (0, 0, i))

    def radial_spec(count):
        return pl.BlockSpec((count, LOCAL_Z, HALF), lambda i, *n: (i, 0, 0))

    def axial_spec(count):
        return pl.BlockSpec((count, NODES, PLANE), lambda i, *n: (i, 0, 0))

    def trace_specs(count):
        return [radial_spec(count), radial_spec(count), radial_spec(count), axial_spec(count)]

    mom_spec = whole((MOMENTS, 128))
    radial_shape = jax.ShapeDtypeStruct((slots, LOCAL_Z, HALF), F32)
    axial_shape = jax.ShapeDtypeStruct((slots, NODES, PLANE), F32)
    mom_shape = jax.ShapeDtypeStruct((MOMENTS, 128), F32)
    big_shape = jax.ShapeDtypeStruct(distribution.shape, F32)
    trace_shapes = [radial_shape, radial_shape, radial_shape, axial_shape]
    square = pltpu.VMEM((NODE_COUNT, 128), F32)

    def call(body, name, count, limit, in_specs, out_specs, out_shape, scratch, args):
        return pl.pallas_call(
            body,
            grid_spec=pltpu.PrefetchScalarGridSpec(
                num_scalar_prefetch=2,
                grid=(slots // count,),
                in_specs=in_specs,
                out_specs=out_specs,
                scratch_shapes=scratch,
            ),
            out_shape=out_shape,
            compiler_params=pltpu.CompilerParams(vmem_limit_bytes=limit * 1024 * 1024),
            name=name,
        )(z_order, codes, *args)

    def all_whole(tables):
        return [whole(x.shape) for x in tables]

    def traces_of(f):
        return call(
            lambda *a: trace_kernel(group, *a), "traces", group, 20, [slab(group)] + all_whole([trace_m]),
            [radial_spec(group), radial_spec(group), axial_spec(group)], [radial_shape, radial_shape, axial_shape],
            [], [f, trace_m],
        )

    def moments_of(f, left):
        return call(
            lambda *a: moment_kernel(group, *a), "moments", group, 20,
            [slab(group), radial_spec(group)] + all_whole([rows, mirror_m]),
            [mom_spec, radial_spec(group)], [mom_shape, radial_shape],
            [pltpu.VMEM((5, NODES, LOCAL_Z, PLANE), F32), square], [f, left, rows, mirror_m],
        )

    def outer(f, ghosts, parts, last):
        count = math.gcd(slots, 2)
        if last:
            f = pltpu.with_memory_space_constraint(f, pltpu.HBM)
        tables = [rows, edge, ghost_r, ghost_z, pos, radial_m, axial_m, rot_m]
        scratch = [
            pltpu.VMEM((3, NODE_COUNT, PLANE), F32),
            pltpu.VMEM((10, NODE_COUNT, 128), F32),
            pltpu.VMEM((NODES, 128), F32),
            pltpu.VMEM((count, 3, NODE_COUNT, 128), F32),
            pltpu.VMEM((count, 2, NODE_COUNT, 128), BF16),
            pltpu.VMEM((count * GHOST_ROWS, PLANE), BF16),
            square,
            square,
            pltpu.VMEM((count, NODE_COUNT, PLANE + 256), BF16),
            pltpu.VMEM((count, 2, NODE_COUNT, 2 * NODE_COUNT), BF16),
            pltpu.VMEM((count, NODE_COUNT, PLANE), F32),
        ]
        return call(
            lambda *a: outer_kernel(count, len(parts), last, *a), "last_update" if last else "update", count, 32 if last else 26,
            [mom_spec] * len(parts) + [slab(count), axial_spec(count)] + [radial_spec(count)] * 3
            + all_whole(tables),
            [slab(count)] + ([mom_spec] if last else []), [big_shape] + ([mom_shape] if last else []),
            ([pltpu.VMEM((5, NODES, LOCAL_Z, PLANE), F32)] if last else []) + scratch,
            [*parts, f, *ghosts, *tables],
        )

    def spread(moments):
        parts = [moments]
        for shift in range(1, verts):
            parts.append(lax.ppermute(moments, "vert", [(i, i ^ shift) for i in range(verts)]))
        return parts

    def halo(near, far, axial):
        from_axial = lax.ppermute(axial, "gz", [(0, 1), (1, 0)])
        pairs = [(i, i ^ 1) for i in range(rows_total)]
        from_near = lax.ppermute(near, "row", pairs)
        between = [(i, i + 1) for i in range(1, rows_total - 1, 2)]
        from_far = lax.ppermute(far, "row", between + [(b, a) for a, b in between])
        return from_axial, from_near, from_far

    current = distribution
    for number in range(STEPS):
        last = number == STEPS - 1
        traces = traces_of(current)
        from_axial, from_near, from_far = halo(*traces)
        moments, turned = moments_of(current, traces[1])
        parts = spread(moments)
        ghosts = [from_axial, from_near, turned, from_far]
        current, *final = outer(current, ghosts, parts, last)
    parts = spread(final[0])
    macro, flux = pl.pallas_call(
        lambda *a: last_kernel(len(parts), *a),
        grid_spec=pltpu.PrefetchScalarGridSpec(
            num_scalar_prefetch=1,
            grid=(1,),
            in_specs=[mom_spec] * len(parts) + [whole(edge.shape)],
            out_specs=[whole((8, NODES, LOCAL_Z)), whole((1, NODES))],
        ),
        out_shape=[
            jax.ShapeDtypeStruct((8, NODES, LOCAL_Z), F32),
            jax.ShapeDtypeStruct((1, NODES), F32),
        ],
        compiler_params=pltpu.CompilerParams(vmem_limit_bytes=4 * 1024 * 1024),
        name="macroscopic",
    )(codes, *parts, edge)
    return (current, macro, flux)


def solution(mesh):
    in_specs = (P("row", "gz", "vert"), P("vert"), P(None, "row"))
    out_specs = (P("row", "gz", "vert"), P(None, "row", "gz"), P("gz", "row"))
    return jax.shard_map(
        on_device, mesh=mesh, in_specs=in_specs, out_specs=out_specs, check_vma=False
    )
```

```python
import math

import jax
import jax.numpy as jnp
import ml_dtypes
import numpy as np
from jax import lax
from jax.experimental import pallas as pl
from jax.experimental.pallas import tpu as pltpu
from jax.sharding import PartitionSpec as P

NODES = 8
NVR = 48
NVT = 48
NVZ = 48
STEPS = 2

ELEMENT_WIDTH = 4.0
TIME_STEP = 0.001
KNUDSEN = 0.005
VISCOUS_RATIO = 2.0 / 3.0
SAT_DENSITY = 1.5
SPEED_LIMIT = 5.0

PLANE = NVR * NVT
HALF = PLANE // 2
THIRD = HALF // 3
BOTTOM, TOP = 0, 1
LOCAL_Z = 2 * NODES
NODE_COUNT = NODES * LOCAL_Z
TILE = 256
WINDOW = 512
GHOST_ROWS = 32
MOMENTS = 16
F32 = jnp.float32
BF16 = jnp.bfloat16
PIECES = [(t, TILE, 0) for t in range(0, 1024, TILE)] + [(1024, 128, 0), (1152, 128, 1)] + [
    (t, TILE, 1) for t in range(1280, PLANE, TILE)
]
HALF_PIECES = [(t, TILE) for t in range(0, 1024, TILE)] + [(1024, 128)]


def legendre_pair(position, point_count):
    previous = 1.0
    current = position
    for degree in range(2, point_count + 1):
        previous, current = (
            current,
            ((2 * degree - 1) * position * current - (degree - 1) * previous) / degree,
        )
    slope = point_count * (position * current - previous) / (position * position - 1.0)
    return (current, slope)


def dg_tables(point_count):
    point_list = []
    weight_list = []
    for number in range(point_count):
        position = math.cos(math.pi * (number + 0.75) / (point_count + 0.5))
        for sweep in range(60):
            value, slope = legendre_pair(position, point_count)
            position = position - value / slope
        value, slope = legendre_pair(position, point_count)
        point_list.append(position)
        weight_list.append(2.0 / ((1.0 - position * position) * slope * slope))
    point_list = point_list[::-1]
    weight_list = weight_list[::-1]
    points = np.array(point_list)
    derivative = np.zeros((point_count, point_count))
    right = np.zeros(point_count)
    left = np.zeros(point_count)
    products = [
        np.prod([points[i] - points[j] for j in range(point_count) if j != i])
        for i in range(point_count)
    ]
    for i in range(point_count):
        others = [j for j in range(point_count) if j != i]
        derivative[i, i] = sum(1.0 / (points[i] - points[j]) for j in others)
        for j in others:
            derivative[i, j] = products[i] / products[j] / (points[i] - points[j])
        right[i] = np.prod([1.0 - points[j] for j in others]) / products[i]
        left[i] = np.prod([-1.0 - points[j] for j in others]) / products[i]
    return points, np.array(weight_list), derivative, right, left


def speed_grid(point_count):
    return -SPEED_LIMIT + (np.arange(point_count) + 0.5) * (2.0 * SPEED_LIMIT / point_count)


POINTS, QUAD, DERIV, END_R, END_L = dg_tables(NODES)
LIFT_R = END_R / QUAD
LIFT_L = END_L / QUAD
GRID_R = speed_grid(NVR)
GRID_T = speed_grid(NVT)
GRID_Z = speed_grid(NVZ)
STEP_V = 2 * SPEED_LIMIT / NVR
WEIGHT = STEP_V**3 / (2 * math.pi) ** 1.5
HALF_FLUX = float(
    WEIGHT
    * np.sum(np.exp(-(GRID_R**2) / 2))
    * np.sum(np.exp(-(GRID_T**2) / 2))
    * np.sum(np.maximum(GRID_Z, 0.0) * np.exp(-(GRID_Z**2) / 2))
)
SCALE = TIME_STEP * 2.0 / ELEMENT_WIDTH


def transport_tables():
    ident = np.eye(NODES)
    up = DERIV + np.outer(LIFT_L, END_L)
    down = DERIV - np.outer(LIFT_R, END_R)
    zero = np.zeros((NODES, NODES))
    wide = np.eye(LOCAL_Z)
    radial = np.stack([np.kron(down, wide), np.kron(up, wide), np.kron(DERIV, wide)])
    zup = np.block([[up, zero], [-np.outer(LIFT_L, END_R), up]])
    zdown = np.block([[down, np.outer(LIFT_R, END_L)], [zero, down]])
    zout = np.block([[down, np.outer(LIFT_R, END_L)], [zero, DERIV]])
    axial = np.stack([np.kron(ident, zdown), np.kron(ident, zup), np.kron(ident, zout)])
    ghost_r = np.zeros((2, NODE_COUNT, 128))
    ghost_z = np.zeros((2, NODE_COUNT, 128))
    for r in range(NODES):
        for z in range(LOCAL_Z):
            n = r * LOCAL_Z + z
            ghost_r[0, n, z] = -LIFT_R[r]
            ghost_r[1, n, z] = LIFT_L[r]
            if z >= NODES:
                ghost_z[0, n, r] = LIFT_R[z - NODES]
            else:
                ghost_z[1, n, r] = LIFT_L[z]
    trace = np.zeros((2, 2, GHOST_ROWS, NODE_COUNT))
    for side in range(2):
        radial_row = END_R if side == 1 else END_L
        for place in range(2):
            for z in range(LOCAL_Z):
                for r in range(NODES):
                    trace[side, place, z, r * LOCAL_Z + z] = radial_row[r]
            for r in range(NODES):
                for k in range(NODES):
                    if place == 0:
                        trace[side, place, LOCAL_Z + r, r * LOCAL_Z + NODES + k] = END_R[k]
                    else:
                        trace[side, place, LOCAL_Z + r, r * LOCAL_Z + k] = END_L[k]
    return (
        (-SCALE * radial).astype(ml_dtypes.bfloat16),
        (-SCALE * axial).astype(np.float32),
        (SCALE * ghost_r).astype(np.float32),
        (SCALE * ghost_z).astype(np.float32),
        trace.astype(ml_dtypes.bfloat16),
    )


def rotation_table():
    full = np.zeros((PLANE + 2 * TILE, PLANE))
    factor = TIME_STEP / (2 * STEP_V)
    for a in range(NVR):
        for b in range(NVT):
            n = a * NVT + b
            first = factor * GRID_T[b] * GRID_T[b]
            second = factor * GRID_R[a] * GRID_T[b]
            if a + 1 < NVR:
                full[TILE + n + NVT, n] = -first
            if a > 0:
                full[TILE + n - NVT, n] = first
            if b + 1 < NVT:
                full[TILE + n + 1, n] = second
            if b > 0:
                full[TILE + n - 1, n] = -second
    tiles = [full[TILE + t - 128 : TILE + t - 128 + WINDOW, t : t + TILE] for t in range(0, PLANE, TILE)]
    return np.stack(tiles).astype(ml_dtypes.bfloat16)


def mirror_table():
    table = np.zeros((THIRD, THIRD))
    groups = THIRD // NVT
    for g in range(groups):
        for b in range(NVT):
            table[(groups - 1 - g) * NVT + b, g * NVT + b] = 1.0
    return table.astype(ml_dtypes.bfloat16)


def plane_rows():
    vr = np.repeat(GRID_R, NVT)
    vt = np.tile(GRID_T, NVR)
    rows = np.zeros((8, PLANE))
    rows[0] = vr
    rows[1] = vt
    rows[2] = np.exp(-(vr**2 + vt**2) / 2)
    return rows.astype(np.float32)


def edge_table():
    table = np.zeros((2, NODES, NODE_COUNT))
    for r in range(NODES):
        for k in range(NODES):
            table[0, r, r * LOCAL_Z + k] = END_L[k]
            table[1, r, r * LOCAL_Z + NODES + k] = END_R[k]
    return table.astype(np.float32)


def node_columns():
    table = np.zeros((NODE_COUNT, 128))
    for r in range(NODES):
        table[r * LOCAL_Z : (r + 1) * LOCAL_Z, :] = (1.0 + POINTS[r]) / 2
    return table.astype(np.float32)


RADIAL_M, AXIAL_M, GHOST_R, GHOST_Z, TRACE_M = transport_tables()
ROTATION_M = rotation_table()
MIRROR_M = mirror_table()
ROWS = plane_rows()
EDGE = edge_table()
NODE_POS = node_columns()


def slot_speed(order, slot):
    return (order[slot].astype(F32) + 0.5) * (2 * SPEED_LIMIT / NVZ) - SPEED_LIMIT


def dot(x, y):
    return jnp.dot(x, y, preferred_element_type=F32)


def macroscopic_of(m):
    rho = m(0)
    inv = 1.0 / rho
    ur, ut, uz = m(1) * inv, m(2) * inv, m(3) * inv
    rr, tt, rt, zz, rz, tz = (m(k) for k in range(4, 10))
    energy = rr + tt + zz
    speed = ur * ur + ut * ut + uz * uz
    temp = (energy * inv - speed) * (1.0 / 3.0)
    tail = 2.0 * rho * speed - energy
    qr = 0.5 * (m(10) - 2.0 * (ur * rr + ut * rt + uz * rz) + ur * tail)
    qt = 0.5 * (m(11) - 2.0 * (ur * rt + ut * tt + uz * tz) + ut * tail)
    qz = 0.5 * (m(12) - 2.0 * (ur * rz + ut * tz + uz * zz) + uz * tail)
    return rho, ur, ut, uz, temp, qr, qt, qz


def add_speed_sums(field, vz, sums):
    one = field * vz
    two = one * vz
    return [
        sums[0] + field,
        sums[1] + one,
        sums[2] + two,
        sums[3] + two * vz,
        sums[4] + field * jnp.abs(vz),
    ]


def finish_moments(sums_ref, rows_ref, table_ref, out_ref):
    lane = lax.broadcasted_iota(jnp.int32, (LOCAL_Z, 128), 1)

    def one_radius(r, carry):
        acc = [jnp.zeros((LOCAL_Z, 128), F32) for _ in range(14)]
        for j in range(PLANE // 128):
            at = pl.ds(j * 128, 128)
            vr = rows_ref[0:1, at]
            vt = rows_ref[1:2, at]
            g0, g1, g2, g3, g4 = (sums_ref[k, r, :, at] for k in range(5))
            a = vr * g0
            b = vt * g0
            aa = vr * a
            bb = vt * b
            c = vr * g1
            d = vt * g1
            perp = aa + bb + g2
            new = [g0, a, b, g1, aa, bb, vr * b, g2, c, d, vr * perp, vt * perp, vr * c + vt * d + g3, g4]
            acc = [x + y for x, y in zip(acc, new)]
        block = jnp.zeros((LOCAL_Z, 128), F32)
        for k in range(14):
            block = jnp.where(lane == k, WEIGHT * jnp.sum(acc[k], axis=1, keepdims=True), block)
        table_ref[pl.ds(pl.multiple_of(r * LOCAL_Z, LOCAL_Z), LOCAL_Z), :] = block
        return carry

    lax.fori_loop(0, NODES, one_radius, 0)
    out_ref[...] = jnp.transpose(table_ref[...])[0:MOMENTS, :]


def clear_sums(sums_ref):
    sums_ref[...] = jnp.zeros(sums_ref.shape, F32)


def places_of():
    return lax.axis_index("row"), lax.axis_index("gz")


def turn_traces(count, row, mirror_ref, left_ref, turned_ref):
    @pl.when(row == 0)
    def _():
        for part in range(3):
            start = (2 - part) * THIRD
            flat = left_ref[:, :, start : start + THIRD].reshape(count * LOCAL_Z, THIRD).astype(BF16)
            got = dot(flat, mirror_ref[...])
            turned_ref[:, :, part * THIRD : (part + 1) * THIRD] = got.reshape(count, LOCAL_Z, THIRD)

    @pl.when(row != 0)
    def _():
        turned_ref[...] = jnp.zeros(turned_ref.shape, F32)


def nodes_of(ref, first, lanes):
    return ref[:, :, first : first + lanes].reshape(NODE_COUNT, lanes)


def trace_kernel(count, order, codes, f_ref, trace_ref, near_ref, far_ref, axial_ref):
    row, place = places_of()
    even = lax.rem(row, 2) == 0
    for s in range(count):
        for first, lanes in HALF_PIECES:
            got = []
            for side in range(2):
                here = side * HALF + first
                narrow = nodes_of(f_ref, s * PLANE + here, lanes).astype(BF16)
                got.append(dot(trace_ref[side, place], narrow))
                axial_ref[s, :, here : here + lanes] = got[side][LOCAL_Z : LOCAL_Z + NODES]
            left, right = got[0][0:LOCAL_Z], got[1][0:LOCAL_Z]
            near_ref[s, :, first : first + lanes] = jnp.where(even, right, left)
            far_ref[s, :, first : first + lanes] = jnp.where(even, left, right)


def moment_kernel(
    count, order, codes, f_ref, left_ref, rows_ref, mirror_ref, mom_ref, turned_ref, sums_ref, table_ref
):
    step = pl.program_id(0)
    row, place = places_of()

    @pl.when(step == 0)
    def _():
        clear_sums(sums_ref)

    turn_traces(count, row, mirror_ref, left_ref, turned_ref)
    speeds = [slot_speed(order, step * count + s) for s in range(count)]
    for j in range(0, PLANE, 128):
        at = pl.ds(j, 128)
        for r in range(NODES):
            sums = [sums_ref[k, r, :, at] for k in range(5)]
            for s in range(count):
                sums = add_speed_sums(f_ref[r, :, pl.ds(s * PLANE + j, 128)], speeds[s], sums)
            for k in range(5):
                sums_ref[k, r, :, at] = sums[k]

    @pl.when(step == pl.num_programs(0) - 1)
    def _():
        finish_moments(sums_ref, rows_ref, table_ref, mom_ref)


def total_of(parts):
    while len(parts) > 1:
        parts = [parts[k] + parts[k + 1] for k in range(0, len(parts), 2)]
    return parts[0]


def edge_sums(total, edge_ref):
    net, gross = total[3:4, :], total[13:14, :]
    down, up = 0.5 * (gross - net), 0.5 * (gross + net)
    pairs = ((0, down), (1, up), (1, down))
    return tuple(jnp.sum(edge_ref[k] * row, axis=1, keepdims=True) for k, row in pairs)


def prepare_nodes(total, codes, place, rows_ref, edge_ref, table_ref, node_ref, wall_ref, plane_ref):
    rho, ur, ut, uz, temp, qr, qt, qz = macroscopic_of(lambda k: total[k : k + 1, :])
    inv_t = 1.0 / temp
    beta = ((1.0 - VISCOUS_RATIO) / 5.0) / (rho * temp * temp)
    kappa = rho * (TIME_STEP / KNUDSEN)
    peak = kappa * rho * inv_t * jnp.sqrt(inv_t)
    values = [uz, -0.5 * inv_t, qz * beta, inv_t, peak, 1.0 - kappa, ur, ut, qr * beta, qt * beta]
    clear_sums(table_ref)
    for k, value in enumerate(values):
        table_ref[k : k + 1, :] = value
    table_ref[...] = jnp.transpose(table_ref[...])
    for k in range(len(values)):
        node_ref[k] = jnp.broadcast_to(table_ref[:, k : k + 1], (NODE_COUNT, 128))
    incident, upward, downward = edge_sums(total, edge_ref)
    bottom = jnp.where(codes[0, BOTTOM] == 1, SAT_DENSITY, incident * (1.0 / HALF_FLUX))
    top = jnp.where(codes[0, TOP] == 2, 0.0, upward * (1.0 / HALF_FLUX))
    wall_ref[...] = jnp.broadcast_to(jnp.where(place == 0, bottom, top), (NODES, 128))

    def one_radius(r, carry):
        rows = pl.ds(pl.multiple_of(r * LOCAL_Z, LOCAL_Z), LOCAL_Z)
        n_half, n_inv = node_ref[1, rows, :], node_ref[3, rows, :]
        n_ur, n_ut = node_ref[6, rows, :], node_ref[7, rows, :]
        n_qr, n_qt = node_ref[8, rows, :], node_ref[9, rows, :]
        for j in range(PLANE // 128):
            at = pl.ds(j * 128, 128)
            cr = rows_ref[0:1, at] - n_ur
            ct = rows_ref[1:2, at] - n_ut
            square = cr * cr + ct * ct
            gauss = jnp.exp(square * n_half)
            along = cr * n_qr + ct * n_qt
            plane_ref[0, rows, at] = gauss
            plane_ref[1, rows, at] = along
            plane_ref[2, rows, at] = square * n_inv
        return carry

    lax.fori_loop(0, NODES, one_radius, 0)


def slot_factors(vz, node_ref):
    cz = vz - node_ref[0]
    square = cz * cz
    return node_ref[4] * jnp.exp(square * node_ref[1]), cz * node_ref[2], square * node_ref[3] - 5.0


def ghost_rows(
    speeds, row, place, in_axial_ref, in_near_ref, in_turned_ref, in_far_ref, rows_ref, wall_ref, ghost_ref
):
    count = len(speeds)
    even = lax.rem(row, 2) == 0
    fill = ghost_ref.shape[0] - count * (LOCAL_Z + NODES)
    strengths = [jnp.exp(-0.5 * vz * vz + jnp.zeros((NODES, 128), F32)) * wall_ref[...] for vz in speeds]
    for j in range(PLANE // 128):
        at = pl.ds(j * 128, 128)
        radials, axials = [], []
        for s in range(count):
            if j * 128 < HALF:
                radial = jnp.where(even, in_near_ref[s, :, at], in_far_ref[s, :, at])
            else:
                back = pl.ds(j * 128 - HALF, 128)
                radial = jnp.where(even, in_far_ref[s, :, back], in_near_ref[s, :, back]) + in_turned_ref[s, :, back]
            own = (place == 0) == (speeds[s] > 0)
            radials.append(rows_ref[0:1, at] * radial)
            axials.append(jnp.where(own, strengths[s] * rows_ref[2:3, at], in_axial_ref[s, :, at]))
        zeros = [jnp.zeros((fill, 128), F32)] if fill else []
        ghost_ref[:, at] = jnp.concatenate(radials + axials + zeros, axis=0).astype(BF16)


def outer_kernel(count, part_count, last, order, codes, *refs):
    part_refs, refs = refs[:part_count], refs[part_count:]
    f_ref, in_axial_ref, in_near_ref, in_turned_ref, in_far_ref = refs[:5]
    rows_ref, edge_ref, ghost_r_ref, ghost_z_ref, pos_ref, radial_m_ref, axial_m_ref, rot_ref, out_ref = refs[5:14]
    refs = refs[14:]
    if last:
        (mom_ref, sums_ref), refs = refs[:2], refs[2:]
    plane_ref, node_ref, wall_ref, slot_ref, lift_ref, ghost_ref, table_ref = refs[:7]
    inverse_ref, pad_ref, lhs_ref, work_ref = refs[7:]
    step = pl.program_id(0)
    row, place = places_of()

    @pl.when(step == 0)
    def _():
        if last:
            clear_sums(sums_ref)
        total = total_of([p[...] for p in part_refs])
        prepare_nodes(total, codes, place, rows_ref, edge_ref, table_ref, node_ref, wall_ref, plane_ref)
        pad_ref[:, :, 0:128] = jnp.zeros((count, NODE_COUNT, 128), BF16)
        pad_ref[:, :, 128 + PLANE :] = jnp.zeros((count, NODE_COUNT, 128), BF16)
        inverse_ref[...] = 1.0 / (ELEMENT_WIDTH * (row.astype(F32) + pos_ref[...]))
        minus = radial_m_ref[jnp.where(row == lax.axis_size("row") - 1, 2, 0)]
        for s in range(count):
            lhs_ref[s, 0, :, 0:NODE_COUNT] = minus
            lhs_ref[s, 1, :, 0:NODE_COUNT] = radial_m_ref[1]

    speeds = [slot_speed(order, step * count + s) for s in range(count)]
    for s in range(count):
        vz = speeds[s]
        for k, value in enumerate(slot_factors(vz, node_ref)):
            slot_ref[s, k] = value
        lean = jnp.abs(vz) * ghost_z_ref[jnp.where(vz > 0, 1, 0)]
        lean = pltpu.roll(lean, count * LOCAL_Z + s * NODES, 1)
        for side in range(2):
            lift = ghost_r_ref[side]
            lift_ref[s, side] = ((pltpu.roll(lift, s * LOCAL_Z, 1) if s else lift) + lean).astype(BF16)
    ghost_rows(
        speeds, row, place, in_axial_ref, in_near_ref, in_turned_ref, in_far_ref, rows_ref, wall_ref, ghost_ref
    )

    kind_out = jnp.where(jnp.logical_and(place == 1, codes[0, TOP] == 2), 2, 0)
    inverse = inverse_ref[...]
    for s in range(count):
        axial = (speeds[s] * axial_m_ref[jnp.where(speeds[s] > 0, 1, kind_out)]).astype(BF16)
        lhs_ref[s, 0, :, NODE_COUNT:] = axial
        lhs_ref[s, 1, :, NODE_COUNT:] = axial
        for j in range(PLANE // 128):
            field = nodes_of(f_ref, s * PLANE + j * 128, 128)
            pad_ref[s, :, 128 + j * 128 : 256 + j * 128] = (field * inverse).astype(BF16)

    held = ghost_ref.shape[0]
    lane = lax.broadcasted_iota(jnp.int32, (count * NODE_COUNT, 128), 1)
    for first, lanes, side in PIECES:
        tile = first // TILE
        start = tile * TILE
        inside = first - start
        lifts = lift_ref[:, side].reshape(count * NODE_COUNT, 128)
        window = pad_ref[:, :, start : start + WINDOW].reshape(count * NODE_COUNT, WINDOW)
        window = jnp.concatenate([jnp.where(lane < held, lifts, window[:, 0:128]), window[:, 128:]], axis=1)
        turning = jnp.concatenate(
            [ghost_ref[:, first : first + lanes], rot_ref[tile, held:, inside : inside + lanes]], axis=0
        )
        turned = dot(window, turning)
        vr = rows_ref[0:1, first : first + lanes]
        for s in range(count):
            field = nodes_of(f_ref, s * PLANE + first, lanes)
            both = jnp.concatenate([(field * vr).astype(BF16), field.astype(BF16)], axis=0)
            work_ref[s, :, first : first + lanes] = turned[s * NODE_COUNT : (s + 1) * NODE_COUNT] + dot(
                lhs_ref[s, side], both
            )

    def update(r, carry):
        rows = pl.ds(pl.multiple_of(r * LOCAL_Z, LOCAL_Z), LOCAL_Z)
        keep = node_ref[5, rows, :]
        factor = [[slot_ref[s, k, rows, :] for k in range(3)] for s in range(count)]
        for j in range(PLANE // 128):
            at = pl.ds(j * 128, 128)
            gauss, along, reach = (plane_ref[k, rows, at] for k in range(3))
            if last:
                sums = [sums_ref[k, r, :, at] for k in range(5)]
            for s in range(count):
                here = pl.ds(s * PLANE + j * 128, 128)
                new = f_ref[r, :, here] * keep + work_ref[s, rows, at]
                bend = (along + factor[s][1]) * (reach + factor[s][2]) + 1.0
                new = new + (gauss * factor[s][0]) * bend
                out_ref[r, :, here] = new
                if last:
                    sums = add_speed_sums(new, speeds[s], sums)
            if last:
                for k in range(5):
                    sums_ref[k, r, :, at] = sums[k]
        return carry

    lax.fori_loop(0, NODES, update, 0)
    if last:

        @pl.when(step == pl.num_programs(0) - 1)
        def _():
            finish_moments(sums_ref, rows_ref, table_ref, mom_ref)


def last_kernel(part_count, codes, *refs):
    total_ref = total_of([p[...] for p in refs[:part_count]])
    edge_ref, macro_ref, flux_ref = refs[part_count:]
    row, place = places_of()
    values = macroscopic_of(lambda k: total_ref[k : k + 1, :])
    for k in range(8):
        for r in range(NODES):
            macro_ref[k, r : r + 1, :] = values[k][:, r * LOCAL_Z : (r + 1) * LOCAL_Z]
    incident, upward, downward = edge_sums(total_ref, edge_ref)
    bottom = jnp.where(codes[0, BOTTOM] == 1, SAT_DENSITY * HALF_FLUX - incident, 0.0)
    top = jnp.where(codes[0, TOP] == 2, upward - downward, 0.0)
    square = jnp.broadcast_to(jnp.where(place == 0, bottom, top), (NODES, 128))
    same = lax.broadcasted_iota(jnp.int32, (NODES, 128), 0) == lax.broadcasted_iota(jnp.int32, (NODES, 128), 1)
    flux_ref[...] = jnp.sum(jnp.where(same, square, 0.0), axis=0, keepdims=True)[:, 0:NODES]


def whole(shape):
    return pl.BlockSpec(shape, lambda *a: (0,) * len(shape), pipeline_mode=pl.Buffered(1))


def on_device(distribution, z_order, edge_codes):
    local_r, local_z, vdev = distribution.shape
    assert local_r == NODES and local_z == LOCAL_Z
    slots = vdev // PLANE
    group = math.gcd(slots, 3)
    rows_total = lax.axis_size("row")
    verts = lax.axis_size("vert")
    assert lax.axis_size("gz") == 2 and rows_total % 2 == 0
    codes = edge_codes.T
    fixed = lambda x: pltpu.with_memory_space_constraint(jnp.asarray(x), pltpu.HBM)
    codes, z_order = fixed(codes), fixed(z_order)
    rows, pos, edge = fixed(ROWS), fixed(NODE_POS), fixed(EDGE)
    radial_m, axial_m = fixed(RADIAL_M), fixed(AXIAL_M)
    ghost_r, ghost_z = fixed(GHOST_R), fixed(GHOST_Z)
    trace_m, mirror_m, rot_m = fixed(TRACE_M), fixed(MIRROR_M), jnp.asarray(ROTATION_M)

    def slab(count):
        return pl.BlockSpec((NODES, LOCAL_Z, count * PLANE), lambda i, *n: (0, 0, i))

    def radial_spec(count):
        return pl.BlockSpec((count, LOCAL_Z, HALF), lambda i, *n: (i, 0, 0))

    def axial_spec(count):
        return pl.BlockSpec((count, NODES, PLANE), lambda i, *n: (i, 0, 0))

    def trace_specs(count):
        return [radial_spec(count), radial_spec(count), radial_spec(count), axial_spec(count)]

    mom_spec = whole((MOMENTS, 128))
    radial_shape = jax.ShapeDtypeStruct((slots, LOCAL_Z, HALF), F32)
    axial_shape = jax.ShapeDtypeStruct((slots, NODES, PLANE), F32)
    mom_shape = jax.ShapeDtypeStruct((MOMENTS, 128), F32)
    big_shape = jax.ShapeDtypeStruct(distribution.shape, F32)
    trace_shapes = [radial_shape, radial_shape, radial_shape, axial_shape]
    square = pltpu.VMEM((NODE_COUNT, 128), F32)

    def call(body, name, count, limit, in_specs, out_specs, out_shape, scratch, args):
        return pl.pallas_call(
            body,
            grid_spec=pltpu.PrefetchScalarGridSpec(
                num_scalar_prefetch=2,
                grid=(slots // count,),
                in_specs=in_specs,
                out_specs=out_specs,
                scratch_shapes=scratch,
            ),
            out_shape=out_shape,
            compiler_params=pltpu.CompilerParams(vmem_limit_bytes=limit * 1024 * 1024),
            name=name,
        )(z_order, codes, *args)

    def all_whole(tables):
        return [whole(x.shape) for x in tables]

    def traces_of(f):
        return call(
            lambda *a: trace_kernel(group, *a), "traces", group, 20, [slab(group)] + all_whole([trace_m]),
            [radial_spec(group), radial_spec(group), axial_spec(group)], [radial_shape, radial_shape, axial_shape],
            [], [f, trace_m],
        )

    def moments_of(f, left):
        return call(
            lambda *a: moment_kernel(group, *a), "moments", group, 20,
            [slab(group), radial_spec(group)] + all_whole([rows, mirror_m]),
            [mom_spec, radial_spec(group)], [mom_shape, radial_shape],
            [pltpu.VMEM((5, NODES, LOCAL_Z, PLANE), F32), square], [f, left, rows, mirror_m],
        )

    def outer(f, ghosts, parts, last):
        count = group
        f = pltpu.with_memory_space_constraint(f, pltpu.HBM)
        tables = [rows, edge, ghost_r, ghost_z, pos, radial_m, axial_m, rot_m]
        scratch = [
            pltpu.VMEM((3, NODE_COUNT, PLANE), F32),
            pltpu.VMEM((10, NODE_COUNT, 128), F32),
            pltpu.VMEM((NODES, 128), F32),
            pltpu.VMEM((count, 3, NODE_COUNT, 128), F32),
            pltpu.VMEM((count, 2, NODE_COUNT, 128), BF16),
            pltpu.VMEM((-(-count * (LOCAL_Z + NODES) // 16) * 16, PLANE), BF16),
            square,
            square,
            pltpu.VMEM((count, NODE_COUNT, PLANE + 256), BF16),
            pltpu.VMEM((count, 2, NODE_COUNT, 2 * NODE_COUNT), BF16),
            pltpu.VMEM((count, NODE_COUNT, PLANE), F32),
        ]
        return call(
            lambda *a: outer_kernel(count, len(parts), last, *a), "last_update" if last else "update", count, 40 if last else 32,
            [mom_spec] * len(parts) + [slab(count), axial_spec(count)] + [radial_spec(count)] * 3
            + all_whole(tables),
            [slab(count)] + ([mom_spec] if last else []), [big_shape] + ([mom_shape] if last else []),
            ([pltpu.VMEM((5, NODES, LOCAL_Z, PLANE), F32)] if last else []) + scratch,
            [*parts, f, *ghosts, *tables],
        )

    def spread(moments):
        parts = [moments]
        for shift in range(1, verts):
            parts.append(lax.ppermute(moments, "vert", [(i, i ^ shift) for i in range(verts)]))
        return parts

    def halo(near, far, axial):
        from_axial = lax.ppermute(axial, "gz", [(0, 1), (1, 0)])
        pairs = [(i, i ^ 1) for i in range(rows_total)]
        from_near = lax.ppermute(near, "row", pairs)
        between = [(i, i + 1) for i in range(1, rows_total - 1, 2)]
        from_far = lax.ppermute(far, "row", between + [(b, a) for a, b in between])
        return from_axial, from_near, from_far

    current = distribution
    for number in range(STEPS):
        last = number == STEPS - 1
        traces = traces_of(current)
        from_axial, from_near, from_far = halo(*traces)
        moments, turned = moments_of(current, traces[1])
        parts = spread(moments)
        ghosts = [from_axial, from_near, turned, from_far]
        current, *final = outer(current, ghosts, parts, last)
    parts = spread(final[0])
    macro, flux = pl.pallas_call(
        lambda *a: last_kernel(len(parts), *a),
        grid_spec=pltpu.PrefetchScalarGridSpec(
            num_scalar_prefetch=1,
            grid=(1,),
            in_specs=[mom_spec] * len(parts) + [whole(edge.shape)],
            out_specs=[whole((8, NODES, LOCAL_Z)), whole((1, NODES))],
        ),
        out_shape=[
            jax.ShapeDtypeStruct((8, NODES, LOCAL_Z), F32),
            jax.ShapeDtypeStruct((1, NODES), F32),
        ],
        compiler_params=pltpu.CompilerParams(vmem_limit_bytes=4 * 1024 * 1024),
        name="macroscopic",
    )(codes, *parts, edge)
    return (current, macro, flux)


def solution(mesh):
    in_specs = (P("row", "gz", "vert"), P("vert"), P(None, "row"))
    out_specs = (P("row", "gz", "vert"), P(None, "row", "gz"), P("gz", "row"))
    return jax.shard_map(
        on_device, mesh=mesh, in_specs=in_specs, out_specs=out_specs, check_vma=False
    )
```

```python
import math

import jax
import jax.numpy as jnp
import ml_dtypes
import numpy as np
from jax import lax
from jax.experimental import pallas as pl
from jax.experimental.pallas import tpu as pltpu
from jax.sharding import PartitionSpec as P

NODES = 8
NVR = 48
NVT = 48
NVZ = 48
STEPS = 2

ELEMENT_WIDTH = 4.0
TIME_STEP = 0.001
KNUDSEN = 0.005
VISCOUS_RATIO = 2.0 / 3.0
SAT_DENSITY = 1.5
SPEED_LIMIT = 5.0

PLANE = NVR * NVT
HALF = PLANE // 2
THIRD = HALF // 3
BOTTOM, TOP = 0, 1
LOCAL_Z = 2 * NODES
NODE_COUNT = NODES * LOCAL_Z
TILE = 256
WINDOW = 512
GHOST_ROWS = 32
MOMENTS = 16
F32 = jnp.float32
BF16 = jnp.bfloat16
PIECES = [(t, TILE, 0) for t in range(0, 1024, TILE)] + [(1024, 128, 0), (1152, 128, 1)] + [
    (t, TILE, 1) for t in range(1280, PLANE, TILE)
]
HALF_PIECES = [(t, TILE) for t in range(0, 1024, TILE)] + [(1024, 128)]


def legendre_pair(position, point_count):
    previous = 1.0
    current = position
    for degree in range(2, point_count + 1):
        previous, current = (
            current,
            ((2 * degree - 1) * position * current - (degree - 1) * previous) / degree,
        )
    slope = point_count * (position * current - previous) / (position * position - 1.0)
    return (current, slope)


def dg_tables(point_count):
    point_list = []
    weight_list = []
    for number in range(point_count):
        position = math.cos(math.pi * (number + 0.75) / (point_count + 0.5))
        for sweep in range(60):
            value, slope = legendre_pair(position, point_count)
            position = position - value / slope
        value, slope = legendre_pair(position, point_count)
        point_list.append(position)
        weight_list.append(2.0 / ((1.0 - position * position) * slope * slope))
    point_list = point_list[::-1]
    weight_list = weight_list[::-1]
    points = np.array(point_list)
    derivative = np.zeros((point_count, point_count))
    right = np.zeros(point_count)
    left = np.zeros(point_count)
    products = [
        np.prod([points[i] - points[j] for j in range(point_count) if j != i])
        for i in range(point_count)
    ]
    for i in range(point_count):
        others = [j for j in range(point_count) if j != i]
        derivative[i, i] = sum(1.0 / (points[i] - points[j]) for j in others)
        for j in others:
            derivative[i, j] = products[i] / products[j] / (points[i] - points[j])
        right[i] = np.prod([1.0 - points[j] for j in others]) / products[i]
        left[i] = np.prod([-1.0 - points[j] for j in others]) / products[i]
    return points, np.array(weight_list), derivative, right, left


def speed_grid(point_count):
    return -SPEED_LIMIT + (np.arange(point_count) + 0.5) * (2.0 * SPEED_LIMIT / point_count)


POINTS, QUAD, DERIV, END_R, END_L = dg_tables(NODES)
LIFT_R = END_R / QUAD
LIFT_L = END_L / QUAD
GRID_R = speed_grid(NVR)
GRID_T = speed_grid(NVT)
GRID_Z = speed_grid(NVZ)
STEP_V = 2 * SPEED_LIMIT / NVR
WEIGHT = STEP_V**3 / (2 * math.pi) ** 1.5
HALF_FLUX = float(
    WEIGHT
    * np.sum(np.exp(-(GRID_R**2) / 2))
    * np.sum(np.exp(-(GRID_T**2) / 2))
    * np.sum(np.maximum(GRID_Z, 0.0) * np.exp(-(GRID_Z**2) / 2))
)
SCALE = TIME_STEP * 2.0 / ELEMENT_WIDTH


def transport_tables():
    ident = np.eye(NODES)
    up = DERIV + np.outer(LIFT_L, END_L)
    down = DERIV - np.outer(LIFT_R, END_R)
    zero = np.zeros((NODES, NODES))
    wide = np.eye(LOCAL_Z)
    radial = np.stack([np.kron(down, wide), np.kron(up, wide), np.kron(DERIV, wide)])
    zup = np.block([[up, zero], [-np.outer(LIFT_L, END_R), up]])
    zdown = np.block([[down, np.outer(LIFT_R, END_L)], [zero, down]])
    zout = np.block([[down, np.outer(LIFT_R, END_L)], [zero, DERIV]])
    axial = np.stack([np.kron(ident, zdown), np.kron(ident, zup), np.kron(ident, zout)])
    ghost_r = np.zeros((2, NODE_COUNT, 128))
    ghost_z = np.zeros((2, NODE_COUNT, 128))
    for r in range(NODES):
        for z in range(LOCAL_Z):
            n = r * LOCAL_Z + z
            ghost_r[0, n, z] = -LIFT_R[r]
            ghost_r[1, n, z] = LIFT_L[r]
            if z >= NODES:
                ghost_z[0, n, r] = LIFT_R[z - NODES]
            else:
                ghost_z[1, n, r] = LIFT_L[z]
    trace = np.zeros((2, 2, GHOST_ROWS, NODE_COUNT))
    for side in range(2):
        radial_row = END_R if side == 1 else END_L
        for place in range(2):
            for z in range(LOCAL_Z):
                for r in range(NODES):
                    trace[side, place, z, r * LOCAL_Z + z] = radial_row[r]
            for r in range(NODES):
                for k in range(NODES):
                    if place == 0:
                        trace[side, place, LOCAL_Z + r, r * LOCAL_Z + NODES + k] = END_R[k]
                    else:
                        trace[side, place, LOCAL_Z + r, r * LOCAL_Z + k] = END_L[k]
    return (
        (-SCALE * radial).astype(ml_dtypes.bfloat16),
        (-SCALE * axial).astype(np.float32),
        (SCALE * ghost_r).astype(np.float32),
        (SCALE * ghost_z).astype(np.float32),
        trace.astype(ml_dtypes.bfloat16),
    )


def rotation_table():
    full = np.zeros((PLANE + 2 * TILE, PLANE))
    factor = TIME_STEP / (2 * STEP_V)
    for a in range(NVR):
        for b in range(NVT):
            n = a * NVT + b
            first = factor * GRID_T[b] * GRID_T[b]
            second = factor * GRID_R[a] * GRID_T[b]
            if a + 1 < NVR:
                full[TILE + n + NVT, n] = -first
            if a > 0:
                full[TILE + n - NVT, n] = first
            if b + 1 < NVT:
                full[TILE + n + 1, n] = second
            if b > 0:
                full[TILE + n - 1, n] = -second
    tiles = [full[TILE + t - 128 : TILE + t - 128 + WINDOW, t : t + TILE] for t in range(0, PLANE, TILE)]
    return np.stack(tiles).astype(ml_dtypes.bfloat16)


def mirror_table():
    table = np.zeros((THIRD, THIRD))
    groups = THIRD // NVT
    for g in range(groups):
        for b in range(NVT):
            table[(groups - 1 - g) * NVT + b, g * NVT + b] = 1.0
    return table.astype(ml_dtypes.bfloat16)


def plane_rows():
    vr = np.repeat(GRID_R, NVT)
    vt = np.tile(GRID_T, NVR)
    rows = np.zeros((8, PLANE))
    rows[0] = vr
    rows[1] = vt
    rows[2] = np.exp(-(vr**2 + vt**2) / 2)
    return rows.astype(np.float32)


def edge_table():
    table = np.zeros((2, NODES, NODE_COUNT))
    for r in range(NODES):
        for k in range(NODES):
            table[0, r, r * LOCAL_Z + k] = END_L[k]
            table[1, r, r * LOCAL_Z + NODES + k] = END_R[k]
    return table.astype(np.float32)


def node_columns():
    table = np.zeros((NODE_COUNT, 128))
    for r in range(NODES):
        table[r * LOCAL_Z : (r + 1) * LOCAL_Z, :] = (1.0 + POINTS[r]) / 2
    return table.astype(np.float32)


RADIAL_M, AXIAL_M, GHOST_R, GHOST_Z, TRACE_M = transport_tables()
ROTATION_M = rotation_table()
MIRROR_M = mirror_table()
ROWS = plane_rows()
EDGE = edge_table()
NODE_POS = node_columns()


def slot_speed(order, slot):
    return (order[slot].astype(F32) + 0.5) * (2 * SPEED_LIMIT / NVZ) - SPEED_LIMIT


def dot(x, y):
    return jnp.dot(x, y, preferred_element_type=F32)


def macroscopic_of(m):
    rho = m(0)
    inv = 1.0 / rho
    ur, ut, uz = m(1) * inv, m(2) * inv, m(3) * inv
    rr, tt, rt, zz, rz, tz = (m(k) for k in range(4, 10))
    energy = rr + tt + zz
    speed = ur * ur + ut * ut + uz * uz
    temp = (energy * inv - speed) * (1.0 / 3.0)
    tail = 2.0 * rho * speed - energy
    qr = 0.5 * (m(10) - 2.0 * (ur * rr + ut * rt + uz * rz) + ur * tail)
    qt = 0.5 * (m(11) - 2.0 * (ur * rt + ut * tt + uz * tz) + ut * tail)
    qz = 0.5 * (m(12) - 2.0 * (ur * rz + ut * tz + uz * zz) + uz * tail)
    return rho, ur, ut, uz, temp, qr, qt, qz


def add_speed_sums(field, vz, sums):
    one = field * vz
    two = one * vz
    return [
        sums[0] + field,
        sums[1] + one,
        sums[2] + two,
        sums[3] + two * vz,
        sums[4] + field * jnp.abs(vz),
    ]


def finish_moments(sums_ref, rows_ref, table_ref, out_ref):
    lane = lax.broadcasted_iota(jnp.int32, (LOCAL_Z, 128), 1)

    def one_radius(r, carry):
        acc = [jnp.zeros((LOCAL_Z, 128), F32) for _ in range(14)]
        for j in range(PLANE // 128):
            at = pl.ds(j * 128, 128)
            vr = rows_ref[0:1, at]
            vt = rows_ref[1:2, at]
            g0, g1, g2, g3, g4 = (sums_ref[k, r, :, at] for k in range(5))
            a = vr * g0
            b = vt * g0
            aa = vr * a
            bb = vt * b
            c = vr * g1
            d = vt * g1
            perp = aa + bb + g2
            new = [g0, a, b, g1, aa, bb, vr * b, g2, c, d, vr * perp, vt * perp, vr * c + vt * d + g3, g4]
            acc = [x + y for x, y in zip(acc, new)]
        block = jnp.zeros((LOCAL_Z, 128), F32)
        for k in range(14):
            block = jnp.where(lane == k, WEIGHT * jnp.sum(acc[k], axis=1, keepdims=True), block)
        table_ref[pl.ds(pl.multiple_of(r * LOCAL_Z, LOCAL_Z), LOCAL_Z), :] = block
        return carry

    lax.fori_loop(0, NODES, one_radius, 0)
    out_ref[...] = jnp.transpose(table_ref[...])[0:MOMENTS, :]


def clear_sums(sums_ref):
    sums_ref[...] = jnp.zeros(sums_ref.shape, F32)


def places_of():
    return lax.axis_index("row"), lax.axis_index("gz")


def turn_traces(count, row, mirror_ref, left_ref, turned_ref):
    @pl.when(row == 0)
    def _():
        for part in range(3):
            start = (2 - part) * THIRD
            flat = left_ref[:, :, start : start + THIRD].reshape(count * LOCAL_Z, THIRD).astype(BF16)
            got = dot(flat, mirror_ref[...])
            turned_ref[:, :, part * THIRD : (part + 1) * THIRD] = got.reshape(count, LOCAL_Z, THIRD)

    @pl.when(row != 0)
    def _():
        turned_ref[...] = jnp.zeros(turned_ref.shape, F32)


def nodes_of(ref, first, lanes):
    return ref[:, :, first : first + lanes].reshape(NODE_COUNT, lanes)


def trace_kernel(count, order, codes, f_ref, trace_ref, near_ref, far_ref, axial_ref):
    row, place = places_of()
    even = lax.rem(row, 2) == 0
    for s in range(count):
        for first, lanes in HALF_PIECES:
            got = []
            for side in range(2):
                here = side * HALF + first
                narrow = nodes_of(f_ref, s * PLANE + here, lanes).astype(BF16)
                got.append(dot(trace_ref[side, place], narrow))
                axial_ref[s, :, here : here + lanes] = got[side][LOCAL_Z : LOCAL_Z + NODES]
            left, right = got[0][0:LOCAL_Z], got[1][0:LOCAL_Z]
            near_ref[s, :, first : first + lanes] = jnp.where(even, right, left)
            far_ref[s, :, first : first + lanes] = jnp.where(even, left, right)


def moment_kernel(
    count, order, codes, f_ref, left_ref, rows_ref, mirror_ref, mom_ref, turned_ref, sums_ref, table_ref
):
    step = pl.program_id(0)
    row, place = places_of()

    @pl.when(step == 0)
    def _():
        clear_sums(sums_ref)

    turn_traces(count, row, mirror_ref, left_ref, turned_ref)
    speeds = [slot_speed(order, step * count + s) for s in range(count)]
    for j in range(0, PLANE, 128):
        at = pl.ds(j, 128)
        for r in range(NODES):
            sums = [sums_ref[k, r, :, at] for k in range(5)]
            for s in range(count):
                sums = add_speed_sums(f_ref[r, :, pl.ds(s * PLANE + j, 128)], speeds[s], sums)
            for k in range(5):
                sums_ref[k, r, :, at] = sums[k]

    @pl.when(step == pl.num_programs(0) - 1)
    def _():
        finish_moments(sums_ref, rows_ref, table_ref, mom_ref)


def total_of(parts):
    while len(parts) > 1:
        parts = [parts[k] + parts[k + 1] for k in range(0, len(parts), 2)]
    return parts[0]


def edge_sums(total, edge_ref):
    net, gross = total[3:4, :], total[13:14, :]
    down, up = 0.5 * (gross - net), 0.5 * (gross + net)
    pairs = ((0, down), (1, up), (1, down))
    return tuple(jnp.sum(edge_ref[k] * row, axis=1, keepdims=True) for k, row in pairs)


def prepare_nodes(total, codes, place, rows_ref, edge_ref, table_ref, node_ref, wall_ref, plane_ref):
    rho, ur, ut, uz, temp, qr, qt, qz = macroscopic_of(lambda k: total[k : k + 1, :])
    inv_t = 1.0 / temp
    beta = ((1.0 - VISCOUS_RATIO) / 5.0) / (rho * temp * temp)
    kappa = rho * (TIME_STEP / KNUDSEN)
    peak = kappa * rho * inv_t * jnp.sqrt(inv_t)
    values = [uz, -0.5 * inv_t, qz * beta, inv_t, peak, 1.0 - kappa, ur, ut, qr * beta, qt * beta]
    clear_sums(table_ref)
    for k, value in enumerate(values):
        table_ref[k : k + 1, :] = value
    table_ref[...] = jnp.transpose(table_ref[...])
    for k in range(len(values)):
        node_ref[k] = jnp.broadcast_to(table_ref[:, k : k + 1], (NODE_COUNT, 128))
    incident, upward, downward = edge_sums(total, edge_ref)
    bottom = jnp.where(codes[0, BOTTOM] == 1, SAT_DENSITY, incident * (1.0 / HALF_FLUX))
    top = jnp.where(codes[0, TOP] == 2, 0.0, upward * (1.0 / HALF_FLUX))
    wall_ref[...] = jnp.broadcast_to(jnp.where(place == 0, bottom, top), (NODES, 128))

    def one_radius(r, carry):
        rows = pl.ds(pl.multiple_of(r * LOCAL_Z, LOCAL_Z), LOCAL_Z)
        n_half, n_inv = node_ref[1, rows, :], node_ref[3, rows, :]
        n_ur, n_ut = node_ref[6, rows, :], node_ref[7, rows, :]
        n_qr, n_qt = node_ref[8, rows, :], node_ref[9, rows, :]
        for j in range(PLANE // 128):
            at = pl.ds(j * 128, 128)
            cr = rows_ref[0:1, at] - n_ur
            ct = rows_ref[1:2, at] - n_ut
            square = cr * cr + ct * ct
            gauss = jnp.exp(square * n_half)
            along = cr * n_qr + ct * n_qt
            plane_ref[0, rows, at] = gauss
            plane_ref[1, rows, at] = along
            plane_ref[2, rows, at] = square * n_inv
        return carry

    lax.fori_loop(0, NODES, one_radius, 0)


def slot_factors(vz, node_ref):
    cz = vz - node_ref[0]
    square = cz * cz
    return node_ref[4] * jnp.exp(square * node_ref[1]), cz * node_ref[2], square * node_ref[3] - 5.0


def ghost_rows(
    speeds, row, place, in_axial_ref, in_near_ref, in_turned_ref, in_far_ref, rows_ref, wall_ref, ghost_ref
):
    count = len(speeds)
    even = lax.rem(row, 2) == 0
    fill = ghost_ref.shape[0] - count * (LOCAL_Z + NODES)
    strengths = [jnp.exp(-0.5 * vz * vz + jnp.zeros((NODES, 128), F32)) * wall_ref[...] for vz in speeds]
    for j in range(PLANE // 128):
        at = pl.ds(j * 128, 128)
        radials, axials = [], []
        for s in range(count):
            if j * 128 < HALF:
                radial = jnp.where(even, in_near_ref[s, :, at], in_far_ref[s, :, at])
            else:
                back = pl.ds(j * 128 - HALF, 128)
                radial = jnp.where(even, in_far_ref[s, :, back], in_near_ref[s, :, back]) + in_turned_ref[s, :, back]
            own = (place == 0) == (speeds[s] > 0)
            radials.append(rows_ref[0:1, at] * radial)
            axials.append(jnp.where(own, strengths[s] * rows_ref[2:3, at], in_axial_ref[s, :, at]))
        zeros = [jnp.zeros((fill, 128), F32)] if fill else []
        ghost_ref[:, at] = jnp.concatenate(radials + axials + zeros, axis=0).astype(BF16)


def outer_kernel(count, part_count, last, order, codes, *refs):
    part_refs, refs = refs[:part_count], refs[part_count:]
    f_ref, in_axial_ref, in_near_ref, in_turned_ref, in_far_ref = refs[:5]
    rows_ref, edge_ref, ghost_r_ref, ghost_z_ref, pos_ref, radial_m_ref, axial_m_ref, rot_ref, out_ref = refs[5:14]
    refs = refs[14:]
    if last:
        (mom_ref, sums_ref), refs = refs[:2], refs[2:]
    plane_ref, node_ref, wall_ref, slot_ref, lift_ref, ghost_ref, table_ref = refs[:7]
    inverse_ref, pad_ref, lhs_ref, work_ref = refs[7:]
    step = pl.program_id(0)
    row, place = places_of()

    @pl.when(step == 0)
    def _():
        if last:
            clear_sums(sums_ref)
        total = total_of([p[...] for p in part_refs])
        prepare_nodes(total, codes, place, rows_ref, edge_ref, table_ref, node_ref, wall_ref, plane_ref)
        pad_ref[:, :, 0:128] = jnp.zeros((count, NODE_COUNT, 128), BF16)
        pad_ref[:, :, 128 + PLANE :] = jnp.zeros((count, NODE_COUNT, 128), BF16)
        inverse_ref[...] = 1.0 / (ELEMENT_WIDTH * (row.astype(F32) + pos_ref[...]))
        minus = radial_m_ref[jnp.where(row == lax.axis_size("row") - 1, 2, 0)]
        for s in range(count):
            lhs_ref[s, 0, :, 0:NODE_COUNT] = minus
            lhs_ref[s, 1, :, 0:NODE_COUNT] = radial_m_ref[1]

    speeds = [slot_speed(order, step * count + s) for s in range(count)]
    for s in range(count):
        vz = speeds[s]
        for k, value in enumerate(slot_factors(vz, node_ref)):
            slot_ref[s, k] = value
        lean = jnp.abs(vz) * ghost_z_ref[jnp.where(vz > 0, 1, 0)]
        lean = pltpu.roll(lean, count * LOCAL_Z + s * NODES, 1)
        for side in range(2):
            lift = ghost_r_ref[side]
            lift_ref[s, side] = ((pltpu.roll(lift, s * LOCAL_Z, 1) if s else lift) + lean).astype(BF16)
    ghost_rows(
        speeds, row, place, in_axial_ref, in_near_ref, in_turned_ref, in_far_ref, rows_ref, wall_ref, ghost_ref
    )

    kind_out = jnp.where(jnp.logical_and(place == 1, codes[0, TOP] == 2), 2, 0)
    inverse = inverse_ref[...]
    for s in range(count):
        axial = (speeds[s] * axial_m_ref[jnp.where(speeds[s] > 0, 1, kind_out)]).astype(BF16)
        lhs_ref[s, 0, :, NODE_COUNT:] = axial
        lhs_ref[s, 1, :, NODE_COUNT:] = axial
        for j in range(PLANE // 128):
            field = nodes_of(f_ref, s * PLANE + j * 128, 128)
            pad_ref[s, :, 128 + j * 128 : 256 + j * 128] = (field * inverse).astype(BF16)

    held = ghost_ref.shape[0]
    lane = lax.broadcasted_iota(jnp.int32, (count * NODE_COUNT, 128), 1)
    for first, lanes, side in PIECES:
        tile = first // TILE
        start = tile * TILE
        inside = first - start
        lifts = lift_ref[:, side].reshape(count * NODE_COUNT, 128)
        window = pad_ref[:, :, start : start + WINDOW].reshape(count * NODE_COUNT, WINDOW)
        window = jnp.concatenate([jnp.where(lane < held, lifts, window[:, 0:128]), window[:, 128:]], axis=1)
        turning = jnp.concatenate(
            [ghost_ref[:, first : first + lanes], rot_ref[tile, held:, inside : inside + lanes]], axis=0
        )
        turned = dot(window, turning)
        vr = rows_ref[0:1, first : first + lanes]
        for s in range(count):
            field = nodes_of(f_ref, s * PLANE + first, lanes)
            both = jnp.concatenate([(field * vr).astype(BF16), field.astype(BF16)], axis=0)
            work_ref[s, :, first : first + lanes] = turned[s * NODE_COUNT : (s + 1) * NODE_COUNT] + dot(
                lhs_ref[s, side], both
            )

    def update(r, carry):
        rows = pl.ds(pl.multiple_of(r * LOCAL_Z, LOCAL_Z), LOCAL_Z)
        keep = node_ref[5, rows, :]
        factor = [[slot_ref[s, k, rows, :] for k in range(3)] for s in range(count)]
        for j in range(PLANE // 128):
            at = pl.ds(j * 128, 128)
            gauss, along, reach = (plane_ref[k, rows, at] for k in range(3))
            if last:
                sums = [sums_ref[k, r, :, at] for k in range(5)]
            for s in range(count):
                here = pl.ds(s * PLANE + j * 128, 128)
                new = f_ref[r, :, here] * keep + work_ref[s, rows, at]
                bend = (along + factor[s][1]) * (reach + factor[s][2]) + 1.0
                new = new + (gauss * factor[s][0]) * bend
                out_ref[r, :, here] = new
                if last:
                    sums = add_speed_sums(new, speeds[s], sums)
            if last:
                for k in range(5):
                    sums_ref[k, r, :, at] = sums[k]
        return carry

    lax.fori_loop(0, NODES, update, 0)
    if last:

        @pl.when(step == pl.num_programs(0) - 1)
        def _():
            finish_moments(sums_ref, rows_ref, table_ref, mom_ref)


def last_kernel(part_count, codes, *refs):
    total_ref = total_of([p[...] for p in refs[:part_count]])
    edge_ref, macro_ref, flux_ref = refs[part_count:]
    row, place = places_of()
    values = macroscopic_of(lambda k: total_ref[k : k + 1, :])
    for k in range(8):
        for r in range(NODES):
            macro_ref[k, r : r + 1, :] = values[k][:, r * LOCAL_Z : (r + 1) * LOCAL_Z]
    incident, upward, downward = edge_sums(total_ref, edge_ref)
    bottom = jnp.where(codes[0, BOTTOM] == 1, SAT_DENSITY * HALF_FLUX - incident, 0.0)
    top = jnp.where(codes[0, TOP] == 2, upward - downward, 0.0)
    square = jnp.broadcast_to(jnp.where(place == 0, bottom, top), (NODES, 128))
    same = lax.broadcasted_iota(jnp.int32, (NODES, 128), 0) == lax.broadcasted_iota(jnp.int32, (NODES, 128), 1)
    flux_ref[...] = jnp.sum(jnp.where(same, square, 0.0), axis=0, keepdims=True)[:, 0:NODES]


def whole(shape):
    return pl.BlockSpec(shape, lambda *a: (0,) * len(shape), pipeline_mode=pl.Buffered(1))


def on_device(distribution, z_order, edge_codes):
    local_r, local_z, vdev = distribution.shape
    assert local_r == NODES and local_z == LOCAL_Z
    slots = vdev // PLANE
    group = math.gcd(slots, 3)
    rows_total = lax.axis_size("row")
    verts = lax.axis_size("vert")
    assert lax.axis_size("gz") == 2 and rows_total % 2 == 0
    codes = edge_codes.T
    fixed = lambda x: pltpu.with_memory_space_constraint(jnp.asarray(x), pltpu.HBM)
    codes, z_order = fixed(codes), fixed(z_order)
    rows, pos, edge = fixed(ROWS), fixed(NODE_POS), fixed(EDGE)
    radial_m, axial_m = fixed(RADIAL_M), fixed(AXIAL_M)
    ghost_r, ghost_z = fixed(GHOST_R), fixed(GHOST_Z)
    trace_m, mirror_m, rot_m = fixed(TRACE_M), fixed(MIRROR_M), jnp.asarray(ROTATION_M)

    def slab(count):
        return pl.BlockSpec((NODES, LOCAL_Z, count * PLANE), lambda i, *n: (0, 0, i))

    def radial_spec(count):
        return pl.BlockSpec((count, LOCAL_Z, HALF), lambda i, *n: (i, 0, 0))

    def axial_spec(count):
        return pl.BlockSpec((count, NODES, PLANE), lambda i, *n: (i, 0, 0))

    def trace_specs(count):
        return [radial_spec(count), radial_spec(count), radial_spec(count), axial_spec(count)]

    mom_spec = whole((MOMENTS, 128))
    radial_shape = jax.ShapeDtypeStruct((slots, LOCAL_Z, HALF), F32)
    axial_shape = jax.ShapeDtypeStruct((slots, NODES, PLANE), F32)
    mom_shape = jax.ShapeDtypeStruct((MOMENTS, 128), F32)
    big_shape = jax.ShapeDtypeStruct(distribution.shape, F32)
    trace_shapes = [radial_shape, radial_shape, radial_shape, axial_shape]
    square = pltpu.VMEM((NODE_COUNT, 128), F32)

    def call(body, name, count, limit, in_specs, out_specs, out_shape, scratch, args):
        return pl.pallas_call(
            body,
            grid_spec=pltpu.PrefetchScalarGridSpec(
                num_scalar_prefetch=2,
                grid=(slots // count,),
                in_specs=in_specs,
                out_specs=out_specs,
                scratch_shapes=scratch,
            ),
            out_shape=out_shape,
            compiler_params=pltpu.CompilerParams(vmem_limit_bytes=limit * 1024 * 1024),
            name=name,
        )(z_order, codes, *args)

    def all_whole(tables):
        return [whole(x.shape) for x in tables]

    def traces_of(f, first):
        if first:
            f = pltpu.with_memory_space_constraint(f, pltpu.HBM)
        return call(
            lambda *a: trace_kernel(group, *a), "traces", group, 20, [slab(group)] + all_whole([trace_m]),
            [radial_spec(group), radial_spec(group), axial_spec(group)], [radial_shape, radial_shape, axial_shape],
            [], [f, trace_m],
        )

    def moments_of(f, left):
        return call(
            lambda *a: moment_kernel(group, *a), "moments", group, 20,
            [slab(group), radial_spec(group)] + all_whole([rows, mirror_m]),
            [mom_spec, radial_spec(group)], [mom_shape, radial_shape],
            [pltpu.VMEM((5, NODES, LOCAL_Z, PLANE), F32), square], [f, left, rows, mirror_m],
        )

    def outer(f, ghosts, parts, last):
        count = group
        if not last:
            f = pltpu.with_memory_space_constraint(f, pltpu.HBM)
        tables = [rows, edge, ghost_r, ghost_z, pos, radial_m, axial_m, rot_m]
        scratch = [
            pltpu.VMEM((3, NODE_COUNT, PLANE), F32),
            pltpu.VMEM((10, NODE_COUNT, 128), F32),
            pltpu.VMEM((NODES, 128), F32),
            pltpu.VMEM((count, 3, NODE_COUNT, 128), F32),
            pltpu.VMEM((count, 2, NODE_COUNT, 128), BF16),
            pltpu.VMEM((-(-count * (LOCAL_Z + NODES) // 16) * 16, PLANE), BF16),
            square,
            square,
            pltpu.VMEM((count, NODE_COUNT, PLANE + 256), BF16),
            pltpu.VMEM((count, 2, NODE_COUNT, 2 * NODE_COUNT), BF16),
            pltpu.VMEM((count, NODE_COUNT, PLANE), F32),
        ]
        return call(
            lambda *a: outer_kernel(count, len(parts), last, *a), "last_update" if last else "update", count, 40 if last else 32,
            [mom_spec] * len(parts) + [slab(count), axial_spec(count)] + [radial_spec(count)] * 3
            + all_whole(tables),
            [slab(count)] + ([mom_spec] if last else []), [big_shape] + ([mom_shape] if last else []),
            ([pltpu.VMEM((5, NODES, LOCAL_Z, PLANE), F32)] if last else []) + scratch,
            [*parts, f, *ghosts, *tables],
        )

    def spread(moments):
        parts = [moments]
        for shift in range(1, verts):
            parts.append(lax.ppermute(moments, "vert", [(i, i ^ shift) for i in range(verts)]))
        return parts

    def halo(near, far, axial):
        from_axial = lax.ppermute(axial, "gz", [(0, 1), (1, 0)])
        pairs = [(i, i ^ 1) for i in range(rows_total)]
        from_near = lax.ppermute(near, "row", pairs)
        between = [(i, i + 1) for i in range(1, rows_total - 1, 2)]
        from_far = lax.ppermute(far, "row", between + [(b, a) for a, b in between])
        return from_axial, from_near, from_far

    current = distribution
    for number in range(STEPS):
        last = number == STEPS - 1
        traces = traces_of(current, number == 0)
        from_axial, from_near, from_far = halo(*traces)
        moments, turned = moments_of(current, traces[1])
        parts = spread(moments)
        ghosts = [from_axial, from_near, turned, from_far]
        current, *final = outer(current, ghosts, parts, last)
    parts = spread(final[0])
    macro, flux = pl.pallas_call(
        lambda *a: last_kernel(len(parts), *a),
        grid_spec=pltpu.PrefetchScalarGridSpec(
            num_scalar_prefetch=1,
            grid=(1,),
            in_specs=[mom_spec] * len(parts) + [whole(edge.shape)],
            out_specs=[whole((8, NODES, LOCAL_Z)), whole((1, NODES))],
        ),
        out_shape=[
            jax.ShapeDtypeStruct((8, NODES, LOCAL_Z), F32),
            jax.ShapeDtypeStruct((1, NODES), F32),
        ],
        compiler_params=pltpu.CompilerParams(vmem_limit_bytes=4 * 1024 * 1024),
        name="macroscopic",
    )(codes, *parts, edge)
    return (current, macro, flux)


def solution(mesh):
    in_specs = (P("row", "gz", "vert"), P("vert"), P(None, "row"))
    out_specs = (P("row", "gz", "vert"), P(None, "row", "gz"), P("gz", "row"))
    return jax.shard_map(
        on_device, mesh=mesh, in_specs=in_specs, out_specs=out_specs, check_vma=False
    )
```
